32 devices in a mesh: section: 2 (over core), tensor: 4 (over y, x), dp: 4 (over z).
Axes of the slice: x: 2, y: 2, z: 4, core: 2. Of those that a mesh axis runs over, the one named last changes fastest.
Arguments:
- inputs: bfloat16 [2, 2048, 1152], P(None, 'dp'), may hold values from -6 to 6
- cotangent: bfloat16 [2, 2048, 1152], P(None, 'dp'), may hold values from -6 to 6
- conditioning: bfloat16 [2, 4, 4, 1152], P(None, 'dp'), may hold values from -6 to 6
- lengths: int32 [2, 4, 4], P(None, 'dp'), may hold values from 1 to 256, 512 in all within a row
- positions: int32 [2, 2, 2048], P(None, None, 'dp'), may hold values from 0 to 63
- modulator: bfloat16 [2, 1152, 6912], P('section', None, 'tensor'), may hold values from -0.1875 to 0.1875
- projections: bfloat16 [2, 3, 1152, 1152], P('section', None, None, 'tensor'), may hold values from -0.1875 to 0.1875
- norm_gains: float32 [2, 2, 72], P('section'), may hold values from 0.1 to 1.9
- out_weight: bfloat16 [2, 1152, 1152], P('section', 'tensor'), may hold values from -1 to 1
- gate_up: bfloat16 [2, 2, 1152, 3072], P('section', None, None, 'tensor'), may hold values from -0.1875 to 0.1875
- down_weight: bfloat16 [2, 3072, 1152], P('section', 'tensor'), may hold values from -0.109375 to 0.109375
Outputs:
- grad_modulator: float32 [2, 1152, 6912], P('section', 'dp', 'tensor')
- grad_projections: float32 [2, 3, 1152, 1152], P('section', None, 'dp', 'tensor')
- grad_norm_gains: float32 [2, 2, 72], P('section')
- grad_out_weight: float32 [2, 1152, 1152], P('section', 'tensor', 'dp')
- grad_gate_up: float32 [2, 2, 1152, 3072], P('section', None, 'dp', 'tensor')
- grad_down_weight: float32 [2, 3072, 1152], P('section', 'tensor', 'dp')
- grad_conditioning: float32 [2, 4, 4, 1152], P(None, 'dp')
- section_results: float32 [2, 2, 2048, 1152], P('section', None, ('dp', 'tensor'))
The draws below stay inside these ranges and needn't reach their ends.
Inputs may be any that keep to these rules, and one draw needn't show every extreme that they name: Each pack's lengths add up to 512; in every pack the largest is exactly 256.
All inputs are finite; a program needn't handle non-finite values.
Results may differ from the reference program's by a relative error of at most 0.019.
Values may be sent and summed in bfloat16 or wider, within the bound.
No kernel may reach another device: no remote copies, remote signals or barrier semaphores. Data moves between devices by JAX's collectives and lax.ppermute only.
A program may use at most 256 MiB of HBM per device.

```python
import math
import jax
import jax.numpy as jnp
import numpy as np
from jax import lax

HEADS = 16
HEAD = 72
FF = 3072
D = 1152
TOK_MB = 512
ITEMS_MB = 4
MICRO = 2
POS = 64
LAYERS = 2
MOST_LEN = 256
TOKENS = 2048
N_DP = 4


def set_ends(values, rng, smallest, top_value):
    longest = values.shape.index(max(values.shape))
    spots = []
    for shift in (0, 1):
        where = [jax.random.randint(jax.random.fold_in(rng, axis), (), 0, length) for axis, length in enumerate(values.shape)]
        where[longest] = (where[longest] + shift) % values.shape[longest]
        spots.append(tuple(where))
    return values.at[spots[0]].set(smallest).at[spots[1]].set(top_value)


def steps_of(stream_key, dims, cuts, low, high):
    level, own = 1.0, jax.random.fold_in(stream_key, 6)
    for position, shards_of in cuts:
        steps = jnp.exp(jax.random.uniform(jax.random.fold_in(own, position), (shards_of,), jnp.float32, low / len(cuts), high / len(cuts)))
        level = level * jnp.repeat(steps, dims[position] // shards_of).reshape([-1 if axis == position else 1 for axis in range(len(dims))])
    return level


def profile(count, total, most, slope):
    loads = [(1 << 20) // math.isqrt(rank ** slope) + 1 for rank in range(2, count + 1)]
    rest, given = total - most - (count - 1), [1] * (count - 1)
    while rest > 0:
        movable = [i for i in range(count - 1) if given[i] < most]
        mass, left = sum([loads[i] for i in movable]), rest
        for i in movable:
            extra = min(most - given[i], max(1, left * loads[i] // mass), rest)
            given[i] = given[i] + extra
            rest = rest - extra
    return np.array([most] + given)


def uneven_parts(key, number_of, total, bound, lean):
    if number_of == 2:
        one = jax.random.randint(key, (), max(1, total - bound), min(bound, total - 1) + 1)
        return jnp.stack([one, total - one])
    sizes = jnp.asarray(profile(number_of, total, bound, lean), jnp.int32)
    twos = (number_of - 1) // 2
    giver, sink = sizes[1:1 + 2 * twos:2], sizes[2:2 + 2 * twos:2]
    slack = jnp.minimum(giver - 1, bound - sink)
    shifted = jax.random.randint(jax.random.fold_in(key, 1), (twos,), 0, 1 << 20) % (slack + 1)
    sizes = sizes.at[1:1 + 2 * twos:2].set(giver - shifted).at[2:2 + 2 * twos:2].set(sink + shifted)
    return sizes[jax.random.permutation(jax.random.fold_in(key, 2), number_of)]


def bell_draw(rng, dims, deviation, most, cuts=(), dtype=jnp.bfloat16):
    result = deviation * jax.random.normal(rng, dims, jnp.float32)
    if cuts:
        result = result * steps_of(rng, dims, cuts, -0.22, 0.18)
    return jnp.clip(result, -most, most).astype(dtype)


def setup_inputs(seed: int = 0) -> dict:
    streams_of = jax.random.split(jax.random.key(seed), 12)
    return {
        "inputs": bell_draw(streams_of[0], (MICRO, TOKENS, D), 1.0, 6.0, ((1, 4),)),
        "cotangent": bell_draw(streams_of[1], (MICRO, TOKENS, D), 1.0, 6.0, ((1, 4),)),
        "conditioning": bell_draw(streams_of[2], (MICRO, N_DP, ITEMS_MB, D), 1.0, 6.0, ((1, 4),)),
        "lengths": jax.vmap(lambda own: uneven_parts(own, ITEMS_MB, TOK_MB, MOST_LEN, 1))(jax.random.split(streams_of[3], MICRO * N_DP)).reshape((MICRO, N_DP, ITEMS_MB)).astype(jnp.int32),
        "positions": set_ends(jax.random.randint(streams_of[4], (MICRO, 2, TOKENS), 0, POS), jax.random.fold_in(streams_of[4], 1), 0, POS - 1).astype(jnp.int32),
        "modulator": bell_draw(streams_of[5], (LAYERS, D, 6 * D), D ** -0.5, 0.1875, ((0, 2), (2, 4))),
        "projections": bell_draw(streams_of[6], (LAYERS, 3, D, D), D ** -0.5, 0.1875, ((0, 2), (3, 4))),
        "norm_gains": jnp.clip(1.0 + 0.18 * jax.random.normal(streams_of[7], (LAYERS, 2, HEAD), jnp.float32), 0.1, 1.9),
        "out_weight": bell_draw(streams_of[8], (LAYERS, D, D), (D // 32) ** -0.5, 1.0, ((0, 2), (1, 4))),
        "gate_up": bell_draw(streams_of[9], (LAYERS, 2, D, FF), D ** -0.5, 0.1875, ((0, 2), (3, 4))),
        "down_weight": bell_draw(streams_of[10], (LAYERS, FF, D), FF ** -0.5, 0.109375, ((0, 2), (1, 4))),
    }


@jax.custom_vjp
def low(v):
    return lax.optimization_barrier(v.astype(jnp.bfloat16)).astype(jnp.float32)

@jax.custom_vjp
def low_back(v):
    return v

def low_keep(v):
    return (low(v), None)

def low_pass(kept, grad):
    return (grad,)

def back_keep(v):
    return (v, None)

def back_low(kept, grad):
    return (low(grad),)
low.defvjp(low_keep, low_pass)
low_back.defvjp(back_keep, back_low)
HIGHEST = lax.Precision.HIGHEST
epsilon = 1e-06

def product(left, right):
    return jnp.dot(left, right, precision=HIGHEST, preferred_element_type=jnp.float32)

def normalize(value):
    return value * lax.rsqrt(lax.optimization_barrier(jnp.mean(value * value, axis=-1, keepdims=True)) + epsilon)

def rotate(value, cosine, sine):
    half = value.shape[-1] // 2
    first = value[..., :half]
    second = value[..., half:]
    return jnp.concatenate([first * cosine - second * sine, first * sine + second * cosine], axis=-1)

def geometry(lens, rows, cols):
    ends = jnp.cumsum(lens).astype(jnp.int32)
    place = jnp.arange(rows.shape[0]).astype(jnp.int32)
    segment = lax.optimization_barrier(jnp.sum((place[:, None] >= ends[None, :]).astype(jnp.int32), axis=1)).astype(jnp.int32)
    labels = jnp.arange(lens.shape[0]).astype(jnp.int32)
    picks = (segment[:, None] == labels[None, :]).astype(jnp.float32)
    same = segment[:, None] == segment[None, :]
    quarter = HEAD // 4
    rates = 10000.0 ** (-jnp.arange(quarter).astype(jnp.float32) / quarter)
    phase = jnp.concatenate([rows.astype(jnp.float32)[:, None] * rates[None, :], cols.astype(jnp.float32)[:, None] * rates[None, :]], axis=1)
    return (picks, same, jnp.cos(phase)[:, None, :], jnp.sin(phase)[:, None, :])

def block(state, tokens_mod, params, shape_info):
    projections, gains, out_weight, gate_up, down_weight = params
    same, cosine, sine = shape_info
    rows = state.shape[0]
    shift1, scale1, gate1, shift2, scale2, gate2 = jnp.split(tokens_mod, 6, axis=1)
    attention_in = low(normalize(state) * (1.0 + scale1) + shift1)
    query_raw = low_back(product(attention_in, projections[0])).reshape(rows, HEADS, HEAD)
    key_raw = low_back(product(attention_in, projections[1])).reshape(rows, HEADS, HEAD)
    value = low(low_back(product(attention_in, projections[2]))).reshape(rows, HEADS, HEAD)
    query = low(rotate(normalize(query_raw) * gains[0], cosine, sine))
    key = low(rotate(normalize(key_raw) * gains[1], cosine, sine))
    scores = low_back(jnp.einsum('thd,shd->hts', query, key, precision=HIGHEST) * HEAD ** (-0.5))
    scores = jnp.where(same[None], scores, -1e+30)
    weights = low(jax.nn.softmax(scores, axis=-1))
    mixed = jnp.einsum('hts,shd->thd', weights, value, precision=HIGHEST).reshape(rows, HEADS * HEAD)
    mixed = low(low_back(mixed))
    attended = low_back(product(mixed, out_weight))
    after = state + gate1 * attended
    mlp_in = low(normalize(after) * (1.0 + scale2) + shift2)
    gate = low_back(product(mlp_in, gate_up[0]))
    upward = low_back(product(mlp_in, gate_up[1]))
    hidden = low(jax.nn.silu(gate) * upward)
    return after + gate2 * low_back(product(hidden, down_weight))

def pack_forward(weights, state, cond, lens, posn):
    picks, same, cosine, sine = geometry(lens, posn[0], posn[1])
    scaled = low(jax.nn.silu(cond))
    for layer in range(LAYERS):
        modulation = low(low_back(product(scaled, weights[0][layer])))
        tokens_mod = product(picks, modulation)
        params = tuple((matrix[layer] for matrix in weights[1:]))
        state = block(state, tokens_mod, params, (same, cosine, sine))
        if layer + 1 < LAYERS:
            state = low(low_back(state))
    return state

def reference(inputs, cotangent, conditioning, lengths, positions, modulator, projections, norm_gains, out_weight, gate_up, down_weight):
    packs = MICRO * N_DP
    states = inputs.astype(jnp.float32).reshape(packs, TOK_MB, D)
    grads_out = cotangent.astype(jnp.float32).reshape(packs, TOK_MB, D)
    conds = conditioning.astype(jnp.float32).reshape(packs, ITEMS_MB, D)
    lens = lengths.reshape(packs, ITEMS_MB)
    posn = positions.reshape(MICRO, 2, N_DP, TOK_MB).transpose(0, 2, 1, 3).reshape(packs, 2, TOK_MB)
    weights = tuple((matrix.astype(jnp.float32) for matrix in (modulator, projections, norm_gains, out_weight, gate_up, down_weight)))

    def whole(weights, states, conds):
        stepper = jax.checkpoint(pack_forward)
        return lax.map(lambda members: stepper(weights, *members), (states, conds, lens, posn))
    outputs, pullback = jax.vjp(whole, weights, states, conds)
    grad_weights, grad_states, grad_conds = pullback(grads_out)
    results = jnp.stack([grad_states.reshape(MICRO, TOKENS, D), outputs.reshape(MICRO, TOKENS, D)])
    return (grad_weights[0], grad_weights[1], grad_weights[2], grad_weights[3], grad_weights[4], grad_weights[5], grad_conds.reshape(MICRO, N_DP, ITEMS_MB, D), results)
```

```python
import functools

import jax
import jax.numpy as jnp
from jax import lax
from jax.experimental import pallas as pl
from jax.experimental.pallas import tpu as pltpu
from jax.sharding import PartitionSpec as P
import numpy as np

HEAD = 72
HALF = HEAD // 2
LANE = 128
epsilon = 1e-06
BF = jnp.bfloat16
F32 = jnp.float32
HIGHEST = lax.Precision.HIGHEST
VM = pl.BlockSpec(memory_space=pltpu.VMEM)
SM = pl.BlockSpec(memory_space=pltpu.SMEM)
ANY = pl.BlockSpec(memory_space=pl.ANY)


def nn(a, b):
    return lax.dot_general(a, b, (((1,), (0,)), ((), ())), preferred_element_type=F32)


def nt(a, b):
    return lax.dot_general(a, b, (((1,), (1,)), ((), ())), preferred_element_type=F32)


def tn(a, b):
    return lax.dot_general(a, b, (((0,), (0,)), ((), ())), preferred_element_type=F32)


def call(body, outs, in_specs, scratch=(), flops=0, size=0, name=None):
    return pl.pallas_call(
        body,
        out_shape=outs,
        in_specs=in_specs,
        out_specs=jax.tree.map(lambda _: VM, outs),
        scratch_shapes=list(scratch),
        compiler_params=pltpu.CompilerParams(vmem_limit_bytes=50 * 2**20),
        cost_estimate=pl.CostEstimate(flops=flops, bytes_accessed=size, transcendentals=0),
        name=name,
    )


def shape(dims, dtype):
    return jax.ShapeDtypeStruct(dims, dtype)


def fetch(is_own, own, other, where, sem):
    @pl.when(is_own)
    def _():
        pltpu.make_async_copy(own, where, sem).start()

    @pl.when(jnp.logical_not(is_own))
    def _():
        pltpu.make_async_copy(other, where, sem).start()


def arrived(own, where, sem):
    pltpu.make_async_copy(own, where, sem).wait()


def inverse_rms(value):
    return lax.rsqrt(jnp.mean(value * value, axis=-1, keepdims=True) + epsilon)


def norm_back(grad, normed, inverse):
    return inverse * (grad - normed * jnp.mean(grad * normed, axis=-1, keepdims=True))


def token_mod(picks, mods_ref, part):
    width = mods_ref.shape[1] // 6
    return nn(picks, mods_ref[:, part * width : (part + 1) * width])


def image_sums(picks, value):
    return lax.dot_general(
        picks.astype(F32),
        value,
        (((0,), (0,)), ((), ())),
        precision=HIGHEST,
        preferred_element_type=F32,
    )


def swap_halves(value):
    return pltpu.roll(value, LANE // 2, 1)


def rotate(value, cosine, sine):
    return value * cosine + swap_halves(value) * sine


def unrotate(grad, cosine, sine):
    return grad * cosine - swap_halves(grad) * sine


def head_inverse(raw):
    return lax.rsqrt(jnp.sum(raw * raw, axis=-1, keepdims=True) * (1.0 / HEAD) + epsilon)


def split_store(value, rows, block_refs):
    own = block_refs[0]
    share = own.shape[0]
    for k, ref in enumerate(block_refs):
        ref[:, rows] = value[k * share : (k + 1) * share].astype(ref.dtype)


def attention_forward(layer, blocks, weights, tables, mods, picks, section):
    (wq_own, wq_got, wo_own, wo_got) = weights
    cosine, sine, gains, seg_col, seg_row = tables
    width = wo_own.shape[1]
    padded = wo_own.shape[0]
    heads = padded // LANE
    raw_input = len(blocks) == 1
    rows = sum(b.shape[0] for b in blocks)
    share = rows // 4
    scale = HEAD**-0.5

    def body(sec_ref, *refs):
        refs = list(refs)
        in_refs = [refs.pop(0) for _ in blocks]
        wq_a, wq_b, wo_a, wo_b, cos_ref, sin_ref, gain_ref, segc_ref, segr_ref, mods_ref, picks_ref = refs[:11]
        refs = refs[11:]
        p_refs = refs[:4]
        qraw_ref, kraw_ref, qrot_ref, krot_ref, v_ref, mixed_ref, a_ref = refs[4:11]
        wq_ref, wo_ref, sems = refs[11:]
        own = sec_ref[0] == layer
        for i in range(3):
            fetch(own, wq_a.at[i], wq_b.at[i], wq_ref.at[i], sems.at[i])
        fetch(own, wo_a, wo_b, wo_ref, sems.at[3])
        for k, ref in enumerate(in_refs):
            if raw_input:
                x = ref[...].astype(F32)
                picked = picks_ref[...]
                shift1 = token_mod(picked, mods_ref, 0)
                scale1 = token_mod(picked, mods_ref, 1)
                a_ref[...] = (x * inverse_rms(x) * (1.0 + scale1) + shift1).astype(BF)
            else:
                a_ref[k * share : (k + 1) * share] = ref[...]
        cos = cos_ref[...]
        sin = sin_ref[...]
        for i, (raw_out, rot_out) in enumerate(((qraw_ref, qrot_ref), (kraw_ref, krot_ref))):
            arrived(wq_a.at[i], wq_ref.at[i], sems.at[i])
            gain = gain_ref[i : i + 1]
            for h in range(heads):
                at = slice(h * LANE, (h + 1) * LANE)
                raw = nn(a_ref[...], wq_ref[i, :, at])
                raw_out[:, at] = raw
                turned = rotate(raw * head_inverse(raw) * gain, cos, sin)
                rot_out[:, at] = turned.astype(BF)
        arrived(wq_a.at[2], wq_ref.at[2], sems.at[2])
        v_ref[...] = nn(a_ref[...], wq_ref[2]).astype(BF)

        def query_block(j, carry):
            at_rows = pl.ds(pl.multiple_of(j * LANE, LANE), LANE)
            same = segc_ref[at_rows] == segr_ref[...]
            for h in range(heads):
                at = slice(h * LANE, (h + 1) * LANE)
                scores = nt(qrot_ref[at_rows, at], krot_ref[:, at]) * scale
                grown = jnp.where(same, jnp.exp(scores), 0.0)
                total = jnp.sum(grown, axis=-1, keepdims=True)
                weights_low = (grown * (1.0 / total)).astype(BF)
                mixed_ref[at_rows, at] = nn(weights_low, v_ref[:, at]).astype(BF)
            return carry

        lax.fori_loop(0, rows // LANE, query_block, 0)
        arrived(wo_a, wo_ref, sems.at[3])
        step = 3 * LANE

        def out_block(j, carry):
            at = pl.ds(pl.multiple_of(j * step, LANE), step)
            split_store(nn(mixed_ref[...], wo_ref[:, at]), at, p_refs)
            return carry

        lax.fori_loop(0, width // step, out_block, 0)

    outs = [shape((share, width), F32)] + [shape((share, width), BF)] * 3
    outs += [shape((rows, padded), F32)] * 2 + [shape((rows, padded), BF)] * 4
    outs += [shape((rows, width), BF)]
    result = call(
        body,
        outs,
        [SM] + [VM] * len(blocks) + [ANY] * 4 + [VM] * 7,
        [
            pltpu.VMEM((3, width, padded), BF),
            pltpu.VMEM((padded, width), BF),
            pltpu.SemaphoreType.DMA((4,)),
        ],
        flops=2 * rows * width * padded * 4 + 4 * rows * rows * padded,
        size=12 * 2**20,
        name=f"attention_forward_{layer}",
    )(section, *blocks, wq_own, wq_got, wo_own, wo_got, cosine, sine, gains, seg_col, seg_row, mods, picks)
    partial, saved = result[:4], result[4:]
    return partial, saved


def after_attention(parts, state, mods, picks):
    def body(p0, p1, p2, p3, state_ref, mods_ref, picks_ref, attended_ref, after_ref, mlp_ref):
        picked = picks_ref[...]
        attended = p0[...] + p1[...].astype(F32) + p2[...].astype(F32) + p3[...].astype(F32)
        attended_ref[...] = attended
        after = state_ref[...].astype(F32) + token_mod(picked, mods_ref, 2) * attended
        after_ref[...] = after
        normed = after * inverse_rms(after)
        mlp_ref[...] = (normed * (1.0 + token_mod(picked, mods_ref, 4)) + token_mod(picked, mods_ref, 3)).astype(BF)

    dims = state.shape
    return call(
        body,
        [shape(dims, F32), shape(dims, F32), shape(dims, BF)],
        [VM] * 7,
        flops=20 * dims[0] * dims[1],
        size=12 * dims[0] * dims[1],
        name="after_attention",
    )(*parts, state, mods, picks)


def after_mlp(parts, after, mods, picks, mods_next):
    last = mods_next is None

    def body(p0, p1, p2, p3, after_ref, mods_ref, picks_ref, *refs):
        picked = picks_ref[...]
        projected = p0[...] + p1[...].astype(F32) + p2[...].astype(F32) + p3[...].astype(F32)
        output = after_ref[...] + token_mod(picked, mods_ref, 5) * projected
        if last:
            projected_ref, output_ref = refs
            output_ref[...] = output
        else:
            next_ref, projected_ref, state_ref, in_ref = refs
            low = output.astype(BF)
            state_ref[...] = low
            state = low.astype(F32)
            normed = state * inverse_rms(state)
            in_ref[...] = (normed * (1.0 + token_mod(picked, next_ref, 1)) + token_mod(picked, next_ref, 0)).astype(BF)
        projected_ref[...] = projected

    dims = after.shape
    outs = [shape(dims, F32)] + ([shape(dims, F32)] if last else [shape(dims, BF)] * 2)
    extra = () if last else (mods_next,)
    return call(
        body,
        outs,
        [VM] * (7 + len(extra)),
        flops=20 * dims[0] * dims[1],
        size=12 * dims[0] * dims[1],
        name="after_mlp",
    )(*parts, after, mods, picks, *extra)


def mlp_forward(layer, blocks, weights, section):
    gu_own, gu_got, wd_own, wd_got = weights
    hidden_size, width = wd_own.shape
    share = blocks[0].shape[0]
    rows = share * 4
    chunk = 2 * LANE

    def body(sec_ref, b0, b1, b2, b3, gu_a, gu_b, wd_a, wd_b, p0, p1, p2, p3, hid_ref, c1_ref, c2_ref, a_ref, gu_ref, wd_ref, sems):
        own = sec_ref[0] == layer
        fetch(own, gu_a.at[0], gu_b.at[0], gu_ref.at[0], sems.at[0])
        fetch(own, gu_a.at[1], gu_b.at[1], gu_ref.at[1], sems.at[1])
        fetch(own, wd_a, wd_b, wd_ref, sems.at[2])
        for k, ref in enumerate((b0, b1, b2, b3)):
            a_ref[k * share : (k + 1) * share] = ref[...]
        arrived(gu_a.at[0], gu_ref.at[0], sems.at[0])
        arrived(gu_a.at[1], gu_ref.at[1], sems.at[1])

        def hidden_block(j, carry):
            at = pl.ds(pl.multiple_of(j * chunk, LANE), chunk)
            gate = nn(a_ref[...], gu_ref[0, :, at])
            up = nn(a_ref[...], gu_ref[1, :, at])
            sigma = jax.nn.sigmoid(gate)
            silu = gate * sigma
            hid_ref[:, at] = (silu * up).astype(BF)
            c1_ref[:, at] = (up * (sigma + silu * (1.0 - sigma))).astype(BF)
            c2_ref[:, at] = silu.astype(BF)
            return carry

        lax.fori_loop(0, hidden_size // chunk, hidden_block, 0)
        arrived(wd_a, wd_ref, sems.at[2])
        step = 3 * LANE

        def out_block(j, carry):
            at = pl.ds(pl.multiple_of(j * step, LANE), step)
            split_store(nn(hid_ref[...], wd_ref[:, at]), at, (p0, p1, p2, p3))
            return carry

        lax.fori_loop(0, width // step, out_block, 0)

    outs = [shape((share, width), F32)] + [shape((share, width), BF)] * 3 + [shape((rows, hidden_size), BF)] * 3
    result = call(
        body,
        outs,
        [SM] + [VM] * 4 + [ANY] * 4,
        [
            pltpu.VMEM((rows, width), BF),
            pltpu.VMEM(gu_own.shape, BF),
            pltpu.VMEM(wd_own.shape, BF),
            pltpu.SemaphoreType.DMA((3,)),
        ],
        flops=6 * rows * width * hidden_size,
        size=10 * 2**20,
        name=f"mlp_forward_{layer}",
    )(section, *blocks, gu_own, gu_got, wd_own, wd_got)
    return result[:4], result[4:]


def mlp_backward(layer, blocks, weights, saved, mods, picks, section):
    gu_own, gu_got, wd_own, wd_got = weights
    hidden, c1, c2 = saved
    hidden_size, width = wd_own.shape
    rows = hidden.shape[0]
    share = rows // 4
    raw_input = len(blocks) == 1
    chunk = 2 * LANE

    def body(sec_ref, *refs):
        refs = list(refs)
        in_refs = [refs.pop(0) for _ in blocks]
        gu_a, gu_b, wd_a, wd_b, c1_ref, c2_ref, mods_ref, picks_ref = refs[:8]
        p_refs = refs[8:12]
        gg_ref, gup_ref, gp_ref = refs[12:15]
        gu_ref, wd_ref, sems = refs[15:]
        own = sec_ref[0] == layer
        fetch(own, wd_a, wd_b, wd_ref, sems.at[2])
        fetch(own, gu_a.at[0], gu_b.at[0], gu_ref.at[0], sems.at[0])
        fetch(own, gu_a.at[1], gu_b.at[1], gu_ref.at[1], sems.at[1])
        for k, ref in enumerate(in_refs):
            if raw_input:
                gp_ref[...] = (ref[...].astype(F32) * token_mod(picks_ref[...], mods_ref, 5)).astype(BF)
            else:
                gp_ref[k * share : (k + 1) * share] = ref[...]
        arrived(wd_a, wd_ref, sems.at[2])

        def hidden_block(j, carry):
            at = pl.ds(pl.multiple_of(j * chunk, LANE), chunk)
            grad_hidden = nt(gp_ref[...], wd_ref[at])
            gg_ref[:, at] = (grad_hidden * c1_ref[:, at].astype(F32)).astype(BF)
            gup_ref[:, at] = (grad_hidden * c2_ref[:, at].astype(F32)).astype(BF)
            return carry

        lax.fori_loop(0, hidden_size // chunk, hidden_block, 0)
        arrived(gu_a.at[0], gu_ref.at[0], sems.at[0])
        arrived(gu_a.at[1], gu_ref.at[1], sems.at[1])
        step = 3 * LANE

        def out_block(j, carry):
            at = pl.ds(pl.multiple_of(j * step, LANE), step)
            split_store(nt(gg_ref[...], gu_ref[0, at]) + nt(gup_ref[...], gu_ref[1, at]), at, p_refs)
            return carry

        lax.fori_loop(0, width // step, out_block, 0)

    outs = [shape((share, width), F32)] + [shape((share, width), BF)] * 3 + [shape((rows, hidden_size), BF)] * 2
    outs += [shape((rows, width), BF)]
    result = call(
        body,
        outs,
        [SM] + [VM] * len(blocks) + [ANY] * 4 + [VM] * 4,
        [
            pltpu.VMEM(gu_own.shape, BF),
            pltpu.VMEM(wd_own.shape, BF),
            pltpu.SemaphoreType.DMA((3,)),
        ],
        flops=6 * rows * width * hidden_size,
        size=10 * 2**20,
        name=f"mlp_backward_{layer}",
    )(section, *blocks, gu_own, gu_got, wd_own, wd_got, c1, c2, mods, picks)
    return result[:4], result[4:]


def mlp_weight_grads(mlp_blocks, grads, hidden, section):
    grad_gate, grad_up, grad_projected = grads
    rows, width = grad_projected.shape
    size = hidden.shape[1]
    share = rows // 4
    half = 3 * size // 2
    step = 3 * LANE

    def body(sec_ref, b0, b1, b2, b3, gg_ref, gu_ref, gp_ref, hid_ref, keep_ref, send_ref, a_ref):
        for k, ref in enumerate((b0, b1, b2, b3)):
            a_ref[k * share : (k + 1) * share] = ref[...]

        def row_block(j, carry):
            at = pl.ds(pl.multiple_of(j * step, LANE), step)
            left = a_ref[:, at]
            first = tn(left, gg_ref[...]).astype(BF)
            middle = tn(left, gu_ref[...]).astype(BF)
            last = tn(gp_ref[:, at], hid_ref[...]).astype(BF)

            def put(low_ref, high_ref):
                low_ref[at, :size] = first
                low_ref[at, size:] = middle[:, : half - size]
                high_ref[at, : half - size] = middle[:, half - size :]
                high_ref[at, half - size :] = last

            @pl.when(sec_ref[0] == 0)
            def _():
                put(keep_ref, send_ref)

            @pl.when(sec_ref[0] != 0)
            def _():
                put(send_ref, keep_ref)

            return carry

        lax.fori_loop(0, width // step, row_block, 0)

    return call(
        body,
        [shape((width, half), BF)] * 2,
        [SM] + [VM] * 8,
        [pltpu.VMEM((rows, width), BF)],
        flops=6 * rows * width * size,
        size=10 * 2**20,
        name="mlp_weight_grads",
    )(section, *mlp_blocks, grad_gate, grad_up, grad_projected, hidden)


def attention_backward(layer, blocks, weights, saved, tables, selects, section):
    wq_own, wq_got, wo_own, wo_got = weights
    q_raw, k_raw, q_rot, k_rot, values, mixed = saved
    cosine, sine, gains, seg_col, seg_row = tables
    pick_qk, pick_v = selects
    rows, padded = q_raw.shape
    width = wo_own.shape[1]
    heads = padded // LANE
    share = rows // 4
    narrow = pick_v.shape[1]
    scale = HEAD**-0.5

    def body(sec_ref, b0, b1, b2, b3, wq_a, wq_b, wo_a, wo_b, qraw_ref, kraw_ref, qrot_ref, krot_ref, v_ref, mixed_ref,
             cos_ref, sin_ref, gain_ref, segc_ref, segr_ref, selqk_ref, selv_ref,
             p0, p1, p2, p3, gqk_out, gv_out, mixed_out, ga_out, ggain_ref,
             wq_ref, wo_ref, gmix_ref, gq_ref, gk_ref, g_ref, gv_ref, sems):
        own = sec_ref[0] == layer
        fetch(own, wo_a, wo_b, wo_ref, sems.at[3])
        for i in range(3):
            fetch(own, wq_a.at[i], wq_b.at[i], wq_ref.at[i], sems.at[i])
        for k, ref in enumerate((b0, b1, b2, b3)):
            ga_out[k * share : (k + 1) * share] = ref[...]
        arrived(wo_a, wo_ref, sems.at[3])
        gmix_ref[...] = nt(ga_out[...], wo_ref[...]).astype(BF)
        gk_ref[...] = jnp.zeros_like(gk_ref)
        gv_ref[...] = jnp.zeros_like(gv_ref)

        def query_block(j, carry):
            at_rows = pl.ds(pl.multiple_of(j * LANE, LANE), LANE)
            same = segc_ref[...] == segr_ref[:, at_rows]
            for h in range(heads):
                at = slice(h * LANE, (h + 1) * LANE)
                query = qrot_ref[at_rows, at]
                grad_mixed = gmix_ref[at_rows, at]
                scores = nt(krot_ref[:, at], query) * scale
                grown = jnp.where(same, jnp.exp(scores), 0.0)
                weights_t = grown * (1.0 / jnp.sum(grown, axis=0, keepdims=True))
                grad_weights = nt(v_ref[:, at], grad_mixed)
                gv_ref[:, at] += nn(weights_t.astype(BF), grad_mixed)
                product = weights_t * grad_weights
                delta = jnp.sum(product, axis=0, keepdims=True)
                grad_scores = (product - weights_t * delta).astype(BF)
                gq_ref[at_rows, at] = tn(grad_scores, krot_ref[:, at])
                gk_ref[:, at] += nn(grad_scores, query)
            return carry

        lax.fori_loop(0, rows // LANE, query_block, 0)
        cos = cos_ref[...]
        sin = sin_ref[...]
        ggain_ref[...] = jnp.zeros_like(ggain_ref)
        for i, (raw_ref, grad_ref) in enumerate(((qraw_ref, gq_ref), (kraw_ref, gk_ref))):
            gain = gain_ref[i : i + 1]
            gain_sum = jnp.zeros((1, LANE), F32)
            for h in range(heads):
                at = slice(h * LANE, (h + 1) * LANE)
                raw = raw_ref[:, at]
                inverse = head_inverse(raw)
                normed = raw * inverse
                turned = unrotate(grad_ref[:, at], cos, sin) * scale
                gain_sum += jnp.sum(turned * normed, axis=0, keepdims=True)
                d = turned * gain
                back = inverse * (d - normed * (jnp.sum(d * normed, axis=-1, keepdims=True) * (1.0 / HEAD)))
                g_ref[:, i * padded + h * LANE : i * padded + (h + 1) * LANE] = back.astype(BF)
            ggain_ref[i : i + 1] = gain_sum
        g_ref[:, 2 * padded :] = gv_ref[...].astype(BF)
        for i in range(3):
            arrived(wq_a.at[i], wq_ref.at[i], sems.at[i])
        step = 3 * LANE

        def out_block(j, carry):
            at = pl.ds(pl.multiple_of(j * step, LANE), step)
            total = nt(g_ref[:, :padded], wq_ref[0, at])
            total += nt(g_ref[:, padded : 2 * padded], wq_ref[1, at])
            total += nt(g_ref[:, 2 * padded :], wq_ref[2, at])
            split_store(total, at, (p0, p1, p2, p3))
            return carry

        lax.fori_loop(0, width // step, out_block, 0)
        gqk_out[...] = nn(g_ref[:, : 2 * padded], selqk_ref[...]).astype(BF)
        gv_out[...] = nn(g_ref[:, 2 * padded :], selv_ref[...]).astype(BF)
        mixed_out[...] = nn(mixed_ref[...], selv_ref[...]).astype(BF)

    outs = [shape((share, width), F32)] + [shape((share, width), BF)] * 3
    outs += [shape((rows, 2 * narrow), BF), shape((rows, narrow), BF), shape((rows, narrow), BF)]
    outs += [shape((rows, width), BF), shape((8, LANE), F32)]
    result = call(
        body,
        outs,
        [SM] + [VM] * 4 + [ANY] * 4 + [VM] * 13,
        [
            pltpu.VMEM((3, width, padded), BF),
            pltpu.VMEM((padded, width), BF),
            pltpu.VMEM((rows, padded), BF),
            pltpu.VMEM((rows, padded), F32),
            pltpu.VMEM((rows, padded), F32),
            pltpu.VMEM((rows, 3 * padded), BF),
            pltpu.VMEM((rows, padded), F32),
            pltpu.SemaphoreType.DMA((4,)),
        ],
        flops=2 * rows * width * padded * 4 + 10 * rows * rows * padded,
        size=14 * 2**20,
        name=f"attention_backward_{layer}",
    )(section, *blocks, wq_own, wq_got, wo_own, wo_got, q_raw, k_raw, q_rot, k_rot, values, mixed,
      cosine, sine, gains, seg_col, seg_row, pick_qk, pick_v)
    return result[:4], result[4:]


def attention_weight_grads(attention_in, grads, section):
    gqk, gv, mixed, grad_attended = grads
    rows, width = attention_in.shape
    narrow = gv.shape[1]
    step = 3 * LANE

    def body(sec_ref, a_ref, gqk_ref, gv_ref, mixed_ref, ga_ref, keep_ref, send_ref):
        def row_block(j, carry):
            at = pl.ds(pl.multiple_of(j * step, LANE), step)
            left = a_ref[:, at]
            first = tn(left, gqk_ref[...]).astype(BF)
            second = tn(left, gv_ref[...]).astype(BF)
            third = tn(ga_ref[:, at], mixed_ref[...]).astype(BF)

            def put(low_ref, high_ref):
                low_ref[at] = first
                high_ref[at] = jnp.concatenate([second, third], axis=1)

            @pl.when(sec_ref[0] == 0)
            def _():
                put(keep_ref, send_ref)

            @pl.when(sec_ref[0] != 0)
            def _():
                put(send_ref, keep_ref)

            return carry

        lax.fori_loop(0, width // step, row_block, 0)

    return call(
        body,
        [shape((width, 2 * narrow), BF)] * 2,
        [SM] + [VM] * 5,
        flops=8 * rows * width * narrow,
        size=6 * 2**20,
        name="attention_weight_grads",
    )(section, attention_in, gqk, gv, mixed, grad_attended)


def back_of_mlp(parts, grad_out, after, attended, projected, mods, picks):
    def body(p0, p1, p2, p3, g_ref, after_ref, attended_ref, projected_ref, mods_ref, picks_ref, ga_ref, grad_ref, sums_ref):
        picked = picks_ref[...]
        g = g_ref[...].astype(F32)
        grad_in = p0[...] + p1[...].astype(F32) + p2[...].astype(F32) + p3[...].astype(F32)
        after = after_ref[...]
        inverse = inverse_rms(after)
        normed = after * inverse
        grad_after = g + norm_back(grad_in * (1.0 + token_mod(picked, mods_ref, 4)), normed, inverse)
        grad_ref[...] = grad_after
        ga_ref[...] = (grad_after * token_mod(picked, mods_ref, 2)).astype(BF)
        sums_ref[0] = image_sums(picked, grad_after * attended_ref[...])
        sums_ref[1] = image_sums(picked, grad_in)
        sums_ref[2] = image_sums(picked, grad_in * normed)
        sums_ref[3] = image_sums(picked, g * projected_ref[...])

    dims = after.shape
    return call(
        body,
        [shape(dims, BF), shape(dims, F32), shape((4, picks.shape[1], dims[1]), F32)],
        [VM] * 10,
        flops=40 * dims[0] * dims[1],
        size=24 * dims[0] * dims[1],
        name="back_of_mlp",
    )(*parts, grad_out, after, attended, projected, mods, picks)


def back_of_attention(parts, grad_after, state, mods, picks, mods_below):
    first = mods_below is None

    def body(p0, p1, p2, p3, grad_ref, state_ref, mods_ref, picks_ref, *refs):
        picked = picks_ref[...]
        grad_in = p0[...] + p1[...].astype(F32) + p2[...].astype(F32) + p3[...].astype(F32)
        state = state_ref[...].astype(F32)
        inverse = inverse_rms(state)
        normed = state * inverse
        grad_state = grad_ref[...] + norm_back(grad_in * (1.0 + token_mod(picked, mods_ref, 1)), normed, inverse)
        if first:
            sums_ref, out_ref = refs
            out_ref[...] = grad_state
        else:
            below_ref, sums_ref, low_ref, gp_ref = refs
            low = grad_state.astype(BF)
            low_ref[...] = low
            gp_ref[...] = (low.astype(F32) * token_mod(picked, below_ref, 5)).astype(BF)
        sums_ref[0] = image_sums(picked, grad_in)
        sums_ref[1] = image_sums(picked, grad_in * normed)

    dims = grad_after.shape
    outs = [shape((2, picks.shape[1], dims[1]), F32)] + ([shape(dims, F32)] if first else [shape(dims, BF)] * 2)
    extra = () if first else (mods_below,)
    return call(
        body,
        outs,
        [VM] * (8 + len(extra)),
        flops=40 * dims[0] * dims[1],
        size=16 * dims[0] * dims[1],
        name="back_of_attention",
    )(*parts, grad_after, state, mods, picks, *extra)


def exchange(value, axis, k):
    return lax.ppermute(value, axis, [(i, i ^ k) for i in range(lax.axis_size(axis))])


def send_parts(parts):
    got = {k: exchange(parts[k], "tensor", k) for k in (3, 1, 2)}
    return [parts[0], got[1], got[2], got[3]]


def gather_blocks(own):
    got = {k: exchange(own, "tensor", k) for k in (3, 1, 2)}
    return [own, got[1], got[2], got[3]]


def group_sum(value, axis):
    k = 1
    while k < lax.axis_size(axis):
        value = value + exchange(value, axis, k)
        k *= 2
    return value


def gather_dp(value):
    count = lax.axis_size("dp")
    if count > 4:
        return lax.all_gather(value, "dp", axis=0)
    me = lax.axis_index("dp")
    got = [value] + [exchange(value, "dp", k) for k in range(1, count)]
    stacked = jnp.stack(got)
    return jnp.stack([lax.dynamic_index_in_dim(stacked, me ^ j, 0, keepdims=False) for j in range(count)])


def head_places(heads):
    place = np.zeros((heads * HEAD, heads * LANE), np.float32)
    for h in range(heads):
        for j in range(HEAD):
            place[h * HEAD + j, h * LANE + (j // HALF) * (LANE // 2) + j % HALF] = 1.0
    return place


def shards(
    inputs,
    cotangent,
    conditioning,
    lengths,
    positions,
    modulator,
    projections,
    norm_gains,
    out_weight,
    gate_up,
    down_weight,
):
    section = lax.axis_index("section")
    other = 1 - section
    tensor = lax.axis_index("tensor")
    data = lax.axis_index("dp")
    micro, rows, width = inputs.shape
    group = lax.axis_size("tensor")
    share = rows // group
    items = lengths.shape[2]
    narrow = projections.shape[3]
    heads = narrow // HEAD
    padded = heads * LANE
    columns = modulator.shape[2]
    sec = section.reshape(1).astype(jnp.int32)

    cond_value = conditioning[:, 0].astype(F32)
    scaled = jax.nn.silu(cond_value).astype(BF)
    part = jnp.einsum("mid,dc->mic", scaled, modulator[0], preferred_element_type=F32).astype(BF)
    mine = lax.dynamic_index_in_dim(part, section, 0, keepdims=False)
    theirs = exchange(lax.dynamic_index_in_dim(part, other, 0, keepdims=False), "section", 1)
    is_first = section == 0
    both = jnp.stack([jnp.where(is_first, mine, theirs), jnp.where(is_first, theirs, mine)])
    pieces = jnp.stack(gather_blocks(both))
    ordered = [lax.dynamic_index_in_dim(pieces, tensor ^ j, 0, keepdims=False) for j in range(group)]
    mods_all = jnp.concatenate(ordered, axis=2)
    mods_all = jnp.pad(mods_all, ((0, 0), (0, 8 - items), (0, 0)))
    mods = [mods_all[0], mods_all[1]]

    place = jnp.asarray(head_places(heads), BF)
    wq_own = jnp.einsum("kde,ec->kdc", projections[0], place, preferred_element_type=F32).astype(BF)
    wo_own = jnp.einsum("ec,ed->cd", place, out_weight[0], preferred_element_type=F32).astype(BF)
    wq_got = exchange(wq_own, "section", 1)
    wo_got = exchange(wo_own, "section", 1)
    gu_got = exchange(gate_up[0], "section", 1)
    wd_got = exchange(down_weight[0], "section", 1)
    attention_weights = (wq_own, wq_got, wo_own, wo_got)
    mlp_weights = (gate_up[0], gu_got, down_weight[0], wd_got)
    select_v = place.T
    zero = jnp.zeros_like(select_v)
    select_qk = jnp.concatenate(
        [jnp.concatenate([select_v, zero], axis=1), jnp.concatenate([zero, select_v], axis=1)], axis=0
    )
    selects = (select_qk, select_v)

    def local(value):
        return jnp.concatenate(
            [
                lax.dynamic_slice_in_dim(value, (tensor ^ k) * share, share, 0)
                for k in range(group)
            ],
            axis=0,
        )

    def of_micro(value):
        return lax.dynamic_index_in_dim(value, section, 0, keepdims=False)

    ends = jnp.cumsum(of_micro(lengths)[0])
    index = jnp.arange(rows)
    index = (tensor ^ (index // share)) * share + index % share
    segment = jnp.sum((index[:, None] >= ends[None, :]).astype(jnp.int32), axis=1)
    picks = (segment[:, None] == jnp.arange(8)[None, :]).astype(BF)
    picks_own = picks[:share]
    lane = np.arange(LANE) % (LANE // 2)
    valid = jnp.asarray(lane < HALF)
    quarter = HEAD // 4
    rates = 10000.0 ** (-jnp.arange(quarter).astype(F32) / quarter)
    rate = jnp.concatenate([rates, rates, jnp.zeros(LANE // 2 - HALF, F32)] * 2)
    place_now = local(of_micro(positions).T).astype(F32)
    phase = jnp.where(jnp.asarray(lane < quarter), place_now[:, :1], place_now[:, 1:]) * rate
    cosine = jnp.where(valid, jnp.cos(phase), 0.0)
    sine = jnp.where(valid, jnp.sin(phase), 0.0) * jnp.where(jnp.asarray(np.arange(LANE) < LANE // 2), -1.0, 1.0)
    own_gains = jnp.dot(
        jnp.pad(norm_gains[0], ((0, 6), (0, 0))), jnp.asarray(head_places(1), F32), precision=HIGHEST
    )
    got_gains = exchange(own_gains, "section", 1)
    gains = [jnp.where(is_first, own_gains, got_gains), jnp.where(is_first, got_gains, own_gains)]
    tables = [(cosine, sine, gains[l], segment[:, None], segment[None, :]) for l in range(2)]
    x = local(of_micro(inputs))
    cotangent_now = local(of_micro(cotangent))

    states = [x[:share]]
    cache = []
    attention_blocks = [x]
    for l in range(2):
        partial, saved = attention_forward(l, attention_blocks, attention_weights, tables[l], mods[l], picks, sec)
        attended, after, mlp_in = after_attention(send_parts(partial), states[l], mods[l], picks_own)
        mlp_blocks = gather_blocks(mlp_in)
        partial, mlp_saved = mlp_forward(l, mlp_blocks, mlp_weights, sec)
        parts = send_parts(partial)
        if l == 0:
            projected, state, attention_in = after_mlp(parts, after, mods[0], picks_own, mods[1])
            states.append(state)
            attention_blocks = gather_blocks(attention_in)
        else:
            projected, output = after_mlp(parts, after, mods[1], picks_own, None)
        cache.append((saved, attended, after, mlp_blocks, mlp_saved, projected))

    grad_blocks = [cotangent_now]
    grad_out = cotangent_now[:share]
    item_sums = [None, None]
    gain_sums = [None, None]
    shares = [None, None]
    for l in (1, 0):
        saved, attended, after, mlp_blocks, mlp_saved, projected = cache[l]
        attention_in = saved[6]
        partial, grads = mlp_backward(l, grad_blocks, mlp_weights, mlp_saved, mods[l], picks, sec)
        parts = send_parts(partial)
        keep, send = mlp_weight_grads(mlp_blocks, grads, mlp_saved[0], sec)
        mlp_half = (keep.astype(F32) + exchange(send, "section", 1).astype(F32)).astype(BF)
        mlp_share = lax.psum_scatter(mlp_half, "dp", scatter_dimension=0, tiled=True)
        grad_attended, grad_after, sums2 = back_of_mlp(
            parts, grad_out, after, attended, projected, mods[l], picks_own
        )
        partial, results = attention_backward(
            l, gather_blocks(grad_attended), attention_weights, saved[:6], tables[l], selects, sec
        )
        gain_sums[l] = results[4]
        parts = send_parts(partial)
        keep, send = attention_weight_grads(attention_in, results[:4], sec)
        attention_half = (keep.astype(F32) + exchange(send, "section", 1).astype(F32)).astype(BF)
        attention_share = lax.psum_scatter(attention_half, "dp", scatter_dimension=0, tiled=True)
        if l == 1:
            sums1, grad_out, grad_projected = back_of_attention(
                parts, grad_after, states[1], mods[1], picks_own, mods[0]
            )
            grad_blocks = gather_blocks(grad_projected)
        else:
            sums1, grad_state = back_of_attention(parts, grad_after, states[0], mods[0], picks_own, None)
        item_sums[l] = jnp.concatenate([sums1, sums2], axis=0)
        shares[l] = (mlp_share, attention_share)

    mine = jnp.where(is_first, grad_state, output)
    theirs = exchange(jnp.where(is_first, output, grad_state), "section", 1)
    results = jnp.stack([jnp.where(is_first, mine, theirs), jnp.where(is_first, theirs, mine)])

    def joined(which):
        mine = jnp.where(is_first, shares[0][which], shares[1][which])
        theirs = exchange(jnp.where(is_first, shares[1][which], shares[0][which]), "section", 1)
        low = jnp.where(is_first, mine, theirs)
        high = jnp.where(is_first, theirs, mine)
        return jnp.concatenate([low, high], axis=1).astype(F32)

    size = down_weight.shape[1]
    mlp_grads = joined(0)
    grad_pair = jnp.stack([mlp_grads[:, :size], mlp_grads[:, size : 2 * size]])
    grad_down = mlp_grads[:, 2 * size :].T
    attention_grads = joined(1)
    grad_qkv = jnp.stack([attention_grads[:, i * narrow : (i + 1) * narrow] for i in range(3)])
    grad_out_w = attention_grads[:, 3 * narrow :].T

    sums = jnp.stack(item_sums)[:, :, :items].transpose(0, 2, 1, 3).reshape(2, items, 6 * width)
    pieces = [
        lax.dynamic_slice_in_dim(sums, (tensor ^ k) * columns, columns, 2) for k in range(group)
    ]
    got = send_parts(pieces)
    mods_grad = (got[0] + got[1] + got[2] + got[3]).astype(BF)
    mine = lax.dynamic_index_in_dim(mods_grad, section, 0, keepdims=False)
    theirs = exchange(lax.dynamic_index_in_dim(mods_grad, other, 0, keepdims=False), "section", 1)
    mods_low = jnp.stack([jnp.where(is_first, mine, theirs), jnp.where(is_first, theirs, mine)])
    all_scaled = gather_dp(scaled)
    all_mods = gather_dp(mods_low)
    deep = width // lax.axis_size("dp")
    scaled_share = lax.dynamic_slice_in_dim(all_scaled, data * deep, deep, 3)
    grad_ada = jnp.einsum("nmid,nmic->dc", scaled_share, all_mods, preferred_element_type=F32)
    sigma = jax.nn.sigmoid(cond_value)
    cond_part = jnp.einsum("mic,dc->mid", mods_low, modulator[0], preferred_element_type=F32)
    cond_part = cond_part * sigma * (1.0 + cond_value * (1.0 - sigma))
    grad_cond = group_sum(group_sum(cond_part, "section"), "tensor")
    gain_parts = jnp.stack(gain_sums)
    gain_own = lax.dynamic_index_in_dim(gain_parts, section, 0, keepdims=False)
    gain_other = lax.dynamic_index_in_dim(gain_parts, other, 0, keepdims=False)
    gain_total = gain_own + exchange(gain_other, "section", 1)
    gain_total = group_sum(group_sum(gain_total, "tensor"), "dp")
    half = LANE // 2
    grad_gains = jnp.concatenate([gain_total[:2, :HALF], gain_total[:2, half : half + HALF]], axis=1)
    return (
        grad_ada[None],
        grad_qkv[None],
        grad_gains[None],
        grad_out_w[None],
        grad_pair[None],
        grad_down[None],
        grad_cond[:, None],
        results[None],
    )


def solution(mesh):
    return jax.shard_map(
        shards,
        mesh=mesh,
        in_specs=(
            P(None, "dp", None),
            P(None, "dp", None),
            P(None, "dp", None, None),
            P(None, "dp", None),
            P(None, None, "dp"),
            P("section", None, "tensor"),
            P("section", None, None, "tensor"),
            P("section", None, None),
            P("section", "tensor", None),
            P("section", None, None, "tensor"),
            P("section", "tensor", None),
        ),
        out_specs=(
            P("section", "dp", "tensor"),
            P("section", None, "dp", "tensor"),
            P("section", None, None),
            P("section", "tensor", "dp"),
            P("section", None, "dp", "tensor"),
            P("section", "tensor", "dp"),
            P(None, "dp", None, None),
            P("section", None, ("dp", "tensor"), None),
        ),
        check_vma=False,
    )
```

```python
import functools

import jax
import jax.numpy as jnp
from jax import lax
from jax.experimental import pallas as pl
from jax.experimental.pallas import tpu as pltpu
from jax.sharding import PartitionSpec as P
import numpy as np

HEAD = 72
HALF = HEAD // 2
LANE = 128
epsilon = 1e-06
BF = jnp.bfloat16
F32 = jnp.float32
HIGHEST = lax.Precision.HIGHEST
VM = pl.BlockSpec(memory_space=pltpu.VMEM)
SM = pl.BlockSpec(memory_space=pltpu.SMEM)
HB = pl.BlockSpec(memory_space=pltpu.HBM)


def nn(a, b):
    return lax.dot_general(a, b, (((1,), (0,)), ((), ())), preferred_element_type=F32)


def nt(a, b):
    return lax.dot_general(a, b, (((1,), (1,)), ((), ())), preferred_element_type=F32)


def tn(a, b):
    return lax.dot_general(a, b, (((0,), (0,)), ((), ())), preferred_element_type=F32)


def call(body, outs, in_specs, scratch=(), name=None, kept=0, limit=24, aliases={}):
    small = len(outs) - kept
    kernel = pl.pallas_call(
        body,
        out_shape=list(outs[:small]) + [pltpu.HBM(o.shape, o.dtype) for o in outs[small:]],
        in_specs=in_specs,
        out_specs=[VM] * small + [HB] * kept,
        scratch_shapes=list(scratch),
        input_output_aliases=aliases,
        compiler_params=pltpu.CompilerParams(vmem_limit_bytes=limit * 2**20),
        cost_estimate=pl.CostEstimate(flops=1000, bytes_accessed=1000, transcendentals=0),
        name=name,
    )

    def run(*args):
        placed = [
            pltpu.with_memory_space_constraint(arg, pltpu.HBM) if spec is HB else arg
            for arg, spec in zip(args, in_specs)
        ]
        return kernel(*placed)

    return run


def shape(dims, dtype):
    return jax.ShapeDtypeStruct(dims, dtype)


def fetch(is_own, own, other, where, sem):
    @pl.when(is_own)
    def _():
        pltpu.make_async_copy(own, where, sem).start()

    @pl.when(jnp.logical_not(is_own))
    def _():
        pltpu.make_async_copy(other, where, sem).start()


def arrived(own, where, sem):
    pltpu.make_async_copy(own, where, sem).wait()


def load(pairs, sems):
    made = [pltpu.make_async_copy(there, here, sems.at[i]) for i, (there, here) in enumerate(pairs)]
    for one in made:
        one.start()
    return made


def finish(copies):
    for one in copies:
        one.wait()


def inverse_rms(value):
    return lax.rsqrt(jnp.mean(value * value, axis=-1, keepdims=True) + epsilon)


def norm_back(grad, normed, inverse):
    return inverse * (grad - normed * jnp.mean(grad * normed, axis=-1, keepdims=True))


def token_mod(picks, mods_ref, part):
    width = mods_ref.shape[1] // 6
    return nn(picks, mods_ref[:, part * width : (part + 1) * width])


def image_sums(picks, value):
    return lax.dot_general(
        picks.astype(F32),
        value,
        (((0,), (0,)), ((), ())),
        precision=HIGHEST,
        preferred_element_type=F32,
    )


def swap_halves(value):
    return pltpu.roll(value, LANE // 2, 1)


def rotate(value, cosine, sine):
    return value * cosine + swap_halves(value) * sine


def unrotate(grad, cosine, sine):
    return grad * cosine - swap_halves(grad) * sine


def head_mean(value):
    return nn(value.astype(BF), jnp.full((LANE, LANE), 1.0, BF)) * (1.0 / HEAD)


def head_inverse(raw):
    return lax.rsqrt(head_mean(raw * raw) + epsilon)


def split_store(value, rows, block_refs):
    own = block_refs[0]
    share = own.shape[0]
    for k, ref in enumerate(block_refs):
        ref[:, rows] = value[k * share : (k + 1) * share].astype(ref.dtype)


def modulation_part(conditioning, modulator_t):
    micro, items = conditioning.shape[0], conditioning.shape[2]
    columns, width = modulator_t.shape
    step = 5 * LANE
    spans = [(j, min(step, columns - j)) for j in range(0, columns, step)]

    def body(cond_ref, mod_in, scaled_ref, part_ref, mod_ref, sems):
        copies = load([(mod_in.at[pl.ds(j, size)], mod_ref.at[pl.ds(j, size)]) for j, size in spans], sems)
        cond = jnp.concatenate([cond_ref[m, 0].astype(F32) for m in range(micro)], axis=0)
        scaled = (cond * jax.nn.sigmoid(cond)).astype(BF)
        scaled_ref[...] = scaled
        for copy, (j, size) in zip(copies, spans):
            copy.wait()
            part_ref[:, j : j + size] = nt(scaled, mod_ref[j : j + size]).astype(BF)

    return call(
        body,
        [shape((micro * items, width), BF), shape((micro * items, columns), BF)],
        [VM, HB],
        [pltpu.VMEM((columns, width), BF), pltpu.SemaphoreType.DMA((len(spans),))],
        name="modulation_part",
        limit=12,
    )(conditioning, modulator_t)


def modulation_rows(pieces, where):
    rows, columns = pieces[0].shape
    count = len(pieces)
    items = rows // 2

    def body(where_ref, *refs):
        piece_refs, (own_ref, send_ref) = refs[:count], refs[count:]
        section, tensor = where_ref[0], where_ref[1]
        values = [ref[...].astype(F32) for ref in piece_refs]
        ordered = []
        for j in range(count):
            picked = jnp.zeros_like(values[0])
            for k in range(count):
                picked = jnp.where((tensor ^ k) == j, values[k], picked)
            ordered.append(picked)
        whole = jnp.concatenate(ordered, axis=1)
        blank = jnp.zeros((8 - items, whole.shape[1]), F32)
        first = jnp.concatenate([whole[:items], blank], axis=0)
        second = jnp.concatenate([whole[items:], blank], axis=0)
        own_ref[...] = jnp.where(section == 0, first, second).astype(BF)
        send_ref[...] = jnp.where(section == 0, second, first).astype(BF)

    return call(
        body,
        [shape((8, count * columns), BF)] * 2,
        [SM] + [VM] * count,
        name="modulation_rows",
        limit=8,
    )(where, *pieces)


def prepare_tables(where, lengths, positions, rates, inputs, cotangent):
    micro, rows, width = inputs.shape
    share = rows // 4
    items = lengths.shape[2]

    def body(where_ref, len_ref, pos_ref, rate_ref, x_in, cot_in,
             cos_ref, sin_ref, segc_ref, segr_ref, picks_ref, x_out, cot_out, xown_out, cown_out, x_ref, cot_ref, sems):
        section, tensor = where_ref[0], where_ref[1]
        pairs = []
        for k in range(4):
            there = pl.ds(pl.multiple_of((tensor ^ k) * share, LANE), share)
            pairs.append((x_in.at[section, there], x_ref.at[pl.ds(k * share, share)]))
            pairs.append((cot_in.at[section, there], cot_ref.at[pl.ds(k * share, share)]))
        copies = load(pairs, sems)

        def segments(index):
            place = (tensor ^ (index // share)) * share + index % share
            segment = jnp.zeros_like(index)
            end = 0
            for i in range(items):
                end = end + len_ref[section, 0, i]
                segment += (place >= end).astype(jnp.int32)
            return segment

        column = segments(lax.broadcasted_iota(jnp.int32, (rows, 1), 0))
        segc_ref[...] = column
        segr_ref[...] = segments(lax.broadcasted_iota(jnp.int32, (1, rows), 1))
        picks_ref[...] = jnp.where(column == lax.broadcasted_iota(jnp.int32, (rows, 8), 1), 1.0, 0.0).astype(BF)
        finish(copies)
        own = pl.ds(0, share)
        pairs = [(x_ref, x_out), (cot_ref, cot_out), (x_ref.at[own], xown_out), (cot_ref.at[own], cown_out)]
        copies = load(pairs, sems)
        blocks = [
            pos_ref[section, :, pl.ds(pl.multiple_of((tensor ^ k) * share, LANE), share)] for k in range(4)
        ]
        place = jnp.concatenate(blocks, axis=1).astype(F32)
        lane = lax.broadcasted_iota(jnp.int32, (LANE // 2, rows), 0)
        phase = jnp.where(lane < HEAD // 4, place[0:1], place[1:2]) * rate_ref[...]
        cosine = jnp.where(lane < HALF, jnp.cos(phase), 0.0)
        sine = jnp.where(lane < HALF, jnp.sin(phase), 0.0)
        cos_ref[...] = jnp.concatenate([cosine, cosine], axis=0).T
        sin_ref[...] = jnp.concatenate([-sine, sine], axis=0).T
        finish(copies)

    own = shape((share, width), BF)
    return call(
        body,
        [
            shape((rows, LANE), F32),
            shape((rows, LANE), F32),
            shape((rows, 1), jnp.int32),
            shape((1, rows), jnp.int32),
            shape((rows, 8), BF),
            shape((rows, width), BF),
            shape((rows, width), BF),
            own,
            own,
        ],
        [SM, SM, VM, VM, HB, HB],
        [pltpu.VMEM((rows, width), BF), pltpu.VMEM((rows, width), BF), pltpu.SemaphoreType.DMA((8,))],
        name="prepare_tables",
        limit=16,
        kept=4,
    )(where, lengths, positions, rates, inputs, cotangent)


def prepare_weights(where, own, got, place, place_one, begun=None):
    wq_own, wo_own, gains_own = own
    wq_got, wo_got, gains_got = got
    narrow, width = wq_own.shape[1:]
    padded = place.shape[1]
    again = begun is not None

    def body(where_ref, *refs):
        refs = list(refs)
        sources = []
        if not again:
            wqa, woa, ga = refs.pop(0), refs.pop(0), refs.pop(0)
            sources.append((wqa, woa))
        wqb, wob, gb = refs.pop(0), refs.pop(0), refs.pop(0)
        place_ref, one_ref = refs.pop(0), refs.pop(0)
        if again:
            refs = refs[2:]
        else:
            gains_ref = refs.pop(0)
        wq_out, wo_out, wq_ref, wo_ref, wide_ref, tall_ref, sems, out_sems = refs
        section = where_ref[0]
        if not again:
            a, b = ga[...], gb[...]
            first = jnp.where(section == 0, a, b)
            second = jnp.where(section == 0, b, a)
            both = jnp.concatenate([first, second, jnp.zeros((4, first.shape[1]), F32)], axis=0)
            gains_ref[...] = lax.dot_general(
                both, one_ref[...], (((1,), (0,)), ((), ())), precision=HIGHEST, preferred_element_type=F32
            )

        def make(wq, wo, layer):
            copies = load([(wq.at[i], wq_ref.at[i]) for i in range(3)] + [(wo, wo_ref)], sems)
            outs = []
            for i in range(3):
                copies[i].wait()
                wide_ref[i] = tn(wq_ref[i], place_ref[...]).astype(BF)
                outs.append(pltpu.make_async_copy(wide_ref.at[i], wq_out.at[layer, i], out_sems.at[i]))
                outs[-1].start()
            copies[3].wait()
            tall_ref[...] = tn(place_ref[...], wo_ref[...]).astype(BF)
            outs.append(pltpu.make_async_copy(tall_ref, wo_out.at[layer], out_sems.at[3]))
            outs[-1].start()
            finish(outs)

        if not again:
            make(wqa, woa, section)

            @pl.when(section == 1)
            def _():
                make(wqb, wob, 0)
        else:

            @pl.when(section == 0)
            def _():
                make(wqb, wob, 1)

    outs = [shape((2, 3, width, padded), BF), shape((2, padded, width), BF)]
    args = [where] + ([] if again else list(own)) + list(got) + [place, place_one] + (list(begun) if again else [])
    return call(
        body,
        ([] if again else [shape((8, LANE), F32)]) + outs,
        [SM] + ([HB] * 2 + [VM]) * (1 if again else 2) + [VM] * 2 + ([HB] * 2 if again else []),
        [
            pltpu.VMEM((3, narrow, width), BF),
            pltpu.VMEM((narrow, width), BF),
            pltpu.VMEM((3, width, padded), BF),
            pltpu.VMEM((padded, width), BF),
            pltpu.SemaphoreType.DMA((4,)),
            pltpu.SemaphoreType.DMA((4,)),
        ],
        name="prepare_weights",
        limit=24,
        kept=2,
        aliases={6: 0, 7: 1} if again else {},
    )(*args)


def attention_forward(layer, blocks, weights, tables, mods, picks):
    wq, wo = weights
    cosine, sine, gains, seg_col, seg_row = tables
    padded, width = wo.shape[1:]
    heads = padded // LANE
    raw_input = len(blocks) == 1
    rows = sum(b.shape[0] for b in blocks)
    share = rows // 4
    scale = HEAD**-0.5
    QB = 512

    def body(*refs):
        refs = list(refs)
        in_refs = [refs.pop(0) for _ in blocks]
        wq_in, wo_in, cos_ref, sin_ref, gain_ref, segc_ref, segr_ref, mods_ref, picks_ref = refs[:9]
        refs = refs[9:]
        p_refs = refs[:4]
        kept = refs[4:11]
        wq_ref, wo_ref, mask_ref = refs[11:14]
        here = refs[14:21]
        sems, out_sems = refs[21:]
        qraw_ref, kraw_ref, qrot_ref, krot_ref, v_ref, mixed_ref, a_ref = here
        weights_in = [(wq_in.at[layer, i], wq_ref.at[i]) for i in range(3)] + [(wo_in.at[layer], wo_ref)]
        weights_in = load(weights_in, sems)

        def keep(i):
            pltpu.make_async_copy(here[i], kept[i], out_sems.at[i]).start()

        for k, ref in enumerate(in_refs):
            if raw_input:
                x = ref[...].astype(F32)
                picked = picks_ref[...]
                shift1 = token_mod(picked, mods_ref, 0)
                scale1 = token_mod(picked, mods_ref, 1)
                a_ref[...] = (x * inverse_rms(x) * (1.0 + scale1) + shift1).astype(BF)
            else:
                a_ref[k * share : (k + 1) * share] = ref[...]
        keep(6)
        mask_ref[...] = jnp.where(segc_ref[...] == segr_ref[...], 1.0, 0.0).astype(BF)
        cos = cos_ref[...]
        sin = sin_ref[...]
        for i, (raw_out, rot_out) in enumerate(((qraw_ref, qrot_ref), (kraw_ref, krot_ref))):
            weights_in[i].wait()
            gain = gain_ref[2 * layer + i : 2 * layer + i + 1]
            for h2 in range(0, heads, 2):
                both = nn(a_ref[...], wq_ref[i, :, h2 * LANE : (h2 + 2) * LANE])
                for h in (h2, h2 + 1):
                    at = slice(h * LANE, (h + 1) * LANE)
                    raw = both[:, (h - h2) * LANE : (h - h2 + 1) * LANE]
                    raw_out[:, at] = raw.astype(BF)
                    turned = rotate(raw * head_inverse(raw) * gain, cos, sin)
                    rot_out[:, at] = turned.astype(BF)
            keep(i)
            keep(2 + i)
        weights_in[2].wait()
        one = jnp.where(lax.broadcasted_iota(jnp.int32, (1, padded), 1) % LANE == LANE - 1, 1.0, 0.0)
        v_ref[...] = (nn(a_ref[...], wq_ref[2]) + one).astype(BF)
        keep(4)

        for j in range(rows // QB):
            at_rows = slice(j * QB, (j + 1) * QB)
            for h in range(heads):
                at = slice(h * LANE, (h + 1) * LANE)
                scores = nt(qrot_ref[at_rows, at], krot_ref[:, at]) * scale
                grown = jnp.exp(scores).astype(BF) * mask_ref[at_rows]
                mixed = nn(grown, v_ref[:, at])
                mixed_ref[at_rows, at] = (mixed * (1.0 / mixed[:, LANE - 1 :])).astype(BF)
        keep(5)
        weights_in[3].wait()
        step = 3 * LANE
        for j in range(width // step):
            at = slice(j * step, (j + 1) * step)
            split_store(nn(mixed_ref[...], wo_ref[:, at]), at, p_refs)
        for i in range(7):
            pltpu.make_async_copy(here[i], kept[i], out_sems.at[i]).wait()

    outs = [shape((share, width), BF)] * 4
    saved_shapes = [shape((rows, padded), BF)] * 6 + [shape((rows, width), BF)]
    result = call(
        body,
        outs + saved_shapes,
        [VM] * len(blocks) + [HB] * 2 + [VM] * 7,
        [
            pltpu.VMEM((3, width, padded), BF),
            pltpu.VMEM((padded, width), BF),
            pltpu.VMEM((rows, rows), BF),
        ] + [pltpu.VMEM(s.shape, BF) for s in saved_shapes] + [
            pltpu.SemaphoreType.DMA((4,)),
            pltpu.SemaphoreType.DMA((7,)),
        ],
        name=f"attention_forward_{layer}",
        limit=28,
        kept=7,
    )(*blocks, wq, wo, cosine, sine, gains, seg_col, seg_row, mods, picks)
    return list(result[:4]), list(result[4:])


def add_parts(refs):
    total = refs[0][...].astype(F32)
    for ref in refs[1:]:
        total += ref[...].astype(F32)
    return total


def after_attention(parts, state, mods, picks):
    dims = state.shape

    def body(p0_in, p1, p2, p3, state_in, mods_ref, picks_ref, mlp_ref, attended_out, after_out,
             p0, state_ref, attended_ref, after_ref, sems, out_sems):
        copies = load([(p0_in, p0), (state_in, state_ref)], sems)
        picked = picks_ref[...]
        finish(copies)
        attended = add_parts((p0, p1, p2, p3))
        attended_ref[...] = attended.astype(BF)
        after = state_ref[...].astype(F32) + token_mod(picked, mods_ref, 2) * attended
        after_ref[...] = after
        kept = load([(attended_ref, attended_out), (after_ref, after_out)], out_sems)
        normed = after * inverse_rms(after)
        mlp_ref[...] = (normed * (1.0 + token_mod(picked, mods_ref, 4)) + token_mod(picked, mods_ref, 3)).astype(BF)
        finish(kept)

    return call(
        body,
        [shape(dims, BF), shape(dims, BF), shape(dims, F32)],
        [HB] + [VM] * 3 + [HB] + [VM] * 2,
        [pltpu.VMEM(dims, BF)] * 3
        + [pltpu.VMEM(dims, F32), pltpu.SemaphoreType.DMA((2,)), pltpu.SemaphoreType.DMA((2,))],
        name="after_attention",
        limit=8,
        kept=2,
    )(*parts, state, mods, picks)


def after_mlp(parts, after, mods, picks, mods_next):
    last = mods_next is None
    dims = after.shape

    def body(p0_in, p1, p2, p3, after_in, mods_ref, picks_ref, *refs):
        refs = list(refs)
        next_ref = None if last else refs.pop(0)
        in_ref = None if last else refs.pop(0)
        projected_out, result_out, p0, after_ref, projected_ref, result_ref, sems, out_sems = refs
        copies = load([(p0_in, p0), (after_in, after_ref)], sems)
        picked = picks_ref[...]
        finish(copies)
        projected = add_parts((p0, p1, p2, p3))
        projected_ref[...] = projected.astype(BF)
        output = after_ref[...] + token_mod(picked, mods_ref, 5) * projected
        result_ref[...] = output.astype(result_ref.dtype)
        kept = load([(projected_ref, projected_out), (result_ref, result_out)], out_sems)
        if not last:
            state = output.astype(BF).astype(F32)
            normed = state * inverse_rms(state)
            in_ref[...] = (normed * (1.0 + token_mod(picked, next_ref, 1)) + token_mod(picked, next_ref, 0)).astype(BF)
        finish(kept)

    result_type = F32 if last else BF
    outs = ([] if last else [shape(dims, BF)]) + [shape(dims, BF), shape(dims, result_type)]
    extra = () if last else (mods_next,)
    return call(
        body,
        outs,
        [HB] + [VM] * 3 + [HB] + [VM] * (2 + len(extra)),
        [
            pltpu.VMEM(dims, BF),
            pltpu.VMEM(dims, F32),
            pltpu.VMEM(dims, BF),
            pltpu.VMEM(dims, result_type),
            pltpu.SemaphoreType.DMA((2,)),
            pltpu.SemaphoreType.DMA((2,)),
        ],
        name="after_mlp",
        limit=8,
        kept=2,
    )(*parts, after, mods, picks, *extra)


def mlp_forward(layer, blocks, weights, section):
    gu_own, gu_got, wd_own, wd_got = weights
    hidden_size, width = wd_own.shape
    share = blocks[0].shape[0]
    rows = share * 4
    chunk = 2 * LANE

    def body(sec_ref, b0, b1, b2, b3, gu_a, gu_b, wd_a, wd_b, p0, p1, p2, p3, hid_out, c1_out, c2_out, a_out,
             a_ref, gu_ref, wd_ref, hid_ref, c1_ref, c2_ref, sems, out_sems):
        own = sec_ref[0] == layer
        fetch(own, gu_a.at[0], gu_b.at[0], gu_ref.at[0], sems.at[0])
        fetch(own, gu_a.at[1], gu_b.at[1], gu_ref.at[1], sems.at[1])
        fetch(own, wd_a, wd_b, wd_ref, sems.at[2])
        for k, ref in enumerate((b0, b1, b2, b3)):
            a_ref[k * share : (k + 1) * share] = ref[...]
        arrived(gu_a.at[0], gu_ref.at[0], sems.at[0])
        arrived(gu_a.at[1], gu_ref.at[1], sems.at[1])
        for j in range(hidden_size // chunk):
            at = slice(j * chunk, (j + 1) * chunk)
            gate = nn(a_ref[...], gu_ref[0, :, at])
            up = nn(a_ref[...], gu_ref[1, :, at])
            sigma = jax.nn.sigmoid(gate)
            silu = gate * sigma
            hid_ref[:, at] = (silu * up).astype(BF)
            c1_ref[:, at] = (up * (sigma + silu * (1.0 - sigma))).astype(BF)
            c2_ref[:, at] = silu.astype(BF)
        kept = load([(hid_ref, hid_out), (c1_ref, c1_out), (c2_ref, c2_out), (a_ref, a_out)], out_sems)
        arrived(wd_a, wd_ref, sems.at[2])
        step = 3 * LANE
        for j in range(width // step):
            at = slice(j * step, (j + 1) * step)
            split_store(nn(hid_ref[...], wd_ref[:, at]), at, (p0, p1, p2, p3))
        finish(kept)

    outs = [shape((share, width), BF)] * 4 + [shape((rows, hidden_size), BF)] * 3 + [shape((rows, width), BF)]
    result = call(
        body,
        outs,
        [SM] + [VM] * 4 + [HB] * 4,
        [
            pltpu.VMEM((rows, width), BF),
            pltpu.VMEM(gu_own.shape, BF),
            pltpu.VMEM(wd_own.shape, BF),
        ]
        + [pltpu.VMEM((rows, hidden_size), BF)] * 3
        + [pltpu.SemaphoreType.DMA((3,)), pltpu.SemaphoreType.DMA((4,))],
        name=f"mlp_forward_{layer}",
        kept=4,
    )(section, *blocks, gu_own, gu_got, wd_own, wd_got)
    return result[:4], result[4:]


def mlp_backward(layer, blocks, weights, saved, mods, picks, section):
    gu_own, gu_got, wd_own, wd_got = weights
    c1, c2 = saved
    hidden_size, width = wd_own.shape
    rows = c1.shape[0]
    share = rows // 4
    raw_input = len(blocks) == 1
    chunk = 2 * LANE

    def body(sec_ref, *refs):
        refs = list(refs)
        in_refs = [refs.pop(0) for _ in blocks]
        gu_a, gu_b, wd_a, wd_b, c1_in, c2_in, mods_ref, picks_ref = refs[:8]
        p_refs = refs[8:12]
        outs = refs[12:15]
        gu_ref, wd_ref, c1_ref, c2_ref, gg_ref, gup_ref, gp_ref, sems, out_sems = refs[15:]
        own = sec_ref[0] == layer
        fetch(own, wd_a, wd_b, wd_ref, sems.at[2])
        pltpu.make_async_copy(c1_in, c1_ref, sems.at[3]).start()
        pltpu.make_async_copy(c2_in, c2_ref, sems.at[4]).start()
        fetch(own, gu_a.at[0], gu_b.at[0], gu_ref.at[0], sems.at[0])
        fetch(own, gu_a.at[1], gu_b.at[1], gu_ref.at[1], sems.at[1])
        for k, ref in enumerate(in_refs):
            if raw_input:
                gp_ref[...] = (ref[...].astype(F32) * token_mod(picks_ref[...], mods_ref, 5)).astype(BF)
            else:
                gp_ref[k * share : (k + 1) * share] = ref[...]
        pltpu.make_async_copy(gp_ref, outs[2], out_sems.at[2]).start()
        arrived(wd_a, wd_ref, sems.at[2])
        pltpu.make_async_copy(c1_in, c1_ref, sems.at[3]).wait()
        pltpu.make_async_copy(c2_in, c2_ref, sems.at[4]).wait()
        for j in range(hidden_size // chunk):
            at = slice(j * chunk, (j + 1) * chunk)
            grad_hidden = nt(gp_ref[...], wd_ref[at])
            gg_ref[:, at] = (grad_hidden * c1_ref[:, at].astype(F32)).astype(BF)
            gup_ref[:, at] = (grad_hidden * c2_ref[:, at].astype(F32)).astype(BF)
        pltpu.make_async_copy(gg_ref, outs[0], out_sems.at[0]).start()
        pltpu.make_async_copy(gup_ref, outs[1], out_sems.at[1]).start()
        arrived(gu_a.at[0], gu_ref.at[0], sems.at[0])
        arrived(gu_a.at[1], gu_ref.at[1], sems.at[1])
        step = 3 * LANE
        for j in range(width // step):
            at = slice(j * step, (j + 1) * step)
            split_store(nt(gg_ref[...], gu_ref[0, at]) + nt(gup_ref[...], gu_ref[1, at]), at, p_refs)
        for i, here in enumerate((gg_ref, gup_ref, gp_ref)):
            pltpu.make_async_copy(here, outs[i], out_sems.at[i]).wait()

    outs = [shape((share, width), BF)] * 4 + [shape((rows, hidden_size), BF)] * 2
    outs += [shape((rows, width), BF)]
    result = call(
        body,
        outs,
        [SM] + [VM] * len(blocks) + [HB] * 6 + [VM] * 2,
        [
            pltpu.VMEM(gu_own.shape, BF),
            pltpu.VMEM(wd_own.shape, BF),
        ]
        + [pltpu.VMEM((rows, hidden_size), BF)] * 4
        + [
            pltpu.VMEM((rows, width), BF),
            pltpu.SemaphoreType.DMA((5,)),
            pltpu.SemaphoreType.DMA((3,)),
        ],
        name=f"mlp_backward_{layer}",
        kept=3,
    )(section, *blocks, gu_own, gu_got, wd_own, wd_got, c1, c2, mods, picks)
    return result[:4], result[4:]


def mlp_weight_grads(mlp_in, grads, hidden):
    grad_gate, grad_up, grad_projected = grads
    rows, width = grad_projected.shape
    size = hidden.shape[1]
    step = 3 * LANE

    def body(a_in, gg_in, gu_in, gp_in, hid_in, out, a_ref, gg_ref, gu_ref, gp_ref, hid_ref, full_ref, in_sems, sems):
        ins = load([(a_in, a_ref), (gg_in, gg_ref), (gu_in, gu_ref), (gp_in, gp_ref), (hid_in, hid_ref)], in_sems)
        finish(ins)
        kept = []
        for j in range(width // step):
            at = slice(j * step, (j + 1) * step)
            left = a_ref[:, at]
            full_ref[at, :size] = tn(left, gg_ref[...]).astype(BF)
            full_ref[at, size : 2 * size] = tn(left, gu_ref[...]).astype(BF)
            full_ref[at, 2 * size :] = tn(gp_ref[:, at], hid_ref[...]).astype(BF)
            here = pl.ds(j * step, step)
            kept.append(pltpu.make_async_copy(full_ref.at[here], out.at[here], sems.at[j]))
            kept[-1].start()
        finish(kept)

    (result,) = call(
        body,
        [shape((width, 3 * size), BF)],
        [HB] * 5,
        [pltpu.VMEM((rows, width), BF)]
        + [pltpu.VMEM((rows, size), BF)] * 2
        + [
            pltpu.VMEM((rows, width), BF),
            pltpu.VMEM((rows, size), BF),
            pltpu.VMEM((width, 3 * size), BF),
            pltpu.SemaphoreType.DMA((5,)),
            pltpu.SemaphoreType.DMA((width // step,)),
        ],
        name="mlp_weight_grads",
        kept=1,
    )(mlp_in, grad_gate, grad_up, grad_projected, hidden)
    return result


def attention_backward(layer, blocks, weights, saved, tables):
    wq, wo = weights
    cosine, sine, gains, seg_col, seg_row = tables
    rows, padded = saved[0].shape
    width = wo.shape[2]
    heads = padded // LANE
    share = rows // 4
    scale = HEAD**-0.5
    QB = 512

    def body(b0, b1, b2, b3, wq_in, wo_in, qraw_in, kraw_in, qrot_in, krot_in, v_in,
             cos_ref, sin_ref, gain_ref, segc_ref, segr_ref,
             p0, p1, p2, p3, ggain_ref, g_out, ga_out,
             wq_ref, wo_ref, qraw_ref, kraw_ref, qrot_ref, krot_ref, v_ref, mask_ref,
             ga_ref, gmix_ref, gq_ref, gk_ref, g_ref, sems, in_sems):
        ins = [(wo_in.at[layer], wo_ref)]
        ins += [(qrot_in, qrot_ref), (krot_in, krot_ref), (v_in, v_ref), (qraw_in, qraw_ref), (kraw_in, kraw_ref)]
        ins += [(wq_in.at[layer, i], wq_ref.at[i]) for i in range(3)]
        ins = load(ins, in_sems)
        for k, ref in enumerate((b0, b1, b2, b3)):
            ga_ref[k * share : (k + 1) * share] = ref[...]
        kept = [pltpu.make_async_copy(ga_ref, ga_out, sems.at[0]), pltpu.make_async_copy(g_ref, g_out, sems.at[1])]
        kept[0].start()
        mask_ref[...] = jnp.where(segc_ref[...] == segr_ref[...], 1.0, 0.0).astype(BF)
        ins[0].wait()
        gmix_ref[...] = nt(ga_ref[...], wo_ref[...]).astype(BF)
        finish(ins[1:4])
        for h in range(heads):
            at = slice(h * LANE, (h + 1) * LANE)
            for j in range(rows // QB):
                at_rows = slice(j * QB, (j + 1) * QB)
                query = qrot_ref[at_rows, at]
                grad_mixed = gmix_ref[at_rows, at]
                scores = nt(krot_ref[:, at], query) * scale
                grown = (jnp.exp(scores).astype(BF) * mask_ref[:, at_rows]).astype(F32)
                weights_t = grown * (1.0 / jnp.sum(grown, axis=0, keepdims=True))
                grad_weights = nt(v_ref[:, at], grad_mixed)
                add_v = nn(weights_t.astype(BF), grad_mixed)
                product = weights_t * grad_weights
                delta = jnp.sum(product, axis=0, keepdims=True)
                grad_scores = (product - weights_t * delta).astype(BF)
                gq_ref[at_rows, at] = tn(grad_scores, krot_ref[:, at])
                add_k = nn(grad_scores, query)
                total_v = add_v if j == 0 else total_v + add_v
                total_k = add_k if j == 0 else total_k + add_k
            gk_ref[:, at] = total_k
            g_ref[:, 2 * padded + h * LANE : 2 * padded + (h + 1) * LANE] = total_v.astype(BF)
        cos = cos_ref[...]
        sin = sin_ref[...]
        finish(ins[4:6])
        ggain_ref[...] = jnp.zeros_like(ggain_ref)
        for i, (raw_ref, grad_ref) in enumerate(((qraw_ref, gq_ref), (kraw_ref, gk_ref))):
            gain = gain_ref[2 * layer + i : 2 * layer + i + 1]
            gain_sum = jnp.zeros((1, LANE), F32)
            for h in range(heads):
                at = slice(h * LANE, (h + 1) * LANE)
                raw = raw_ref[:, at].astype(F32)
                inverse = head_inverse(raw)
                normed = raw * inverse
                turned = unrotate(grad_ref[:, at], cos, sin) * scale
                product = turned * normed
                gain_sum += jnp.sum(product, axis=0, keepdims=True)
                back = inverse * (turned * gain - normed * head_mean(product * gain))
                g_ref[:, i * padded + h * LANE : i * padded + (h + 1) * LANE] = back.astype(BF)
            ggain_ref[i : i + 1] = gain_sum
        kept[1].start()
        finish(ins[6:])
        step = 3 * LANE
        for j in range(width // step):
            at = slice(j * step, (j + 1) * step)
            total = nt(g_ref[:, :padded], wq_ref[0, at])
            total += nt(g_ref[:, padded : 2 * padded], wq_ref[1, at])
            total += nt(g_ref[:, 2 * padded :], wq_ref[2, at])
            split_store(total, at, (p0, p1, p2, p3))
        finish(kept)

    outs = [shape((share, width), BF)] * 4
    outs += [shape((8, LANE), F32), shape((rows, 3 * padded), BF), shape((rows, width), BF)]
    result = call(
        body,
        outs,
        [VM] * 4 + [HB] * 7 + [VM] * 5,
        [
            pltpu.VMEM((3, width, padded), BF),
            pltpu.VMEM((padded, width), BF),
        ]
        + [pltpu.VMEM((rows, padded), BF)] * 5
        + [
            pltpu.VMEM((rows, rows), BF),
            pltpu.VMEM((rows, width), BF),
            pltpu.VMEM((rows, padded), BF),
            pltpu.VMEM((rows, padded), F32),
            pltpu.VMEM((rows, padded), F32),
            pltpu.VMEM((rows, 3 * padded), BF),
            pltpu.SemaphoreType.DMA((2,)),
            pltpu.SemaphoreType.DMA((9,)),
        ],
        name=f"attention_backward_{layer}",
        limit=32,
        kept=2,
    )(*blocks, wq, wo, *saved[:5], cosine, sine, gains, seg_col, seg_row)
    return result[:4], result[4:]


def attention_weight_grads(attention_in, grads, mixed, grad_attended, place):
    rows, width = attention_in.shape
    padded, narrow = place.shape
    step = 3 * LANE

    def body(a_in, g_in, mixed_in, ga_in, place_ref, out, a_ref, g_ref, mixed_ref, ga_ref, right_ref, full_ref, in_sems, sems):
        ins = load([(g_in, g_ref), (mixed_in, mixed_ref), (a_in, a_ref), (ga_in, ga_ref)], in_sems)
        finish(ins[:2])
        for i in range(3):
            right_ref[i] = nn(g_ref[:, i * padded : (i + 1) * padded], place_ref[...]).astype(BF)
        right_ref[3] = nn(mixed_ref[...], place_ref[...]).astype(BF)
        finish(ins[2:])
        kept = []
        for j in range(width // step):
            at = slice(j * step, (j + 1) * step)
            left = a_ref[:, at]
            for i in range(3):
                full_ref[at, i * narrow : (i + 1) * narrow] = tn(left, right_ref[i]).astype(BF)
            full_ref[at, 3 * narrow :] = tn(ga_ref[:, at], right_ref[3]).astype(BF)
            here = pl.ds(j * step, step)
            kept.append(pltpu.make_async_copy(full_ref.at[here], out.at[here], sems.at[j]))
            kept[-1].start()
        finish(kept)

    (result,) = call(
        body,
        [shape((width, 4 * narrow), BF)],
        [HB] * 4 + [VM],
        [
            pltpu.VMEM((rows, width), BF),
            pltpu.VMEM((rows, 3 * padded), BF),
            pltpu.VMEM((rows, padded), BF),
            pltpu.VMEM((rows, width), BF),
            pltpu.VMEM((4, rows, narrow), BF),
            pltpu.VMEM((width, 4 * narrow), BF),
            pltpu.SemaphoreType.DMA((4,)),
            pltpu.SemaphoreType.DMA((width // step,)),
        ],
        name="attention_weight_grads",
        kept=1,
    )(attention_in, grads, mixed, grad_attended, place)
    return result


def back_of_mlp(parts, grad_out, after, attended, projected, mods, picks):
    dims = after.shape

    def body(p0_in, p1, p2, p3, g_in, after_in, attended_in, projected_in, mods_ref, picks_ref, ga_ref, sums_ref, grad_out_ref,
             p0, g_ref, after_ref, attended_ref, projected_ref, grad_ref, sems, out_sems):
        ins = [(p0_in, p0), (after_in, after_ref), (g_in, g_ref), (attended_in, attended_ref), (projected_in, projected_ref)]
        ins = load(ins, sems)
        picked = picks_ref[...]
        ins[0].wait()
        grad_in = add_parts((p0, p1, p2, p3))
        ins[1].wait()
        after = after_ref[...]
        inverse = inverse_rms(after)
        normed = after * inverse
        ins[2].wait()
        g = g_ref[...].astype(F32)
        grad_after = g + norm_back(grad_in * (1.0 + token_mod(picked, mods_ref, 4)), normed, inverse)
        grad_ref[...] = grad_after
        kept = load([(grad_ref, grad_out_ref)], out_sems)
        ga_ref[...] = (grad_after * token_mod(picked, mods_ref, 2)).astype(BF)
        finish(ins[3:])
        sums_ref[0] = image_sums(picked, grad_after * attended_ref[...].astype(F32))
        sums_ref[1] = image_sums(picked, grad_in)
        sums_ref[2] = image_sums(picked, grad_in * normed)
        sums_ref[3] = image_sums(picked, g * projected_ref[...].astype(F32))
        finish(kept)

    return call(
        body,
        [shape(dims, BF), shape((4, picks.shape[1], dims[1]), F32), shape(dims, F32)],
        [HB] + [VM] * 3 + [HB] * 4 + [VM] * 2,
        [
            pltpu.VMEM(dims, BF),
            pltpu.VMEM(dims, BF),
            pltpu.VMEM(dims, F32),
            pltpu.VMEM(dims, BF),
            pltpu.VMEM(dims, BF),
            pltpu.VMEM(dims, F32),
            pltpu.SemaphoreType.DMA((5,)),
            pltpu.SemaphoreType.DMA((1,)),
        ],
        name="back_of_mlp",
        limit=12,
        kept=1,
    )(*parts, grad_out, after, attended, projected, mods, picks)


def back_of_attention(parts, grad_after, state, mods, picks, mods_below):
    first = mods_below is None
    dims = grad_after.shape

    def body(p0_in, p1, p2, p3, grad_in_ref, state_in, mods_ref, picks_ref, *refs):
        refs = list(refs)
        below_ref = None if first else refs.pop(0)
        sums_ref = refs.pop(0)
        gp_ref = None if first else refs.pop(0)
        result_out, p0, grad_ref, state_ref, result_ref, sems, out_sems = refs
        ins = load([(p0_in, p0), (state_in, state_ref), (grad_in_ref, grad_ref)], sems)
        picked = picks_ref[...]
        ins[0].wait()
        grad_in = add_parts((p0, p1, p2, p3))
        ins[1].wait()
        state = state_ref[...].astype(F32)
        inverse = inverse_rms(state)
        normed = state * inverse
        ins[2].wait()
        grad_state = grad_ref[...] + norm_back(grad_in * (1.0 + token_mod(picked, mods_ref, 1)), normed, inverse)
        result_ref[...] = grad_state.astype(result_ref.dtype)
        kept = load([(result_ref, result_out)], out_sems)
        if not first:
            gp_ref[...] = (grad_state.astype(BF).astype(F32) * token_mod(picked, below_ref, 5)).astype(BF)
        sums_ref[0] = image_sums(picked, grad_in)
        sums_ref[1] = image_sums(picked, grad_in * normed)
        finish(kept)

    result_type = F32 if first else BF
    outs = [shape((2, picks.shape[1], dims[1]), F32)] + ([] if first else [shape(dims, BF)]) + [shape(dims, result_type)]
    extra = () if first else (mods_below,)
    return call(
        body,
        outs,
        [HB] + [VM] * 3 + [HB] * 2 + [VM] * (2 + len(extra)),
        [
            pltpu.VMEM(dims, BF),
            pltpu.VMEM(dims, F32),
            pltpu.VMEM(dims, BF),
            pltpu.VMEM(dims, result_type),
            pltpu.SemaphoreType.DMA((3,)),
            pltpu.SemaphoreType.DMA((1,)),
        ],
        name="back_of_attention",
        limit=12,
        kept=1,
    )(*parts, grad_after, state, mods, picks, *extra)


def exchange(value, axis, k):
    return lax.ppermute(value, axis, [(i, i ^ k) for i in range(lax.axis_size(axis))])


def send_parts(parts):
    got = {k: exchange(parts[k], "tensor", k) for k in (3, 1, 2)}
    return [parts[0], got[1], got[2], got[3]]


def gather_blocks(own):
    got = {k: exchange(own, "tensor", k) for k in (3, 1, 2)}
    return [own, got[1], got[2], got[3]]


def group_sum(value, axis):
    k = 1
    while k < lax.axis_size(axis):
        value = value + exchange(value, axis, k)
        k *= 2
    return value


def gather_dp(value):
    count = lax.axis_size("dp")
    if count > 4:
        return lax.all_gather(value, "dp", axis=0)
    me = lax.axis_index("dp")
    got = [value] + [exchange(value, "dp", k) for k in range(1, count)]
    stacked = jnp.stack(got)
    return jnp.stack([lax.dynamic_index_in_dim(stacked, me ^ j, 0, keepdims=False) for j in range(count)])


def head_places(heads):
    place = np.zeros((heads * HEAD, heads * LANE), np.float32)
    for h in range(heads):
        for j in range(HEAD):
            place[h * HEAD + j, h * LANE + (j // HALF) * (LANE // 2) + j % HALF] = 1.0
    return place


def shards(
    inputs,
    cotangent,
    conditioning,
    lengths,
    positions,
    modulator,
    projections,
    norm_gains,
    out_weight,
    gate_up,
    down_weight,
):
    section = lax.axis_index("section")
    other = 1 - section
    tensor = lax.axis_index("tensor")
    data = lax.axis_index("dp")
    micro, _, width = inputs.shape
    rows = inputs.shape[1]
    group = lax.axis_size("tensor")
    share = rows // group
    items = lengths.shape[2]
    narrow = projections.shape[3]
    heads = narrow // HEAD
    columns = modulator.shape[2]
    sec = section.reshape(1).astype(jnp.int32)

    where = jnp.stack([section, tensor]).astype(jnp.int32)
    is_first = section == 0

    own = (jnp.swapaxes(projections[0], 1, 2), out_weight[0], norm_gains[0])
    got = tuple(exchange(value, "section", 1) for value in own)
    scaled, part = modulation_part(conditioning, jnp.swapaxes(modulator[0], 0, 1))
    pieces = gather_blocks(part)
    quarter = HEAD // 4
    rates = 10000.0 ** (-jnp.arange(quarter).astype(F32) / quarter)
    rates = jnp.concatenate([rates, rates, jnp.zeros(LANE // 2 - HALF, F32)])[:, None]
    where_late, part = lax.optimization_barrier((where, part))
    cosine, sine, seg_col, seg_row, picks, x, cotangent_now, x_own, cotangent_own = prepare_tables(
        where_late, lengths, positions, rates, inputs, cotangent
    )
    pieces, cosine = lax.optimization_barrier((pieces, cosine))
    mods_own, mods_send = modulation_rows([part] + pieces[1:], where)
    mods_got = exchange(mods_send, "section", 1)
    place = jnp.asarray(head_places(heads), BF)
    place_one = jnp.asarray(head_places(1), F32)
    got, mods_own = lax.optimization_barrier((got, mods_own))
    gu_send, wd_send, mods_got = lax.optimization_barrier((gate_up[0], down_weight[0], mods_got))
    got, mods_got = lax.optimization_barrier((got, mods_got))
    gains, wq, wo = prepare_weights(where, own, got, place, place_one)
    mods = [jnp.where(is_first, mods_own, mods_got), jnp.where(is_first, mods_got, mods_own)]
    gu_got = exchange(gu_send, "section", 1)
    wd_got = exchange(wd_send, "section", 1)
    mlp_weights = (gate_up[0], gu_got, down_weight[0], wd_got)

    picks_own = picks[:share]
    tables = (cosine, sine, gains, seg_col, seg_row)

    states = [x_own]
    cache = []
    attention_blocks = [x]
    for l in range(2):
        partial, saved = attention_forward(l, attention_blocks, (wq, wo), tables, mods[l], picks)
        parts = send_parts(partial)
        if l == 0:
            wq, mixed = lax.optimization_barrier((wq, saved[5]))
            saved[5] = mixed
            wq, wo = prepare_weights(where, own, got, place, place_one, (wq, wo))
            parts, wq = lax.optimization_barrier((parts, wq))
            attention_weights = (wq, wo)
        mlp_in, attended, after = after_attention(parts, states[l], mods[l], picks_own)
        partial, mlp_saved = mlp_forward(l, gather_blocks(mlp_in), mlp_weights, sec)
        parts = send_parts(partial)
        if l == 0:
            attention_in, projected, state = after_mlp(parts, after, mods[0], picks_own, mods[1])
            states.append(state)
            attention_blocks = gather_blocks(attention_in)
        else:
            projected, output = after_mlp(parts, after, mods[1], picks_own, None)
        cache.append((saved, attended, after, mlp_saved, projected))

    grad_blocks = [cotangent_now]
    grad_out = cotangent_own
    item_sums = [None, None]
    gain_sums = [None, None]
    shares = [None, None]
    earlier = None

    def data_sum(value):
        return lax.psum_scatter(value, ("dp", "section"), scatter_dimension=0, tiled=True)

    for l in (1, 0):
        saved, attended, after, (hidden, c1, c2, mlp_in), projected = cache[l]
        mixed, attention_in = saved[5:]
        partial, grads = mlp_backward(l, grad_blocks, mlp_weights, (c1, c2), mods[l], picks, sec)
        parts = send_parts(partial)
        mlp_grads = mlp_weight_grads(mlp_in, grads, hidden)
        if earlier is not None:
            parts, earlier = lax.optimization_barrier((parts, earlier))
            shares[1] = (shares[1][0], earlier)
            mlp_grads, earlier = lax.optimization_barrier((mlp_grads, earlier))
        parts, mlp_grads = lax.optimization_barrier((parts, mlp_grads))
        mlp_share = data_sum(mlp_grads)
        grad_attended, sums2, grad_after = back_of_mlp(
            parts, grad_out, after, attended, projected, mods[l], picks_own
        )
        blocks = gather_blocks(grad_attended)
        partial, (gain_sums[l], grads, grad_attended) = attention_backward(l, blocks, (wq, wo), saved, tables)
        parts = send_parts(partial)
        attention_grads = attention_weight_grads(attention_in, grads, mixed, grad_attended, place.T)
        if l == 1:
            parts, mlp_share = lax.optimization_barrier((parts, mlp_share))
        attention_grads, mlp_share = lax.optimization_barrier((attention_grads, mlp_share))
        parts, attention_grads = lax.optimization_barrier((parts, attention_grads))
        attention_share = data_sum(attention_grads)
        if l == 1:
            sums1, grad_projected, grad_out = back_of_attention(
                parts, grad_after, states[1], mods[1], picks_own, mods[0]
            )
            grad_blocks = gather_blocks(grad_projected)
            earlier = attention_share
        else:
            sums1, grad_state = back_of_attention(parts, grad_after, states[0], mods[0], picks_own, None)
        item_sums[l] = jnp.concatenate([sums1, sums2], axis=0)
        shares[l] = (mlp_share, attention_share)
    shares[1] = (shares[1][0], earlier)

    mine = jnp.where(is_first, grad_state, output)
    theirs = exchange(jnp.where(is_first, output, grad_state), "section", 1)
    results = jnp.stack([jnp.where(is_first, mine, theirs), jnp.where(is_first, theirs, mine)])

    def joined(which):
        mine = jnp.where(is_first, shares[0][which], shares[1][which])
        theirs = exchange(jnp.where(is_first, shares[1][which], shares[0][which]), "section", 1)
        low = jnp.where(is_first, mine, theirs)
        high = jnp.where(is_first, theirs, mine)
        return jnp.concatenate([low, high], axis=0).astype(F32)

    size = down_weight.shape[1]
    mlp_grads = joined(0)
    grad_pair = jnp.stack([mlp_grads[:, :size], mlp_grads[:, size : 2 * size]])
    grad_down = mlp_grads[:, 2 * size :].T
    attention_grads = joined(1)
    grad_qkv = jnp.stack([attention_grads[:, i * narrow : (i + 1) * narrow] for i in range(3)])
    grad_out_w = attention_grads[:, 3 * narrow :].T

    sums = jnp.stack(item_sums)[:, :, :items].transpose(0, 2, 1, 3).reshape(2, items, 6 * width)
    pieces = [
        lax.dynamic_slice_in_dim(sums, (tensor ^ k) * columns, columns, 2) for k in range(group)
    ]
    got = send_parts(pieces)
    mods_grad = (got[0] + got[1] + got[2] + got[3]).astype(BF)
    mine = lax.dynamic_index_in_dim(mods_grad, section, 0, keepdims=False)
    theirs = exchange(lax.dynamic_index_in_dim(mods_grad, other, 0, keepdims=False), "section", 1)
    mods_low = jnp.stack([jnp.where(is_first, mine, theirs), jnp.where(is_first, theirs, mine)])
    all_scaled = gather_dp(scaled.reshape(micro, items, width))
    all_mods = gather_dp(mods_low)
    deep = width // lax.axis_size("dp")
    scaled_share = lax.dynamic_slice_in_dim(all_scaled, data * deep, deep, 3)
    grad_ada = jnp.einsum("nmid,nmic->dc", scaled_share, all_mods, preferred_element_type=F32)
    cond_value = conditioning[:, 0].astype(F32)
    sigma = jax.nn.sigmoid(cond_value)
    cond_part = jnp.einsum("mic,dc->mid", mods_low, modulator[0], preferred_element_type=F32)
    cond_part = cond_part * sigma * (1.0 + cond_value * (1.0 - sigma))
    grad_cond = group_sum(group_sum(cond_part, "section"), "tensor")
    gain_parts = jnp.stack(gain_sums)
    gain_own = lax.dynamic_index_in_dim(gain_parts, section, 0, keepdims=False)
    gain_other = lax.dynamic_index_in_dim(gain_parts, other, 0, keepdims=False)
    gain_total = gain_own + exchange(gain_other, "section", 1)
    gain_total = group_sum(group_sum(gain_total, "tensor"), "dp")
    half = LANE // 2
    grad_gains = jnp.concatenate([gain_total[:2, :HALF], gain_total[:2, half : half + HALF]], axis=1)
    return (
        grad_ada[None],
        grad_qkv[None],
        grad_gains[None],
        grad_out_w[None],
        grad_pair[None],
        grad_down[None],
        grad_cond[:, None],
        results[None],
    )


def solution(mesh):
    return jax.shard_map(
        shards,
        mesh=mesh,
        in_specs=(
            P(None, "dp", None),
            P(None, "dp", None),
            P(None, "dp", None, None),
            P(None, "dp", None),
            P(None, None, "dp"),
            P("section", None, "tensor"),
            P("section", None, None, "tensor"),
            P("section", None, None),
            P("section", "tensor", None),
            P("section", None, None, "tensor"),
            P("section", "tensor", None),
        ),
        out_specs=(
            P("section", "dp", "tensor"),
            P("section", None, "dp", "tensor"),
            P("section", None, None),
            P("section", "tensor", "dp"),
            P("section", None, "dp", "tensor"),
            P("section", "tensor", "dp"),
            P(None, "dp", None, None),
            P("section", None, ("dp", "tensor"), None),
        ),
        check_vma=False,
    )
```

```python
import functools

import jax
import jax.numpy as jnp
from jax import lax
from jax.experimental import pallas as pl
from jax.experimental.pallas import tpu as pltpu
from jax.sharding import PartitionSpec as P
import numpy as np

HEAD = 72
HALF = HEAD // 2
LANE = 128
epsilon = 1e-06
BF = jnp.bfloat16
F32 = jnp.float32
HIGHEST = lax.Precision.HIGHEST
VM = pl.BlockSpec(memory_space=pltpu.VMEM)
SM = pl.BlockSpec(memory_space=pltpu.SMEM)
HB = pl.BlockSpec(memory_space=pltpu.HBM)
FREE = pl.BlockSpec(memory_space=pltpu.VMEM)


def nn(a, b):
    return lax.dot_general(a, b, (((1,), (0,)), ((), ())), preferred_element_type=F32)


def nt(a, b):
    return lax.dot_general(a, b, (((1,), (1,)), ((), ())), preferred_element_type=F32)


def tn(a, b):
    return lax.dot_general(a, b, (((0,), (0,)), ((), ())), preferred_element_type=F32)


def call(body, outs, in_specs, scratch=(), name=None, kept=0, limit=24, aliases={}):
    small = len(outs) - kept
    kernel = pl.pallas_call(
        body,
        out_shape=[pltpu.VMEM(o.shape, o.dtype) for o in outs[:small]] + [pltpu.HBM(o.shape, o.dtype) for o in outs[small:]],
        in_specs=in_specs,
        out_specs=[VM] * small + [HB] * kept,
        scratch_shapes=list(scratch),
        input_output_aliases=aliases,
        compiler_params=pltpu.CompilerParams(vmem_limit_bytes=limit * 2**20),
        cost_estimate=pl.CostEstimate(flops=1000, bytes_accessed=1000, transcendentals=0),
        name=name,
    )

    def run(*args):
        spaces = {id(HB): pltpu.HBM, id(VM): pltpu.VMEM}
        placed = [
            pltpu.with_memory_space_constraint(arg, spaces[id(spec)]) if id(spec) in spaces else arg
            for arg, spec in zip(args, in_specs)
        ]
        return kernel(*placed)

    return run


def shape(dims, dtype):
    return jax.ShapeDtypeStruct(dims, dtype)


def fetch(is_own, own, other, where, sem):
    @pl.when(is_own)
    def _():
        pltpu.make_async_copy(own, where, sem).start()

    @pl.when(jnp.logical_not(is_own))
    def _():
        pltpu.make_async_copy(other, where, sem).start()


def arrived(own, where, sem):
    pltpu.make_async_copy(own, where, sem).wait()


def load(pairs, sems):
    made = [pltpu.make_async_copy(there, here, sems.at[i]) for i, (there, here) in enumerate(pairs)]
    for one in made:
        one.start()
    return made


def finish(copies):
    for one in copies:
        one.wait()


def rows_of(whole, where_ref, here):
    share = whole.shape[1] // 4
    pairs = []
    for k in range(here.shape[0] // share):
        there = pl.ds(pl.multiple_of((where_ref[1] ^ k) * share, LANE), share)
        pairs.append((whole.at[where_ref[0], there], here.at[pl.ds(k * share, share)]))
    return pairs


def inverse_rms(value):
    return lax.rsqrt(jnp.mean(value * value, axis=-1, keepdims=True) + epsilon)


def norm_back(grad, normed, inverse):
    return inverse * (grad - normed * jnp.mean(grad * normed, axis=-1, keepdims=True))


def token_mod(picks, mods_ref, part):
    width = mods_ref.shape[1] // 6
    return nn(picks, mods_ref[:, part * width : (part + 1) * width])


def image_sums(picks, value):
    return lax.dot_general(
        picks.astype(F32),
        value,
        (((0,), (0,)), ((), ())),
        precision=HIGHEST,
        preferred_element_type=F32,
    )


def swap_halves(value):
    return pltpu.roll(value, LANE // 2, 1)


def rotate(value, cosine, sine):
    return value * cosine + swap_halves(value) * sine


def unrotate(grad, cosine, sine):
    return grad * cosine - swap_halves(grad) * sine


def head_mean(value):
    return nn(value.astype(BF), jnp.full((LANE, LANE), 1.0, BF)) * (1.0 / HEAD)


def head_inverse(raw):
    return lax.rsqrt(head_mean(raw * raw) + epsilon)


def split_store(value, rows, block_refs):
    own = block_refs[0]
    share = own.shape[0]
    for k, ref in enumerate(block_refs):
        ref[:, rows] = value[k * share : (k + 1) * share].astype(ref.dtype)


def modulation_part(conditioning, modulator_t):
    micro, items = conditioning.shape[0], conditioning.shape[2]
    columns, width = modulator_t.shape
    step = 5 * LANE
    spans = [(j, min(step, columns - j)) for j in range(0, columns, step)]

    def body(cond_ref, mod_in, scaled_ref, part_ref, mod_ref, sems):
        copies = load([(mod_in.at[pl.ds(j, size)], mod_ref.at[pl.ds(j, size)]) for j, size in spans], sems)
        cond = jnp.concatenate([cond_ref[m, 0].astype(F32) for m in range(micro)], axis=0)
        scaled = (cond * jax.nn.sigmoid(cond)).astype(BF)
        scaled_ref[...] = scaled
        for copy, (j, size) in zip(copies, spans):
            copy.wait()
            part_ref[:, j : j + size] = nt(scaled, mod_ref[j : j + size]).astype(BF)

    return call(
        body,
        [shape((micro * items, width), BF), shape((micro * items, columns), BF)],
        [FREE, HB],
        [pltpu.VMEM((columns, width), BF), pltpu.SemaphoreType.DMA((len(spans),))],
        name="modulation_part",
        limit=12,
    )(conditioning, modulator_t)


def modulation_rows(pieces, gains, where, place_one):
    rows, columns = pieces[0].shape
    count = len(pieces)
    items = rows // 2

    def body(where_ref, *refs):
        piece_refs, (ga, gb, one_ref, own_ref, send_ref, gains_ref) = refs[:count], refs[count:]
        section, tensor = where_ref[0], where_ref[1]
        values = [ref[...].astype(F32) for ref in piece_refs]
        ordered = []
        for j in range(count):
            picked = jnp.zeros_like(values[0])
            for k in range(count):
                picked = jnp.where((tensor ^ k) == j, values[k], picked)
            ordered.append(picked)
        whole = jnp.concatenate(ordered, axis=1)
        blank = jnp.zeros((8 - items, whole.shape[1]), F32)
        first = jnp.concatenate([whole[:items], blank], axis=0)
        second = jnp.concatenate([whole[items:], blank], axis=0)
        own_ref[...] = jnp.where(section == 0, first, second).astype(BF)
        send_ref[...] = jnp.where(section == 0, second, first).astype(BF)
        a, b = ga[...], gb[...]
        first = jnp.where(section == 0, a, b)
        second = jnp.where(section == 0, b, a)
        both = jnp.concatenate([first, second, jnp.zeros((4, first.shape[1]), F32)], axis=0)
        gains_ref[...] = lax.dot_general(
            both, one_ref[...], (((1,), (0,)), ((), ())), precision=HIGHEST, preferred_element_type=F32
        )

    return call(
        body,
        [shape((8, count * columns), BF)] * 2 + [shape((8, LANE), F32)],
        [SM] + [VM] * count + [FREE] * 3,
        name="modulation_rows",
        limit=8,
    )(where, *pieces, *gains, place_one)


def prepare_tables(where, lengths, positions, rates):
    rows = positions.shape[2]
    share = rows // 4
    items = lengths.shape[2]

    def body(where_ref, len_ref, pos_ref, rate_ref, cos_ref, sin_ref, segc_ref, segr_ref, picks_ref, own_ref):
        section, tensor = where_ref[0], where_ref[1]

        def segments(index):
            place = (tensor ^ (index // share)) * share + index % share
            segment = jnp.zeros_like(index)
            end = 0
            for i in range(items):
                end = end + len_ref[section, 0, i]
                segment += (place >= end).astype(jnp.int32)
            return segment

        column = segments(lax.broadcasted_iota(jnp.int32, (rows, 1), 0))
        segc_ref[...] = column
        segr_ref[...] = segments(lax.broadcasted_iota(jnp.int32, (1, rows), 1))
        picks = jnp.where(column == lax.broadcasted_iota(jnp.int32, (rows, 8), 1), 1.0, 0.0).astype(BF)
        picks_ref[...] = picks
        own_ref[...] = picks[:share]
        blocks = [
            pos_ref[section, :, pl.ds(pl.multiple_of((tensor ^ k) * share, LANE), share)] for k in range(4)
        ]
        place = jnp.concatenate(blocks, axis=1).astype(F32)
        lane = lax.broadcasted_iota(jnp.int32, (LANE // 2, rows), 0)
        phase = jnp.where(lane < HEAD // 4, place[0:1], place[1:2]) * rate_ref[...]
        cosine = jnp.where(lane < HALF, jnp.cos(phase), 0.0)
        sine = jnp.where(lane < HALF, jnp.sin(phase), 0.0)
        cos_ref[...] = jnp.concatenate([cosine, cosine], axis=0).T
        sin_ref[...] = jnp.concatenate([-sine, sine], axis=0).T

    return call(
        body,
        [
            shape((rows, LANE), F32),
            shape((rows, LANE), F32),
            shape((rows, 1), jnp.int32),
            shape((1, rows), jnp.int32),
            shape((rows, 8), BF),
            shape((share, 8), BF),
        ],
        [SM, SM, FREE, FREE],
        name="prepare_tables",
        limit=16,
    )(where, lengths, positions, rates)


def prepare_weights(where, source, place, begun=None, only=None):
    wq, wo = source
    narrow, width = wq.shape[1:]
    padded = place.shape[1]

    def body(where_ref, wq_in, wo_in, place_ref, *refs):
        wq_out, wo_out, wq_ref, wo_ref, wide_ref, tall_ref, sems, out_sems = refs if begun is None else refs[2:]
        section = where_ref[0]

        def make(layer):
            copies = load([(wq_in.at[i], wq_ref.at[i]) for i in range(3)] + [(wo_in, wo_ref)], sems)
            outs = []
            for i in range(3):
                copies[i].wait()
                wide_ref[i] = tn(wq_ref[i], place_ref[...]).astype(BF)
                outs.append(pltpu.make_async_copy(wide_ref.at[i], wq_out.at[layer, i], out_sems.at[i]))
                outs[-1].start()
            copies[3].wait()
            tall_ref[...] = tn(place_ref[...], wo_ref[...]).astype(BF)
            outs.append(pltpu.make_async_copy(tall_ref, wo_out.at[layer], out_sems.at[3]))
            outs[-1].start()
            finish(outs)

        if only is None:
            make(section)
        else:

            @pl.when(section == only)
            def _():
                make(1 - only)

    args = [where, wq, wo, place] + ([] if begun is None else list(begun))
    return call(
        body,
        [shape((2, 3, width, padded), BF), shape((2, padded, width), BF)],
        [SM, HB, HB, FREE] + ([] if begun is None else [HB, HB]),
        [
            pltpu.VMEM((3, narrow, width), BF),
            pltpu.VMEM((narrow, width), BF),
            pltpu.VMEM((3, width, padded), BF),
            pltpu.VMEM((padded, width), BF),
            pltpu.SemaphoreType.DMA((4,)),
            pltpu.SemaphoreType.DMA((4,)),
        ],
        name="prepare_weights",
        limit=24,
        kept=2,
        aliases={} if begun is None else {4: 0, 5: 1},
    )(*args)


def attention_forward(layer, where, blocks, weights, tables, mods, picks, carried=()):
    wq, wo = weights
    cosine, sine, gains, seg_col, seg_row = tables
    padded, width = wo.shape[1:]
    heads = padded // LANE
    raw_input = len(blocks) == 1
    rows = cosine.shape[0]
    share = rows // 4
    scale = HEAD**-0.5
    QB = 512

    def body(where_ref, *refs):
        refs = list(refs)
        in_refs = [refs.pop(0) for _ in blocks]
        wq_in, wo_in, cos_ref, sin_ref, gain_ref, segc_ref, segr_ref, mods_ref, picks_ref = refs[:9]
        refs = refs[9:]
        carried_refs = [refs.pop(0) for _ in carried]
        p_refs = [refs.pop(0) for _ in range(4)]
        state_ref = refs.pop(0) if raw_input else None
        kept = [refs.pop(0) for _ in range(7)]
        carried_outs = [refs.pop(0) for _ in carried]
        wq_ref, wo_ref, mask_ref = refs[:3]
        here = refs[3:10]
        sems, out_sems, carried_sems, a_x_ref, x_sems = refs[10:]
        carried_copies = load(list(zip(carried_refs, carried_outs)), carried_sems)
        if raw_input:
            x_ref = a_x_ref
            x_copies = load(rows_of(in_refs[0], where_ref, x_ref), x_sems)
        qraw_ref, kraw_ref, qrot_ref, krot_ref, v_ref, mixed_ref, a_ref = here
        weights_in = [(wq_in.at[layer, i], wq_ref.at[i]) for i in range(3)] + [(wo_in.at[layer], wo_ref)]
        weights_in = load(weights_in, sems)

        def keep(i):
            pltpu.make_async_copy(here[i], kept[i], out_sems.at[i]).start()

        if raw_input:
            picked = picks_ref[...]
            shift1 = token_mod(picked, mods_ref, 0)
            scale1 = token_mod(picked, mods_ref, 1)
            finish(x_copies)
            state_ref[...] = x_ref[:share]
            x = x_ref[...].astype(F32)
            a_ref[...] = (x * inverse_rms(x) * (1.0 + scale1) + shift1).astype(BF)
        else:
            for k, ref in enumerate(in_refs):
                a_ref[k * share : (k + 1) * share] = ref[...]
        keep(6)
        mask_ref[...] = jnp.where(segc_ref[...] == segr_ref[...], 1.0, 0.0).astype(BF)
        cos = cos_ref[...]
        sin = sin_ref[...]
        for i, (raw_out, rot_out) in enumerate(((qraw_ref, qrot_ref), (kraw_ref, krot_ref))):
            weights_in[i].wait()
            gain = gain_ref[2 * layer + i : 2 * layer + i + 1]
            for h2 in range(0, heads, 2):
                both = nn(a_ref[...], wq_ref[i, :, h2 * LANE : (h2 + 2) * LANE])
                for h in (h2, h2 + 1):
                    at = slice(h * LANE, (h + 1) * LANE)
                    raw = both[:, (h - h2) * LANE : (h - h2 + 1) * LANE]
                    raw_out[:, at] = raw.astype(BF)
                    turned = rotate(raw * head_inverse(raw) * gain, cos, sin)
                    rot_out[:, at] = turned.astype(BF)
            keep(i)
            keep(2 + i)
        weights_in[2].wait()
        one = jnp.where(lax.broadcasted_iota(jnp.int32, (1, padded), 1) % LANE == LANE - 1, 1.0, 0.0)
        v_ref[...] = (nn(a_ref[...], wq_ref[2]) + one).astype(BF)
        keep(4)

        for j in range(rows // QB):
            at_rows = slice(j * QB, (j + 1) * QB)
            for h in range(heads):
                at = slice(h * LANE, (h + 1) * LANE)
                scores = nt(qrot_ref[at_rows, at], krot_ref[:, at]) * scale
                grown = jnp.exp(scores).astype(BF) * mask_ref[at_rows]
                mixed = nn(grown, v_ref[:, at])
                mixed_ref[at_rows, at] = (mixed * (1.0 / mixed[:, LANE - 1 :])).astype(BF)
        keep(5)
        weights_in[3].wait()
        step = 3 * LANE
        for j in range(width // step):
            at = slice(j * step, (j + 1) * step)
            split_store(nn(mixed_ref[...], wo_ref[:, at]), at, p_refs)
        for i in range(7):
            pltpu.make_async_copy(here[i], kept[i], out_sems.at[i]).wait()
        finish(carried_copies)

    outs = [shape((share, width), BF)] * (5 if raw_input else 4)
    saved_shapes = [shape((rows, padded), BF)] * 6 + [shape((rows, width), BF)]
    result = call(
        body,
        outs + saved_shapes + [shape(c.shape, c.dtype) for c in carried],
        [SM] + ([HB] if raw_input else [VM] * 4) + [HB] * 2 + [VM] * (7 + len(carried)),
        [
            pltpu.VMEM((3, width, padded), BF),
            pltpu.VMEM((padded, width), BF),
            pltpu.VMEM((rows, rows), BF),
        ] + [pltpu.VMEM(s.shape, BF) for s in saved_shapes] + [
            pltpu.SemaphoreType.DMA((4,)),
            pltpu.SemaphoreType.DMA((7,)),
            pltpu.SemaphoreType.DMA((max(1, len(carried)),)),
            pltpu.VMEM((rows if raw_input else 16, width), BF),
            pltpu.SemaphoreType.DMA((4,)),
        ],
        name=f"attention_forward_{layer}",
        limit=28,
        kept=7 + len(carried),
    )(where, *blocks, wq, wo, cosine, sine, gains, seg_col, seg_row, mods, picks, *carried)
    n = len(outs)
    return list(result[:4]), list(result[4:n]), list(result[n : n + 7]), list(result[n + 7 :])


def add_parts(refs):
    total = refs[0][...].astype(F32)
    for ref in refs[1:]:
        total += ref[...].astype(F32)
    return total


def after_attention(parts, state, mods, picks):
    dims = state.shape

    def body(p0, p1, p2, p3, state_ref, mods_ref, picks_ref, mlp_ref, attended_ref, after_ref):
        picked = picks_ref[...]
        attended = add_parts((p0, p1, p2, p3))
        attended_ref[...] = attended.astype(BF)
        after = state_ref[...].astype(F32) + token_mod(picked, mods_ref, 2) * attended
        after_ref[...] = after
        normed = after * inverse_rms(after)
        mlp_ref[...] = (normed * (1.0 + token_mod(picked, mods_ref, 4)) + token_mod(picked, mods_ref, 3)).astype(BF)

    return call(
        body,
        [shape(dims, BF), shape(dims, BF), shape(dims, F32)],
        [VM] * 7,
        name="after_attention",
        limit=8,
    )(*parts, state, mods, picks)


def after_mlp(parts, after, mods, picks, mods_next):
    dims = after.shape

    def body(p0, p1, p2, p3, after_ref, mods_ref, picks_ref, next_ref, in_ref, projected_ref, state_ref):
        picked = picks_ref[...]
        projected = add_parts((p0, p1, p2, p3))
        output = after_ref[...] + token_mod(picked, mods_ref, 5) * projected
        low = output.astype(BF)
        state_ref[...] = low
        state = low.astype(F32)
        normed = state * inverse_rms(state)
        in_ref[...] = (normed * (1.0 + token_mod(picked, next_ref, 1)) + token_mod(picked, next_ref, 0)).astype(BF)
        projected_ref[...] = projected.astype(BF)

    return call(
        body,
        [shape(dims, BF)] * 3,
        [VM] * 8,
        name="after_mlp",
        limit=8,
    )(*parts, after, mods, picks, mods_next)


def last_output(parts, after, mods, picks):
    dims = after.shape

    def body(p0_in, p1, p2, p3, after_in, mods_ref, picks_ref, output_ref, projected_out, p0, after_ref, projected_ref, sems, out_sems):
        copies = load([(p0_in, p0), (after_in, after_ref)], sems)
        gate2 = token_mod(picks_ref[...], mods_ref, 5)
        finish(copies)
        projected = add_parts((p0, p1, p2, p3))
        projected_ref[...] = projected.astype(BF)
        kept = load([(projected_ref, projected_out)], out_sems)
        output_ref[...] = after_ref[...] + gate2 * projected
        finish(kept)

    return call(
        body,
        [shape(dims, F32), shape(dims, BF)],
        [HB] + [VM] * 3 + [HB] + [VM] * 2,
        [
            pltpu.VMEM(dims, BF),
            pltpu.VMEM(dims, F32),
            pltpu.VMEM(dims, BF),
            pltpu.SemaphoreType.DMA((2,)),
            pltpu.SemaphoreType.DMA((1,)),
        ],
        name="last_output",
        limit=8,
        kept=1,
    )(*parts, after, mods, picks)


def mlp_forward(layer, blocks, weights, section, carried):
    gu_own, gu_got, wd_own, wd_got = weights
    hidden_size, width = wd_own.shape
    share = blocks[0].shape[0]
    rows = share * 4
    chunk = 2 * LANE
    chunks = hidden_size // chunk

    def body(sec_ref, b0, b1, b2, b3, gu_a, gu_b, wd_a, wd_b, attended_ref, after_ref,
             p0, p1, p2, p3, hid_out, c1_out, c2_out, a_out, attended_out, after_out, p0_out,
             a_ref, gu_ref, wd_ref, hid_ref, c1_ref, c2_ref, sems, out_sems, carried_sems):
        own = sec_ref[0] == layer
        for j in range(chunks):
            at = pl.ds(j * chunk, chunk)
            for i in range(2):
                fetch(own, gu_a.at[i, :, at], gu_b.at[i, :, at], gu_ref.at[i, :, at], sems.at[2 * j + i])
        fetch(own, wd_a, wd_b, wd_ref, sems.at[2 * chunks])
        carried_copies = load([(attended_ref, attended_out), (after_ref, after_out)], carried_sems)
        for k, ref in enumerate((b0, b1, b2, b3)):
            a_ref[k * share : (k + 1) * share] = ref[...]
        for j in range(chunks):
            at = slice(j * chunk, (j + 1) * chunk)
            for i in range(2):
                arrived(gu_a.at[i, :, pl.ds(j * chunk, chunk)], gu_ref.at[i, :, pl.ds(j * chunk, chunk)], sems.at[2 * j + i])
            gate = nn(a_ref[...], gu_ref[0, :, at])
            up = nn(a_ref[...], gu_ref[1, :, at])
            sigma = jax.nn.sigmoid(gate)
            silu = gate * sigma
            hid_ref[:, at] = (silu * up).astype(BF)
            c1_ref[:, at] = (up * (sigma + silu * (1.0 - sigma))).astype(BF)
            c2_ref[:, at] = silu.astype(BF)
        kept = load([(hid_ref, hid_out), (c1_ref, c1_out), (c2_ref, c2_out), (a_ref, a_out)], out_sems)
        arrived(wd_a, wd_ref, sems.at[2 * chunks])
        step = 3 * LANE
        for j in range(width // step):
            at = slice(j * step, (j + 1) * step)
            split_store(nn(hid_ref[...], wd_ref[:, at]), at, (p0, p1, p2, p3))
        kept.append(pltpu.make_async_copy(p0, p0_out, out_sems.at[4]))
        kept[-1].start()
        finish(kept + carried_copies)

    outs = [shape((share, width), BF)] * 4 + [shape((rows, hidden_size), BF)] * 3 + [shape((rows, width), BF)]
    outs += [shape(c.shape, c.dtype) for c in carried] + [shape((share, width), BF)]
    result = call(
        body,
        outs,
        [SM] + [VM] * 4 + [HB] * 4 + [VM] * 2,
        [
            pltpu.VMEM((rows, width), BF),
            pltpu.VMEM(gu_own.shape, BF),
            pltpu.VMEM(wd_own.shape, BF),
        ]
        + [pltpu.VMEM((rows, hidden_size), BF)] * 3
        + [
            pltpu.SemaphoreType.DMA((2 * chunks + 1,)),
            pltpu.SemaphoreType.DMA((5,)),
            pltpu.SemaphoreType.DMA((2,)),
        ],
        name=f"mlp_forward_{layer}",
        kept=7,
    )(section, *blocks, gu_own, gu_got, wd_own, wd_got, *carried)
    return list(result[:4]), list(result[4:8]), list(result[8:])


def mlp_backward(layer, where, blocks, weights, saved, carried):
    gu_own, gu_got, wd_own, wd_got = weights
    c1, c2 = saved
    hidden_size, width = wd_own.shape
    rows = c1.shape[0]
    share = rows // 4
    chunk = 2 * LANE
    chunks = hidden_size // chunk

    def body(where_ref, *refs):
        refs = list(refs)
        in_refs = [refs.pop(0) for _ in blocks]
        gu_a, gu_b, wd_a, wd_b, c1_in, c2_in = refs[:6]
        refs = refs[6:]
        carried_refs = [refs.pop(0) for _ in carried]
        p_refs = [refs.pop(0) for _ in range(3)]
        outs = [refs.pop(0) for _ in range(4)]
        carried_outs = [refs.pop(0) for _ in carried]
        gu_ref, wd_ref, c1_ref, c2_ref, gg_ref, gup_ref, gp_ref, p0, sems, in_sems, out_sems, carried_sems = refs
        own = where_ref[0] == layer
        for j in range(chunks):
            at = pl.ds(j * chunk, chunk)
            fetch(own, wd_a.at[at], wd_b.at[at], wd_ref.at[at], sems.at[j])
        saved_copies = load([(c1_in, c1_ref), (c2_in, c2_ref)], in_sems)
        for i in range(2):
            fetch(own, gu_a.at[i], gu_b.at[i], gu_ref.at[i], sems.at[chunks + i])
        kept = load(list(zip(carried_refs, carried_outs)), carried_sems)
        for k, ref in enumerate(in_refs):
            gp_ref[k * share : (k + 1) * share] = ref[...]

        def keep(i, here):
            kept.append(pltpu.make_async_copy(here, outs[i], out_sems.at[i]))
            kept[-1].start()

        keep(0, gp_ref)
        for j in range(chunks):
            at = slice(j * chunk, (j + 1) * chunk)
            arrived(wd_a.at[pl.ds(j * chunk, chunk)], wd_ref.at[pl.ds(j * chunk, chunk)], sems.at[j])
            grad_hidden = nt(gp_ref[...], wd_ref[at])
            if j == 0:
                finish(saved_copies)
            gg_ref[:, at] = (grad_hidden * c1_ref[:, at].astype(F32)).astype(BF)
            gup_ref[:, at] = (grad_hidden * c2_ref[:, at].astype(F32)).astype(BF)
        keep(1, gg_ref)
        keep(2, gup_ref)
        for i in range(2):
            arrived(gu_a.at[i], gu_ref.at[i], sems.at[chunks + i])
        step = 3 * LANE
        for j in range(width // step):
            at = slice(j * step, (j + 1) * step)
            split_store(nt(gg_ref[...], gu_ref[0, at]) + nt(gup_ref[...], gu_ref[1, at]), at, [p0] + p_refs)
        keep(3, p0)
        finish(kept)

    outs = [shape((share, width), BF)] * 3
    outs += [shape((rows, width), BF)] + [shape((rows, hidden_size), BF)] * 2 + [shape((share, width), BF)]
    outs += [shape(c.shape, c.dtype) for c in carried]
    result = call(
        body,
        outs,
        [SM] + [VM] * 4 + [HB] * 6 + [VM] * len(carried),
        [
            pltpu.VMEM(gu_own.shape, BF),
            pltpu.VMEM(wd_own.shape, BF),
        ]
        + [pltpu.VMEM((rows, hidden_size), BF)] * 4
        + [
            pltpu.VMEM((rows, width), BF),
            pltpu.VMEM((share, width), BF),
            pltpu.SemaphoreType.DMA((chunks + 2,)),
            pltpu.SemaphoreType.DMA((2,)),
            pltpu.SemaphoreType.DMA((4,)),
            pltpu.SemaphoreType.DMA((max(1, len(carried)),)),
        ],
        name=f"mlp_backward_{layer}",
        kept=4 + len(carried),
    )(where, *blocks, gu_own, gu_got, wd_own, wd_got, c1, c2, *carried)
    return list(result[:3]), list(result[3:6]), list(result[6:])


def mlp_backward_last(layer, where, cotangent, weights, saved, mods, picks):
    gu_own, gu_got, wd_own, wd_got = weights
    hidden, c1, c2, mlp_in = saved
    hidden_size, width = wd_own.shape
    rows = c1.shape[0]
    share = rows // 4
    chunk = 2 * LANE
    chunks = hidden_size // chunk
    step = 3 * LANE
    size = hidden_size

    def body(where_ref, cot_in, gu_a, gu_b, wd_a, wd_b, hid_in, c1_in, c2_in, a_in, mods_ref, picks_ref, *refs):
        refs = list(refs)
        p_refs = [refs.pop(0) for _ in range(3)]
        (out, p0_out, p0, gu_ref, wd_ref, c1_ref, c2_ref, gg_ref, gup_ref, hid_ref, gp_ref, a_ref, full_ref,
         sems, in_sems, cot_sems, out_sems) = refs
        own = where_ref[0] == layer
        cot_copies = load(rows_of(cot_in, where_ref, gp_ref), cot_sems)
        for j in range(chunks):
            at = pl.ds(j * chunk, chunk)
            fetch(own, wd_a.at[at], wd_b.at[at], wd_ref.at[at], sems.at[j])
        ins = load([(c1_in, c1_ref), (c2_in, c2_ref), (hid_in, hid_ref), (a_in, a_ref)], in_sems)
        for i in range(2):
            fetch(own, gu_a.at[i], gu_b.at[i], gu_ref.at[i], sems.at[chunks + i])
        kept = []
        finish(cot_copies)
        gp_ref[...] = (gp_ref[...].astype(F32) * token_mod(picks_ref[...], mods_ref, 5)).astype(BF)
        for j in range(chunks):
            at = slice(j * chunk, (j + 1) * chunk)
            arrived(wd_a.at[pl.ds(j * chunk, chunk)], wd_ref.at[pl.ds(j * chunk, chunk)], sems.at[j])
            grad_hidden = nt(gp_ref[...], wd_ref[at])
            if j == 0:
                finish(ins[:2])
            gg_ref[:, at] = (grad_hidden * c1_ref[:, at].astype(F32)).astype(BF)
            gup_ref[:, at] = (grad_hidden * c2_ref[:, at].astype(F32)).astype(BF)
        finish(ins[2:])
        for j in range(width // step):
            at = slice(j * step, (j + 1) * step)
            left = a_ref[:, at]
            full_ref[at, :size] = tn(left, gg_ref[...]).astype(BF)
            full_ref[at, size : 2 * size] = tn(left, gup_ref[...]).astype(BF)
            full_ref[at, 2 * size :] = tn(gp_ref[:, at], hid_ref[...]).astype(BF)
            here = pl.ds(j * step, step)
            kept.append(pltpu.make_async_copy(full_ref.at[here], out.at[here], out_sems.at[j]))
            kept[-1].start()
        for i in range(2):
            arrived(gu_a.at[i], gu_ref.at[i], sems.at[chunks + i])
        for j in range(width // step):
            at = slice(j * step, (j + 1) * step)
            split_store(nt(gg_ref[...], gu_ref[0, at]) + nt(gup_ref[...], gu_ref[1, at]), at, [p0] + p_refs)
        kept += load([(p0, p0_out)], cot_sems)
        finish(kept)

    outs = [shape((share, width), BF)] * 3 + [shape((width, 3 * size), BF), shape((share, width), BF)]
    result = call(
        body,
        outs,
        [SM] + [HB] * 9 + [VM] * 2,
        [
            pltpu.VMEM((share, width), BF),
            pltpu.VMEM(gu_own.shape, BF),
            pltpu.VMEM(wd_own.shape, BF),
        ]
        + [pltpu.VMEM((rows, hidden_size), BF)] * 5
        + [
            pltpu.VMEM((rows, width), BF),
            pltpu.VMEM((rows, width), BF),
            pltpu.VMEM((width, 3 * size), BF),
            pltpu.SemaphoreType.DMA((chunks + 2,)),
            pltpu.SemaphoreType.DMA((4,)),
            pltpu.SemaphoreType.DMA((4,)),
            pltpu.SemaphoreType.DMA((width // step,)),
        ],
        name=f"mlp_backward_{layer}",
        kept=2,
        limit=32,
    )(where, cotangent, gu_own, gu_got, wd_own, wd_got, hidden, c1, c2, mlp_in, mods, picks)
    return [result[4]] + list(result[:3]), result[3]


def mlp_weight_grads(mlp_in, grads, hidden):
    grad_projected, grad_gate, grad_up = grads
    rows, width = grad_projected.shape
    size = hidden.shape[1]
    step = 3 * LANE

    def body(a_in, gg_in, gu_in, gp_in, hid_in, *refs):
        out, a_ref, gg_ref, gu_ref, gp_ref, hid_ref, full_ref, in_sems, sems = refs
        ins = load([(a_in, a_ref), (gg_in, gg_ref), (gu_in, gu_ref), (gp_in, gp_ref), (hid_in, hid_ref)], in_sems)
        kept = []
        finish(ins[:2])
        for j in range(width // step):
            at = slice(j * step, (j + 1) * step)
            left = a_ref[:, at]
            full_ref[at, :size] = tn(left, gg_ref[...]).astype(BF)
            if j == 0:
                ins[2].wait()
            full_ref[at, size : 2 * size] = tn(left, gu_ref[...]).astype(BF)
            if j == 0:
                finish(ins[3:])
            full_ref[at, 2 * size :] = tn(gp_ref[:, at], hid_ref[...]).astype(BF)
            here = pl.ds(j * step, step)
            kept.append(pltpu.make_async_copy(full_ref.at[here], out.at[here], sems.at[j]))
            kept[-1].start()
        finish(kept)

    result = call(
        body,
        [shape((width, 3 * size), BF)],
        [HB] * 5,
        [pltpu.VMEM((rows, width), BF)]
        + [pltpu.VMEM((rows, size), BF)] * 2
        + [
            pltpu.VMEM((rows, width), BF),
            pltpu.VMEM((rows, size), BF),
            pltpu.VMEM((width, 3 * size), BF),
            pltpu.SemaphoreType.DMA((5,)),
            pltpu.SemaphoreType.DMA((width // step,)),
        ],
        name="mlp_weight_grads",
        kept=1,
    )(mlp_in, grad_gate, grad_up, grad_projected, hidden)
    return result[0]


def attention_backward(layer, blocks, weights, saved, tables, grad_after):
    wq, wo = weights
    cosine, sine, gains, seg_col, seg_row = tables
    rows, padded = saved[0].shape
    width = wo.shape[2]
    heads = padded // LANE
    share = rows // 4
    scale = HEAD**-0.5
    QB = 512

    def body(b0, b1, b2, b3, wq_in, wo_in, qraw_in, kraw_in, qrot_in, krot_in, v_in,
             cos_ref, sin_ref, gain_ref, segc_ref, segr_ref, grad_ref,
             p1, p2, p3, g_out, ga_out, p0_out, ggain_out, grad_out,
             wq_ref, wo_ref, qraw_ref, kraw_ref, qrot_ref, krot_ref, v_ref, mask_ref,
             ga_ref, gmix_ref, gq_ref, gk_ref, g_ref, p0, ggain_ref, sems, in_sems):
        ins = [(wo_in.at[layer], wo_ref)]
        ins += [(qrot_in, qrot_ref), (krot_in, krot_ref), (v_in, v_ref), (qraw_in, qraw_ref), (kraw_in, kraw_ref)]
        ins += [(wq_in.at[layer, i], wq_ref.at[i]) for i in range(3)]
        ins = load(ins, in_sems)
        for k, ref in enumerate((b0, b1, b2, b3)):
            ga_ref[k * share : (k + 1) * share] = ref[...]
        kept = []

        def keep(here, there):
            kept.append(pltpu.make_async_copy(here, there, sems.at[len(kept)]))
            kept[-1].start()

        keep(ga_ref, ga_out)
        keep(grad_ref, grad_out)
        mask_ref[...] = jnp.where(segc_ref[...] == segr_ref[...], 1.0, 0.0).astype(BF)
        ins[0].wait()
        gmix_ref[...] = nt(ga_ref[...], wo_ref[...]).astype(BF)
        finish(ins[1:4])
        for h in range(heads):
            at = slice(h * LANE, (h + 1) * LANE)
            for j in range(rows // QB):
                at_rows = slice(j * QB, (j + 1) * QB)
                query = qrot_ref[at_rows, at]
                grad_mixed = gmix_ref[at_rows, at]
                scores = nt(krot_ref[:, at], query) * scale
                grown = (jnp.exp(scores).astype(BF) * mask_ref[:, at_rows]).astype(F32)
                weights_t = grown * (1.0 / jnp.sum(grown, axis=0, keepdims=True))
                grad_weights = nt(v_ref[:, at], grad_mixed)
                add_v = nn(weights_t.astype(BF), grad_mixed)
                product = weights_t * grad_weights
                delta = jnp.sum(product, axis=0, keepdims=True)
                grad_scores = (product - weights_t * delta).astype(BF)
                gq_ref[at_rows, at] = tn(grad_scores, krot_ref[:, at])
                add_k = nn(grad_scores, query)
                total_v = add_v if j == 0 else total_v + add_v
                total_k = add_k if j == 0 else total_k + add_k
            gk_ref[:, at] = total_k
            g_ref[:, 2 * padded + h * LANE : 2 * padded + (h + 1) * LANE] = total_v.astype(BF)
        cos = cos_ref[...]
        sin = sin_ref[...]
        finish(ins[4:6])
        ggain_ref[...] = jnp.zeros_like(ggain_ref)
        for i, (raw_ref, grad_ref) in enumerate(((qraw_ref, gq_ref), (kraw_ref, gk_ref))):
            gain = gain_ref[2 * layer + i : 2 * layer + i + 1]
            gain_sum = jnp.zeros((1, LANE), F32)
            for h in range(heads):
                at = slice(h * LANE, (h + 1) * LANE)
                raw = raw_ref[:, at].astype(F32)
                inverse = head_inverse(raw)
                normed = raw * inverse
                turned = unrotate(grad_ref[:, at], cos, sin) * scale
                product = turned * normed
                gain_sum += jnp.sum(product, axis=0, keepdims=True)
                back = inverse * (turned * gain - normed * head_mean(product * gain))
                g_ref[:, i * padded + h * LANE : i * padded + (h + 1) * LANE] = back.astype(BF)
            ggain_ref[i : i + 1] = gain_sum
        keep(g_ref, g_out)
        keep(ggain_ref, ggain_out)
        finish(ins[6:])
        step = 3 * LANE
        for j in range(width // step):
            at = slice(j * step, (j + 1) * step)
            total = nt(g_ref[:, :padded], wq_ref[0, at])
            total += nt(g_ref[:, padded : 2 * padded], wq_ref[1, at])
            total += nt(g_ref[:, 2 * padded :], wq_ref[2, at])
            split_store(total, at, (p0, p1, p2, p3))
        keep(p0, p0_out)
        finish(kept)

    outs = [shape((share, width), BF)] * 3
    outs += [shape((rows, 3 * padded), BF), shape((rows, width), BF), shape((share, width), BF), shape((8, LANE), F32)]
    outs += [shape(grad_after.shape, F32)]
    result = call(
        body,
        outs,
        [VM] * 4 + [HB] * 7 + [VM] * 6,
        [
            pltpu.VMEM((3, width, padded), BF),
            pltpu.VMEM((padded, width), BF),
        ]
        + [pltpu.VMEM((rows, padded), BF)] * 5
        + [
            pltpu.VMEM((rows, rows), BF),
            pltpu.VMEM((rows, width), BF),
            pltpu.VMEM((rows, padded), BF),
            pltpu.VMEM((rows, padded), F32),
            pltpu.VMEM((rows, padded), F32),
            pltpu.VMEM((rows, 3 * padded), BF),
            pltpu.VMEM((share, width), BF),
            pltpu.VMEM((8, LANE), F32),
            pltpu.SemaphoreType.DMA((5,)),
            pltpu.SemaphoreType.DMA((9,)),
        ],
        name=f"attention_backward_{layer}",
        limit=32,
        kept=5,
    )(*blocks, wq, wo, *saved[:5], cosine, sine, gains, seg_col, seg_row, grad_after)
    return list(result[:3]), list(result[3:])


def attention_weight_grads(attention_in, grads, mixed, grad_attended, place):
    rows, width = attention_in.shape
    padded, narrow = place.shape
    step = 3 * LANE


    def body(a_in, g_in, mixed_in, ga_in, place_ref, out, a_ref, g_ref, mixed_ref, ga_ref, right_ref, full_ref, in_sems, sems):
        ins = load([(g_in, g_ref), (mixed_in, mixed_ref), (a_in, a_ref), (ga_in, ga_ref)], in_sems)
        finish(ins[:2])
        for i in range(3):
            right_ref[i] = nn(g_ref[:, i * padded : (i + 1) * padded], place_ref[...]).astype(BF)
        right_ref[3] = nn(mixed_ref[...], place_ref[...]).astype(BF)
        finish(ins[2:])
        kept = []
        for j in range(width // step):
            at = slice(j * step, (j + 1) * step)
            left = a_ref[:, at]
            for i in range(3):
                full_ref[at, i * narrow : (i + 1) * narrow] = tn(left, right_ref[i]).astype(BF)
            full_ref[at, 3 * narrow :] = tn(ga_ref[:, at], right_ref[3]).astype(BF)
            here = pl.ds(j * step, step)
            kept.append(pltpu.make_async_copy(full_ref.at[here], out.at[here], sems.at[j]))
            kept[-1].start()
        finish(kept)

    result = call(
        body,
        [shape((width, 4 * narrow), BF)],
        [HB] * 4 + [FREE],
        [
            pltpu.VMEM((rows, width), BF),
            pltpu.VMEM((rows, 3 * padded), BF),
            pltpu.VMEM((rows, padded), BF),
            pltpu.VMEM((rows, width), BF),
            pltpu.VMEM((4, rows, narrow), BF),
            pltpu.VMEM((width, 4 * narrow), BF),
            pltpu.SemaphoreType.DMA((4,)),
            pltpu.SemaphoreType.DMA((width // step,)),
        ],
        name="attention_weight_grads",
        kept=1,
    )(attention_in, grads, mixed, grad_attended, place)
    return result[0]


def own_rows(whole, where_ref, here):
    return rows_of(whole, where_ref, here) if len(whole.shape) == 3 else [(whole, here)]


def back_of_mlp(where, parts, grad_out, after, attended, projected, mods, picks):
    dims = after.shape

    def body(where_ref, p0_in, p1, p2, p3, g_in, after_in, attended_in, projected_in, mods_ref, picks_ref,
             ga_ref, grad_ref, sums_out,
             p0, g_ref, after_ref, attended_ref, projected_ref, sums_ref, sems, out_sems):
        pairs = [(p0_in, p0), (after_in, after_ref)] + own_rows(g_in, where_ref, g_ref)
        ins = load(pairs + [(attended_in, attended_ref), (projected_in, projected_ref)], sems)
        picked = picks_ref[...]
        scale2 = token_mod(picked, mods_ref, 4)
        gate1 = token_mod(picked, mods_ref, 2)
        finish(ins[:2])
        grad_in = add_parts((p0, p1, p2, p3))
        after = after_ref[...]
        inverse = inverse_rms(after)
        normed = after * inverse
        finish(ins[2:])
        g = g_ref[...].astype(F32)
        grad_after = g + norm_back(grad_in * (1.0 + scale2), normed, inverse)
        sums_ref[0] = image_sums(picked, grad_after * attended_ref[...].astype(F32))
        sums_ref[1] = image_sums(picked, grad_in)
        sums_ref[2] = image_sums(picked, grad_in * normed)
        sums_ref[3] = image_sums(picked, g * projected_ref[...].astype(F32))
        kept = load([(sums_ref, sums_out)], out_sems)
        grad_ref[...] = grad_after
        ga_ref[...] = (grad_after * gate1).astype(BF)
        finish(kept)

    return call(
        body,
        [shape(dims, BF), shape(dims, F32), shape((4, picks.shape[1], dims[1]), F32)],
        [SM, HB] + [VM] * 3 + [HB] * 4 + [VM] * 2,
        [
            pltpu.VMEM(dims, BF),
            pltpu.VMEM(dims, BF),
            pltpu.VMEM(dims, F32),
            pltpu.VMEM(dims, BF),
            pltpu.VMEM(dims, BF),
            pltpu.VMEM((4, picks.shape[1], dims[1]), F32),
            pltpu.SemaphoreType.DMA((5,)),
            pltpu.SemaphoreType.DMA((1,)),
        ],
        name="back_of_mlp",
        limit=10,
        kept=1,
    )(where, *parts, grad_out, after, attended, projected, mods, picks)


def back_of_attention(where, parts, grad_after, state, mods, picks, mods_below):
    first = mods_below is None
    dims = grad_after.shape

    def body(where_ref, p0_in, p1, p2, p3, grad_in_ref, state_in, mods_ref, picks_ref, *refs):
        refs = list(refs)
        below_ref = None if first else refs.pop(0)
        sums_ref = refs.pop(0)
        gp_ref = None if first else refs.pop(0)
        out_ref, p0, grad_ref, state_ref, sems = refs
        ins = load([(p0_in, p0), (grad_in_ref, grad_ref)] + own_rows(state_in, where_ref, state_ref), sems)
        picked = picks_ref[...]
        scale1 = token_mod(picked, mods_ref, 1)
        finish(ins)
        grad_in = add_parts((p0, p1, p2, p3))
        state = state_ref[...].astype(F32)
        inverse = inverse_rms(state)
        normed = state * inverse
        grad_state = grad_ref[...] + norm_back(grad_in * (1.0 + scale1), normed, inverse)
        out_ref[...] = grad_state.astype(out_ref.dtype)
        if not first:
            gp_ref[...] = (grad_state.astype(BF).astype(F32) * token_mod(picked, below_ref, 5)).astype(BF)
        sums_ref[0] = image_sums(picked, grad_in)
        sums_ref[1] = image_sums(picked, grad_in * normed)

    outs = [shape((2, picks.shape[1], dims[1]), F32)] + ([shape(dims, F32)] if first else [shape(dims, BF)] * 2)
    extra = () if first else (mods_below,)
    return call(
        body,
        outs,
        [SM, HB] + [VM] * 3 + [HB] * 2 + [VM] * (2 + len(extra)),
        [
            pltpu.VMEM(dims, BF),
            pltpu.VMEM(dims, F32),
            pltpu.VMEM(dims, BF),
            pltpu.SemaphoreType.DMA((3,)),
        ],
        name="back_of_attention",
        limit=10,
    )(where, *parts, grad_after, state, mods, picks, *extra)


def exchange(value, axis, k):
    return lax.ppermute(value, axis, [(i, i ^ k) for i in range(lax.axis_size(axis))])


def send_parts(parts):
    got = {k: exchange(parts[k], "tensor", k) for k in (3, 1, 2)}
    return [parts[0], got[1], got[2], got[3]]


def gather_blocks(own):
    got = {k: exchange(own, "tensor", k) for k in (3, 1, 2)}
    return [own, got[1], got[2], got[3]]


def group_sum(value, axis):
    k = 1
    while k < lax.axis_size(axis):
        value = value + exchange(value, axis, k)
        k *= 2
    return value


def gather_dp(value):
    count = lax.axis_size("dp")
    if count > 4:
        return lax.all_gather(value, "dp", axis=0)
    me = lax.axis_index("dp")
    got = [value] + [exchange(value, "dp", k) for k in range(1, count)]
    stacked = jnp.stack(got)
    return jnp.stack([lax.dynamic_index_in_dim(stacked, me ^ j, 0, keepdims=False) for j in range(count)])


def head_places(heads):
    place = np.zeros((heads * HEAD, heads * LANE), np.float32)
    for h in range(heads):
        for j in range(HEAD):
            place[h * HEAD + j, h * LANE + (j // HALF) * (LANE // 2) + j % HALF] = 1.0
    return place


def shards(
    inputs,
    cotangent,
    conditioning,
    lengths,
    positions,
    modulator,
    projections,
    norm_gains,
    out_weight,
    gate_up,
    down_weight,
):
    section = lax.axis_index("section")
    other = 1 - section
    tensor = lax.axis_index("tensor")
    data = lax.axis_index("dp")
    micro, _, width = inputs.shape
    rows = inputs.shape[1]
    group = lax.axis_size("tensor")
    share = rows // group
    items = lengths.shape[2]
    narrow = projections.shape[3]
    heads = narrow // HEAD
    columns = modulator.shape[2]
    sec = section.reshape(1).astype(jnp.int32)

    where = jnp.stack([section, tensor]).astype(jnp.int32)
    is_first = section == 0

    where = jnp.stack([section, tensor]).astype(jnp.int32)
    is_first = section == 0
    place = jnp.asarray(head_places(heads), BF)
    place_one = jnp.asarray(head_places(1), F32)

    own = (jnp.swapaxes(projections[0], 1, 2), out_weight[0])
    got = [exchange(value, "section", 1) for value in own]
    got_gains = exchange(norm_gains[0], "section", 1)
    scaled, part = modulation_part(conditioning, jnp.swapaxes(modulator[0], 0, 1))
    pieces = gather_blocks(part)
    quarter = HEAD // 4
    rates = 10000.0 ** (-jnp.arange(quarter).astype(F32) / quarter)
    rates = jnp.concatenate([rates, rates, jnp.zeros(LANE // 2 - HALF, F32)])[:, None]
    where_late, part = lax.optimization_barrier((where, part))
    cosine, sine, seg_col, seg_row, picks, picks_own = prepare_tables(where_late, lengths, positions, rates)
    wq, wo = prepare_weights(where_late, own, place)
    pieces, got, cosine, wq = lax.optimization_barrier((pieces, got, cosine, wq))
    mods_own, mods_send, gains = modulation_rows([part] + pieces[1:], (norm_gains[0], got_gains), where, place_one)
    mods_got = exchange(mods_send, "section", 1)
    gu_send, wd_send, mods_got = lax.optimization_barrier((gate_up[0], down_weight[0], mods_got))
    mods = [jnp.where(is_first, mods_own, mods_got), jnp.where(is_first, mods_got, mods_own)]
    gu_got = exchange(gu_send, "section", 1)
    wd_got = exchange(wd_send, "section", 1)
    mlp_weights = (gate_up[0], gu_got, down_weight[0], wd_got)
    wq, mods_first = lax.optimization_barrier((wq, mods[0]))
    mods[0] = mods_first
    wq, wo = prepare_weights(where, got, place, (wq, wo), 1)
    tables = (cosine, sine, gains, seg_col, seg_row)

    cache = []
    attention_blocks = [inputs]
    carried = ()
    for l in range(2):
        partial, state, saved, kept = attention_forward(
            l, where, attention_blocks, (wq, wo), tables, mods[l], picks, carried
        )
        parts = send_parts(partial)
        if l == 0:
            state = state[0]
            wq, mixed = lax.optimization_barrier((wq, saved[5]))
            saved[5] = mixed
            wq, wo = prepare_weights(where, got, place, (wq, wo), 0)
            parts, wq = lax.optimization_barrier((parts, wq))
        else:
            cache[0].append(kept[0])
            state = carried[1]
            state_kept = kept[1]
        mlp_in, attended, after = after_attention(parts, state, mods[l], picks_own)
        partial, mlp_saved, kept = mlp_forward(l, gather_blocks(mlp_in), mlp_weights, sec, (attended, after))
        parts = send_parts(partial)
        cache.append([saved, mlp_saved] + kept)
        if l == 0:
            attention_in, projected, state = after_mlp(parts, after, mods[0], picks_own, mods[1])
            carried = (projected, state)
            attention_blocks = gather_blocks(attention_in)

    item_sums = [None, None]
    gain_sums = [None, None]
    shares = [None, None]

    def data_sum(value):
        return lax.psum_scatter(value, ("dp", "section"), scatter_dimension=0, tiled=True)

    for l in (1, 0):
        saved, (hidden, c1, c2, mlp_in), attended, after, own_partial = cache[l][:5]
        mixed, attention_in = saved[5:]
        if l == 1:
            partial, mlp_grads = mlp_backward_last(l, where, cotangent, mlp_weights, cache[1][1], mods[1], picks)
            parts, partial[1:], mlp_grads = lax.optimization_barrier((parts, partial[1:], mlp_grads))
            output, projected = last_output([own_partial] + parts[1:], after, mods[1], picks_own)
            mlp_share = data_sum(mlp_grads)
            parts = send_parts(partial)
            grad_out = cotangent
        else:
            partial, grads, kept = mlp_backward(
                l, where, grad_blocks, mlp_weights, (c1, c2), [grad_out]
            )
            projected = cache[0][5]
            grad_out = kept[1]
            mlp_grads = mlp_weight_grads(mlp_in, grads, hidden)
            parts, mlp_grads, earlier = lax.optimization_barrier(
                (send_parts([kept[0]] + partial)[1:], mlp_grads, shares[1][1])
            )
            parts = [kept[0]] + parts
            shares[1] = (shares[1][0], earlier)
            mlp_share = data_sum(mlp_grads)
        grad_attended, grad_after, sums2 = back_of_mlp(
            where, parts, grad_out, after, attended, projected, mods[l], picks_own
        )
        blocks = gather_blocks(grad_attended)
        partial, kept = attention_backward(l, blocks, (wq, wo), saved, tables, grad_after)
        grads, grad_attended, own, gain_sums[l], grad_after = kept
        attention_grads = attention_weight_grads(attention_in, grads, mixed, grad_attended, place.T)
        parts, attention_grads, mlp_share = lax.optimization_barrier(
            (send_parts([own] + partial)[1:], attention_grads, mlp_share)
        )
        parts = [own] + parts
        attention_share = data_sum(attention_grads)
        if l == 1:
            sums1, grad_projected, grad_out = back_of_attention(
                where, parts, grad_after, state_kept, mods[1], picks_own, mods[0]
            )
            grad_blocks = gather_blocks(grad_projected)
        else:
            sums1, grad_state = back_of_attention(where, parts, grad_after, inputs, mods[0], picks_own, None)
        item_sums[l] = jnp.concatenate([sums1, sums2], axis=0)
        shares[l] = (mlp_share, attention_share)

    mine = jnp.where(is_first, grad_state, output)
    theirs = exchange(jnp.where(is_first, output, grad_state), "section", 1)
    results = jnp.stack([jnp.where(is_first, mine, theirs), jnp.where(is_first, theirs, mine)])

    def joined(which):
        mine = jnp.where(is_first, shares[0][which], shares[1][which])
        theirs = exchange(jnp.where(is_first, shares[1][which], shares[0][which]), "section", 1)
        low = jnp.where(is_first, mine, theirs)
        high = jnp.where(is_first, theirs, mine)
        return jnp.concatenate([low, high], axis=0).astype(F32)

    size = down_weight.shape[1]
    mlp_grads = joined(0)
    grad_pair = jnp.stack([mlp_grads[:, :size], mlp_grads[:, size : 2 * size]])
    grad_down = mlp_grads[:, 2 * size :].T
    attention_grads = joined(1)
    grad_qkv = jnp.stack([attention_grads[:, i * narrow : (i + 1) * narrow] for i in range(3)])
    grad_out_w = attention_grads[:, 3 * narrow :].T

    sums = jnp.stack(item_sums)[:, :, :items].transpose(0, 2, 1, 3).reshape(2 * items, 6 * width)
    gain_parts = jnp.concatenate([jnp.concatenate([g[0:1], g[1:2]], axis=1) for g in gain_sums])
    gain_parts = jnp.pad(gain_parts, ((0, 2 * items - 2), (0, 0)))
    pieces = [
        jnp.concatenate([lax.dynamic_slice_in_dim(sums, (tensor ^ k) * columns, columns, 1), gain_parts], axis=1)
        for k in range(group)
    ]
    got = send_parts(pieces)
    total = (got[0] + got[1]) + (got[2] + got[3])
    layers = total[:, :columns].reshape(2, items, columns).astype(BF).astype(F32)
    gain_rows = jnp.pad(total[:2, None, columns:], ((0, 0), (0, items - 1), (0, 0)))
    layers = jnp.concatenate([layers, gain_rows], axis=2)
    mine = jnp.where(is_first, layers[0], layers[1])
    theirs = exchange(jnp.where(is_first, layers[1], layers[0]), "section", 1)
    gain_total = mine[0:1, columns:] + theirs[0:1, columns:]
    mods_grad = jnp.concatenate(
        [jnp.where(is_first, mine, theirs)[:, :columns], jnp.where(is_first, theirs, mine)[:, :columns]]
    )
    packed = jnp.concatenate(
        [mods_grad, scaled.astype(F32), jnp.pad(gain_total, ((0, 2 * items - 1), (0, 0)))], axis=1
    )
    gathered = gather_dp(packed)
    all_mods = gathered[:, :, :columns].astype(BF)
    deep = width // lax.axis_size("dp")
    scaled_share = lax.dynamic_slice_in_dim(gathered, columns + data * deep, deep, 2).astype(BF)
    grad_ada = jnp.einsum("nid,nic->dc", scaled_share, all_mods, preferred_element_type=F32)
    gain_total = jnp.sum(gathered[:, 0, columns + width :], axis=0)
    cond_value = conditioning[:, 0].astype(F32)
    sigma = jax.nn.sigmoid(cond_value)
    cond_part = jnp.einsum("ic,dc->id", mods_grad.astype(BF), modulator[0], preferred_element_type=F32)
    cond_part = cond_part.reshape(micro, items, width) * sigma * (1.0 + cond_value * (1.0 - sigma))
    grad_cond = group_sum(group_sum(cond_part, "section"), "tensor")
    half = LANE // 2
    gain_total = gain_total.reshape(2, LANE)
    grad_gains = jnp.concatenate([gain_total[:, :HALF], gain_total[:, half : half + HALF]], axis=1)
    return (
        grad_ada[None],
        grad_qkv[None],
        grad_gains[None],
        grad_out_w[None],
        grad_pair[None],
        grad_down[None],
        grad_cond[:, None],
        results[None],
    )


def solution(mesh):
    return jax.shard_map(
        shards,
        mesh=mesh,
        in_specs=(
            P(None, "dp", None),
            P(None, "dp", None),
            P(None, "dp", None, None),
            P(None, "dp", None),
            P(None, None, "dp"),
            P("section", None, "tensor"),
            P("section", None, None, "tensor"),
            P("section", None, None),
            P("section", "tensor", None),
            P("section", None, None, "tensor"),
            P("section", "tensor", None),
        ),
        out_specs=(
            P("section", "dp", "tensor"),
            P("section", None, "dp", "tensor"),
            P("section", None, None),
            P("section", "tensor", "dp"),
            P("section", None, "dp", "tensor"),
            P("section", "tensor", "dp"),
            P(None, "dp", None, None),
            P("section", None, ("dp", "tensor"), None),
        ),
        check_vma=False,
    )
```

```python
import functools

import jax
import jax.numpy as jnp
from jax import lax
from jax.experimental import pallas as pl
from jax.experimental.pallas import tpu as pltpu
from jax.sharding import PartitionSpec as P
import numpy as np

HEAD = 72
HALF = HEAD // 2
LANE = 128
epsilon = 1e-06
BF = jnp.bfloat16
F32 = jnp.float32
HIGHEST = lax.Precision.HIGHEST
VM = pl.BlockSpec(memory_space=pltpu.VMEM)
SM = pl.BlockSpec(memory_space=pltpu.SMEM)
HB = pl.BlockSpec(memory_space=pltpu.HBM)
FREE = pl.BlockSpec(memory_space=pltpu.VMEM)


def nn(a, b):
    return lax.dot_general(a, b, (((1,), (0,)), ((), ())), preferred_element_type=F32)


def nt(a, b):
    return lax.dot_general(a, b, (((1,), (1,)), ((), ())), preferred_element_type=F32)


def tn(a, b):
    return lax.dot_general(a, b, (((0,), (0,)), ((), ())), preferred_element_type=F32)


def call(body, outs, in_specs, scratch=(), name=None, kept=0, limit=24, aliases={}):
    small = len(outs) - kept
    kernel = pl.pallas_call(
        body,
        out_shape=[pltpu.VMEM(o.shape, o.dtype) for o in outs[:small]] + [pltpu.HBM(o.shape, o.dtype) for o in outs[small:]],
        in_specs=in_specs,
        out_specs=[VM] * small + [HB] * kept,
        scratch_shapes=list(scratch),
        input_output_aliases=aliases,
        compiler_params=pltpu.CompilerParams(vmem_limit_bytes=limit * 2**20),
        cost_estimate=pl.CostEstimate(flops=1000, bytes_accessed=1000, transcendentals=0),
        name=name,
    )

    def run(*args):
        spaces = {id(HB): pltpu.HBM, id(VM): pltpu.VMEM}
        placed = [
            pltpu.with_memory_space_constraint(arg, spaces[id(spec)]) if id(spec) in spaces else arg
            for arg, spec in zip(args, in_specs)
        ]
        return kernel(*placed)

    return run


def shape(dims, dtype):
    return jax.ShapeDtypeStruct(dims, dtype)


def fetch(is_own, own, other, where, sem):
    @pl.when(is_own)
    def _():
        pltpu.make_async_copy(own, where, sem).start()

    @pl.when(jnp.logical_not(is_own))
    def _():
        pltpu.make_async_copy(other, where, sem).start()


def arrived(own, where, sem):
    pltpu.make_async_copy(own, where, sem).wait()


def load(pairs, sems):
    made = [pltpu.make_async_copy(there, here, sems.at[i]) for i, (there, here) in enumerate(pairs)]
    for one in made:
        one.start()
    return made


def finish(copies):
    for one in copies:
        one.wait()


def rows_of(whole, where_ref, here):
    share = whole.shape[1] // 4
    pairs = []
    for k in range(here.shape[0] // share):
        there = pl.ds(pl.multiple_of((where_ref[1] ^ k) * share, LANE), share)
        pairs.append((whole.at[where_ref[0], there], here.at[pl.ds(k * share, share)]))
    return pairs


def own_rows(whole, where_ref, here):
    return rows_of(whole, where_ref, here) if len(whole.shape) == 3 else [(whole, here)]


def inverse_rms(value):
    return lax.rsqrt(jnp.mean(value * value, axis=-1, keepdims=True) + epsilon)


def norm_back(grad, normed, inverse):
    return inverse * (grad - normed * jnp.mean(grad * normed, axis=-1, keepdims=True))


def token_mod(picks, mods_ref, part):
    width = mods_ref.shape[1] // 6
    return nn(picks, mods_ref[:, part * width : (part + 1) * width])


def image_sums(picks, value):
    return lax.dot_general(
        picks.astype(F32),
        value,
        (((0,), (0,)), ((), ())),
        precision=HIGHEST,
        preferred_element_type=F32,
    )


def swap_halves(value):
    return pltpu.roll(value, LANE // 2, 1)


def rotate(value, cosine, sine):
    return value * cosine + swap_halves(value) * sine


def unrotate(grad, cosine, sine):
    return grad * cosine - swap_halves(grad) * sine


def head_mean(value):
    return nn(value.astype(BF), jnp.full((LANE, LANE), 1.0, BF)) * (1.0 / HEAD)


def head_inverse(raw):
    return lax.rsqrt(head_mean(raw * raw) + epsilon)


def split_store(value, rows, block_refs):
    own = block_refs[0]
    share = own.shape[0]
    for k, ref in enumerate(block_refs):
        ref[:, rows] = value[k * share : (k + 1) * share].astype(ref.dtype)


def modulation_part(conditioning, modulator_t):
    micro, items = conditioning.shape[0], conditioning.shape[2]
    columns, width = modulator_t.shape
    step = 5 * LANE
    spans = [(j, min(step, columns - j)) for j in range(0, columns, step)]

    def body(cond_ref, mod_in, scaled_ref, part_ref, mod_ref, sems):
        copies = load([(mod_in.at[pl.ds(j, size)], mod_ref.at[pl.ds(j, size)]) for j, size in spans], sems)
        cond = jnp.concatenate([cond_ref[m, 0].astype(F32) for m in range(micro)], axis=0)
        scaled = (cond * jax.nn.sigmoid(cond)).astype(BF)
        scaled_ref[...] = scaled
        for copy, (j, size) in zip(copies, spans):
            copy.wait()
            part_ref[:, j : j + size] = nt(scaled, mod_ref[j : j + size]).astype(BF)

    return call(
        body,
        [shape((micro * items, width), BF), shape((micro * items, columns), BF)],
        [FREE, HB],
        [pltpu.VMEM((columns, width), BF), pltpu.SemaphoreType.DMA((len(spans),))],
        name="modulation_part",
        limit=12,
    )(conditioning, modulator_t)


def modulation_rows(pieces, gains, where, place_one):
    rows, columns = pieces[0].shape
    count = len(pieces)
    items = rows // 2

    def body(where_ref, *refs):
        piece_refs, (ga, gb, one_ref, own_ref, send_ref, gains_ref) = refs[:count], refs[count:]
        section, tensor = where_ref[0], where_ref[1]
        values = [ref[...].astype(F32) for ref in piece_refs]
        ordered = []
        for j in range(count):
            picked = jnp.zeros_like(values[0])
            for k in range(count):
                picked = jnp.where((tensor ^ k) == j, values[k], picked)
            ordered.append(picked)
        whole = jnp.concatenate(ordered, axis=1)
        blank = jnp.zeros((8 - items, whole.shape[1]), F32)
        first = jnp.concatenate([whole[:items], blank], axis=0)
        second = jnp.concatenate([whole[items:], blank], axis=0)
        own_ref[...] = jnp.where(section == 0, first, second).astype(BF)
        send_ref[...] = jnp.where(section == 0, second, first).astype(BF)
        a, b = ga[...], gb[...]
        first = jnp.where(section == 0, a, b)
        second = jnp.where(section == 0, b, a)
        both = jnp.concatenate([first, second, jnp.zeros((4, first.shape[1]), F32)], axis=0)
        gains_ref[...] = lax.dot_general(
            both, one_ref[...], (((1,), (0,)), ((), ())), precision=HIGHEST, preferred_element_type=F32
        )

    return call(
        body,
        [shape((8, count * columns), BF)] * 2 + [shape((8, LANE), F32)],
        [SM] + [VM] * count + [FREE] * 3,
        name="modulation_rows",
        limit=8,
    )(where, *pieces, *gains, place_one)


def prepare_tables(where, lengths, positions, rates):
    rows = positions.shape[2]
    share = rows // 4
    items = lengths.shape[2]

    def body(where_ref, len_ref, pos_ref, rate_ref, cos_ref, sin_ref, segc_ref, segr_ref, picks_ref, own_ref):
        section, tensor = where_ref[0], where_ref[1]

        def segments(index):
            place = (tensor ^ (index // share)) * share + index % share
            segment = jnp.zeros_like(index)
            end = 0
            for i in range(items):
                end = end + len_ref[section, 0, i]
                segment += (place >= end).astype(jnp.int32)
            return segment

        column = segments(lax.broadcasted_iota(jnp.int32, (rows, 1), 0))
        segc_ref[...] = column
        segr_ref[...] = segments(lax.broadcasted_iota(jnp.int32, (1, rows), 1))
        picks = jnp.where(column == lax.broadcasted_iota(jnp.int32, (rows, 8), 1), 1.0, 0.0).astype(BF)
        picks_ref[...] = picks
        own_ref[...] = picks[:share]
        blocks = [
            pos_ref[section, :, pl.ds(pl.multiple_of((tensor ^ k) * share, LANE), share)] for k in range(4)
        ]
        place = jnp.concatenate(blocks, axis=1).astype(F32)
        lane = lax.broadcasted_iota(jnp.int32, (LANE // 2, rows), 0)
        phase = jnp.where(lane < HEAD // 4, place[0:1], place[1:2]) * rate_ref[...]
        cosine = jnp.where(lane < HALF, jnp.cos(phase), 0.0)
        sine = jnp.where(lane < HALF, jnp.sin(phase), 0.0)
        cos_ref[...] = jnp.concatenate([cosine, cosine], axis=0).T
        sin_ref[...] = jnp.concatenate([-sine, sine], axis=0).T

    return call(
        body,
        [
            shape((rows, LANE), F32),
            shape((rows, LANE), F32),
            shape((rows, 1), jnp.int32),
            shape((1, rows), jnp.int32),
            shape((rows, 8), BF),
            shape((share, 8), BF),
        ],
        [SM, SM, FREE, FREE],
        name="prepare_tables",
        limit=16,
    )(where, lengths, positions, rates)


def prepare_weights(where, source, place, begun=None, only=None):
    wq, wo = source
    narrow, width = wq.shape[1:]
    padded = place.shape[1]

    def body(where_ref, wq_in, wo_in, place_ref, *refs):
        wq_out, wo_out, wq_ref, wo_ref, wide_ref, tall_ref, sems, out_sems = refs if begun is None else refs[2:]
        section = where_ref[0]

        def make(layer):
            copies = load([(wq_in.at[i], wq_ref.at[i]) for i in range(3)] + [(wo_in, wo_ref)], sems)
            outs = []
            for i in range(3):
                copies[i].wait()
                wide_ref[i] = tn(wq_ref[i], place_ref[...]).astype(BF)
                outs += load([(wide_ref.at[i], wq_out.at[layer, i])], out_sems.at[pl.ds(i, 1)])
            copies[3].wait()
            tall_ref[...] = tn(place_ref[...], wo_ref[...]).astype(BF)
            finish(outs + load([(tall_ref, wo_out.at[layer])], out_sems.at[pl.ds(3, 1)]))

        if only is None:
            make(section)
        else:

            @pl.when(section == only)
            def _():
                make(1 - only)

    args = [where, wq, wo, place] + ([] if begun is None else list(begun))
    return call(
        body,
        [shape((2, 3, width, padded), BF), shape((2, padded, width), BF)],
        [SM, HB, HB, FREE] + ([] if begun is None else [HB, HB]),
        [
            pltpu.VMEM((3, narrow, width), BF),
            pltpu.VMEM((narrow, width), BF),
            pltpu.VMEM((3, width, padded), BF),
            pltpu.VMEM((padded, width), BF),
            pltpu.SemaphoreType.DMA((4,)),
            pltpu.SemaphoreType.DMA((4,)),
        ],
        name="prepare_weights",
        limit=24,
        kept=2,
        aliases={} if begun is None else {4: 0, 5: 1},
    )(*args)


def last_ahead(where, cotangent, down_own, down_got, mods, picks):
    rows = picks.shape[0]
    size, width = down_own.shape

    def body(where_ref, cot_in, wd_a, wd_b, mods_ref, picks_ref, gp_out, gh_out, gp_ref, gh_ref, wd_ref, sems):
        copies = load(rows_of(cot_in, where_ref, gp_ref), sems)
        fetch(where_ref[0] == 1, wd_a, wd_b, wd_ref, sems.at[4])
        finish(copies)
        gp_ref[...] = (gp_ref[...].astype(F32) * token_mod(picks_ref[...], mods_ref, 5)).astype(BF)
        outs = load([(gp_ref, gp_out)], sems)
        arrived(wd_a, wd_ref, sems.at[4])
        gh_ref[...] = nt(gp_ref[...], wd_ref[...]).astype(BF)
        finish(outs + load([(gh_ref, gh_out)], sems.at[pl.ds(1, 1)]))

    return call(
        body,
        [shape((rows, width), BF), shape((rows, size), BF)],
        [SM] + [HB] * 3 + [VM] * 2,
        [
            pltpu.VMEM((rows, width), BF),
            pltpu.VMEM((rows, size), BF),
            pltpu.VMEM((size, width), BF),
            pltpu.SemaphoreType.DMA((5,)),
        ],
        name="last_ahead",
        limit=16,
        kept=2,
    )(where, cotangent, down_own, down_got, mods, picks)


def attention_forward(layer, where, blocks, weights, tables, mods, picks, carried=()):
    wq, wo = weights
    cosine, sine, gains, seg_col, seg_row = tables
    padded, width = wo.shape[1:]
    heads = padded // LANE
    raw_input = len(blocks) == 1
    rows = cosine.shape[0]
    share = rows // 4
    scale = HEAD**-0.5
    QB = 512

    def body(where_ref, *refs):
        refs = list(refs)
        in_refs = [refs.pop(0) for _ in blocks]
        wq_in, wo_in, cos_ref, sin_ref, gain_ref, segc_ref, segr_ref, mods_ref, picks_ref = refs[:9]
        refs = refs[9:]
        carried_refs = [refs.pop(0) for _ in carried]
        p_refs = [refs.pop(0) for _ in range(4)]
        state_ref = refs.pop(0) if raw_input else None
        kept = [refs.pop(0) for _ in range(7)]
        carried_outs = [refs.pop(0) for _ in carried]
        wq_ref, wo_ref, mask_ref = refs[:3]
        here = refs[3:10]
        sems, out_sems, carried_sems, a_x_ref, x_sems = refs[10:]
        carried_copies = load(list(zip(carried_refs, carried_outs)), carried_sems)
        if raw_input:
            x_ref = a_x_ref
            x_copies = load(rows_of(in_refs[0], where_ref, x_ref), x_sems)
        qraw_ref, kraw_ref, qrot_ref, krot_ref, v_ref, mixed_ref, a_ref = here
        weights_in = [(wq_in.at[layer, i], wq_ref.at[i]) for i in range(3)] + [(wo_in.at[layer], wo_ref)]
        weights_in = load(weights_in, sems)

        def keep(i):
            pltpu.make_async_copy(here[i], kept[i], out_sems.at[i]).start()

        if raw_input:
            picked = picks_ref[...]
            shift1 = token_mod(picked, mods_ref, 0)
            scale1 = token_mod(picked, mods_ref, 1)
            finish(x_copies)
            state_ref[...] = x_ref[:share]
            x = x_ref[...].astype(F32)
            a_ref[...] = (x * inverse_rms(x) * (1.0 + scale1) + shift1).astype(BF)
        else:
            for k, ref in enumerate(in_refs):
                a_ref[k * share : (k + 1) * share] = ref[...]
        keep(6)
        mask_ref[...] = jnp.where(segc_ref[...] == segr_ref[...], 1.0, 0.0).astype(BF)
        cos = cos_ref[...]
        sin = sin_ref[...]
        for i, (raw_out, rot_out) in enumerate(((qraw_ref, qrot_ref), (kraw_ref, krot_ref))):
            weights_in[i].wait()
            gain = gain_ref[2 * layer + i : 2 * layer + i + 1]
            for h2 in range(0, heads, 2):
                both = nn(a_ref[...], wq_ref[i, :, h2 * LANE : (h2 + 2) * LANE])
                for h in (h2, h2 + 1):
                    at = slice(h * LANE, (h + 1) * LANE)
                    raw = both[:, (h - h2) * LANE : (h - h2 + 1) * LANE]
                    raw_out[:, at] = raw.astype(BF)
                    turned = rotate(raw * head_inverse(raw) * gain, cos, sin)
                    rot_out[:, at] = turned.astype(BF)
            keep(i)
            keep(2 + i)
        weights_in[2].wait()
        one = jnp.where(lax.broadcasted_iota(jnp.int32, (1, padded), 1) % LANE == LANE - 1, 1.0, 0.0)
        v_ref[...] = (nn(a_ref[...], wq_ref[2]) + one).astype(BF)
        keep(4)

        for j in range(rows // QB):
            at_rows = slice(j * QB, (j + 1) * QB)
            for h in range(heads):
                at = slice(h * LANE, (h + 1) * LANE)
                scores = nt(qrot_ref[at_rows, at], krot_ref[:, at]) * scale
                grown = jnp.exp(scores).astype(BF) * mask_ref[at_rows]
                mixed = nn(grown, v_ref[:, at])
                mixed_ref[at_rows, at] = (mixed * (1.0 / mixed[:, LANE - 1 :])).astype(BF)
        keep(5)
        weights_in[3].wait()
        step = 3 * LANE
        for j in range(width // step):
            at = slice(j * step, (j + 1) * step)
            split_store(nn(mixed_ref[...], wo_ref[:, at]), at, p_refs)
        for i in range(7):
            pltpu.make_async_copy(here[i], kept[i], out_sems.at[i]).wait()
        finish(carried_copies)

    outs = [shape((share, width), BF)] * (5 if raw_input else 4)
    saved_shapes = [shape((rows, padded), BF)] * 6 + [shape((rows, width), BF)]
    result = call(
        body,
        outs + saved_shapes + [shape(c.shape, c.dtype) for c in carried],
        [SM] + ([HB] if raw_input else [VM] * 4) + [HB] * 2 + [VM] * (7 + len(carried)),
        [
            pltpu.VMEM((3, width, padded), BF),
            pltpu.VMEM((padded, width), BF),
            pltpu.VMEM((rows, rows), BF),
        ] + [pltpu.VMEM(s.shape, BF) for s in saved_shapes] + [
            pltpu.SemaphoreType.DMA((4,)),
            pltpu.SemaphoreType.DMA((7,)),
            pltpu.SemaphoreType.DMA((max(1, len(carried)),)),
            pltpu.VMEM((rows if raw_input else 16, width), BF),
            pltpu.SemaphoreType.DMA((4,)),
        ],
        name=f"attention_forward_{layer}",
        limit=28,
        kept=7 + len(carried),
    )(where, *blocks, wq, wo, cosine, sine, gains, seg_col, seg_row, mods, picks, *carried)
    n = len(outs)
    return list(result[:4]), list(result[4:n]), list(result[n : n + 7]), list(result[n + 7 :])


def add_parts(refs):
    total = refs[0][...].astype(F32)
    for ref in refs[1:]:
        total += ref[...].astype(F32)
    return total


def after_attention(parts, state, mods, picks):
    dims = state.shape

    def body(p0, p1, p2, p3, state_ref, mods_ref, picks_ref, mlp_ref, attended_ref, after_ref):
        picked = picks_ref[...]
        attended = add_parts((p0, p1, p2, p3))
        attended_ref[...] = attended.astype(BF)
        after = state_ref[...].astype(F32) + token_mod(picked, mods_ref, 2) * attended
        after_ref[...] = after
        normed = after * inverse_rms(after)
        mlp_ref[...] = (normed * (1.0 + token_mod(picked, mods_ref, 4)) + token_mod(picked, mods_ref, 3)).astype(BF)

    return call(
        body,
        [shape(dims, BF), shape(dims, BF), shape(dims, F32)],
        [VM] * 7,
        name="after_attention",
        limit=8,
    )(*parts, state, mods, picks)


def after_mlp(parts, after, mods, picks, mods_next):
    dims = after.shape

    def body(p0, p1, p2, p3, after_ref, mods_ref, picks_ref, next_ref, in_ref, projected_ref, state_ref):
        picked = picks_ref[...]
        projected = add_parts((p0, p1, p2, p3))
        output = after_ref[...] + token_mod(picked, mods_ref, 5) * projected
        low = output.astype(BF)
        state_ref[...] = low
        state = low.astype(F32)
        normed = state * inverse_rms(state)
        in_ref[...] = (normed * (1.0 + token_mod(picked, next_ref, 1)) + token_mod(picked, next_ref, 0)).astype(BF)
        projected_ref[...] = projected.astype(BF)

    return call(
        body,
        [shape(dims, BF)] * 3,
        [VM] * 8,
        name="after_mlp",
        limit=8,
    )(*parts, after, mods, picks, mods_next)


def last_output(parts, after, mods, picks):
    dims = after.shape

    def body(p0_in, p1, p2, p3, after_in, mods_ref, picks_ref, output_ref, p0, after_ref, sems):
        copies = load([(p0_in, p0), (after_in, after_ref)], sems)
        gate2 = token_mod(picks_ref[...], mods_ref, 5)
        finish(copies)
        output_ref[...] = after_ref[...] + gate2 * add_parts((p0, p1, p2, p3))

    return call(
        body,
        [shape(dims, F32)],
        [HB] + [VM] * 3 + [HB] + [VM] * 2,
        [pltpu.VMEM(dims, BF), pltpu.VMEM(dims, F32), pltpu.SemaphoreType.DMA((2,))],
        name="last_output",
        limit=8,
    )(*parts, after, mods, picks)[0]


def last_gate_sums(where, parts, cotangent, picks):
    share, width = parts[0].shape
    rows = picks.shape[0]

    def body(where_ref, *refs):
        part_refs = refs[:4]
        cot_in, picks_ref, sums_out, p_ref, g_ref, sums_ref, sems, cot_sems, out_sems = refs[4:]
        copies = load([(ref, p_ref.at[pl.ds(k * share, share)]) for k, ref in enumerate(part_refs)], sems)
        copies += load(rows_of(cot_in, where_ref, g_ref), cot_sems)
        finish(copies)
        sums_ref[0] = image_sums(picks_ref[...], g_ref[...].astype(F32) * p_ref[...].astype(F32))
        finish(load([(sums_ref, sums_out)], out_sems))

    sums = (1, picks.shape[1], width)
    return call(
        body,
        [shape(sums, F32)],
        [SM] + [HB] * 5 + [VM],
        [
            pltpu.VMEM((rows, width), BF),
            pltpu.VMEM((rows, width), BF),
            pltpu.VMEM(sums, F32),
            pltpu.SemaphoreType.DMA((4,)),
            pltpu.SemaphoreType.DMA((4,)),
            pltpu.SemaphoreType.DMA((1,)),
        ],
        name="last_gate_sums",
        limit=16,
        kept=1,
    )(where, *parts, cotangent, picks)[0]


def mlp_forward(layer, blocks, weights, section, carried, late):
    gu_own, gu_got, wd_own, wd_got = weights
    hidden_size, width = wd_own.shape
    share = blocks[0].shape[0]
    rows = share * 4
    chunk = 2 * LANE
    chunks = hidden_size // chunk

    def body(sec_ref, b0, b1, b2, b3, gu_a, gu_b, wd_a, wd_b, attended_ref, after_ref,
             *refs):
        refs = list(refs)
        p_refs = [] if late else [refs.pop(0) for _ in range(4)]
        hid_out, c1_out, c2_out, a_out, attended_out, after_out = refs[:6]
        refs = refs[6:]
        p_outs = [refs.pop(0) for _ in range(4)] if late else []
        a_ref, gu_ref, wd_ref, hid_ref, c1_ref, c2_ref, sems, out_sems, carried_sems = refs[:9]
        if late:
            p_refs, p_sems = refs[9:13], refs[13]
        own = sec_ref[0] == layer
        for j in range(chunks):
            at = pl.ds(j * chunk, chunk)
            for i in range(2):
                fetch(own, gu_a.at[i, :, at], gu_b.at[i, :, at], gu_ref.at[i, :, at], sems.at[2 * j + i])
        fetch(own, wd_a, wd_b, wd_ref, sems.at[2 * chunks])
        carried_copies = load([(attended_ref, attended_out), (after_ref, after_out)], carried_sems)
        for k, ref in enumerate((b0, b1, b2, b3)):
            a_ref[k * share : (k + 1) * share] = ref[...]
        for j in range(chunks):
            at = slice(j * chunk, (j + 1) * chunk)
            for i in range(2):
                arrived(gu_a.at[i, :, pl.ds(j * chunk, chunk)], gu_ref.at[i, :, pl.ds(j * chunk, chunk)], sems.at[2 * j + i])
            gate = nn(a_ref[...], gu_ref[0, :, at])
            up = nn(a_ref[...], gu_ref[1, :, at])
            sigma = jax.nn.sigmoid(gate)
            silu = gate * sigma
            hid_ref[:, at] = (silu * up).astype(BF)
            c1_ref[:, at] = (up * (sigma + silu * (1.0 - sigma))).astype(BF)
            c2_ref[:, at] = silu.astype(BF)
        kept = load([(hid_ref, hid_out), (c1_ref, c1_out), (c2_ref, c2_out), (a_ref, a_out)], out_sems)
        arrived(wd_a, wd_ref, sems.at[2 * chunks])
        step = 3 * LANE
        for j in range(width // step):
            at = slice(j * step, (j + 1) * step)
            split_store(nn(hid_ref[...], wd_ref[:, at]), at, p_refs)
        if late:
            kept += load(list(zip(p_refs, p_outs)), p_sems)
        finish(kept + carried_copies)

    parts = [shape((share, width), BF)] * 4
    outs = ([] if late else parts) + [shape((rows, hidden_size), BF)] * 3 + [shape((rows, width), BF)]
    outs += [shape(c.shape, c.dtype) for c in carried] + (parts if late else [])
    result = call(
        body,
        outs,
        [SM] + [VM] * 4 + [HB] * 4 + [VM] * 2,
        [
            pltpu.VMEM((rows, width), BF),
            pltpu.VMEM(gu_own.shape, BF),
            pltpu.VMEM(wd_own.shape, BF),
        ]
        + [pltpu.VMEM((rows, hidden_size), BF)] * 3
        + [
            pltpu.SemaphoreType.DMA((2 * chunks + 1,)),
            pltpu.SemaphoreType.DMA((4,)),
            pltpu.SemaphoreType.DMA((2,)),
        ]
        + ([pltpu.VMEM((share, width), BF)] * 4 + [pltpu.SemaphoreType.DMA((4,))] if late else []),
        name=f"mlp_forward_{layer}",
        kept=10 if late else 6,
    )(section, *blocks, gu_own, gu_got, wd_own, wd_got, *carried)
    result = list(result)
    partial = result[6:] if late else result[:4]
    result = result[:6] if late else result[4:]
    return partial, result[:4], result[4:]


def mlp_backward(layer, where, blocks, weights, saved, carried):
    gu_own, gu_got, wd_own, wd_got = weights
    c1, c2 = saved
    hidden_size, width = wd_own.shape
    rows = c1.shape[0]
    share = rows // 4
    chunk = 2 * LANE
    chunks = hidden_size // chunk

    def body(where_ref, *refs):
        refs = list(refs)
        in_refs = [refs.pop(0) for _ in blocks]
        gu_a, gu_b, wd_a, wd_b, c1_in, c2_in = refs[:6]
        refs = refs[6:]
        carried_refs = [refs.pop(0) for _ in carried]
        p_refs = [refs.pop(0) for _ in range(3)]
        outs = [refs.pop(0) for _ in range(4)]
        carried_outs = [refs.pop(0) for _ in carried]
        gu_ref, wd_ref, c1_ref, c2_ref, gg_ref, gup_ref, gp_ref, p0, sems, in_sems, out_sems, carried_sems = refs
        own = where_ref[0] == layer
        for j in range(chunks):
            at = pl.ds(j * chunk, chunk)
            fetch(own, wd_a.at[at], wd_b.at[at], wd_ref.at[at], sems.at[j])
        saved_copies = load([(c1_in, c1_ref), (c2_in, c2_ref)], in_sems)
        for i in range(2):
            fetch(own, gu_a.at[i], gu_b.at[i], gu_ref.at[i], sems.at[chunks + i])
        kept = load(list(zip(carried_refs, carried_outs)), carried_sems)
        for k, ref in enumerate(in_refs):
            gp_ref[k * share : (k + 1) * share] = ref[...]

        def keep(i, here):
            kept.append(pltpu.make_async_copy(here, outs[i], out_sems.at[i]))
            kept[-1].start()

        keep(0, gp_ref)
        for j in range(chunks):
            at = slice(j * chunk, (j + 1) * chunk)
            arrived(wd_a.at[pl.ds(j * chunk, chunk)], wd_ref.at[pl.ds(j * chunk, chunk)], sems.at[j])
            grad_hidden = nt(gp_ref[...], wd_ref[at])
            if j == 0:
                finish(saved_copies)
            gg_ref[:, at] = (grad_hidden * c1_ref[:, at].astype(F32)).astype(BF)
            gup_ref[:, at] = (grad_hidden * c2_ref[:, at].astype(F32)).astype(BF)
        keep(1, gg_ref)
        keep(2, gup_ref)
        for i in range(2):
            arrived(gu_a.at[i], gu_ref.at[i], sems.at[chunks + i])
        step = 3 * LANE
        for j in range(width // step):
            at = slice(j * step, (j + 1) * step)
            split_store(nt(gg_ref[...], gu_ref[0, at]) + nt(gup_ref[...], gu_ref[1, at]), at, [p0] + p_refs)
        keep(3, p0)
        finish(kept)

    outs = [shape((share, width), BF)] * 3
    outs += [shape((rows, width), BF)] + [shape((rows, hidden_size), BF)] * 2 + [shape((share, width), BF)]
    outs += [shape(c.shape, c.dtype) for c in carried]
    result = call(
        body,
        outs,
        [SM] + [VM] * 4 + [HB] * 6 + [VM] * len(carried),
        [
            pltpu.VMEM(gu_own.shape, BF),
            pltpu.VMEM(wd_own.shape, BF),
        ]
        + [pltpu.VMEM((rows, hidden_size), BF)] * 4
        + [
            pltpu.VMEM((rows, width), BF),
            pltpu.VMEM((share, width), BF),
            pltpu.SemaphoreType.DMA((chunks + 2,)),
            pltpu.SemaphoreType.DMA((2,)),
            pltpu.SemaphoreType.DMA((4,)),
            pltpu.SemaphoreType.DMA((max(1, len(carried)),)),
        ],
        name=f"mlp_backward_{layer}",
        kept=4 + len(carried),
    )(where, *blocks, gu_own, gu_got, wd_own, wd_got, c1, c2, *carried)
    return list(result[:3]), list(result[3:6]), list(result[6:])


def mlp_backward_last(layer, ahead, saved):
    grad_projected, grad_hidden = ahead
    hidden, c1, c2, mlp_in = saved
    rows, width = grad_projected.shape
    size = hidden.shape[1]
    step = 3 * LANE

    def body(gp_in, gh_in, hid_in, c1_in, c2_in, a_in, gg_ref, gup_ref, out,
             gh_ref, c1_ref, c2_ref, hid_ref, gp_ref, a_ref, full_ref, in_sems, out_sems):
        ins = [(gh_in, gh_ref), (c1_in, c1_ref), (c2_in, c2_ref), (a_in, a_ref), (gp_in, gp_ref), (hid_in, hid_ref)]
        ins = load(ins, in_sems)
        finish(ins[:2])
        gg_ref[...] = gh_ref[...] * c1_ref[...]
        ins[2].wait()
        gup_ref[...] = gh_ref[...] * c2_ref[...]
        finish(ins[3:])
        kept = []
        for j in range(width // step):
            at = slice(j * step, (j + 1) * step)
            left = a_ref[:, at]
            full_ref[at, :size] = tn(left, gg_ref[...]).astype(BF)
            full_ref[at, size : 2 * size] = tn(left, gup_ref[...]).astype(BF)
            full_ref[at, 2 * size :] = tn(gp_ref[:, at], hid_ref[...]).astype(BF)
            here = pl.ds(j * step, step)
            kept.append(pltpu.make_async_copy(full_ref.at[here], out.at[here], out_sems.at[j]))
            kept[-1].start()
        finish(kept)

    return call(
        body,
        [shape((rows, size), BF)] * 2 + [shape((width, 3 * size), BF)],
        [HB] * 6,
        [pltpu.VMEM((rows, size), BF)] * 4
        + [
            pltpu.VMEM((rows, width), BF),
            pltpu.VMEM((rows, width), BF),
            pltpu.VMEM((width, 3 * size), BF),
            pltpu.SemaphoreType.DMA((6,)),
            pltpu.SemaphoreType.DMA((width // step,)),
        ],
        name=f"mlp_backward_{layer}",
        kept=1,
        limit=24,
    )(grad_projected, grad_hidden, hidden, c1, c2, mlp_in)


def mlp_input_grad(layer, section, grad_gate, grad_up, weights):
    gu_own, gu_got = weights[:2]
    rows = grad_gate.shape[0]
    width = gu_own.shape[1]
    share = rows // 4
    step = 3 * LANE

    def body(sec_ref, gg_ref, gup_ref, gu_a, gu_b, p1, p2, p3, p0_out, p0, gu_ref, sems, out_sems):
        own = sec_ref[0] == layer
        spans = [pl.ds(j * step, step) for j in range(width // step)]
        for j, at in enumerate(spans):
            for i in range(2):
                fetch(own, gu_a.at[i, at], gu_b.at[i, at], gu_ref.at[i, at], sems.at[2 * j + i])
        for j, at in enumerate(spans):
            for i in range(2):
                arrived(gu_a.at[i, at], gu_ref.at[i, at], sems.at[2 * j + i])
            here = slice(j * step, (j + 1) * step)
            split_store(
                nt(gg_ref[...], gu_ref[0, here]) + nt(gup_ref[...], gu_ref[1, here]), here, (p0, p1, p2, p3)
            )
        finish(load([(p0, p0_out)], out_sems))

    result = call(
        body,
        [shape((share, width), BF)] * 4,
        [SM, VM, VM, HB, HB],
        [
            pltpu.VMEM((share, width), BF),
            pltpu.VMEM(gu_own.shape, BF),
            pltpu.SemaphoreType.DMA((2 * (width // step),)),
            pltpu.SemaphoreType.DMA((1,)),
        ],
        name="mlp_input_grad",
        kept=1,
        limit=16,
    )(section, grad_gate, grad_up, gu_own, gu_got)
    return [result[3]] + list(result[:3])


def mlp_weight_grads(mlp_in, grads, hidden):
    grad_projected, grad_gate, grad_up = grads
    rows, width = grad_projected.shape
    size = hidden.shape[1]
    step = 3 * LANE

    def body(a_in, gg_in, gu_in, gp_in, hid_in, *refs):
        out, a_ref, gg_ref, gu_ref, gp_ref, hid_ref, full_ref, in_sems, sems = refs
        ins = load([(a_in, a_ref), (gg_in, gg_ref), (gu_in, gu_ref), (gp_in, gp_ref), (hid_in, hid_ref)], in_sems)
        kept = []
        finish(ins[:2])
        for j in range(width // step):
            at = slice(j * step, (j + 1) * step)
            left = a_ref[:, at]
            full_ref[at, :size] = tn(left, gg_ref[...]).astype(BF)
            if j == 0:
                ins[2].wait()
            full_ref[at, size : 2 * size] = tn(left, gu_ref[...]).astype(BF)
            if j == 0:
                finish(ins[3:])
            full_ref[at, 2 * size :] = tn(gp_ref[:, at], hid_ref[...]).astype(BF)
            here = pl.ds(j * step, step)
            kept.append(pltpu.make_async_copy(full_ref.at[here], out.at[here], sems.at[j]))
            kept[-1].start()
        finish(kept)

    result = call(
        body,
        [shape((width, 3 * size), BF)],
        [HB] * 5,
        [pltpu.VMEM((rows, width), BF)]
        + [pltpu.VMEM((rows, size), BF)] * 2
        + [
            pltpu.VMEM((rows, width), BF),
            pltpu.VMEM((rows, size), BF),
            pltpu.VMEM((width, 3 * size), BF),
            pltpu.SemaphoreType.DMA((5,)),
            pltpu.SemaphoreType.DMA((width // step,)),
        ],
        name="mlp_weight_grads",
        kept=1,
    )(mlp_in, grad_gate, grad_up, grad_projected, hidden)
    return result[0]


def attention_backward(layer, blocks, weights, saved, tables, grad_after):
    wq, wo = weights
    cosine, sine, gains, seg_col, seg_row = tables
    rows, padded = saved[0].shape
    width = wo.shape[2]
    heads = padded // LANE
    share = rows // 4
    scale = HEAD**-0.5
    QB = 512

    def body(b0, b1, b2, b3, wq_in, wo_in, qraw_in, kraw_in, qrot_in, krot_in, v_in,
             cos_ref, sin_ref, gain_ref, segc_ref, segr_ref, grad_ref,
             p1, p2, p3, g_out, ga_out, p0_out, ggain_out, grad_out,
             wq_ref, wo_ref, qraw_ref, kraw_ref, qrot_ref, krot_ref, v_ref, mask_ref,
             ga_ref, gmix_ref, gq_ref, gk_ref, g_ref, p0, ggain_ref, sems, in_sems):
        ins = [(wo_in.at[layer], wo_ref)]
        ins += [(qrot_in, qrot_ref), (krot_in, krot_ref), (v_in, v_ref), (qraw_in, qraw_ref), (kraw_in, kraw_ref)]
        ins += [(wq_in.at[layer, i], wq_ref.at[i]) for i in range(3)]
        ins = load(ins, in_sems)
        for k, ref in enumerate((b0, b1, b2, b3)):
            ga_ref[k * share : (k + 1) * share] = ref[...]
        kept = []

        def keep(here, there):
            kept.append(pltpu.make_async_copy(here, there, sems.at[len(kept)]))
            kept[-1].start()

        keep(ga_ref, ga_out)
        keep(grad_ref, grad_out)
        mask_ref[...] = jnp.where(segc_ref[...] == segr_ref[...], 1.0, 0.0).astype(BF)
        ins[0].wait()
        gmix_ref[...] = nt(ga_ref[...], wo_ref[...]).astype(BF)
        finish(ins[1:4])
        for h in range(heads):
            at = slice(h * LANE, (h + 1) * LANE)
            for j in range(rows // QB):
                at_rows = slice(j * QB, (j + 1) * QB)
                query = qrot_ref[at_rows, at]
                grad_mixed = gmix_ref[at_rows, at]
                scores = nt(krot_ref[:, at], query) * scale
                grown = (jnp.exp(scores).astype(BF) * mask_ref[:, at_rows]).astype(F32)
                weights_t = grown * (1.0 / jnp.sum(grown, axis=0, keepdims=True))
                grad_weights = nt(v_ref[:, at], grad_mixed)
                add_v = nn(weights_t.astype(BF), grad_mixed)
                product = weights_t * grad_weights
                delta = jnp.sum(product, axis=0, keepdims=True)
                grad_scores = (product - weights_t * delta).astype(BF)
                gq_ref[at_rows, at] = tn(grad_scores, krot_ref[:, at])
                add_k = nn(grad_scores, query)
                total_v = add_v if j == 0 else total_v + add_v
                total_k = add_k if j == 0 else total_k + add_k
            gk_ref[:, at] = total_k
            g_ref[:, 2 * padded + h * LANE : 2 * padded + (h + 1) * LANE] = total_v.astype(BF)
        cos = cos_ref[...]
        sin = sin_ref[...]
        finish(ins[4:6])
        ggain_ref[...] = jnp.zeros_like(ggain_ref)
        for i, (raw_ref, grad_ref) in enumerate(((qraw_ref, gq_ref), (kraw_ref, gk_ref))):
            gain = gain_ref[2 * layer + i : 2 * layer + i + 1]
            gain_sum = jnp.zeros((1, LANE), F32)
            for h in range(heads):
                at = slice(h * LANE, (h + 1) * LANE)
                raw = raw_ref[:, at].astype(F32)
                inverse = head_inverse(raw)
                normed = raw * inverse
                turned = unrotate(grad_ref[:, at], cos, sin) * scale
                product = turned * normed
                gain_sum += jnp.sum(product, axis=0, keepdims=True)
                back = inverse * (turned * gain - normed * head_mean(product * gain))
                g_ref[:, i * padded + h * LANE : i * padded + (h + 1) * LANE] = back.astype(BF)
            ggain_ref[i : i + 1] = gain_sum
        keep(g_ref, g_out)
        keep(ggain_ref, ggain_out)
        finish(ins[6:])
        step = 3 * LANE
        for j in range(width // step):
            at = slice(j * step, (j + 1) * step)
            total = nt(g_ref[:, :padded], wq_ref[0, at])
            total += nt(g_ref[:, padded : 2 * padded], wq_ref[1, at])
            total += nt(g_ref[:, 2 * padded :], wq_ref[2, at])
            split_store(total, at, (p0, p1, p2, p3))
        keep(p0, p0_out)
        finish(kept)

    outs = [shape((share, width), BF)] * 3
    outs += [shape((rows, 3 * padded), BF), shape((rows, width), BF), shape((share, width), BF), shape((8, LANE), F32)]
    outs += [shape(grad_after.shape, F32)]
    result = call(
        body,
        outs,
        [VM] * 4 + [HB] * 7 + [VM] * 6,
        [
            pltpu.VMEM((3, width, padded), BF),
            pltpu.VMEM((padded, width), BF),
        ]
        + [pltpu.VMEM((rows, padded), BF)] * 5
        + [
            pltpu.VMEM((rows, rows), BF),
            pltpu.VMEM((rows, width), BF),
            pltpu.VMEM((rows, padded), BF),
            pltpu.VMEM((rows, padded), F32),
            pltpu.VMEM((rows, padded), F32),
            pltpu.VMEM((rows, 3 * padded), BF),
            pltpu.VMEM((share, width), BF),
            pltpu.VMEM((8, LANE), F32),
            pltpu.SemaphoreType.DMA((5,)),
            pltpu.SemaphoreType.DMA((9,)),
        ],
        name=f"attention_backward_{layer}",
        limit=32,
        kept=5,
    )(*blocks, wq, wo, *saved[:5], cosine, sine, gains, seg_col, seg_row, grad_after)
    return list(result[:3]), list(result[3:])


def attention_weight_grads(attention_in, grads, mixed, grad_attended, place):
    rows, width = attention_in.shape
    padded, narrow = place.shape
    step = 3 * LANE


    def body(a_in, g_in, mixed_in, ga_in, place_ref, out, a_ref, g_ref, mixed_ref, ga_ref, right_ref, full_ref, in_sems, sems):
        ins = load([(g_in, g_ref), (mixed_in, mixed_ref), (a_in, a_ref), (ga_in, ga_ref)], in_sems)
        finish(ins[:2])
        for i in range(3):
            right_ref[i] = nn(g_ref[:, i * padded : (i + 1) * padded], place_ref[...]).astype(BF)
        right_ref[3] = nn(mixed_ref[...], place_ref[...]).astype(BF)
        finish(ins[2:])
        kept = []
        for j in range(width // step):
            at = slice(j * step, (j + 1) * step)
            left = a_ref[:, at]
            for i in range(3):
                full_ref[at, i * narrow : (i + 1) * narrow] = tn(left, right_ref[i]).astype(BF)
            full_ref[at, 3 * narrow :] = tn(ga_ref[:, at], right_ref[3]).astype(BF)
            here = pl.ds(j * step, step)
            kept.append(pltpu.make_async_copy(full_ref.at[here], out.at[here], sems.at[j]))
            kept[-1].start()
        finish(kept)

    result = call(
        body,
        [shape((width, 4 * narrow), BF)],
        [HB] * 4 + [FREE],
        [
            pltpu.VMEM((rows, width), BF),
            pltpu.VMEM((rows, 3 * padded), BF),
            pltpu.VMEM((rows, padded), BF),
            pltpu.VMEM((rows, width), BF),
            pltpu.VMEM((4, rows, narrow), BF),
            pltpu.VMEM((width, 4 * narrow), BF),
            pltpu.SemaphoreType.DMA((4,)),
            pltpu.SemaphoreType.DMA((width // step,)),
        ],
        name="attention_weight_grads",
        kept=1,
    )(attention_in, grads, mixed, grad_attended, place)
    return result[0]


def back_of_mlp(where, parts, grad_out, after, attended, projected, mods, picks):
    dims = after.shape
    extra = [] if projected is None else [projected]
    sums = (3 + len(extra), picks.shape[1], dims[1])

    def body(where_ref, p0_in, p1, p2, p3, g_in, after_in, attended_in, *refs):
        refs = list(refs)
        extra_refs = [refs.pop(0) for _ in extra]
        (mods_ref, picks_ref, ga_ref, grad_ref, sums_out,
         p0, g_ref, after_ref, attended_ref, projected_ref, sums_ref, sems, out_sems) = refs
        pairs = [(p0_in, p0), (after_in, after_ref)] + own_rows(g_in, where_ref, g_ref)
        ins = load(pairs + [(attended_in, attended_ref)] + [(ref, projected_ref) for ref in extra_refs], sems)
        picked = picks_ref[...]
        scale2 = token_mod(picked, mods_ref, 4)
        gate1 = token_mod(picked, mods_ref, 2)
        finish(ins[:2])
        grad_in = add_parts((p0, p1, p2, p3))
        after = after_ref[...]
        inverse = inverse_rms(after)
        normed = after * inverse
        finish(ins[2:])
        g = g_ref[...].astype(F32)
        grad_after = g + norm_back(grad_in * (1.0 + scale2), normed, inverse)
        sums_ref[0] = image_sums(picked, grad_after * attended_ref[...].astype(F32))
        sums_ref[1] = image_sums(picked, grad_in)
        sums_ref[2] = image_sums(picked, grad_in * normed)
        if extra:
            sums_ref[3] = image_sums(picked, g * projected_ref[...].astype(F32))
        kept = load([(sums_ref, sums_out)], out_sems)
        grad_ref[...] = grad_after
        ga_ref[...] = (grad_after * gate1).astype(BF)
        finish(kept)

    return call(
        body,
        [shape(dims, BF), shape(dims, F32), shape(sums, F32)],
        [SM, HB] + [VM] * 3 + [HB] * (3 + len(extra)) + [VM] * 2,
        [
            pltpu.VMEM(dims, BF),
            pltpu.VMEM(dims, BF),
            pltpu.VMEM(dims, F32),
            pltpu.VMEM(dims, BF),
            pltpu.VMEM(dims, BF),
            pltpu.VMEM(sums, F32),
            pltpu.SemaphoreType.DMA((5,)),
            pltpu.SemaphoreType.DMA((1,)),
        ],
        name="back_of_mlp",
        limit=10,
        kept=1,
    )(where, *parts, grad_out, after, attended, *extra, mods, picks)


def back_of_attention(where, parts, grad_after, state, mods, picks, mods_below):
    first = mods_below is None
    dims = grad_after.shape

    def body(where_ref, p0_in, p1, p2, p3, grad_in_ref, state_in, mods_ref, picks_ref, *refs):
        refs = list(refs)
        below_ref = None if first else refs.pop(0)
        sums_ref = refs.pop(0)
        gp_ref = None if first else refs.pop(0)
        out_ref, p0, grad_ref, state_ref, sems = refs
        ins = load([(p0_in, p0), (grad_in_ref, grad_ref)] + own_rows(state_in, where_ref, state_ref), sems)
        picked = picks_ref[...]
        scale1 = token_mod(picked, mods_ref, 1)
        finish(ins)
        grad_in = add_parts((p0, p1, p2, p3))
        state = state_ref[...].astype(F32)
        inverse = inverse_rms(state)
        normed = state * inverse
        grad_state = grad_ref[...] + norm_back(grad_in * (1.0 + scale1), normed, inverse)
        out_ref[...] = grad_state.astype(out_ref.dtype)
        if not first:
            gp_ref[...] = (grad_state.astype(BF).astype(F32) * token_mod(picked, below_ref, 5)).astype(BF)
        sums_ref[0] = image_sums(picked, grad_in)
        sums_ref[1] = image_sums(picked, grad_in * normed)

    outs = [shape((2, picks.shape[1], dims[1]), F32)] + ([shape(dims, F32)] if first else [shape(dims, BF)] * 2)
    extra = () if first else (mods_below,)
    return call(
        body,
        outs,
        [SM, HB] + [VM] * 3 + [HB] * 2 + [VM] * (2 + len(extra)),
        [
            pltpu.VMEM(dims, BF),
            pltpu.VMEM(dims, F32),
            pltpu.VMEM(dims, BF),
            pltpu.SemaphoreType.DMA((3,)),
        ],
        name="back_of_attention",
        limit=10,
    )(where, *parts, grad_after, state, mods, picks, *extra)


def exchange(value, axis, k):
    return lax.ppermute(value, axis, [(i, i ^ k) for i in range(lax.axis_size(axis))])


def handed_on(value):
    def body(source, target):
        target[...] = source[...]

    return call(body, [shape(value.shape, value.dtype)], [VM], name="handed_on", limit=4)(value)[0]


def in_order(got, order):
    for place, k in enumerate(order):
        for _ in range(len(order) - 1 - place):
            got[k] = handed_on(got[k])


def send_parts(parts, beside=None, whole=False):
    got = {k: exchange(parts[k], "tensor", k) for k in (3, 1, 2)}
    if beside is not None and not whole:
        got[1], beside = lax.optimization_barrier((got[1], beside))
    if whole:
        got, beside = lax.optimization_barrier((got, beside))
    else:
        in_order(got, (1, 2, 3))
    result = [parts[0], got[1], got[2], got[3]]
    return result if beside is None else (result, beside)


def gather_blocks(own):
    got = {k: exchange(own, "tensor", k) for k in (3, 1, 2)}
    in_order(got, (3, 2, 1))
    return [own, got[1], got[2], got[3]]


def group_sum(value, axis):
    k = 1
    while k < lax.axis_size(axis):
        value = value + exchange(value, axis, k)
        k *= 2
    return value


def gather_dp(value):
    count = lax.axis_size("dp")
    if count > 4:
        return lax.all_gather(value, "dp", axis=0)
    me = lax.axis_index("dp")
    got = [value] + [exchange(value, "dp", k) for k in range(1, count)]
    stacked = jnp.stack(got)
    return jnp.stack([lax.dynamic_index_in_dim(stacked, me ^ j, 0, keepdims=False) for j in range(count)])


def head_places(heads):
    place = np.zeros((heads * HEAD, heads * LANE), np.float32)
    for h in range(heads):
        for j in range(HEAD):
            place[h * HEAD + j, h * LANE + (j // HALF) * (LANE // 2) + j % HALF] = 1.0
    return place


def shards(
    inputs,
    cotangent,
    conditioning,
    lengths,
    positions,
    modulator,
    projections,
    norm_gains,
    out_weight,
    gate_up,
    down_weight,
):
    section = lax.axis_index("section")
    other = 1 - section
    tensor = lax.axis_index("tensor")
    data = lax.axis_index("dp")
    micro, _, width = inputs.shape
    rows = inputs.shape[1]
    group = lax.axis_size("tensor")
    share = rows // group
    items = lengths.shape[2]
    narrow = projections.shape[3]
    heads = narrow // HEAD
    columns = modulator.shape[2]
    sec = section.reshape(1).astype(jnp.int32)

    where = jnp.stack([section, tensor]).astype(jnp.int32)
    is_first = section == 0

    where = jnp.stack([section, tensor]).astype(jnp.int32)
    is_first = section == 0
    place = jnp.asarray(head_places(heads), BF)
    place_one = jnp.asarray(head_places(1), F32)

    own = (jnp.swapaxes(projections[0], 1, 2), out_weight[0])
    got = [exchange(value, "section", 1) for value in own]
    got_gains = exchange(norm_gains[0], "section", 1)
    scaled, part = modulation_part(conditioning, jnp.swapaxes(modulator[0], 0, 1))
    pieces = gather_blocks(part)
    quarter = HEAD // 4
    rates = 10000.0 ** (-jnp.arange(quarter).astype(F32) / quarter)
    rates = jnp.concatenate([rates, rates, jnp.zeros(LANE // 2 - HALF, F32)])[:, None]
    where_late, part = lax.optimization_barrier((where, part))
    cosine, sine, seg_col, seg_row, picks, picks_own = prepare_tables(where_late, lengths, positions, rates)
    wq, wo = prepare_weights(where_late, own, place)
    pieces, got, cosine, wq = lax.optimization_barrier((pieces, got, cosine, wq))
    mods_own, mods_send, gains = modulation_rows([part] + pieces[1:], (norm_gains[0], got_gains), where, place_one)
    mods_got = exchange(mods_send, "section", 1)
    gu_send, wd_send, mods_got = lax.optimization_barrier((gate_up[0], down_weight[0], mods_got))
    mods = [jnp.where(is_first, mods_own, mods_got), jnp.where(is_first, mods_got, mods_own)]
    gu_got = exchange(gu_send, "section", 1)
    wd_got = exchange(wd_send, "section", 1)
    mlp_weights = (gate_up[0], gu_got, down_weight[0], wd_got)
    wq, mods_first = lax.optimization_barrier((wq, mods[0]))
    mods[0] = mods_first
    wq, wo = prepare_weights(where, got, place, (wq, wo), 1)
    tables = (cosine, sine, gains, seg_col, seg_row)

    cache = []
    attention_blocks = [inputs]
    carried = ()
    for l in range(2):
        partial, state, saved, kept = attention_forward(
            l, where, attention_blocks, (wq, wo), tables, mods[l], picks, carried
        )
        if l == 0:
            state = state[0]
            wq, mixed = lax.optimization_barrier((wq, saved[5]))
            saved[5] = mixed
            wq, wo = prepare_weights(where, got, place, (wq, wo), 0)
            parts, wq = send_parts(partial, wq)
        else:
            parts = send_parts(partial)
            cache[0].append(kept[0])
            state = carried[1]
            state_kept = kept[1]
        mlp_in, attended, after = after_attention(parts, state, mods[l], picks_own)
        partial, mlp_saved, kept = mlp_forward(l, gather_blocks(mlp_in), mlp_weights, sec, (attended, after), l == 1)
        cache.append([saved, mlp_saved] + kept)
        if l == 0:
            where_late, partial[0] = lax.optimization_barrier((where, partial[0]))
            ahead = last_ahead(where_late, cotangent, down_weight[0], wd_got, mods[1], picks)
            parts, ahead = send_parts(partial, ahead)
            attention_in, projected, state = after_mlp(parts, after, mods[0], picks_own, mods[1])
            carried = (projected, state)
            attention_blocks = gather_blocks(attention_in)

    item_sums = [None, None]
    gain_sums = [None, None]
    shares = [None, None]

    def data_sum(value):
        return lax.psum_scatter(value, ("dp", "section"), scatter_dimension=0, tiled=True)

    for l in (1, 0):
        saved, (hidden, c1, c2, mlp_in), attended, after = cache[l][:4]
        mixed, attention_in = saved[5:]
        if l == 1:
            last_partial = partial
            grad_gate, grad_up, mlp_grads = mlp_backward_last(l, ahead, cache[1][1])
            mlp_share = data_sum(mlp_grads)
            partial = mlp_input_grad(l, sec, grad_gate, grad_up, mlp_weights)
            where_late, partial[0] = lax.optimization_barrier((where, partial[0]))
            last_sums = last_gate_sums(where_late, last_partial, cotangent, picks)
            parts, last_sums = send_parts(partial, last_sums, True)
            grad_out = cotangent
            projected = None
        else:
            partial, grads, kept = mlp_backward(
                l, where, grad_blocks, mlp_weights, (c1, c2), [grad_out]
            )
            projected = cache[0][4]
            grad_out = kept[1]
            mlp_grads = mlp_weight_grads(mlp_in, grads, hidden)
            parts, (mlp_grads, earlier) = send_parts([kept[0]] + partial, (mlp_grads, shares[1][1]), True)
            shares[1] = (shares[1][0], earlier)
            mlp_share = data_sum(mlp_grads)
        grad_attended, grad_after, sums2 = back_of_mlp(
            where, parts, grad_out, after, attended, projected, mods[l], picks_own
        )
        blocks = gather_blocks(grad_attended)
        partial, kept = attention_backward(l, blocks, (wq, wo), saved, tables, grad_after)
        grads, grad_attended, own, gain_sums[l], grad_after = kept
        attention_grads = attention_weight_grads(attention_in, grads, mixed, grad_attended, place.T)
        if l == 1:
            parts, (attention_grads, mlp_share) = send_parts([own] + partial, (attention_grads, mlp_share), True)
            attention_share = data_sum(attention_grads)
            sums1, grad_projected, grad_out = back_of_attention(
                where, parts, grad_after, state_kept, mods[1], picks_own, mods[0]
            )
            grad_blocks = gather_blocks(grad_projected)
            shares[1] = (mlp_share, attention_share)
        else:
            parts, attention_grads = send_parts([own] + partial, attention_grads, True)
            sums1, grad_state = back_of_attention(where, parts, grad_after, inputs, mods[0], picks_own, None)
        item_sums[l] = jnp.concatenate([sums1, sums2], axis=0)

    item_sums[1] = jnp.concatenate([item_sums[1], last_sums], axis=0)
    sums = jnp.stack(item_sums)[:, :, :items].transpose(0, 2, 1, 3).reshape(2 * items, 6 * width)
    gain_parts = jnp.concatenate([jnp.concatenate([g[0:1], g[1:2]], axis=1) for g in gain_sums])
    gain_parts = jnp.pad(gain_parts, ((0, 2 * items - 2), (0, 0)))
    pieces = [
        jnp.concatenate([lax.dynamic_slice_in_dim(sums, (tensor ^ k) * columns, columns, 1), gain_parts], axis=1)
        for k in range(group)
    ]
    got = send_parts(pieces)
    total = (got[0] + got[1]) + (got[2] + got[3])
    total, attention_grads, mlp_share = lax.optimization_barrier((total, attention_grads, mlp_share))
    shares[0] = (mlp_share, data_sum(attention_grads))
    last_partial[1:], total = lax.optimization_barrier((last_partial[1:], total))
    output = last_output(send_parts(last_partial), cache[1][3], mods[1], picks_own)
    layers = total[:, :columns].reshape(2, items, columns).astype(BF).astype(F32)
    gain_rows = jnp.pad(total[:2, None, columns:], ((0, 0), (0, items - 1), (0, 0)))
    layers = jnp.concatenate([layers, gain_rows], axis=2)
    mine = jnp.where(is_first, layers[0], layers[1])
    theirs = exchange(jnp.where(is_first, layers[1], layers[0]), "section", 1)
    gain_total = mine[0:1, columns:] + theirs[0:1, columns:]
    mods_grad = jnp.concatenate(
        [jnp.where(is_first, mine, theirs)[:, :columns], jnp.where(is_first, theirs, mine)[:, :columns]]
    )
    packed = jnp.concatenate(
        [mods_grad, scaled.astype(F32), jnp.pad(gain_total, ((0, 2 * items - 1), (0, 0)))], axis=1
    )
    gathered = gather_dp(packed)
    all_mods = gathered[:, :, :columns].astype(BF)
    deep = width // lax.axis_size("dp")
    scaled_share = lax.dynamic_slice_in_dim(gathered, columns + data * deep, deep, 2).astype(BF)
    grad_ada = jnp.einsum("nid,nic->dc", scaled_share, all_mods, preferred_element_type=F32)
    gain_total = jnp.sum(gathered[:, 0, columns + width :], axis=0)
    cond_value = conditioning[:, 0].astype(F32)
    sigma = jax.nn.sigmoid(cond_value)
    cond_part = jnp.einsum("ic,dc->id", mods_grad.astype(BF), modulator[0], preferred_element_type=F32)
    cond_part = cond_part.reshape(micro, items, width) * sigma * (1.0 + cond_value * (1.0 - sigma))
    grad_cond = group_sum(group_sum(cond_part, "section"), "tensor")
    half = LANE // 2
    gain_total = gain_total.reshape(2, LANE)
    grad_gains = jnp.concatenate([gain_total[:, :HALF], gain_total[:, half : half + HALF]], axis=1)
    mine = jnp.where(is_first, grad_state, output)
    theirs = exchange(jnp.where(is_first, output, grad_state), "section", 1)
    results = jnp.stack([jnp.where(is_first, mine, theirs), jnp.where(is_first, theirs, mine)])

    def joined(which):
        mine = jnp.where(is_first, shares[0][which], shares[1][which])
        theirs = exchange(jnp.where(is_first, shares[1][which], shares[0][which]), "section", 1)
        low = jnp.where(is_first, mine, theirs)
        high = jnp.where(is_first, theirs, mine)
        return jnp.concatenate([low, high], axis=0).astype(F32)

    size = down_weight.shape[1]
    mlp_grads = joined(0)
    grad_pair = jnp.stack([mlp_grads[:, :size], mlp_grads[:, size : 2 * size]])
    grad_down = mlp_grads[:, 2 * size :].T
    attention_grads = joined(1)
    grad_qkv = jnp.stack([attention_grads[:, i * narrow : (i + 1) * narrow] for i in range(3)])
    grad_out_w = attention_grads[:, 3 * narrow :].T

    return (
        grad_ada[None],
        grad_qkv[None],
        grad_gains[None],
        grad_out_w[None],
        grad_pair[None],
        grad_down[None],
        grad_cond[:, None],
        results[None],
    )


def solution(mesh):
    return jax.shard_map(
        shards,
        mesh=mesh,
        in_specs=(
            P(None, "dp", None),
            P(None, "dp", None),
            P(None, "dp", None, None),
            P(None, "dp", None),
            P(None, None, "dp"),
            P("section", None, "tensor"),
            P("section", None, None, "tensor"),
            P("section", None, None),
            P("section", "tensor", None),
            P("section", None, None, "tensor"),
            P("section", "tensor", None),
        ),
        out_specs=(
            P("section", "dp", "tensor"),
            P("section", None, "dp", "tensor"),
            P("section", None, None),
            P("section", "tensor", "dp"),
            P("section", None, "dp", "tensor"),
            P("section", "tensor", "dp"),
            P(None, "dp", None, None),
            P("section", None, ("dp", "tensor"), None),
        ),
        check_vma=False,
    )
```

```python
import functools

import jax
import jax.numpy as jnp
from jax import lax
from jax.experimental import pallas as pl
from jax.experimental.pallas import tpu as pltpu
from jax.sharding import PartitionSpec as P
import numpy as np

HEAD = 72
HALF = HEAD // 2
LANE = 128
epsilon = 1e-06
BF = jnp.bfloat16
F32 = jnp.float32
HIGHEST = lax.Precision.HIGHEST
VM = pl.BlockSpec(memory_space=pltpu.VMEM)
SM = pl.BlockSpec(memory_space=pltpu.SMEM)
HB = pl.BlockSpec(memory_space=pltpu.HBM)
FREE = pl.BlockSpec(memory_space=pltpu.VMEM)


def nn(a, b):
    return lax.dot_general(a, b, (((1,), (0,)), ((), ())), preferred_element_type=F32)


def nt(a, b):
    return lax.dot_general(a, b, (((1,), (1,)), ((), ())), preferred_element_type=F32)


def tn(a, b):
    return lax.dot_general(a, b, (((0,), (0,)), ((), ())), preferred_element_type=F32)


def call(body, outs, in_specs, scratch=(), name=None, kept=0, limit=24, aliases={}):
    small = len(outs) - kept
    kernel = pl.pallas_call(
        body,
        out_shape=[pltpu.VMEM(o.shape, o.dtype) for o in outs[:small]] + [pltpu.HBM(o.shape, o.dtype) for o in outs[small:]],
        in_specs=in_specs,
        out_specs=[VM] * small + [HB] * kept,
        scratch_shapes=list(scratch),
        input_output_aliases=aliases,
        compiler_params=pltpu.CompilerParams(vmem_limit_bytes=limit * 2**20),
        cost_estimate=pl.CostEstimate(flops=1000, bytes_accessed=1000, transcendentals=0),
        name=name,
    )

    def run(*args):
        spaces = {id(HB): pltpu.HBM, id(VM): pltpu.VMEM}
        placed = [
            pltpu.with_memory_space_constraint(arg, spaces[id(spec)]) if id(spec) in spaces else arg
            for arg, spec in zip(args, in_specs)
        ]
        return kernel(*placed)

    return run


def shape(dims, dtype):
    return jax.ShapeDtypeStruct(dims, dtype)


def fetch(is_own, own, other, where, sem):
    @pl.when(is_own)
    def _():
        pltpu.make_async_copy(own, where, sem).start()

    @pl.when(jnp.logical_not(is_own))
    def _():
        pltpu.make_async_copy(other, where, sem).start()


def arrived(own, where, sem):
    pltpu.make_async_copy(own, where, sem).wait()


def load(pairs, sems):
    made = [pltpu.make_async_copy(there, here, sems.at[i]) for i, (there, here) in enumerate(pairs)]
    for one in made:
        one.start()
    return made


def finish(copies):
    for one in copies:
        one.wait()


def rows_of(whole, where_ref, here):
    share = whole.shape[1] // 4
    pairs = []
    for k in range(here.shape[0] // share):
        there = pl.ds(pl.multiple_of((where_ref[1] ^ k) * share, LANE), share)
        pairs.append((whole.at[where_ref[0], there], here.at[pl.ds(k * share, share)]))
    return pairs


def own_rows(whole, where_ref, here):
    return rows_of(whole, where_ref, here) if len(whole.shape) == 3 else [(whole, here)]


def inverse_rms(value):
    return lax.rsqrt(jnp.mean(value * value, axis=-1, keepdims=True) + epsilon)


def norm_back(grad, normed, inverse):
    return inverse * (grad - normed * jnp.mean(grad * normed, axis=-1, keepdims=True))


def token_mod(picks, mods_ref, part):
    width = mods_ref.shape[1] // 6
    return nn(picks, mods_ref[:, part * width : (part + 1) * width])


def image_sums(picks, value):
    return lax.dot_general(
        picks.astype(F32),
        value,
        (((0,), (0,)), ((), ())),
        precision=HIGHEST,
        preferred_element_type=F32,
    )


def swap_halves(value):
    return pltpu.roll(value, LANE // 2, 1)


def rotate(value, cosine, sine):
    return value * cosine + swap_halves(value) * sine


def unrotate(grad, cosine, sine):
    return grad * cosine - swap_halves(grad) * sine


def head_mean(value):
    return nn(value.astype(BF), jnp.full((LANE, LANE), 1.0, BF)) * (1.0 / HEAD)


def head_inverse(raw):
    return lax.rsqrt(head_mean(raw * raw) + epsilon)


def split_store(value, rows, block_refs):
    own = block_refs[0]
    share = own.shape[0]
    for k, ref in enumerate(block_refs):
        ref[:, rows] = value[k * share : (k + 1) * share].astype(ref.dtype)


def modulation_part(conditioning, modulator_t):
    micro, items = conditioning.shape[0], conditioning.shape[2]
    columns, width = modulator_t.shape
    step = 5 * LANE
    spans = [(j, min(step, columns - j)) for j in range(0, columns, step)]

    def body(cond_ref, mod_in, scaled_ref, part_ref, mod_ref, sems):
        copies = load([(mod_in.at[pl.ds(j, size)], mod_ref.at[pl.ds(j, size)]) for j, size in spans], sems)
        cond = jnp.concatenate([cond_ref[m, 0].astype(F32) for m in range(micro)], axis=0)
        scaled = (cond * jax.nn.sigmoid(cond)).astype(BF)
        scaled_ref[...] = scaled
        for copy, (j, size) in zip(copies, spans):
            copy.wait()
            part_ref[:, j : j + size] = nt(scaled, mod_ref[j : j + size]).astype(BF)

    return call(
        body,
        [shape((micro * items, width), BF), shape((micro * items, columns), BF)],
        [FREE, HB],
        [pltpu.VMEM((columns, width), BF), pltpu.SemaphoreType.DMA((len(spans),))],
        name="modulation_part",
        limit=12,
    )(conditioning, modulator_t)


def modulation_rows(pieces, gains, where, place_one):
    rows, columns = pieces[0].shape
    count = len(pieces)
    items = rows // 2

    def body(where_ref, *refs):
        piece_refs, (ga, gb, one_ref, own_ref, send_ref, gains_ref) = refs[:count], refs[count:]
        section, tensor = where_ref[0], where_ref[1]
        values = [ref[...].astype(F32) for ref in piece_refs]
        ordered = []
        for j in range(count):
            picked = jnp.zeros_like(values[0])
            for k in range(count):
                picked = jnp.where((tensor ^ k) == j, values[k], picked)
            ordered.append(picked)
        whole = jnp.concatenate(ordered, axis=1)
        blank = jnp.zeros((8 - items, whole.shape[1]), F32)
        first = jnp.concatenate([whole[:items], blank], axis=0)
        second = jnp.concatenate([whole[items:], blank], axis=0)
        own_ref[...] = jnp.where(section == 0, first, second).astype(BF)
        send_ref[...] = jnp.where(section == 0, second, first).astype(BF)
        a, b = ga[...], gb[...]
        first = jnp.where(section == 0, a, b)
        second = jnp.where(section == 0, b, a)
        both = jnp.concatenate([first, second, jnp.zeros((4, first.shape[1]), F32)], axis=0)
        gains_ref[...] = lax.dot_general(
            both, one_ref[...], (((1,), (0,)), ((), ())), precision=HIGHEST, preferred_element_type=F32
        )

    return call(
        body,
        [shape((8, count * columns), BF)] * 2 + [shape((8, LANE), F32)],
        [SM] + [VM] * count + [FREE] * 3,
        name="modulation_rows",
        limit=8,
    )(where, *pieces, *gains, place_one)


def prepare_tables(where, lengths, positions, rates):
    rows = positions.shape[2]
    share = rows // 4
    items = lengths.shape[2]

    def body(where_ref, len_ref, pos_ref, rate_ref, cos_ref, sin_ref, segc_ref, segr_ref, picks_ref, own_ref):
        section, tensor = where_ref[0], where_ref[1]

        def segments(index):
            place = (tensor ^ (index // share)) * share + index % share
            segment = jnp.zeros_like(index)
            end = 0
            for i in range(items):
                end = end + len_ref[section, 0, i]
                segment += (place >= end).astype(jnp.int32)
            return segment

        column = segments(lax.broadcasted_iota(jnp.int32, (rows, 1), 0))
        segc_ref[...] = column
        segr_ref[...] = segments(lax.broadcasted_iota(jnp.int32, (1, rows), 1))
        picks = jnp.where(column == lax.broadcasted_iota(jnp.int32, (rows, 8), 1), 1.0, 0.0).astype(BF)
        picks_ref[...] = picks
        own_ref[...] = picks[:share]
        blocks = [
            pos_ref[section, :, pl.ds(pl.multiple_of((tensor ^ k) * share, LANE), share)] for k in range(4)
        ]
        place = jnp.concatenate(blocks, axis=1).astype(F32)
        lane = lax.broadcasted_iota(jnp.int32, (LANE // 2, rows), 0)
        phase = jnp.where(lane < HEAD // 4, place[0:1], place[1:2]) * rate_ref[...]
        cosine = jnp.where(lane < HALF, jnp.cos(phase), 0.0)
        sine = jnp.where(lane < HALF, jnp.sin(phase), 0.0)
        cos_ref[...] = jnp.concatenate([cosine, cosine], axis=0).T
        sin_ref[...] = jnp.concatenate([-sine, sine], axis=0).T

    return call(
        body,
        [
            shape((rows, LANE), F32),
            shape((rows, LANE), F32),
            shape((rows, 1), jnp.int32),
            shape((1, rows), jnp.int32),
            shape((rows, 8), BF),
            shape((share, 8), BF),
        ],
        [SM, SM, FREE, FREE],
        name="prepare_tables",
        limit=16,
    )(where, lengths, positions, rates)


def prepare_weights(where, source, place, begun=None, only=None):
    wq, wo = source
    narrow, width = wq.shape[1:]
    padded = place.shape[1]

    def body(where_ref, wq_in, wo_in, place_ref, *refs):
        wq_out, wo_out, wq_ref, wo_ref, wide_ref, tall_ref, sems, out_sems = refs if begun is None else refs[2:]
        section = where_ref[0]

        def make(layer):
            copies = load([(wq_in.at[i], wq_ref.at[i]) for i in range(3)] + [(wo_in, wo_ref)], sems)
            outs = []
            for i in range(3):
                copies[i].wait()
                wide_ref[i] = tn(wq_ref[i], place_ref[...]).astype(BF)
                outs += load([(wide_ref.at[i], wq_out.at[layer, i])], out_sems.at[pl.ds(i, 1)])
            copies[3].wait()
            tall_ref[...] = tn(place_ref[...], wo_ref[...]).astype(BF)
            finish(outs + load([(tall_ref, wo_out.at[layer])], out_sems.at[pl.ds(3, 1)]))

        if only is None:
            make(section)
        else:

            @pl.when(section == only)
            def _():
                make(1 - only)

    args = [where, wq, wo, place] + ([] if begun is None else list(begun))
    return call(
        body,
        [shape((2, 3, width, padded), BF), shape((2, padded, width), BF)],
        [SM, HB, HB, FREE] + ([] if begun is None else [HB, HB]),
        [
            pltpu.VMEM((3, narrow, width), BF),
            pltpu.VMEM((narrow, width), BF),
            pltpu.VMEM((3, width, padded), BF),
            pltpu.VMEM((padded, width), BF),
            pltpu.SemaphoreType.DMA((4,)),
            pltpu.SemaphoreType.DMA((4,)),
        ],
        name="prepare_weights",
        limit=24,
        kept=2,
        aliases={} if begun is None else {4: 0, 5: 1},
    )(*args)


def last_ahead(where, cotangent, down_own, down_got, mods, picks):
    rows = picks.shape[0]
    size, width = down_own.shape

    def body(where_ref, cot_in, wd_a, wd_b, mods_ref, picks_ref, gp_out, gh_out, gp_ref, gh_ref, wd_ref, sems):
        copies = load(rows_of(cot_in, where_ref, gp_ref), sems)
        fetch(where_ref[0] == 1, wd_a, wd_b, wd_ref, sems.at[4])
        finish(copies)
        gp_ref[...] = (gp_ref[...].astype(F32) * token_mod(picks_ref[...], mods_ref, 5)).astype(BF)
        outs = load([(gp_ref, gp_out)], sems)
        arrived(wd_a, wd_ref, sems.at[4])
        gh_ref[...] = nt(gp_ref[...], wd_ref[...]).astype(BF)
        finish(outs + load([(gh_ref, gh_out)], sems.at[pl.ds(1, 1)]))

    return call(
        body,
        [shape((rows, width), BF), shape((rows, size), BF)],
        [SM] + [HB] * 3 + [VM] * 2,
        [
            pltpu.VMEM((rows, width), BF),
            pltpu.VMEM((rows, size), BF),
            pltpu.VMEM((size, width), BF),
            pltpu.SemaphoreType.DMA((5,)),
        ],
        name="last_ahead",
        limit=16,
        kept=2,
    )(where, cotangent, down_own, down_got, mods, picks)


def attention_forward(layer, where, blocks, weights, tables, mods, picks, carried=()):
    wq, wo = weights
    cosine, sine, gains, seg_col, seg_row = tables
    padded, width = wo.shape[1:]
    heads = padded // LANE
    raw_input = len(blocks) == 1
    rows = cosine.shape[0]
    share = rows // 4
    scale = HEAD**-0.5
    QB = 512

    def body(where_ref, *refs):
        refs = list(refs)
        in_refs = [refs.pop(0) for _ in blocks]
        wq_in, wo_in, cos_ref, sin_ref, gain_ref, segc_ref, segr_ref, mods_ref, picks_ref = refs[:9]
        refs = refs[9:]
        carried_refs = [refs.pop(0) for _ in carried]
        p_refs = [refs.pop(0) for _ in range(4)]
        state_ref = refs.pop(0) if raw_input else None
        kept = [refs.pop(0) for _ in range(7)]
        carried_outs = [refs.pop(0) for _ in carried]
        wq_ref, wo_ref, mask_ref = refs[:3]
        here = refs[3:10]
        sems, out_sems, carried_sems, a_x_ref, x_sems = refs[10:]
        if raw_input:
            x_ref = a_x_ref
            x_copies = load(rows_of(in_refs[0], where_ref, x_ref), x_sems)
        qraw_ref, kraw_ref, qrot_ref, krot_ref, v_ref, mixed_ref, a_ref = here
        pairs = [(wq_in.at[layer, i], wq_ref.at[i]) for i in range(3)] + [(wo_in.at[layer], wo_ref)]
        weights_in = load(pairs[:1], sems)

        def keep(i):
            pltpu.make_async_copy(here[i], kept[i], out_sems.at[i]).start()

        if raw_input:
            picked = picks_ref[...]
            shift1 = token_mod(picked, mods_ref, 0)
            scale1 = token_mod(picked, mods_ref, 1)
            finish(x_copies)
            state_ref[...] = x_ref[:share]
            x = x_ref[...].astype(F32)
            a_ref[...] = (x * inverse_rms(x) * (1.0 + scale1) + shift1).astype(BF)
        else:
            for k, ref in enumerate(in_refs):
                a_ref[k * share : (k + 1) * share] = ref[...]
        mask_ref[...] = jnp.where(segc_ref[...] == segr_ref[...], 1.0, 0.0).astype(BF)
        cos = cos_ref[...]
        sin = sin_ref[...]
        for i, (raw_out, rot_out) in enumerate(((qraw_ref, qrot_ref), (kraw_ref, krot_ref))):
            weights_in[i].wait()
            if i == 0:
                weights_in += load(pairs[1:], sems.at[pl.ds(1, 3)])
                carried_copies = load(list(zip(carried_refs, carried_outs)), carried_sems)
                keep(6)
            gain = gain_ref[2 * layer + i : 2 * layer + i + 1]
            for h2 in range(0, heads, 2):
                both = nn(a_ref[...], wq_ref[i, :, h2 * LANE : (h2 + 2) * LANE])
                for h in (h2, h2 + 1):
                    at = slice(h * LANE, (h + 1) * LANE)
                    raw = both[:, (h - h2) * LANE : (h - h2 + 1) * LANE]
                    raw_out[:, at] = raw.astype(BF)
                    turned = rotate(raw * head_inverse(raw) * gain, cos, sin)
                    rot_out[:, at] = turned.astype(BF)
            keep(i)
            keep(2 + i)
        weights_in[2].wait()
        one = jnp.where(lax.broadcasted_iota(jnp.int32, (1, padded), 1) % LANE == LANE - 1, 1.0, 0.0)
        v_ref[...] = (nn(a_ref[...], wq_ref[2]) + one).astype(BF)
        keep(4)

        for j in range(rows // QB):
            at_rows = slice(j * QB, (j + 1) * QB)
            for h in range(heads):
                at = slice(h * LANE, (h + 1) * LANE)
                scores = nt(qrot_ref[at_rows, at], krot_ref[:, at]) * scale
                grown = jnp.exp(scores).astype(BF) * mask_ref[at_rows]
                mixed = nn(grown, v_ref[:, at])
                mixed_ref[at_rows, at] = (mixed * (1.0 / mixed[:, LANE - 1 :])).astype(BF)
        keep(5)
        weights_in[3].wait()
        step = 3 * LANE
        for j in range(width // step):
            at = slice(j * step, (j + 1) * step)
            split_store(nn(mixed_ref[...], wo_ref[:, at]), at, p_refs)
        for i in range(7):
            pltpu.make_async_copy(here[i], kept[i], out_sems.at[i]).wait()
        finish(carried_copies)

    outs = [shape((share, width), BF)] * (5 if raw_input else 4)
    saved_shapes = [shape((rows, padded), BF)] * 6 + [shape((rows, width), BF)]
    result = call(
        body,
        outs + saved_shapes + [shape(c.shape, c.dtype) for c in carried],
        [SM] + ([HB] if raw_input else [VM] * 4) + [HB] * 2 + [VM] * (7 + len(carried)),
        [
            pltpu.VMEM((3, width, padded), BF),
            pltpu.VMEM((padded, width), BF),
            pltpu.VMEM((rows, rows), BF),
        ] + [pltpu.VMEM(s.shape, BF) for s in saved_shapes] + [
            pltpu.SemaphoreType.DMA((4,)),
            pltpu.SemaphoreType.DMA((7,)),
            pltpu.SemaphoreType.DMA((max(1, len(carried)),)),
            pltpu.VMEM((rows if raw_input else 16, width), BF),
            pltpu.SemaphoreType.DMA((4,)),
        ],
        name=f"attention_forward_{layer}",
        limit=28,
        kept=7 + len(carried),
    )(where, *blocks, wq, wo, cosine, sine, gains, seg_col, seg_row, mods, picks, *carried)
    n = len(outs)
    return list(result[:4]), list(result[4:n]), list(result[n : n + 7]), list(result[n + 7 :])


def add_parts(refs):
    total = refs[0][...].astype(F32)
    for ref in refs[1:]:
        total += ref[...].astype(F32)
    return total


def after_attention(parts, state, mods, picks):
    dims = state.shape

    def body(p0, p1, p2, p3, state_ref, mods_ref, picks_ref, mlp_ref, attended_ref, after_ref):
        picked = picks_ref[...]
        attended = add_parts((p0, p1, p2, p3))
        attended_ref[...] = attended.astype(BF)
        after = state_ref[...].astype(F32) + token_mod(picked, mods_ref, 2) * attended
        after_ref[...] = after
        normed = after * inverse_rms(after)
        mlp_ref[...] = (normed * (1.0 + token_mod(picked, mods_ref, 4)) + token_mod(picked, mods_ref, 3)).astype(BF)

    return call(
        body,
        [shape(dims, BF), shape(dims, BF), shape(dims, F32)],
        [VM] * 7,
        name="after_attention",
        limit=8,
    )(*parts, state, mods, picks)


def after_mlp(parts, after, mods, picks, mods_next):
    dims = after.shape

    def body(p0, p1, p2, p3, after_ref, mods_ref, picks_ref, next_ref, in_ref, projected_ref, state_ref):
        picked = picks_ref[...]
        projected = add_parts((p0, p1, p2, p3))
        output = after_ref[...] + token_mod(picked, mods_ref, 5) * projected
        low = output.astype(BF)
        state_ref[...] = low
        state = low.astype(F32)
        normed = state * inverse_rms(state)
        in_ref[...] = (normed * (1.0 + token_mod(picked, next_ref, 1)) + token_mod(picked, next_ref, 0)).astype(BF)
        projected_ref[...] = projected.astype(BF)

    return call(
        body,
        [shape(dims, BF)] * 3,
        [VM] * 8,
        name="after_mlp",
        limit=8,
    )(*parts, after, mods, picks, mods_next)


def last_output(parts, after, mods, picks):
    dims = after.shape

    def body(p0_in, p1, p2, p3, after_in, mods_ref, picks_ref, output_ref, p0, after_ref, sems):
        copies = load([(p0_in, p0), (after_in, after_ref)], sems)
        gate2 = token_mod(picks_ref[...], mods_ref, 5)
        finish(copies)
        output_ref[...] = after_ref[...] + gate2 * add_parts((p0, p1, p2, p3))

    return call(
        body,
        [shape(dims, F32)],
        [HB] + [VM] * 3 + [HB] + [VM] * 2,
        [pltpu.VMEM(dims, BF), pltpu.VMEM(dims, F32), pltpu.SemaphoreType.DMA((2,))],
        name="last_output",
        limit=8,
    )(*parts, after, mods, picks)[0]


def last_projection(layer, where, hidden, weights, cotangent, picks):
    wd_own, wd_got = weights[2:]
    rows, size = hidden.shape
    width = wd_own.shape[1]
    share = rows // 4
    step = 3 * LANE

    def body(where_ref, hid_in, wd_a, wd_b, cot_in, picks_ref, p0, p1, p2, p3, sums_out,
             hid_ref, wd_ref, g_ref, q0, q1, q2, q3, sums_ref, sems, cot_sems, out_sems):
        fetch(where_ref[0] == layer, wd_a, wd_b, wd_ref, sems.at[0])
        copies = load([(hid_in, hid_ref)], sems.at[pl.ds(1, 1)]) + load(rows_of(cot_in, where_ref, g_ref), cot_sems)
        arrived(wd_a, wd_ref, sems.at[0])
        finish(copies)
        picked = picks_ref[...]
        for j in range(width // step):
            at = slice(j * step, (j + 1) * step)
            part = nn(hid_ref[...], wd_ref[:, at])
            split_store(part, at, (q0, q1, q2, q3))
            sums_ref[0, :, at] = image_sums(picked, g_ref[:, at].astype(F32) * part)
        finish(load([(q0, p0), (q1, p1), (q2, p2), (q3, p3), (sums_ref, sums_out)], out_sems))

    sums = (1, picks.shape[1], width)
    result = call(
        body,
        [shape((share, width), BF)] * 4 + [shape(sums, F32)],
        [SM] + [HB] * 4 + [VM],
        [
            pltpu.VMEM((rows, size), BF),
            pltpu.VMEM((size, width), BF),
            pltpu.VMEM((rows, width), BF),
        ]
        + [pltpu.VMEM((share, width), BF)] * 4
        + [
            pltpu.VMEM(sums, F32),
            pltpu.SemaphoreType.DMA((2,)),
            pltpu.SemaphoreType.DMA((4,)),
            pltpu.SemaphoreType.DMA((5,)),
        ],
        name="last_projection",
        limit=16,
        kept=5,
    )(where, hidden, wd_own, wd_got, cotangent, picks)
    return list(result[:4]), result[4]


def attention_results(where, mine, theirs):
    half, columns = mine.shape
    narrow = columns // 4
    eye = jnp.eye(2 * half, dtype=BF)

    def body(where_ref, mine_ref, theirs_ref, eye_ref, qkv_out, out_out, qkv_ref, out_ref, sems):
        a, b = mine_ref[...].astype(F32), theirs_ref[...].astype(F32)
        first = where_ref[0] == 0
        full = jnp.concatenate([jnp.where(first, a, b), jnp.where(first, b, a)], axis=0)
        for i in range(3):
            qkv_ref[i] = full[:, i * narrow : (i + 1) * narrow]
        copies = load([(qkv_ref, qkv_out)], sems)
        out_ref[...] = tn(full[:, 3 * narrow :].astype(BF), eye_ref[...])
        finish(copies + load([(out_ref, out_out)], sems.at[pl.ds(1, 1)]))

    return call(
        body,
        [shape((3, 2 * half, narrow), F32), shape((narrow, 2 * half), F32)],
        [SM, VM, VM, FREE],
        [
            pltpu.VMEM((3, 2 * half, narrow), F32),
            pltpu.VMEM((narrow, 2 * half), F32),
            pltpu.SemaphoreType.DMA((2,)),
        ],
        name="attention_results",
        limit=12,
        kept=2,
    )(where, mine, theirs, eye)


def mlp_forward(layer, blocks, weights, section, carried, late):
    gu_own, gu_got, wd_own, wd_got = weights
    hidden_size, width = wd_own.shape
    share = blocks[0].shape[0]
    rows = share * 4
    chunk = 2 * LANE
    chunks = hidden_size // chunk

    def body(sec_ref, b0, b1, b2, b3, gu_a, gu_b, wd_a, wd_b, attended_ref, after_ref,
             *refs):
        refs = list(refs)
        p_refs = [] if late else [refs.pop(0) for _ in range(4)]
        hid_out, c1_out, c2_out, a_out, attended_out, after_out = refs[:6]
        refs = refs[6:]
        p_outs = [refs.pop(0) for _ in range(4)] if late else []
        a_ref, gu_ref, wd_ref, hid_ref, c1_ref, c2_ref, sems, out_sems, carried_sems = refs[:9]
        if late:
            p_refs, p_sems = refs[9:13], refs[13]
        own = sec_ref[0] == layer
        for j in range(chunks):
            at = pl.ds(j * chunk, chunk)
            for i in range(2):
                fetch(own, gu_a.at[i, :, at], gu_b.at[i, :, at], gu_ref.at[i, :, at], sems.at[2 * j + i])
        fetch(own, wd_a, wd_b, wd_ref, sems.at[2 * chunks])
        carried_copies = load([(attended_ref, attended_out), (after_ref, after_out)], carried_sems)
        for k, ref in enumerate((b0, b1, b2, b3)):
            a_ref[k * share : (k + 1) * share] = ref[...]
        for j in range(chunks):
            at = slice(j * chunk, (j + 1) * chunk)
            for i in range(2):
                arrived(gu_a.at[i, :, pl.ds(j * chunk, chunk)], gu_ref.at[i, :, pl.ds(j * chunk, chunk)], sems.at[2 * j + i])
            gate = nn(a_ref[...], gu_ref[0, :, at])
            up = nn(a_ref[...], gu_ref[1, :, at])
            sigma = jax.nn.sigmoid(gate)
            silu = gate * sigma
            hid_ref[:, at] = (silu * up).astype(BF)
            c1_ref[:, at] = (up * (sigma + silu * (1.0 - sigma))).astype(BF)
            c2_ref[:, at] = silu.astype(BF)
        kept = load([(hid_ref, hid_out), (c1_ref, c1_out), (c2_ref, c2_out), (a_ref, a_out)], out_sems)
        arrived(wd_a, wd_ref, sems.at[2 * chunks])
        step = 3 * LANE
        for j in range(width // step):
            at = slice(j * step, (j + 1) * step)
            split_store(nn(hid_ref[...], wd_ref[:, at]), at, p_refs)
        if late:
            kept += load(list(zip(p_refs, p_outs)), p_sems)
        finish(kept + carried_copies)

    parts = [shape((share, width), BF)] * 4
    outs = ([] if late else parts) + [shape((rows, hidden_size), BF)] * 3 + [shape((rows, width), BF)]
    outs += [shape(c.shape, c.dtype) for c in carried] + (parts if late else [])
    result = call(
        body,
        outs,
        [SM] + [VM] * 4 + [HB] * 4 + [VM] * 2,
        [
            pltpu.VMEM((rows, width), BF),
            pltpu.VMEM(gu_own.shape, BF),
            pltpu.VMEM(wd_own.shape, BF),
        ]
        + [pltpu.VMEM((rows, hidden_size), BF)] * 3
        + [
            pltpu.SemaphoreType.DMA((2 * chunks + 1,)),
            pltpu.SemaphoreType.DMA((4,)),
            pltpu.SemaphoreType.DMA((2,)),
        ]
        + ([pltpu.VMEM((share, width), BF)] * 4 + [pltpu.SemaphoreType.DMA((4,))] if late else []),
        name=f"mlp_forward_{layer}",
        kept=10 if late else 6,
    )(section, *blocks, gu_own, gu_got, wd_own, wd_got, *carried)
    result = list(result)
    partial = result[6:] if late else result[:4]
    result = result[:6] if late else result[4:]
    return partial, result[:4], result[4:]


def mlp_backward(layer, where, blocks, weights, saved, carried):
    gu_own, gu_got, wd_own, wd_got = weights
    c1, c2 = saved
    hidden_size, width = wd_own.shape
    rows = c1.shape[0]
    share = rows // 4
    chunk = 2 * LANE
    chunks = hidden_size // chunk

    def body(where_ref, *refs):
        refs = list(refs)
        in_refs = [refs.pop(0) for _ in blocks]
        gu_a, gu_b, wd_a, wd_b, c1_in, c2_in = refs[:6]
        refs = refs[6:]
        carried_refs = [refs.pop(0) for _ in carried]
        p_refs = [refs.pop(0) for _ in range(3)]
        outs = [refs.pop(0) for _ in range(4)]
        carried_outs = [refs.pop(0) for _ in carried]
        gu_ref, wd_ref, c1_ref, c2_ref, gg_ref, gup_ref, gp_ref, p0, sems, in_sems, out_sems, carried_sems = refs
        own = where_ref[0] == layer
        for j in range(chunks):
            at = pl.ds(j * chunk, chunk)
            fetch(own, wd_a.at[at], wd_b.at[at], wd_ref.at[at], sems.at[j])
        saved_copies = load([(c1_in, c1_ref), (c2_in, c2_ref)], in_sems)
        for i in range(2):
            fetch(own, gu_a.at[i], gu_b.at[i], gu_ref.at[i], sems.at[chunks + i])
        kept = load(list(zip(carried_refs, carried_outs)), carried_sems)
        for k, ref in enumerate(in_refs):
            gp_ref[k * share : (k + 1) * share] = ref[...]

        def keep(i, here):
            kept.append(pltpu.make_async_copy(here, outs[i], out_sems.at[i]))
            kept[-1].start()

        keep(0, gp_ref)
        for j in range(chunks):
            at = slice(j * chunk, (j + 1) * chunk)
            arrived(wd_a.at[pl.ds(j * chunk, chunk)], wd_ref.at[pl.ds(j * chunk, chunk)], sems.at[j])
            grad_hidden = nt(gp_ref[...], wd_ref[at])
            if j == 0:
                finish(saved_copies)
            gg_ref[:, at] = (grad_hidden * c1_ref[:, at].astype(F32)).astype(BF)
            gup_ref[:, at] = (grad_hidden * c2_ref[:, at].astype(F32)).astype(BF)
        keep(1, gg_ref)
        keep(2, gup_ref)
        for i in range(2):
            arrived(gu_a.at[i], gu_ref.at[i], sems.at[chunks + i])
        step = 3 * LANE
        for j in range(width // step):
            at = slice(j * step, (j + 1) * step)
            split_store(nt(gg_ref[...], gu_ref[0, at]) + nt(gup_ref[...], gu_ref[1, at]), at, [p0] + p_refs)
        keep(3, p0)
        finish(kept)

    outs = [shape((share, width), BF)] * 3
    outs += [shape((rows, width), BF)] + [shape((rows, hidden_size), BF)] * 2 + [shape((share, width), BF)]
    outs += [shape(c.shape, c.dtype) for c in carried]
    result = call(
        body,
        outs,
        [SM] + [VM] * 4 + [HB] * 6 + [VM] * len(carried),
        [
            pltpu.VMEM(gu_own.shape, BF),
            pltpu.VMEM(wd_own.shape, BF),
        ]
        + [pltpu.VMEM((rows, hidden_size), BF)] * 4
        + [
            pltpu.VMEM((rows, width), BF),
            pltpu.VMEM((share, width), BF),
            pltpu.SemaphoreType.DMA((chunks + 2,)),
            pltpu.SemaphoreType.DMA((2,)),
            pltpu.SemaphoreType.DMA((4,)),
            pltpu.SemaphoreType.DMA((max(1, len(carried)),)),
        ],
        name=f"mlp_backward_{layer}",
        kept=4 + len(carried),
    )(where, *blocks, gu_own, gu_got, wd_own, wd_got, c1, c2, *carried)
    return list(result[:3]), list(result[3:6]), list(result[6:])


def mlp_last(layer, blocks, weights, ahead, section, carried):
    gu_own, gu_got = weights[:2]
    grad_projected, grad_hidden = ahead
    rows, size = grad_hidden.shape
    width = gu_own.shape[1]
    share = rows // 4
    chunk = 2 * LANE
    chunks = size // chunk
    step = 3 * LANE

    def body(sec_ref, b0, b1, b2, b3, gu_a, gu_b, gp_in, gh_in, attended_ref, after_ref,
             gg_ref, gup_ref, out, hid_out, attended_out, after_out,
             a_ref, gu_ref, hid_ref, gh_ref, gp_ref, full_ref, sems, in_sems, out_sems, kept_sems):
        own = sec_ref[0] == layer
        for j in range(chunks):
            at = pl.ds(j * chunk, chunk)
            for i in range(2):
                fetch(own, gu_a.at[i, :, at], gu_b.at[i, :, at], gu_ref.at[i, :, at], sems.at[2 * j + i])
        ins = load([(gh_in, gh_ref), (gp_in, gp_ref)], in_sems)
        kept = load([(attended_ref, attended_out), (after_ref, after_out)], kept_sems)
        for k, ref in enumerate((b0, b1, b2, b3)):
            a_ref[k * share : (k + 1) * share] = ref[...]
        for j in range(chunks):
            at = slice(j * chunk, (j + 1) * chunk)
            for i in range(2):
                here = pl.ds(j * chunk, chunk)
                arrived(gu_a.at[i, :, here], gu_ref.at[i, :, here], sems.at[2 * j + i])
            gate = nn(a_ref[...], gu_ref[0, :, at])
            up = nn(a_ref[...], gu_ref[1, :, at])
            if j == 0:
                ins[0].wait()
            sigma = jax.nn.sigmoid(gate)
            silu = gate * sigma
            grad = gh_ref[:, at].astype(F32)
            hid_ref[:, at] = (silu * up).astype(BF)
            gg_ref[:, at] = (grad * (up * (sigma + silu * (1.0 - sigma)))).astype(BF)
            gup_ref[:, at] = (grad * silu).astype(BF)
        kept += load([(hid_ref, hid_out)], kept_sems.at[pl.ds(2, 1)])
        ins[1].wait()
        for j in range(width // step):
            at = slice(j * step, (j + 1) * step)
            left = a_ref[:, at]
            full_ref[at, :size] = tn(left, gg_ref[...]).astype(BF)
            full_ref[at, size : 2 * size] = tn(left, gup_ref[...]).astype(BF)
            full_ref[at, 2 * size :] = tn(gp_ref[:, at], hid_ref[...]).astype(BF)
            here = pl.ds(j * step, step)
            kept += load([(full_ref.at[here], out.at[here])], out_sems.at[pl.ds(j, 1)])
        finish(kept)

    result = call(
        body,
        [shape((rows, size), BF)] * 2
        + [shape((width, 3 * size), BF), shape((rows, size), BF)]
        + [shape(c.shape, c.dtype) for c in carried],
        [SM] + [VM] * 4 + [HB] * 4 + [VM] * 2,
        [
            pltpu.VMEM((rows, width), BF),
            pltpu.VMEM(gu_own.shape, BF),
            pltpu.VMEM((rows, size), BF),
            pltpu.VMEM((rows, size), BF),
            pltpu.VMEM((rows, width), BF),
            pltpu.VMEM((width, 3 * size), BF),
            pltpu.SemaphoreType.DMA((2 * chunks,)),
            pltpu.SemaphoreType.DMA((2,)),
            pltpu.SemaphoreType.DMA((width // step,)),
            pltpu.SemaphoreType.DMA((3,)),
        ],
        name=f"mlp_last_{layer}",
        kept=4,
        limit=28,
    )(section, *blocks, gu_own, gu_got, grad_projected, grad_hidden, *carried)
    return list(result[:2]), result[2], result[3], list(result[4:])


def mlp_input_grad(layer, section, grad_gate, grad_up, weights):
    gu_own, gu_got = weights[:2]
    rows = grad_gate.shape[0]
    width = gu_own.shape[1]
    share = rows // 4
    step = 3 * LANE

    def body(sec_ref, gg_ref, gup_ref, gu_a, gu_b, p1, p2, p3, p0_out, p0, gu_ref, sems, out_sems):
        own = sec_ref[0] == layer
        spans = [pl.ds(j * step, step) for j in range(width // step)]
        for j, at in enumerate(spans):
            for i in range(2):
                fetch(own, gu_a.at[i, at], gu_b.at[i, at], gu_ref.at[i, at], sems.at[2 * j + i])
        for j, at in enumerate(spans):
            for i in range(2):
                arrived(gu_a.at[i, at], gu_ref.at[i, at], sems.at[2 * j + i])
            here = slice(j * step, (j + 1) * step)
            split_store(
                nt(gg_ref[...], gu_ref[0, here]) + nt(gup_ref[...], gu_ref[1, here]), here, (p0, p1, p2, p3)
            )
        finish(load([(p0, p0_out)], out_sems))

    result = call(
        body,
        [shape((share, width), BF)] * 4,
        [SM, VM, VM, HB, HB],
        [
            pltpu.VMEM((share, width), BF),
            pltpu.VMEM(gu_own.shape, BF),
            pltpu.SemaphoreType.DMA((2 * (width // step),)),
            pltpu.SemaphoreType.DMA((1,)),
        ],
        name="mlp_input_grad",
        kept=1,
        limit=16,
    )(section, grad_gate, grad_up, gu_own, gu_got)
    return [result[3]] + list(result[:3])


def mlp_weight_grads(mlp_in, grads, hidden):
    grad_projected, grad_gate, grad_up = grads
    rows, width = grad_projected.shape
    size = hidden.shape[1]
    step = 3 * LANE

    def body(a_in, gg_in, gu_in, gp_in, hid_in, *refs):
        out, a_ref, gg_ref, gu_ref, gp_ref, hid_ref, full_ref, in_sems, sems = refs
        ins = load([(a_in, a_ref), (gg_in, gg_ref), (gu_in, gu_ref), (gp_in, gp_ref), (hid_in, hid_ref)], in_sems)
        kept = []
        finish(ins[:2])
        for j in range(width // step):
            at = slice(j * step, (j + 1) * step)
            left = a_ref[:, at]
            full_ref[at, :size] = tn(left, gg_ref[...]).astype(BF)
            if j == 0:
                ins[2].wait()
            full_ref[at, size : 2 * size] = tn(left, gu_ref[...]).astype(BF)
            if j == 0:
                finish(ins[3:])
            full_ref[at, 2 * size :] = tn(gp_ref[:, at], hid_ref[...]).astype(BF)
            here = pl.ds(j * step, step)
            kept.append(pltpu.make_async_copy(full_ref.at[here], out.at[here], sems.at[j]))
            kept[-1].start()
        finish(kept)

    result = call(
        body,
        [shape((width, 3 * size), BF)],
        [HB] * 5,
        [pltpu.VMEM((rows, width), BF)]
        + [pltpu.VMEM((rows, size), BF)] * 2
        + [
            pltpu.VMEM((rows, width), BF),
            pltpu.VMEM((rows, size), BF),
            pltpu.VMEM((width, 3 * size), BF),
            pltpu.SemaphoreType.DMA((5,)),
            pltpu.SemaphoreType.DMA((width // step,)),
        ],
        name="mlp_weight_grads",
        kept=1,
    )(mlp_in, grad_gate, grad_up, grad_projected, hidden)
    return result[0]


def attention_backward(layer, blocks, weights, saved, tables, grad_after):
    wq, wo = weights
    cosine, sine, gains, seg_col, seg_row = tables
    rows, padded = saved[0].shape
    width = wo.shape[2]
    heads = padded // LANE
    share = rows // 4
    scale = HEAD**-0.5
    QB = 512

    def body(b0, b1, b2, b3, wq_in, wo_in, qraw_in, kraw_in, qrot_in, krot_in, v_in,
             cos_ref, sin_ref, gain_ref, segc_ref, segr_ref, grad_ref,
             p1, p2, p3, g_out, ga_out, p0_out, ggain_out, grad_out,
             wq_ref, wo_ref, qraw_ref, kraw_ref, qrot_ref, krot_ref, v_ref, mask_ref,
             ga_ref, gmix_ref, gq_ref, gk_ref, g_ref, p0, ggain_ref, sems, in_sems):
        ins = [(wo_in.at[layer], wo_ref)]
        ins += [(qrot_in, qrot_ref), (krot_in, krot_ref), (v_in, v_ref), (qraw_in, qraw_ref), (kraw_in, kraw_ref)]
        ins += [(wq_in.at[layer, i], wq_ref.at[i]) for i in range(3)]
        ins = load(ins, in_sems)
        for k, ref in enumerate((b0, b1, b2, b3)):
            ga_ref[k * share : (k + 1) * share] = ref[...]
        kept = []

        def keep(here, there):
            kept.append(pltpu.make_async_copy(here, there, sems.at[len(kept)]))
            kept[-1].start()

        keep(ga_ref, ga_out)
        keep(grad_ref, grad_out)
        mask_ref[...] = jnp.where(segc_ref[...] == segr_ref[...], 1.0, 0.0).astype(BF)
        ins[0].wait()
        gmix_ref[...] = nt(ga_ref[...], wo_ref[...]).astype(BF)
        finish(ins[1:4])
        for h in range(heads):
            at = slice(h * LANE, (h + 1) * LANE)
            for j in range(rows // QB):
                at_rows = slice(j * QB, (j + 1) * QB)
                query = qrot_ref[at_rows, at]
                grad_mixed = gmix_ref[at_rows, at]
                scores = nt(krot_ref[:, at], query) * scale
                grown = (jnp.exp(scores).astype(BF) * mask_ref[:, at_rows]).astype(F32)
                weights_t = grown * (1.0 / jnp.sum(grown, axis=0, keepdims=True))
                grad_weights = nt(v_ref[:, at], grad_mixed)
                add_v = nn(weights_t.astype(BF), grad_mixed)
                product = weights_t * grad_weights
                delta = jnp.sum(product, axis=0, keepdims=True)
                grad_scores = (product - weights_t * delta).astype(BF)
                gq_ref[at_rows, at] = tn(grad_scores, krot_ref[:, at])
                add_k = nn(grad_scores, query)
                total_v = add_v if j == 0 else total_v + add_v
                total_k = add_k if j == 0 else total_k + add_k
            gk_ref[:, at] = total_k
            g_ref[:, 2 * padded + h * LANE : 2 * padded + (h + 1) * LANE] = total_v.astype(BF)
        cos = cos_ref[...]
        sin = sin_ref[...]
        finish(ins[4:6])
        ggain_ref[...] = jnp.zeros_like(ggain_ref)
        for i, (raw_ref, grad_ref) in enumerate(((qraw_ref, gq_ref), (kraw_ref, gk_ref))):
            gain = gain_ref[2 * layer + i : 2 * layer + i + 1]
            gain_sum = jnp.zeros((1, LANE), F32)
            for h in range(heads):
                at = slice(h * LANE, (h + 1) * LANE)
                raw = raw_ref[:, at].astype(F32)
                inverse = head_inverse(raw)
                normed = raw * inverse
                turned = unrotate(grad_ref[:, at], cos, sin) * scale
                product = turned * normed
                gain_sum += jnp.sum(product, axis=0, keepdims=True)
                back = inverse * (turned * gain - normed * head_mean(product * gain))
                g_ref[:, i * padded + h * LANE : i * padded + (h + 1) * LANE] = back.astype(BF)
            ggain_ref[i : i + 1] = gain_sum
        keep(g_ref, g_out)
        keep(ggain_ref, ggain_out)
        finish(ins[6:])
        step = 3 * LANE
        for j in range(width // step):
            at = slice(j * step, (j + 1) * step)
            total = nt(g_ref[:, :padded], wq_ref[0, at])
            total += nt(g_ref[:, padded : 2 * padded], wq_ref[1, at])
            total += nt(g_ref[:, 2 * padded :], wq_ref[2, at])
            split_store(total, at, (p0, p1, p2, p3))
        keep(p0, p0_out)
        finish(kept)

    outs = [shape((share, width), BF)] * 3
    outs += [shape((rows, 3 * padded), BF), shape((rows, width), BF), shape((share, width), BF), shape((8, LANE), F32)]
    outs += [shape(grad_after.shape, F32)]
    result = call(
        body,
        outs,
        [VM] * 4 + [HB] * 7 + [VM] * 6,
        [
            pltpu.VMEM((3, width, padded), BF),
            pltpu.VMEM((padded, width), BF),
        ]
        + [pltpu.VMEM((rows, padded), BF)] * 5
        + [
            pltpu.VMEM((rows, rows), BF),
            pltpu.VMEM((rows, width), BF),
            pltpu.VMEM((rows, padded), BF),
            pltpu.VMEM((rows, padded), F32),
            pltpu.VMEM((rows, padded), F32),
            pltpu.VMEM((rows, 3 * padded), BF),
            pltpu.VMEM((share, width), BF),
            pltpu.VMEM((8, LANE), F32),
            pltpu.SemaphoreType.DMA((5,)),
            pltpu.SemaphoreType.DMA((9,)),
        ],
        name=f"attention_backward_{layer}",
        limit=32,
        kept=5,
    )(*blocks, wq, wo, *saved[:5], cosine, sine, gains, seg_col, seg_row, grad_after)
    return list(result[:3]), list(result[3:])


def attention_weight_grads(attention_in, grads, mixed, grad_attended, place):
    rows, width = attention_in.shape
    padded, narrow = place.shape
    step = 3 * LANE


    def body(a_in, g_in, mixed_in, ga_in, place_ref, out, a_ref, g_ref, mixed_ref, ga_ref, right_ref, full_ref, in_sems, sems):
        ins = load([(g_in, g_ref), (mixed_in, mixed_ref), (a_in, a_ref), (ga_in, ga_ref)], in_sems)
        finish(ins[:2])
        for i in range(3):
            right_ref[i] = nn(g_ref[:, i * padded : (i + 1) * padded], place_ref[...]).astype(BF)
        right_ref[3] = nn(mixed_ref[...], place_ref[...]).astype(BF)
        finish(ins[2:])
        kept = []
        for j in range(width // step):
            at = slice(j * step, (j + 1) * step)
            left = a_ref[:, at]
            for i in range(3):
                full_ref[at, i * narrow : (i + 1) * narrow] = tn(left, right_ref[i]).astype(BF)
            full_ref[at, 3 * narrow :] = tn(ga_ref[:, at], right_ref[3]).astype(BF)
            here = pl.ds(j * step, step)
            kept.append(pltpu.make_async_copy(full_ref.at[here], out.at[here], sems.at[j]))
            kept[-1].start()
        finish(kept)

    result = call(
        body,
        [shape((width, 4 * narrow), BF)],
        [HB] * 4 + [FREE],
        [
            pltpu.VMEM((rows, width), BF),
            pltpu.VMEM((rows, 3 * padded), BF),
            pltpu.VMEM((rows, padded), BF),
            pltpu.VMEM((rows, width), BF),
            pltpu.VMEM((4, rows, narrow), BF),
            pltpu.VMEM((width, 4 * narrow), BF),
            pltpu.SemaphoreType.DMA((4,)),
            pltpu.SemaphoreType.DMA((width // step,)),
        ],
        name="attention_weight_grads",
        kept=1,
    )(attention_in, grads, mixed, grad_attended, place)
    return result[0]


def back_of_mlp(where, parts, grad_out, after, attended, projected, mods, picks):
    dims = after.shape
    extra = [] if projected is None else [projected]
    sums = (3 + len(extra), picks.shape[1], dims[1])

    def body(where_ref, p0_in, p1, p2, p3, g_in, after_in, attended_in, *refs):
        refs = list(refs)
        extra_refs = [refs.pop(0) for _ in extra]
        (mods_ref, picks_ref, ga_ref, grad_ref, sums_out,
         p0, g_ref, after_ref, attended_ref, projected_ref, sums_ref, sems, out_sems) = refs
        pairs = [(p0_in, p0), (after_in, after_ref)] + own_rows(g_in, where_ref, g_ref)
        ins = load(pairs + [(attended_in, attended_ref)] + [(ref, projected_ref) for ref in extra_refs], sems)
        picked = picks_ref[...]
        scale2 = token_mod(picked, mods_ref, 4)
        gate1 = token_mod(picked, mods_ref, 2)
        finish(ins[:2])
        grad_in = add_parts((p0, p1, p2, p3))
        after = after_ref[...]
        inverse = inverse_rms(after)
        normed = after * inverse
        finish(ins[2:])
        g = g_ref[...].astype(F32)
        grad_after = g + norm_back(grad_in * (1.0 + scale2), normed, inverse)
        sums_ref[0] = image_sums(picked, grad_after * attended_ref[...].astype(F32))
        sums_ref[1] = image_sums(picked, grad_in)
        sums_ref[2] = image_sums(picked, grad_in * normed)
        if extra:
            sums_ref[3] = image_sums(picked, g * projected_ref[...].astype(F32))
        kept = load([(sums_ref, sums_out)], out_sems)
        grad_ref[...] = grad_after
        ga_ref[...] = (grad_after * gate1).astype(BF)
        finish(kept)

    return call(
        body,
        [shape(dims, BF), shape(dims, F32), shape(sums, F32)],
        [SM, HB] + [VM] * 3 + [HB] * (3 + len(extra)) + [VM] * 2,
        [
            pltpu.VMEM(dims, BF),
            pltpu.VMEM(dims, BF),
            pltpu.VMEM(dims, F32),
            pltpu.VMEM(dims, BF),
            pltpu.VMEM(dims, BF),
            pltpu.VMEM(sums, F32),
            pltpu.SemaphoreType.DMA((5,)),
            pltpu.SemaphoreType.DMA((1,)),
        ],
        name="back_of_mlp",
        limit=10,
        kept=1,
    )(where, *parts, grad_out, after, attended, *extra, mods, picks)


def back_of_attention(where, parts, grad_after, state, mods, picks, mods_below):
    first = mods_below is None
    dims = grad_after.shape

    def body(where_ref, p0_in, p1, p2, p3, grad_in_ref, state_in, mods_ref, picks_ref, *refs):
        refs = list(refs)
        below_ref = None if first else refs.pop(0)
        sums_ref = refs.pop(0)
        gp_ref = None if first else refs.pop(0)
        out_ref, p0, grad_ref, state_ref, sems = refs
        ins = load([(p0_in, p0), (grad_in_ref, grad_ref)] + own_rows(state_in, where_ref, state_ref), sems)
        picked = picks_ref[...]
        scale1 = token_mod(picked, mods_ref, 1)
        finish(ins)
        grad_in = add_parts((p0, p1, p2, p3))
        state = state_ref[...].astype(F32)
        inverse = inverse_rms(state)
        normed = state * inverse
        grad_state = grad_ref[...] + norm_back(grad_in * (1.0 + scale1), normed, inverse)
        out_ref[...] = grad_state.astype(out_ref.dtype)
        if not first:
            gp_ref[...] = (grad_state.astype(BF).astype(F32) * token_mod(picked, below_ref, 5)).astype(BF)
        sums_ref[0] = image_sums(picked, grad_in)
        sums_ref[1] = image_sums(picked, grad_in * normed)

    outs = [shape((2, picks.shape[1], dims[1]), F32)] + ([shape(dims, F32)] if first else [shape(dims, BF)] * 2)
    extra = () if first else (mods_below,)
    return call(
        body,
        outs,
        [SM, HB] + [VM] * 3 + [HB] * 2 + [VM] * (2 + len(extra)),
        [
            pltpu.VMEM(dims, BF),
            pltpu.VMEM(dims, F32),
            pltpu.VMEM(dims, BF),
            pltpu.SemaphoreType.DMA((3,)),
        ],
        name="back_of_attention",
        limit=10,
    )(where, *parts, grad_after, state, mods, picks, *extra)


def exchange(value, axis, k):
    return lax.ppermute(value, axis, [(i, i ^ k) for i in range(lax.axis_size(axis))])


def handed_on(value):
    def body(source, target):
        target[...] = source[...]

    return call(body, [shape(value.shape, value.dtype)], [VM], name="handed_on", limit=4)(value)[0]


def in_order(got, order):
    for place, k in enumerate(order):
        for _ in range(len(order) - 1 - place):
            got[k] = handed_on(got[k])


def send_parts(parts, beside=None, whole=False):
    got = {k: exchange(parts[k], "tensor", k) for k in (3, 1, 2)}
    if beside is not None and not whole:
        got[1], beside = lax.optimization_barrier((got[1], beside))
    if whole:
        got, beside = lax.optimization_barrier((got, beside))
    else:
        in_order(got, (1, 2, 3))
    result = [parts[0], got[1], got[2], got[3]]
    return result if beside is None else (result, beside)


def gather_blocks(own):
    got = {k: exchange(own, "tensor", k) for k in (3, 1, 2)}
    in_order(got, (3, 2, 1))
    return [own, got[1], got[2], got[3]]


def group_sum(value, axis):
    k = 1
    while k < lax.axis_size(axis):
        value = value + exchange(value, axis, k)
        k *= 2
    return value


def gather_dp(value):
    count = lax.axis_size("dp")
    if count > 4:
        return lax.all_gather(value, "dp", axis=0)
    me = lax.axis_index("dp")
    got = [value] + [exchange(value, "dp", k) for k in range(1, count)]
    stacked = jnp.stack(got)
    return jnp.stack([lax.dynamic_index_in_dim(stacked, me ^ j, 0, keepdims=False) for j in range(count)])


def head_places(heads):
    place = np.zeros((heads * HEAD, heads * LANE), np.float32)
    for h in range(heads):
        for j in range(HEAD):
            place[h * HEAD + j, h * LANE + (j // HALF) * (LANE // 2) + j % HALF] = 1.0
    return place


def shards(
    inputs,
    cotangent,
    conditioning,
    lengths,
    positions,
    modulator,
    projections,
    norm_gains,
    out_weight,
    gate_up,
    down_weight,
):
    section = lax.axis_index("section")
    other = 1 - section
    tensor = lax.axis_index("tensor")
    data = lax.axis_index("dp")
    micro, _, width = inputs.shape
    rows = inputs.shape[1]
    group = lax.axis_size("tensor")
    share = rows // group
    items = lengths.shape[2]
    narrow = projections.shape[3]
    heads = narrow // HEAD
    columns = modulator.shape[2]
    sec = section.reshape(1).astype(jnp.int32)

    where = jnp.stack([section, tensor]).astype(jnp.int32)
    is_first = section == 0

    where = jnp.stack([section, tensor]).astype(jnp.int32)
    is_first = section == 0
    place = jnp.asarray(head_places(heads), BF)
    place_one = jnp.asarray(head_places(1), F32)

    own = (jnp.swapaxes(projections[0], 1, 2), out_weight[0])
    got = [exchange(value, "section", 1) for value in own]
    got_gains = exchange(norm_gains[0], "section", 1)
    scaled, part = modulation_part(conditioning, jnp.swapaxes(modulator[0], 0, 1))
    pieces = gather_blocks(part)
    quarter = HEAD // 4
    rates = 10000.0 ** (-jnp.arange(quarter).astype(F32) / quarter)
    rates = jnp.concatenate([rates, rates, jnp.zeros(LANE // 2 - HALF, F32)])[:, None]
    where_late, part = lax.optimization_barrier((where, part))
    cosine, sine, seg_col, seg_row, picks, picks_own = prepare_tables(where_late, lengths, positions, rates)
    wq, wo = prepare_weights(where_late, own, place)
    pieces, got, cosine, wq = lax.optimization_barrier((pieces, got, cosine, wq))
    mods_own, mods_send, gains = modulation_rows([part] + pieces[1:], (norm_gains[0], got_gains), where, place_one)
    mods_got = exchange(mods_send, "section", 1)
    gu_send, wd_send, mods_got = lax.optimization_barrier((gate_up[0], down_weight[0], mods_got))
    mods = [jnp.where(is_first, mods_own, mods_got), jnp.where(is_first, mods_got, mods_own)]
    gu_got = exchange(gu_send, "section", 1)
    wd_got = exchange(wd_send, "section", 1)
    mlp_weights = (gate_up[0], gu_got, down_weight[0], wd_got)
    wq, mods_first = lax.optimization_barrier((wq, mods[0]))
    mods[0] = mods_first
    wq, wo = prepare_weights(where, got, place, (wq, wo), 1)
    tables = (cosine, sine, gains, seg_col, seg_row)

    cache = []
    attention_blocks = [inputs]
    carried = ()
    for l in range(2):
        partial, state, saved, kept = attention_forward(
            l, where, attention_blocks, (wq, wo), tables, mods[l], picks, carried
        )
        if l == 0:
            state = state[0]
            wq, mixed = lax.optimization_barrier((wq, saved[5]))
            saved[5] = mixed
            wq, wo = prepare_weights(where, got, place, (wq, wo), 0)
            parts, wq = send_parts(partial, wq)
        else:
            parts = send_parts(partial)
            cache[0].append(kept[0])
            state = carried[1]
            state_kept = kept[1]
        mlp_in, attended, after = after_attention(parts, state, mods[l], picks_own)
        if l == 1:
            grads, mlp_grads, hidden, kept = mlp_last(
                l, gather_blocks(mlp_in), mlp_weights, ahead, sec, (attended, after)
            )
            cache.append([saved] + kept)
            break
        partial, mlp_saved, kept = mlp_forward(l, gather_blocks(mlp_in), mlp_weights, sec, (attended, after), False)
        cache.append([saved, mlp_saved] + kept)
        if l == 0:
            where_late, partial[0] = lax.optimization_barrier((where, partial[0]))
            ahead = last_ahead(where_late, cotangent, down_weight[0], wd_got, mods[1], picks)
            parts, ahead = send_parts(partial, ahead)
            attention_in, projected, state = after_mlp(parts, after, mods[0], picks_own, mods[1])
            carried = (projected, state)
            attention_blocks = gather_blocks(attention_in)

    item_sums = [None, None]
    gain_sums = [None, None]
    shares = [None, None]

    def data_sum(value):
        return lax.psum_scatter(value, ("dp", "section"), scatter_dimension=0, tiled=True)

    for l in (1, 0):
        if l == 1:
            saved, attended, after = cache[1]
            mlp_share = data_sum(mlp_grads)
            partial = mlp_input_grad(l, sec, *grads, mlp_weights)
            where_late, partial[0] = lax.optimization_barrier((where, partial[0]))
            last_partial, last_sums = last_projection(l, where_late, hidden, mlp_weights, cotangent, picks)
            parts, last_sums = send_parts(partial, last_sums, True)
            grad_out = cotangent
            projected = None
        else:
            saved, (hidden, c1, c2, mlp_in), attended, after = cache[0][:4]
            partial, grads, kept = mlp_backward(
                l, where, grad_blocks, mlp_weights, (c1, c2), [grad_out]
            )
            projected = cache[0][4]
            grad_out = kept[1]
            mlp_grads = mlp_weight_grads(mlp_in, grads, hidden)
            parts, (mlp_grads, earlier) = send_parts([kept[0]] + partial, (mlp_grads, shares[1][1]), True)
            shares[1] = (shares[1][0], earlier)
            mlp_share = data_sum(mlp_grads)
        mixed, attention_in = saved[5:]
        grad_attended, grad_after, sums2 = back_of_mlp(
            where, parts, grad_out, after, attended, projected, mods[l], picks_own
        )
        blocks = gather_blocks(grad_attended)
        partial, kept = attention_backward(l, blocks, (wq, wo), saved, tables, grad_after)
        grads, grad_attended, own, gain_sums[l], grad_after = kept
        attention_grads = attention_weight_grads(attention_in, grads, mixed, grad_attended, place.T)
        if l == 1:
            parts, (attention_grads, mlp_share) = send_parts([own] + partial, (attention_grads, mlp_share), True)
            attention_share = data_sum(attention_grads)
            sums1, grad_projected, grad_out = back_of_attention(
                where, parts, grad_after, state_kept, mods[1], picks_own, mods[0]
            )
            grad_blocks = gather_blocks(grad_projected)
            shares[1] = (mlp_share, attention_share)
        else:
            parts, attention_grads = send_parts([own] + partial, attention_grads, True)
            sums1, grad_state = back_of_attention(where, parts, grad_after, inputs, mods[0], picks_own, None)
        item_sums[l] = jnp.concatenate([sums1, sums2], axis=0)

    item_sums[1] = jnp.concatenate([item_sums[1], last_sums], axis=0)
    sums = jnp.stack(item_sums)[:, :, :items].transpose(0, 2, 1, 3).reshape(2 * items, 6 * width)
    gain_parts = jnp.concatenate([jnp.concatenate([g[0:1], g[1:2]], axis=1) for g in gain_sums])
    gain_parts = jnp.pad(gain_parts, ((0, 2 * items - 2), (0, 0)))
    pieces = [
        jnp.concatenate([lax.dynamic_slice_in_dim(sums, (tensor ^ k) * columns, columns, 1), gain_parts], axis=1)
        for k in range(group)
    ]
    got = send_parts(pieces)
    total = (got[0] + got[1]) + (got[2] + got[3])
    total, attention_grads, mlp_share = lax.optimization_barrier((total, attention_grads, mlp_share))
    shares[0] = (mlp_share, data_sum(attention_grads))
    last_partial[1:], total = lax.optimization_barrier((last_partial[1:], total))
    output = last_output(send_parts(last_partial), cache[1][2], mods[1], picks_own)
    layers = total[:, :columns].reshape(2, items, columns).astype(BF).astype(F32)
    gain_rows = jnp.pad(total[:2, None, columns:], ((0, 0), (0, items - 1), (0, 0)))
    layers = jnp.concatenate([layers, gain_rows], axis=2)
    mine = jnp.where(is_first, layers[0], layers[1])
    theirs = exchange(jnp.where(is_first, layers[1], layers[0]), "section", 1)
    gain_total = mine[0:1, columns:] + theirs[0:1, columns:]
    mods_grad = jnp.concatenate(
        [jnp.where(is_first, mine, theirs)[:, :columns], jnp.where(is_first, theirs, mine)[:, :columns]]
    )
    packed = jnp.concatenate(
        [mods_grad, scaled.astype(F32), jnp.pad(gain_total, ((0, 2 * items - 1), (0, 0)))], axis=1
    )
    gathered = gather_dp(packed)
    all_mods = gathered[:, :, :columns].astype(BF)
    deep = width // lax.axis_size("dp")
    scaled_share = lax.dynamic_slice_in_dim(gathered, columns + data * deep, deep, 2).astype(BF)
    grad_ada = jnp.einsum("nid,nic->dc", scaled_share, all_mods, preferred_element_type=F32)
    gain_total = jnp.sum(gathered[:, 0, columns + width :], axis=0)
    cond_value = conditioning[:, 0].astype(F32)
    sigma = jax.nn.sigmoid(cond_value)
    cond_part = jnp.einsum("ic,dc->id", mods_grad.astype(BF), modulator[0], preferred_element_type=F32)
    cond_part = cond_part.reshape(micro, items, width) * sigma * (1.0 + cond_value * (1.0 - sigma))
    grad_cond = group_sum(group_sum(cond_part, "section"), "tensor")
    half = LANE // 2
    gain_total = gain_total.reshape(2, LANE)
    grad_gains = jnp.concatenate([gain_total[:, :HALF], gain_total[:, half : half + HALF]], axis=1)
    mine = jnp.where(is_first, grad_state, output)
    theirs = exchange(jnp.where(is_first, output, grad_state), "section", 1)
    results = jnp.stack([jnp.where(is_first, mine, theirs), jnp.where(is_first, theirs, mine)])

    def joined(which):
        mine = jnp.where(is_first, shares[0][which], shares[1][which])
        theirs = exchange(jnp.where(is_first, shares[1][which], shares[0][which]), "section", 1)
        low = jnp.where(is_first, mine, theirs)
        high = jnp.where(is_first, theirs, mine)
        return jnp.concatenate([low, high], axis=0).astype(F32)

    size = down_weight.shape[1]
    mlp_grads = joined(0)
    grad_pair = jnp.stack([mlp_grads[:, :size], mlp_grads[:, size : 2 * size]])
    grad_down = mlp_grads[:, 2 * size :].T
    mine = jnp.where(is_first, shares[0][1], shares[1][1])
    theirs = exchange(jnp.where(is_first, shares[1][1], shares[0][1]), "section", 1)
    grad_qkv, grad_out_w = attention_results(where, mine, theirs)
    return (
        grad_ada[None],
        grad_qkv[None],
        grad_gains[None],
        grad_out_w[None],
        grad_pair[None],
        grad_down[None],
        grad_cond[:, None],
        results[None],
    )


def solution(mesh):
    return jax.shard_map(
        shards,
        mesh=mesh,
        in_specs=(
            P(None, "dp", None),
            P(None, "dp", None),
            P(None, "dp", None, None),
            P(None, "dp", None),
            P(None, None, "dp"),
            P("section", None, "tensor"),
            P("section", None, None, "tensor"),
            P("section", None, None),
            P("section", "tensor", None),
            P("section", None, None, "tensor"),
            P("section", "tensor", None),
        ),
        out_specs=(
            P("section", "dp", "tensor"),
            P("section", None, "dp", "tensor"),
            P("section", None, None),
            P("section", "tensor", "dp"),
            P("section", None, "dp", "tensor"),
            P("section", "tensor", "dp"),
            P(None, "dp", None, None),
            P("section", None, ("dp", "tensor"), None),
        ),
        check_vma=False,
    )
```

```python
import functools

import jax
import jax.numpy as jnp
from jax import lax
from jax.experimental import pallas as pl
from jax.experimental.pallas import tpu as pltpu
from jax.sharding import PartitionSpec as P
import numpy as np

HEAD = 72
HALF = HEAD // 2
LANE = 128
epsilon = 1e-06
BF = jnp.bfloat16
F32 = jnp.float32
HIGHEST = lax.Precision.HIGHEST
VM = pl.BlockSpec(memory_space=pltpu.VMEM)
SM = pl.BlockSpec(memory_space=pltpu.SMEM)
HB = pl.BlockSpec(memory_space=pltpu.HBM)
FREE = pl.BlockSpec(memory_space=pltpu.VMEM)


def nn(a, b):
    return lax.dot_general(a, b, (((1,), (0,)), ((), ())), preferred_element_type=F32)


def nt(a, b):
    return lax.dot_general(a, b, (((1,), (1,)), ((), ())), preferred_element_type=F32)


def tn(a, b):
    return lax.dot_general(a, b, (((0,), (0,)), ((), ())), preferred_element_type=F32)


def call(body, outs, in_specs, scratch=(), name=None, kept=0, limit=24, aliases={}):
    small = len(outs) - kept
    kernel = pl.pallas_call(
        body,
        out_shape=[pltpu.VMEM(o.shape, o.dtype) for o in outs[:small]] + [pltpu.HBM(o.shape, o.dtype) for o in outs[small:]],
        in_specs=in_specs,
        out_specs=[VM] * small + [HB] * kept,
        scratch_shapes=list(scratch),
        input_output_aliases=aliases,
        compiler_params=pltpu.CompilerParams(vmem_limit_bytes=limit * 2**20),
        cost_estimate=pl.CostEstimate(flops=1000, bytes_accessed=1000, transcendentals=0),
        name=name,
    )

    def run(*args):
        spaces = {id(HB): pltpu.HBM, id(VM): pltpu.VMEM}
        placed = [
            pltpu.with_memory_space_constraint(arg, spaces[id(spec)]) if id(spec) in spaces else arg
            for arg, spec in zip(args, in_specs)
        ]
        return kernel(*placed)

    return run


def shape(dims, dtype):
    return jax.ShapeDtypeStruct(dims, dtype)


def fetch(is_own, own, other, where, sem):
    @pl.when(is_own)
    def _():
        pltpu.make_async_copy(own, where, sem).start()

    @pl.when(jnp.logical_not(is_own))
    def _():
        pltpu.make_async_copy(other, where, sem).start()


def arrived(own, where, sem):
    pltpu.make_async_copy(own, where, sem).wait()


def load(pairs, sems):
    made = [pltpu.make_async_copy(there, here, sems.at[i]) for i, (there, here) in enumerate(pairs)]
    for one in made:
        one.start()
    return made


def finish(copies):
    for one in copies:
        one.wait()


def rows_of(whole, where_ref, here):
    share = whole.shape[1] // 4
    pairs = []
    for k in range(here.shape[0] // share):
        there = pl.ds(pl.multiple_of((where_ref[1] ^ k) * share, LANE), share)
        pairs.append((whole.at[where_ref[0], there], here.at[pl.ds(k * share, share)]))
    return pairs


def own_rows(whole, where_ref, here):
    return rows_of(whole, where_ref, here) if len(whole.shape) == 3 else [(whole, here)]


def inverse_rms(value):
    return lax.rsqrt(jnp.mean(value * value, axis=-1, keepdims=True) + epsilon)


def norm_back(grad, normed, inverse):
    return inverse * (grad - normed * jnp.mean(grad * normed, axis=-1, keepdims=True))


def token_mod(picks, mods_ref, part):
    width = mods_ref.shape[1] // 6
    return nn(picks, mods_ref[:, part * width : (part + 1) * width])


def image_sums(picks, value):
    return lax.dot_general(
        picks.astype(F32),
        value,
        (((0,), (0,)), ((), ())),
        precision=HIGHEST,
        preferred_element_type=F32,
    )


def swap_halves(value):
    return pltpu.roll(value, LANE // 2, 1)


def rotate(value, cosine, sine):
    return value * cosine + swap_halves(value) * sine


def unrotate(grad, cosine, sine):
    return grad * cosine - swap_halves(grad) * sine


def head_mean(value):
    return nn(value.astype(BF), jnp.full((LANE, LANE), 1.0, BF)) * (1.0 / HEAD)


def head_inverse(raw):
    return lax.rsqrt(head_mean(raw * raw) + epsilon)


def split_store(value, rows, block_refs):
    own = block_refs[0]
    share = own.shape[0]
    for k, ref in enumerate(block_refs):
        ref[:, rows] = value[k * share : (k + 1) * share].astype(ref.dtype)


def modulation_part(conditioning, modulator_t):
    micro, items = conditioning.shape[0], conditioning.shape[2]
    columns, width = modulator_t.shape
    step = 5 * LANE
    spans = [(j, min(step, columns - j)) for j in range(0, columns, step)]

    def body(cond_ref, mod_in, scaled_ref, part_ref, mod_ref, sems):
        copies = load([(mod_in.at[pl.ds(j, size)], mod_ref.at[pl.ds(j, size)]) for j, size in spans], sems)
        cond = jnp.concatenate([cond_ref[m, 0].astype(F32) for m in range(micro)], axis=0)
        scaled = (cond * jax.nn.sigmoid(cond)).astype(BF)
        scaled_ref[...] = scaled
        for copy, (j, size) in zip(copies, spans):
            copy.wait()
            part_ref[:, j : j + size] = nt(scaled, mod_ref[j : j + size]).astype(BF)

    return call(
        body,
        [shape((micro * items, width), BF), shape((micro * items, columns), BF)],
        [FREE, HB],
        [pltpu.VMEM((columns, width), BF), pltpu.SemaphoreType.DMA((len(spans),))],
        name="modulation_part",
        limit=12,
    )(conditioning, modulator_t)


def modulation_rows(pieces, gains, where, place_one):
    rows, columns = pieces[0].shape
    count = len(pieces)
    items = rows // 2

    def body(where_ref, *refs):
        piece_refs, (ga, gb, one_ref, own_ref, send_ref, gains_ref) = refs[:count], refs[count:]
        section, tensor = where_ref[0], where_ref[1]
        values = [ref[...].astype(F32) for ref in piece_refs]
        ordered = []
        for j in range(count):
            picked = jnp.zeros_like(values[0])
            for k in range(count):
                picked = jnp.where((tensor ^ k) == j, values[k], picked)
            ordered.append(picked)
        whole = jnp.concatenate(ordered, axis=1)
        blank = jnp.zeros((8 - items, whole.shape[1]), F32)
        first = jnp.concatenate([whole[:items], blank], axis=0)
        second = jnp.concatenate([whole[items:], blank], axis=0)
        own_ref[...] = jnp.where(section == 0, first, second).astype(BF)
        send_ref[...] = jnp.where(section == 0, second, first).astype(BF)
        a, b = ga[...], gb[...]
        first = jnp.where(section == 0, a, b)
        second = jnp.where(section == 0, b, a)
        both = jnp.concatenate([first, second, jnp.zeros((4, first.shape[1]), F32)], axis=0)
        gains_ref[...] = lax.dot_general(
            both, one_ref[...], (((1,), (0,)), ((), ())), precision=HIGHEST, preferred_element_type=F32
        )

    return call(
        body,
        [shape((8, count * columns), BF)] * 2 + [shape((8, LANE), F32)],
        [SM] + [VM] * count + [FREE] * 3,
        name="modulation_rows",
        limit=8,
    )(where, *pieces, *gains, place_one)


def prepare_tables(where, lengths, positions, rates):
    rows = positions.shape[2]
    share = rows // 4
    items = lengths.shape[2]

    def body(where_ref, len_ref, pos_ref, rate_ref, cos_ref, sin_ref, segc_ref, segr_ref, picks_ref, own_ref):
        section, tensor = where_ref[0], where_ref[1]

        def segments(index):
            place = (tensor ^ (index // share)) * share + index % share
            segment = jnp.zeros_like(index)
            end = 0
            for i in range(items):
                end = end + len_ref[section, 0, i]
                segment += (place >= end).astype(jnp.int32)
            return segment

        column = segments(lax.broadcasted_iota(jnp.int32, (rows, 1), 0))
        segc_ref[...] = column
        segr_ref[...] = segments(lax.broadcasted_iota(jnp.int32, (1, rows), 1))
        picks = jnp.where(column == lax.broadcasted_iota(jnp.int32, (rows, 8), 1), 1.0, 0.0).astype(BF)
        picks_ref[...] = picks
        own_ref[...] = picks[:share]
        blocks = [
            pos_ref[section, :, pl.ds(pl.multiple_of((tensor ^ k) * share, LANE), share)] for k in range(4)
        ]
        place = jnp.concatenate(blocks, axis=1).astype(F32)
        lane = lax.broadcasted_iota(jnp.int32, (LANE // 2, rows), 0)
        phase = jnp.where(lane < HEAD // 4, place[0:1], place[1:2]) * rate_ref[...]
        cosine = jnp.where(lane < HALF, jnp.cos(phase), 0.0)
        sine = jnp.where(lane < HALF, jnp.sin(phase), 0.0)
        cos_ref[...] = jnp.concatenate([cosine, cosine], axis=0).T
        sin_ref[...] = jnp.concatenate([-sine, sine], axis=0).T

    return call(
        body,
        [
            shape((rows, LANE), F32),
            shape((rows, LANE), F32),
            shape((rows, 1), jnp.int32),
            shape((1, rows), jnp.int32),
            shape((rows, 8), BF),
            shape((share, 8), BF),
        ],
        [SM, SM, FREE, FREE],
        name="prepare_tables",
        limit=16,
    )(where, lengths, positions, rates)


def prepare_weights(where, source, place, begun=None, only=None):
    wq, wo = source
    narrow, width = wq.shape[1:]
    padded = place.shape[1]

    def body(where_ref, wq_in, wo_in, place_ref, *refs):
        wq_out, wo_out, wq_ref, wo_ref, wide_ref, tall_ref, sems, out_sems = refs if begun is None else refs[2:]
        section = where_ref[0]

        def make(layer):
            copies = load([(wq_in.at[i], wq_ref.at[i]) for i in range(3)] + [(wo_in, wo_ref)], sems)
            outs = []
            for i in range(3):
                copies[i].wait()
                wide_ref[i] = tn(wq_ref[i], place_ref[...]).astype(BF)
                outs += load([(wide_ref.at[i], wq_out.at[layer, i])], out_sems.at[pl.ds(i, 1)])
            copies[3].wait()
            tall_ref[...] = tn(place_ref[...], wo_ref[...]).astype(BF)
            finish(outs + load([(tall_ref, wo_out.at[layer])], out_sems.at[pl.ds(3, 1)]))

        if only is None:
            make(section)
        else:

            @pl.when(section == only)
            def _():
                make(1 - only)

    args = [where, wq, wo, place] + ([] if begun is None else list(begun))
    return call(
        body,
        [shape((2, 3, width, padded), BF), shape((2, padded, width), BF)],
        [SM, HB, HB, FREE] + ([] if begun is None else [HB, HB]),
        [
            pltpu.VMEM((3, narrow, width), BF),
            pltpu.VMEM((narrow, width), BF),
            pltpu.VMEM((3, width, padded), BF),
            pltpu.VMEM((padded, width), BF),
            pltpu.SemaphoreType.DMA((4,)),
            pltpu.SemaphoreType.DMA((4,)),
        ],
        name="prepare_weights",
        limit=24,
        kept=2,
        aliases={} if begun is None else {4: 0, 5: 1},
    )(*args)


def last_ahead(where, cotangent, down_own, down_got, mods, picks):
    rows = picks.shape[0]
    size, width = down_own.shape

    def body(where_ref, cot_in, wd_a, wd_b, mods_ref, picks_ref, gp_out, gh_out, gp_ref, gh_ref, wd_ref, sems):
        copies = load(rows_of(cot_in, where_ref, gp_ref), sems)
        fetch(where_ref[0] == 1, wd_a, wd_b, wd_ref, sems.at[4])
        finish(copies)
        gp_ref[...] = (gp_ref[...].astype(F32) * token_mod(picks_ref[...], mods_ref, 5)).astype(BF)
        outs = load([(gp_ref, gp_out)], sems)
        arrived(wd_a, wd_ref, sems.at[4])
        gh_ref[...] = nt(gp_ref[...], wd_ref[...]).astype(BF)
        finish(outs + load([(gh_ref, gh_out)], sems.at[pl.ds(1, 1)]))

    return call(
        body,
        [shape((rows, width), BF), shape((rows, size), BF)],
        [SM] + [HB] * 3 + [VM] * 2,
        [
            pltpu.VMEM((rows, width), BF),
            pltpu.VMEM((rows, size), BF),
            pltpu.VMEM((size, width), BF),
            pltpu.SemaphoreType.DMA((5,)),
        ],
        name="last_ahead",
        limit=16,
        kept=2,
    )(where, cotangent, down_own, down_got, mods, picks)


def attention_forward(layer, where, blocks, weights, tables, mods, picks, carried=()):
    wq, wo = weights
    cosine, sine, gains, seg_col, seg_row = tables
    padded, width = wo.shape[1:]
    heads = padded // LANE
    raw_input = len(blocks) == 1
    rows = cosine.shape[0]
    share = rows // 4
    scale = HEAD**-0.5
    QB = 512

    def body(where_ref, *refs):
        refs = list(refs)
        in_refs = [refs.pop(0) for _ in blocks]
        wq_in, wo_in, cos_ref, sin_ref, gain_ref, segc_ref, segr_ref, mods_ref, picks_ref = refs[:9]
        refs = refs[9:]
        carried_refs = [refs.pop(0) for _ in carried]
        p_refs = [refs.pop(0) for _ in range(4)]
        state_ref = refs.pop(0) if raw_input else None
        kept = [refs.pop(0) for _ in range(7)]
        carried_outs = [refs.pop(0) for _ in carried]
        wq_ref, wo_ref, mask_ref = refs[:3]
        here = refs[3:10]
        sems, out_sems, carried_sems, a_x_ref, x_sems = refs[10:]
        if raw_input:
            x_ref = a_x_ref
            x_copies = load(rows_of(in_refs[0], where_ref, x_ref), x_sems)
        qraw_ref, kraw_ref, qrot_ref, krot_ref, v_ref, mixed_ref, a_ref = here
        pairs = [(wq_in.at[layer, i], wq_ref.at[i]) for i in range(3)] + [(wo_in.at[layer], wo_ref)]
        weights_in = load(pairs[:1], sems)

        def keep(i):
            pltpu.make_async_copy(here[i], kept[i], out_sems.at[i]).start()

        if raw_input:
            picked = picks_ref[...]
            shift1 = token_mod(picked, mods_ref, 0)
            scale1 = token_mod(picked, mods_ref, 1)
            finish(x_copies)
            state_ref[...] = x_ref[:share]
            x = x_ref[...].astype(F32)
            a_ref[...] = (x * inverse_rms(x) * (1.0 + scale1) + shift1).astype(BF)
        else:
            for k, ref in enumerate(in_refs):
                a_ref[k * share : (k + 1) * share] = ref[...]
        mask_ref[...] = jnp.where(segc_ref[...] == segr_ref[...], 1.0, 0.0).astype(BF)
        cos = cos_ref[...]
        sin = sin_ref[...]
        for i, (raw_out, rot_out) in enumerate(((qraw_ref, qrot_ref), (kraw_ref, krot_ref))):
            weights_in[i].wait()
            if i == 0:
                weights_in += load(pairs[1:], sems.at[pl.ds(1, 3)])
                carried_copies = load(list(zip(carried_refs, carried_outs)), carried_sems)
                keep(6)
            gain = gain_ref[2 * layer + i : 2 * layer + i + 1]
            all_raw = nn(a_ref[...], wq_ref[i])
            for h in range(heads):
                at = slice(h * LANE, (h + 1) * LANE)
                raw = all_raw[:, at]
                raw_out[:, at] = raw.astype(BF)
                turned = rotate(raw * head_inverse(raw) * gain, cos, sin)
                rot_out[:, at] = turned.astype(BF)
            keep(i)
            keep(2 + i)
        weights_in[2].wait()
        one = jnp.where(lax.broadcasted_iota(jnp.int32, (1, padded), 1) % LANE == LANE - 1, 1.0, 0.0)
        v_ref[...] = (nn(a_ref[...], wq_ref[2]) + one).astype(BF)
        keep(4)

        for j in range(rows // QB):
            at_rows = slice(j * QB, (j + 1) * QB)
            for h in range(heads):
                at = slice(h * LANE, (h + 1) * LANE)
                scores = nt(qrot_ref[at_rows, at], krot_ref[:, at]) * scale
                grown = jnp.exp(scores).astype(BF) * mask_ref[at_rows]
                mixed = nn(grown, v_ref[:, at])
                mixed_ref[at_rows, at] = (mixed * (1.0 / mixed[:, LANE - 1 :])).astype(BF)
        keep(5)
        weights_in[3].wait()
        step = 3 * LANE
        for j in range(width // step):
            at = slice(j * step, (j + 1) * step)
            split_store(nn(mixed_ref[...], wo_ref[:, at]), at, p_refs)
        for i in range(7):
            pltpu.make_async_copy(here[i], kept[i], out_sems.at[i]).wait()
        finish(carried_copies)

    outs = [shape((share, width), BF)] * (5 if raw_input else 4)
    saved_shapes = [shape((rows, padded), BF)] * 6 + [shape((rows, width), BF)]
    result = call(
        body,
        outs + saved_shapes + [shape(c.shape, c.dtype) for c in carried],
        [SM] + ([HB] if raw_input else [VM] * 4) + [HB] * 2 + [VM] * (7 + len(carried)),
        [
            pltpu.VMEM((3, width, padded), BF),
            pltpu.VMEM((padded, width), BF),
            pltpu.VMEM((rows, rows), BF),
        ] + [pltpu.VMEM(s.shape, BF) for s in saved_shapes] + [
            pltpu.SemaphoreType.DMA((4,)),
            pltpu.SemaphoreType.DMA((7,)),
            pltpu.SemaphoreType.DMA((max(1, len(carried)),)),
            pltpu.VMEM((rows if raw_input else 16, width), BF),
            pltpu.SemaphoreType.DMA((4,)),
        ],
        name=f"attention_forward_{layer}",
        limit=28,
        kept=7 + len(carried),
    )(where, *blocks, wq, wo, cosine, sine, gains, seg_col, seg_row, mods, picks, *carried)
    n = len(outs)
    return list(result[:4]), list(result[4:n]), list(result[n : n + 7]), list(result[n + 7 :])


def add_parts(refs):
    total = refs[0][...].astype(F32)
    for ref in refs[1:]:
        total += ref[...].astype(F32)
    return total


def after_attention(parts, state, mods, picks):
    dims = state.shape

    def body(p0, p1, p2, p3, state_ref, mods_ref, picks_ref, mlp_ref, attended_ref, after_ref):
        picked = picks_ref[...]
        attended = add_parts((p0, p1, p2, p3))
        attended_ref[...] = attended.astype(BF)
        after = state_ref[...].astype(F32) + token_mod(picked, mods_ref, 2) * attended
        after_ref[...] = after
        normed = after * inverse_rms(after)
        mlp_ref[...] = (normed * (1.0 + token_mod(picked, mods_ref, 4)) + token_mod(picked, mods_ref, 3)).astype(BF)

    return call(
        body,
        [shape(dims, BF), shape(dims, BF), shape(dims, F32)],
        [VM] * 7,
        name="after_attention",
        limit=8,
    )(*parts, state, mods, picks)


def after_mlp(parts, after, mods, picks, mods_next):
    dims = after.shape

    def body(p0, p1, p2, p3, after_ref, mods_ref, picks_ref, next_ref, in_ref, projected_ref, state_ref):
        picked = picks_ref[...]
        projected = add_parts((p0, p1, p2, p3))
        output = after_ref[...] + token_mod(picked, mods_ref, 5) * projected
        low = output.astype(BF)
        state_ref[...] = low
        state = low.astype(F32)
        normed = state * inverse_rms(state)
        in_ref[...] = (normed * (1.0 + token_mod(picked, next_ref, 1)) + token_mod(picked, next_ref, 0)).astype(BF)
        projected_ref[...] = projected.astype(BF)

    return call(
        body,
        [shape(dims, BF)] * 3,
        [VM] * 8,
        name="after_mlp",
        limit=8,
    )(*parts, after, mods, picks, mods_next)


def last_output(parts, after, mods, picks):
    dims = after.shape

    def body(p0_in, p1, p2, p3, after_in, mods_ref, picks_ref, output_ref, p0, after_ref, sems):
        copies = load([(p0_in, p0), (after_in, after_ref)], sems)
        gate2 = token_mod(picks_ref[...], mods_ref, 5)
        finish(copies)
        output_ref[...] = after_ref[...] + gate2 * add_parts((p0, p1, p2, p3))

    return call(
        body,
        [shape(dims, F32)],
        [HB] + [VM] * 3 + [HB] + [VM] * 2,
        [pltpu.VMEM(dims, BF), pltpu.VMEM(dims, F32), pltpu.SemaphoreType.DMA((2,))],
        name="last_output",
        limit=8,
    )(*parts, after, mods, picks)[0]


def last_projection(layer, where, hidden, weights, cotangent, picks):
    wd_own, wd_got = weights[2:]
    rows, size = hidden.shape
    width = wd_own.shape[1]
    share = rows // 4
    step = 3 * LANE

    def body(where_ref, hid_in, wd_a, wd_b, cot_in, picks_ref, p0, p1, p2, p3, sums_out,
             hid_ref, wd_ref, g_ref, q0, q1, q2, q3, sums_ref, sems, cot_sems, out_sems):
        fetch(where_ref[0] == layer, wd_a, wd_b, wd_ref, sems.at[0])
        copies = load([(hid_in, hid_ref)], sems.at[pl.ds(1, 1)]) + load(rows_of(cot_in, where_ref, g_ref), cot_sems)
        arrived(wd_a, wd_ref, sems.at[0])
        finish(copies)
        picked = picks_ref[...]
        for j in range(width // step):
            at = slice(j * step, (j + 1) * step)
            part = nn(hid_ref[...], wd_ref[:, at])
            split_store(part, at, (q0, q1, q2, q3))
            sums_ref[0, :, at] = image_sums(picked, g_ref[:, at].astype(F32) * part)
        finish(load([(q0, p0), (q1, p1), (q2, p2), (q3, p3), (sums_ref, sums_out)], out_sems))

    sums = (1, picks.shape[1], width)
    result = call(
        body,
        [shape((share, width), BF)] * 4 + [shape(sums, F32)],
        [SM] + [HB] * 4 + [VM],
        [
            pltpu.VMEM((rows, size), BF),
            pltpu.VMEM((size, width), BF),
            pltpu.VMEM((rows, width), BF),
        ]
        + [pltpu.VMEM((share, width), BF)] * 4
        + [
            pltpu.VMEM(sums, F32),
            pltpu.SemaphoreType.DMA((2,)),
            pltpu.SemaphoreType.DMA((4,)),
            pltpu.SemaphoreType.DMA((5,)),
        ],
        name="last_projection",
        limit=16,
        kept=5,
    )(where, hidden, wd_own, wd_got, cotangent, picks)
    return list(result[:4]), result[4]


def attention_results(where, mine, theirs):
    half, columns = mine.shape
    narrow = columns // 4
    eye = jnp.eye(2 * half, dtype=BF)

    def body(where_ref, mine_ref, theirs_ref, eye_ref, qkv_out, out_out, qkv_ref, out_ref, sems):
        a, b = mine_ref[...].astype(F32), theirs_ref[...].astype(F32)
        first = where_ref[0] == 0
        full = jnp.concatenate([jnp.where(first, a, b), jnp.where(first, b, a)], axis=0)
        for i in range(3):
            qkv_ref[i] = full[:, i * narrow : (i + 1) * narrow]
        copies = load([(qkv_ref, qkv_out)], sems)
        out_ref[...] = tn(full[:, 3 * narrow :].astype(BF), eye_ref[...])
        finish(copies + load([(out_ref, out_out)], sems.at[pl.ds(1, 1)]))

    return call(
        body,
        [shape((3, 2 * half, narrow), F32), shape((narrow, 2 * half), F32)],
        [SM, VM, VM, FREE],
        [
            pltpu.VMEM((3, 2 * half, narrow), F32),
            pltpu.VMEM((narrow, 2 * half), F32),
            pltpu.SemaphoreType.DMA((2,)),
        ],
        name="attention_results",
        limit=12,
        kept=2,
    )(where, mine, theirs, eye)


def mlp_forward(layer, blocks, weights, section, carried, late):
    gu_own, gu_got, wd_own, wd_got = weights
    hidden_size, width = wd_own.shape
    share = blocks[0].shape[0]
    rows = share * 4
    chunk = 2 * LANE
    chunks = hidden_size // chunk

    def body(sec_ref, b0, b1, b2, b3, gu_a, gu_b, wd_a, wd_b, attended_ref, after_ref,
             *refs):
        refs = list(refs)
        p_refs = [] if late else [refs.pop(0) for _ in range(4)]
        hid_out, c1_out, c2_out, a_out, attended_out, after_out = refs[:6]
        refs = refs[6:]
        p_outs = [refs.pop(0) for _ in range(4)] if late else []
        a_ref, gu_ref, wd_ref, hid_ref, c1_ref, c2_ref, sems, out_sems, carried_sems = refs[:9]
        if late:
            p_refs, p_sems = refs[9:13], refs[13]
        own = sec_ref[0] == layer
        for j in range(chunks):
            at = pl.ds(j * chunk, chunk)
            for i in range(2):
                fetch(own, gu_a.at[i, :, at], gu_b.at[i, :, at], gu_ref.at[i, :, at], sems.at[2 * j + i])
        fetch(own, wd_a, wd_b, wd_ref, sems.at[2 * chunks])
        carried_copies = load([(attended_ref, attended_out), (after_ref, after_out)], carried_sems)
        for k, ref in enumerate((b0, b1, b2, b3)):
            a_ref[k * share : (k + 1) * share] = ref[...]
        for j in range(chunks):
            at = slice(j * chunk, (j + 1) * chunk)
            for i in range(2):
                arrived(gu_a.at[i, :, pl.ds(j * chunk, chunk)], gu_ref.at[i, :, pl.ds(j * chunk, chunk)], sems.at[2 * j + i])
            gate = nn(a_ref[...], gu_ref[0, :, at])
            up = nn(a_ref[...], gu_ref[1, :, at])
            sigma = jax.nn.sigmoid(gate)
            silu = gate * sigma
            hid_ref[:, at] = (silu * up).astype(BF)
            c1_ref[:, at] = (up * (sigma + silu * (1.0 - sigma))).astype(BF)
            c2_ref[:, at] = silu.astype(BF)
        kept = load([(hid_ref, hid_out), (c1_ref, c1_out), (c2_ref, c2_out), (a_ref, a_out)], out_sems)
        arrived(wd_a, wd_ref, sems.at[2 * chunks])
        step = 3 * LANE
        for j in range(width // step):
            at = slice(j * step, (j + 1) * step)
            split_store(nn(hid_ref[...], wd_ref[:, at]), at, p_refs)
        if late:
            kept += load(list(zip(p_refs, p_outs)), p_sems)
        finish(kept + carried_copies)

    parts = [shape((share, width), BF)] * 4
    outs = ([] if late else parts) + [shape((rows, hidden_size), BF)] * 3 + [shape((rows, width), BF)]
    outs += [shape(c.shape, c.dtype) for c in carried] + (parts if late else [])
    result = call(
        body,
        outs,
        [SM] + [VM] * 4 + [HB] * 4 + [VM] * 2,
        [
            pltpu.VMEM((rows, width), BF),
            pltpu.VMEM(gu_own.shape, BF),
            pltpu.VMEM(wd_own.shape, BF),
        ]
        + [pltpu.VMEM((rows, hidden_size), BF)] * 3
        + [
            pltpu.SemaphoreType.DMA((2 * chunks + 1,)),
            pltpu.SemaphoreType.DMA((4,)),
            pltpu.SemaphoreType.DMA((2,)),
        ]
        + ([pltpu.VMEM((share, width), BF)] * 4 + [pltpu.SemaphoreType.DMA((4,))] if late else []),
        name=f"mlp_forward_{layer}",
        kept=10 if late else 6,
    )(section, *blocks, gu_own, gu_got, wd_own, wd_got, *carried)
    result = list(result)
    partial = result[6:] if late else result[:4]
    result = result[:6] if late else result[4:]
    return partial, result[:4], result[4:]


def mlp_backward(layer, where, blocks, weights, saved, carried):
    gu_own, gu_got, wd_own, wd_got = weights
    c1, c2 = saved
    hidden_size, width = wd_own.shape
    rows = c1.shape[0]
    share = rows // 4
    chunk = 3 * LANE
    chunks = hidden_size // chunk

    def body(where_ref, *refs):
        refs = list(refs)
        in_refs = [refs.pop(0) for _ in blocks]
        gu_a, gu_b, wd_a, wd_b, c1_in, c2_in = refs[:6]
        refs = refs[6:]
        carried_refs = [refs.pop(0) for _ in carried]
        p_refs = [refs.pop(0) for _ in range(3)]
        outs = [refs.pop(0) for _ in range(4)]
        carried_outs = [refs.pop(0) for _ in carried]
        gu_ref, wd_ref, c1_ref, c2_ref, gg_ref, gup_ref, gp_ref, p0, sems, in_sems, out_sems, carried_sems = refs
        own = where_ref[0] == layer
        for j in range(chunks):
            at = pl.ds(j * chunk, chunk)
            fetch(own, wd_a.at[at], wd_b.at[at], wd_ref.at[at], sems.at[j])
        saved_copies = load([(c1_in, c1_ref), (c2_in, c2_ref)], in_sems)
        for i in range(2):
            fetch(own, gu_a.at[i], gu_b.at[i], gu_ref.at[i], sems.at[chunks + i])
        kept = load(list(zip(carried_refs, carried_outs)), carried_sems)
        for k, ref in enumerate(in_refs):
            gp_ref[k * share : (k + 1) * share] = ref[...]

        def keep(i, here):
            kept.append(pltpu.make_async_copy(here, outs[i], out_sems.at[i]))
            kept[-1].start()

        keep(0, gp_ref)
        for j in range(chunks):
            at = slice(j * chunk, (j + 1) * chunk)
            arrived(wd_a.at[pl.ds(j * chunk, chunk)], wd_ref.at[pl.ds(j * chunk, chunk)], sems.at[j])
            grad_hidden = nt(gp_ref[...], wd_ref[at])
            if j == 0:
                finish(saved_copies)
            gg_ref[:, at] = (grad_hidden * c1_ref[:, at].astype(F32)).astype(BF)
            gup_ref[:, at] = (grad_hidden * c2_ref[:, at].astype(F32)).astype(BF)
        keep(1, gg_ref)
        keep(2, gup_ref)
        for i in range(2):
            arrived(gu_a.at[i], gu_ref.at[i], sems.at[chunks + i])
        step = 3 * LANE
        for j in range(width // step):
            at = slice(j * step, (j + 1) * step)
            split_store(nt(gg_ref[...], gu_ref[0, at]) + nt(gup_ref[...], gu_ref[1, at]), at, [p0] + p_refs)
        keep(3, p0)
        finish(kept)

    outs = [shape((share, width), BF)] * 3
    outs += [shape((rows, width), BF)] + [shape((rows, hidden_size), BF)] * 2 + [shape((share, width), BF)]
    outs += [shape(c.shape, c.dtype) for c in carried]
    result = call(
        body,
        outs,
        [SM] + [VM] * 4 + [HB] * 6 + [VM] * len(carried),
        [
            pltpu.VMEM(gu_own.shape, BF),
            pltpu.VMEM(wd_own.shape, BF),
        ]
        + [pltpu.VMEM((rows, hidden_size), BF)] * 4
        + [
            pltpu.VMEM((rows, width), BF),
            pltpu.VMEM((share, width), BF),
            pltpu.SemaphoreType.DMA((chunks + 2,)),
            pltpu.SemaphoreType.DMA((2,)),
            pltpu.SemaphoreType.DMA((4,)),
            pltpu.SemaphoreType.DMA((max(1, len(carried)),)),
        ],
        name=f"mlp_backward_{layer}",
        kept=4 + len(carried),
    )(where, *blocks, gu_own, gu_got, wd_own, wd_got, c1, c2, *carried)
    return list(result[:3]), list(result[3:6]), list(result[6:])


def mlp_last(layer, blocks, weights, ahead, section, carried):
    gu_own, gu_got = weights[:2]
    grad_projected, grad_hidden = ahead
    rows, size = grad_hidden.shape
    width = gu_own.shape[1]
    share = rows // 4
    chunk = 2 * LANE
    chunks = size // chunk
    step = 3 * LANE

    def body(sec_ref, b0, b1, b2, b3, gu_a, gu_b, gp_in, gh_in, attended_ref, after_ref,
             gg_ref, gup_ref, out, hid_out, attended_out, after_out,
             a_ref, gu_ref, hid_ref, gh_ref, gp_ref, full_ref, sems, in_sems, out_sems, kept_sems):
        own = sec_ref[0] == layer
        for j in range(chunks):
            at = pl.ds(j * chunk, chunk)
            for i in range(2):
                fetch(own, gu_a.at[i, :, at], gu_b.at[i, :, at], gu_ref.at[i, :, at], sems.at[2 * j + i])
        ins = load([(gh_in, gh_ref), (gp_in, gp_ref)], in_sems)
        kept = load([(attended_ref, attended_out), (after_ref, after_out)], kept_sems)
        for k, ref in enumerate((b0, b1, b2, b3)):
            a_ref[k * share : (k + 1) * share] = ref[...]
        for j in range(chunks):
            at = slice(j * chunk, (j + 1) * chunk)
            for i in range(2):
                here = pl.ds(j * chunk, chunk)
                arrived(gu_a.at[i, :, here], gu_ref.at[i, :, here], sems.at[2 * j + i])
            gate = nn(a_ref[...], gu_ref[0, :, at])
            up = nn(a_ref[...], gu_ref[1, :, at])
            if j == 0:
                ins[0].wait()
            sigma = jax.nn.sigmoid(gate)
            silu = gate * sigma
            grad = gh_ref[:, at].astype(F32)
            hid_ref[:, at] = (silu * up).astype(BF)
            gg_ref[:, at] = (grad * (up * (sigma + silu * (1.0 - sigma)))).astype(BF)
            gup_ref[:, at] = (grad * silu).astype(BF)
        kept += load([(hid_ref, hid_out)], kept_sems.at[pl.ds(2, 1)])
        ins[1].wait()
        for j in range(width // step):
            at = slice(j * step, (j + 1) * step)
            left = a_ref[:, at]
            full_ref[at, :size] = tn(left, gg_ref[...]).astype(BF)
            full_ref[at, size : 2 * size] = tn(left, gup_ref[...]).astype(BF)
            full_ref[at, 2 * size :] = tn(gp_ref[:, at], hid_ref[...]).astype(BF)
            here = pl.ds(j * step, step)
            kept += load([(full_ref.at[here], out.at[here])], out_sems.at[pl.ds(j, 1)])
        finish(kept)

    result = call(
        body,
        [shape((rows, size), BF)] * 2
        + [shape((width, 3 * size), BF), shape((rows, size), BF)]
        + [shape(c.shape, c.dtype) for c in carried],
        [SM] + [VM] * 4 + [HB] * 4 + [VM] * 2,
        [
            pltpu.VMEM((rows, width), BF),
            pltpu.VMEM(gu_own.shape, BF),
            pltpu.VMEM((rows, size), BF),
            pltpu.VMEM((rows, size), BF),
            pltpu.VMEM((rows, width), BF),
            pltpu.VMEM((width, 3 * size), BF),
            pltpu.SemaphoreType.DMA((2 * chunks,)),
            pltpu.SemaphoreType.DMA((2,)),
            pltpu.SemaphoreType.DMA((width // step,)),
            pltpu.SemaphoreType.DMA((3,)),
        ],
        name=f"mlp_last_{layer}",
        kept=4,
        limit=28,
    )(section, *blocks, gu_own, gu_got, grad_projected, grad_hidden, *carried)
    return list(result[:2]), result[2], result[3], list(result[4:])


def mlp_input_grad(layer, section, grad_gate, grad_up, weights):
    gu_own, gu_got = weights[:2]
    rows = grad_gate.shape[0]
    width = gu_own.shape[1]
    share = rows // 4
    step = 3 * LANE

    def body(sec_ref, gg_ref, gup_ref, gu_a, gu_b, p1, p2, p3, p0_out, p0, gu_ref, sems, out_sems):
        own = sec_ref[0] == layer
        spans = [pl.ds(j * step, step) for j in range(width // step)]
        for j, at in enumerate(spans):
            for i in range(2):
                fetch(own, gu_a.at[i, at], gu_b.at[i, at], gu_ref.at[i, at], sems.at[2 * j + i])
        for j, at in enumerate(spans):
            for i in range(2):
                arrived(gu_a.at[i, at], gu_ref.at[i, at], sems.at[2 * j + i])
            here = slice(j * step, (j + 1) * step)
            split_store(
                nt(gg_ref[...], gu_ref[0, here]) + nt(gup_ref[...], gu_ref[1, here]), here, (p0, p1, p2, p3)
            )
        finish(load([(p0, p0_out)], out_sems))

    result = call(
        body,
        [shape((share, width), BF)] * 4,
        [SM, VM, VM, HB, HB],
        [
            pltpu.VMEM((share, width), BF),
            pltpu.VMEM(gu_own.shape, BF),
            pltpu.SemaphoreType.DMA((2 * (width // step),)),
            pltpu.SemaphoreType.DMA((1,)),
        ],
        name="mlp_input_grad",
        kept=1,
        limit=16,
    )(section, grad_gate, grad_up, gu_own, gu_got)
    return [result[3]] + list(result[:3])


def mlp_weight_grads(mlp_in, grads, hidden):
    grad_projected, grad_gate, grad_up = grads
    rows, width = grad_projected.shape
    size = hidden.shape[1]
    step = 3 * LANE

    def body(a_in, gg_in, gu_in, gp_in, hid_in, *refs):
        out, a_ref, gg_ref, gu_ref, gp_ref, hid_ref, full_ref, in_sems, sems = refs
        ins = load([(a_in, a_ref), (gg_in, gg_ref), (gu_in, gu_ref), (gp_in, gp_ref), (hid_in, hid_ref)], in_sems)
        kept = []
        finish(ins[:2])
        for j in range(width // step):
            at = slice(j * step, (j + 1) * step)
            left = a_ref[:, at]
            full_ref[at, :size] = tn(left, gg_ref[...]).astype(BF)
            if j == 0:
                ins[2].wait()
            full_ref[at, size : 2 * size] = tn(left, gu_ref[...]).astype(BF)
            if j == 0:
                finish(ins[3:])
            full_ref[at, 2 * size :] = tn(gp_ref[:, at], hid_ref[...]).astype(BF)
            here = pl.ds(j * step, step)
            kept.append(pltpu.make_async_copy(full_ref.at[here], out.at[here], sems.at[j]))
            kept[-1].start()
        finish(kept)

    result = call(
        body,
        [shape((width, 3 * size), BF)],
        [HB] * 5,
        [pltpu.VMEM((rows, width), BF)]
        + [pltpu.VMEM((rows, size), BF)] * 2
        + [
            pltpu.VMEM((rows, width), BF),
            pltpu.VMEM((rows, size), BF),
            pltpu.VMEM((width, 3 * size), BF),
            pltpu.SemaphoreType.DMA((5,)),
            pltpu.SemaphoreType.DMA((width // step,)),
        ],
        name="mlp_weight_grads",
        kept=1,
    )(mlp_in, grad_gate, grad_up, grad_projected, hidden)
    return result[0]


def attention_backward(layer, blocks, weights, saved, tables, grad_after):
    wq, wo = weights
    cosine, sine, gains, seg_col, seg_row = tables
    rows, padded = saved[0].shape
    width = wo.shape[2]
    heads = padded // LANE
    share = rows // 4
    scale = HEAD**-0.5
    QB = 512

    def body(b0, b1, b2, b3, wq_in, wo_in, qraw_in, kraw_in, qrot_in, krot_in, v_in,
             cos_ref, sin_ref, gain_ref, segc_ref, segr_ref, grad_ref,
             p1, p2, p3, g_out, ga_out, p0_out, ggain_out, grad_out,
             wq_ref, wo_ref, qraw_ref, kraw_ref, qrot_ref, krot_ref, v_ref, mask_ref,
             ga_ref, gmix_ref, gq_ref, gk_ref, g_ref, p0, ggain_ref, sems, in_sems):
        ins = [(wo_in.at[layer], wo_ref)]
        ins += [(qrot_in, qrot_ref), (krot_in, krot_ref), (v_in, v_ref), (qraw_in, qraw_ref), (kraw_in, kraw_ref)]
        ins += [(wq_in.at[layer, i], wq_ref.at[i]) for i in range(3)]
        ins = load(ins, in_sems)
        for k, ref in enumerate((b0, b1, b2, b3)):
            ga_ref[k * share : (k + 1) * share] = ref[...]
        kept = []

        def keep(here, there):
            kept.append(pltpu.make_async_copy(here, there, sems.at[len(kept)]))
            kept[-1].start()

        keep(ga_ref, ga_out)
        keep(grad_ref, grad_out)
        mask_ref[...] = jnp.where(segc_ref[...] == segr_ref[...], 1.0, 0.0).astype(BF)
        ins[0].wait()
        gmix_ref[...] = nt(ga_ref[...], wo_ref[...]).astype(BF)
        finish(ins[1:4])
        for h in range(heads):
            at = slice(h * LANE, (h + 1) * LANE)
            for j in range(rows // QB):
                at_rows = slice(j * QB, (j + 1) * QB)
                query = qrot_ref[at_rows, at]
                grad_mixed = gmix_ref[at_rows, at]
                scores = nt(krot_ref[:, at], query) * scale
                grown = (jnp.exp(scores).astype(BF) * mask_ref[:, at_rows]).astype(F32)
                weights_t = grown * (1.0 / jnp.sum(grown, axis=0, keepdims=True))
                grad_weights = nt(v_ref[:, at], grad_mixed)
                add_v = nn(weights_t.astype(BF), grad_mixed)
                product = weights_t * grad_weights
                delta = jnp.sum(product, axis=0, keepdims=True)
                grad_scores = (product - weights_t * delta).astype(BF)
                gq_ref[at_rows, at] = tn(grad_scores, krot_ref[:, at])
                add_k = nn(grad_scores, query)
                total_v = add_v if j == 0 else total_v + add_v
                total_k = add_k if j == 0 else total_k + add_k
            gk_ref[:, at] = total_k
            g_ref[:, 2 * padded + h * LANE : 2 * padded + (h + 1) * LANE] = total_v.astype(BF)
        cos = cos_ref[...]
        sin = sin_ref[...]
        finish(ins[4:6])
        ggain_ref[...] = jnp.zeros_like(ggain_ref)
        for i, (raw_ref, grad_ref) in enumerate(((qraw_ref, gq_ref), (kraw_ref, gk_ref))):
            gain = gain_ref[2 * layer + i : 2 * layer + i + 1]
            gain_sum = jnp.zeros((1, LANE), F32)
            for h in range(heads):
                at = slice(h * LANE, (h + 1) * LANE)
                raw = raw_ref[:, at].astype(F32)
                inverse = head_inverse(raw)
                normed = raw * inverse
                turned = unrotate(grad_ref[:, at], cos, sin) * scale
                product = turned * normed
                gain_sum += jnp.sum(product, axis=0, keepdims=True)
                back = inverse * (turned * gain - normed * head_mean(product * gain))
                g_ref[:, i * padded + h * LANE : i * padded + (h + 1) * LANE] = back.astype(BF)
            ggain_ref[i : i + 1] = gain_sum
        keep(g_ref, g_out)
        keep(ggain_ref, ggain_out)
        finish(ins[6:])
        step = 3 * LANE
        for j in range(width // step):
            at = slice(j * step, (j + 1) * step)
            total = nt(g_ref[:, :padded], wq_ref[0, at])
            total += nt(g_ref[:, padded : 2 * padded], wq_ref[1, at])
            total += nt(g_ref[:, 2 * padded :], wq_ref[2, at])
            split_store(total, at, (p0, p1, p2, p3))
        keep(p0, p0_out)
        finish(kept)

    outs = [shape((share, width), BF)] * 3
    outs += [shape((rows, 3 * padded), BF), shape((rows, width), BF), shape((share, width), BF), shape((8, LANE), F32)]
    outs += [shape(grad_after.shape, F32)]
    result = call(
        body,
        outs,
        [VM] * 4 + [HB] * 7 + [VM] * 6,
        [
            pltpu.VMEM((3, width, padded), BF),
            pltpu.VMEM((padded, width), BF),
        ]
        + [pltpu.VMEM((rows, padded), BF)] * 5
        + [
            pltpu.VMEM((rows, rows), BF),
            pltpu.VMEM((rows, width), BF),
            pltpu.VMEM((rows, padded), BF),
            pltpu.VMEM((rows, padded), F32),
            pltpu.VMEM((rows, padded), F32),
            pltpu.VMEM((rows, 3 * padded), BF),
            pltpu.VMEM((share, width), BF),
            pltpu.VMEM((8, LANE), F32),
            pltpu.SemaphoreType.DMA((5,)),
            pltpu.SemaphoreType.DMA((9,)),
        ],
        name=f"attention_backward_{layer}",
        limit=32,
        kept=5,
    )(*blocks, wq, wo, *saved[:5], cosine, sine, gains, seg_col, seg_row, grad_after)
    return list(result[:3]), list(result[3:])


def attention_weight_grads(attention_in, grads, mixed, grad_attended, place):
    rows, width = attention_in.shape
    padded, narrow = place.shape
    step = 3 * LANE


    def body(a_in, g_in, mixed_in, ga_in, place_ref, out, a_ref, g_ref, mixed_ref, ga_ref, right_ref, full_ref, in_sems, sems):
        ins = load([(g_in, g_ref), (mixed_in, mixed_ref), (a_in, a_ref), (ga_in, ga_ref)], in_sems)
        finish(ins[:2])
        for i in range(3):
            right_ref[i] = nn(g_ref[:, i * padded : (i + 1) * padded], place_ref[...]).astype(BF)
        right_ref[3] = nn(mixed_ref[...], place_ref[...]).astype(BF)
        finish(ins[2:])
        kept = []
        for j in range(width // step):
            at = slice(j * step, (j + 1) * step)
            left = a_ref[:, at]
            for i in range(3):
                full_ref[at, i * narrow : (i + 1) * narrow] = tn(left, right_ref[i]).astype(BF)
            full_ref[at, 3 * narrow :] = tn(ga_ref[:, at], right_ref[3]).astype(BF)
            here = pl.ds(j * step, step)
            kept.append(pltpu.make_async_copy(full_ref.at[here], out.at[here], sems.at[j]))
            kept[-1].start()
        finish(kept)

    result = call(
        body,
        [shape((width, 4 * narrow), BF)],
        [HB] * 4 + [FREE],
        [
            pltpu.VMEM((rows, width), BF),
            pltpu.VMEM((rows, 3 * padded), BF),
            pltpu.VMEM((rows, padded), BF),
            pltpu.VMEM((rows, width), BF),
            pltpu.VMEM((4, rows, narrow), BF),
            pltpu.VMEM((width, 4 * narrow), BF),
            pltpu.SemaphoreType.DMA((4,)),
            pltpu.SemaphoreType.DMA((width // step,)),
        ],
        name="attention_weight_grads",
        kept=1,
    )(attention_in, grads, mixed, grad_attended, place)
    return result[0]


def back_of_mlp(where, parts, grad_out, after, attended, projected, mods, picks):
    dims = after.shape
    extra = [] if projected is None else [projected]
    sums = (3 + len(extra), picks.shape[1], dims[1])

    def body(where_ref, p0_in, p1, p2, p3, g_in, after_in, attended_in, *refs):
        refs = list(refs)
        extra_refs = [refs.pop(0) for _ in extra]
        (mods_ref, picks_ref, ga_ref, grad_ref, sums_out,
         p0, g_ref, after_ref, attended_ref, projected_ref, sums_ref, sems, out_sems) = refs
        pairs = [(p0_in, p0), (after_in, after_ref)] + own_rows(g_in, where_ref, g_ref)
        ins = load(pairs + [(attended_in, attended_ref)] + [(ref, projected_ref) for ref in extra_refs], sems)
        picked = picks_ref[...]
        scale2 = token_mod(picked, mods_ref, 4)
        gate1 = token_mod(picked, mods_ref, 2)
        finish(ins[:2])
        grad_in = add_parts((p0, p1, p2, p3))
        after = after_ref[...]
        inverse = inverse_rms(after)
        normed = after * inverse
        finish(ins[2:])
        g = g_ref[...].astype(F32)
        grad_after = g + norm_back(grad_in * (1.0 + scale2), normed, inverse)
        sums_ref[0] = image_sums(picked, grad_after * attended_ref[...].astype(F32))
        sums_ref[1] = image_sums(picked, grad_in)
        sums_ref[2] = image_sums(picked, grad_in * normed)
        if extra:
            sums_ref[3] = image_sums(picked, g * projected_ref[...].astype(F32))
        kept = load([(sums_ref, sums_out)], out_sems)
        grad_ref[...] = grad_after
        ga_ref[...] = (grad_after * gate1).astype(BF)
        finish(kept)

    return call(
        body,
        [shape(dims, BF), shape(dims, F32), shape(sums, F32)],
        [SM, HB] + [VM] * 3 + [HB] * (3 + len(extra)) + [VM] * 2,
        [
            pltpu.VMEM(dims, BF),
            pltpu.VMEM(dims, BF),
            pltpu.VMEM(dims, F32),
            pltpu.VMEM(dims, BF),
            pltpu.VMEM(dims, BF),
            pltpu.VMEM(sums, F32),
            pltpu.SemaphoreType.DMA((5,)),
            pltpu.SemaphoreType.DMA((1,)),
        ],
        name="back_of_mlp",
        limit=10,
        kept=1,
    )(where, *parts, grad_out, after, attended, *extra, mods, picks)


def back_of_attention(where, parts, grad_after, state, mods, picks, mods_below):
    first = mods_below is None
    dims = grad_after.shape

    def body(where_ref, p0_in, p1, p2, p3, grad_in_ref, state_in, mods_ref, picks_ref, *refs):
        refs = list(refs)
        below_ref = None if first else refs.pop(0)
        sums_ref = refs.pop(0)
        gp_ref = None if first else refs.pop(0)
        out_ref, p0, grad_ref, state_ref, sems = refs
        ins = load([(p0_in, p0), (grad_in_ref, grad_ref)] + own_rows(state_in, where_ref, state_ref), sems)
        picked = picks_ref[...]
        scale1 = token_mod(picked, mods_ref, 1)
        finish(ins)
        grad_in = add_parts((p0, p1, p2, p3))
        state = state_ref[...].astype(F32)
        inverse = inverse_rms(state)
        normed = state * inverse
        grad_state = grad_ref[...] + norm_back(grad_in * (1.0 + scale1), normed, inverse)
        out_ref[...] = grad_state.astype(out_ref.dtype)
        if not first:
            gp_ref[...] = (grad_state.astype(BF).astype(F32) * token_mod(picked, below_ref, 5)).astype(BF)
        sums_ref[0] = image_sums(picked, grad_in)
        sums_ref[1] = image_sums(picked, grad_in * normed)

    outs = [shape((2, picks.shape[1], dims[1]), F32)] + ([shape(dims, F32)] if first else [shape(dims, BF)] * 2)
    extra = () if first else (mods_below,)
    return call(
        body,
        outs,
        [SM, HB] + [VM] * 3 + [HB] * 2 + [VM] * (2 + len(extra)),
        [
            pltpu.VMEM(dims, BF),
            pltpu.VMEM(dims, F32),
            pltpu.VMEM(dims, BF),
            pltpu.SemaphoreType.DMA((3,)),
        ],
        name="back_of_attention",
        limit=10,
    )(where, *parts, grad_after, state, mods, picks, *extra)


def exchange(value, axis, k):
    return lax.ppermute(value, axis, [(i, i ^ k) for i in range(lax.axis_size(axis))])


def handed_on(value):
    def body(source, target):
        target[...] = source[...]

    return call(body, [shape(value.shape, value.dtype)], [VM], name="handed_on", limit=4)(value)[0]


def in_order(got, order):
    for place, k in enumerate(order):
        for _ in range(len(order) - 1 - place):
            got[k] = handed_on(got[k])


def send_parts(parts, beside=None, whole=False):
    got = {k: exchange(parts[k], "tensor", k) for k in (3, 1, 2)}
    if beside is not None and not whole:
        got[1], beside = lax.optimization_barrier((got[1], beside))
    if whole:
        got, beside = lax.optimization_barrier((got, beside))
    else:
        in_order(got, (1, 2, 3))
    result = [parts[0], got[1], got[2], got[3]]
    return result if beside is None else (result, beside)


def gather_blocks(own):
    got = {k: exchange(own, "tensor", k) for k in (3, 1, 2)}
    in_order(got, (3, 2, 1))
    return [own, got[1], got[2], got[3]]


def group_sum(value, axis):
    k = 1
    while k < lax.axis_size(axis):
        value = value + exchange(value, axis, k)
        k *= 2
    return value


def gather_dp(value):
    count = lax.axis_size("dp")
    if count > 4:
        return lax.all_gather(value, "dp", axis=0)
    me = lax.axis_index("dp")
    got = [value] + [exchange(value, "dp", k) for k in range(1, count)]
    stacked = jnp.stack(got)
    return jnp.stack([lax.dynamic_index_in_dim(stacked, me ^ j, 0, keepdims=False) for j in range(count)])


def head_places(heads):
    place = np.zeros((heads * HEAD, heads * LANE), np.float32)
    for h in range(heads):
        for j in range(HEAD):
            place[h * HEAD + j, h * LANE + (j // HALF) * (LANE // 2) + j % HALF] = 1.0
    return place


def shards(
    inputs,
    cotangent,
    conditioning,
    lengths,
    positions,
    modulator,
    projections,
    norm_gains,
    out_weight,
    gate_up,
    down_weight,
):
    section = lax.axis_index("section")
    other = 1 - section
    tensor = lax.axis_index("tensor")
    data = lax.axis_index("dp")
    micro, _, width = inputs.shape
    rows = inputs.shape[1]
    group = lax.axis_size("tensor")
    share = rows // group
    items = lengths.shape[2]
    narrow = projections.shape[3]
    heads = narrow // HEAD
    columns = modulator.shape[2]
    sec = section.reshape(1).astype(jnp.int32)

    where = jnp.stack([section, tensor]).astype(jnp.int32)
    is_first = section == 0

    where = jnp.stack([section, tensor]).astype(jnp.int32)
    is_first = section == 0
    place = jnp.asarray(head_places(heads), BF)
    place_one = jnp.asarray(head_places(1), F32)

    own = (jnp.swapaxes(projections[0], 1, 2), out_weight[0])
    got = [exchange(value, "section", 1) for value in own]
    got_gains = exchange(norm_gains[0], "section", 1)
    scaled, part = modulation_part(conditioning, jnp.swapaxes(modulator[0], 0, 1))
    pieces = gather_blocks(part)
    quarter = HEAD // 4
    rates = 10000.0 ** (-jnp.arange(quarter).astype(F32) / quarter)
    rates = jnp.concatenate([rates, rates, jnp.zeros(LANE // 2 - HALF, F32)])[:, None]
    where_late, part = lax.optimization_barrier((where, part))
    cosine, sine, seg_col, seg_row, picks, picks_own = prepare_tables(where_late, lengths, positions, rates)
    wq, wo = prepare_weights(where_late, own, place)
    pieces, got, cosine, wq = lax.optimization_barrier((pieces, got, cosine, wq))
    mods_own, mods_send, gains = modulation_rows([part] + pieces[1:], (norm_gains[0], got_gains), where, place_one)
    mods_got = exchange(mods_send, "section", 1)
    gu_send, wd_send, mods_got = lax.optimization_barrier((gate_up[0], down_weight[0], mods_got))
    mods = [jnp.where(is_first, mods_own, mods_got), jnp.where(is_first, mods_got, mods_own)]
    gu_got = exchange(gu_send, "section", 1)
    wd_got = exchange(wd_send, "section", 1)
    mlp_weights = (gate_up[0], gu_got, down_weight[0], wd_got)
    wq, mods_first = lax.optimization_barrier((wq, mods[0]))
    mods[0] = mods_first
    wq, wo = prepare_weights(where, got, place, (wq, wo), 1)
    tables = (cosine, sine, gains, seg_col, seg_row)

    cache = []
    attention_blocks = [inputs]
    carried = ()
    for l in range(2):
        partial, state, saved, kept = attention_forward(
            l, where, attention_blocks, (wq, wo), tables, mods[l], picks, carried
        )
        if l == 0:
            state = state[0]
            wq, mixed = lax.optimization_barrier((wq, saved[5]))
            saved[5] = mixed
            wq, wo = prepare_weights(where, got, place, (wq, wo), 0)
            parts, wq = send_parts(partial, wq)
        else:
            parts = send_parts(partial)
            cache[0].append(kept[0])
            state = carried[1]
            state_kept = kept[1]
        mlp_in, attended, after = after_attention(parts, state, mods[l], picks_own)
        if l == 1:
            grads, mlp_grads, hidden, kept = mlp_last(
                l, gather_blocks(mlp_in), mlp_weights, ahead, sec, (attended, after)
            )
            cache.append([saved] + kept)
            break
        partial, mlp_saved, kept = mlp_forward(l, gather_blocks(mlp_in), mlp_weights, sec, (attended, after), False)
        cache.append([saved, mlp_saved] + kept)
        if l == 0:
            where_late, partial[0] = lax.optimization_barrier((where, partial[0]))
            ahead = last_ahead(where_late, cotangent, down_weight[0], wd_got, mods[1], picks)
            parts, ahead = send_parts(partial, ahead)
            attention_in, projected, state = after_mlp(parts, after, mods[0], picks_own, mods[1])
            carried = (projected, state)
            attention_blocks = gather_blocks(attention_in)

    item_sums = [None, None]
    gain_sums = [None, None]
    shares = [None, None]

    def data_sum(value):
        return lax.psum_scatter(value, ("dp", "section"), scatter_dimension=0, tiled=True)

    for l in (1, 0):
        if l == 1:
            saved, attended, after = cache[1]
            mlp_share = data_sum(mlp_grads)
            partial = mlp_input_grad(l, sec, *grads, mlp_weights)
            where_late, partial[0] = lax.optimization_barrier((where, partial[0]))
            last_partial, last_sums = last_projection(l, where_late, hidden, mlp_weights, cotangent, picks)
            parts, last_sums = send_parts(partial, last_sums, True)
            grad_out = cotangent
            projected = None
        else:
            saved, (hidden, c1, c2, mlp_in), attended, after = cache[0][:4]
            partial, grads, kept = mlp_backward(
                l, where, grad_blocks, mlp_weights, (c1, c2), [grad_out]
            )
            projected = cache[0][4]
            grad_out = kept[1]
            mlp_grads = mlp_weight_grads(mlp_in, grads, hidden)
            parts, (mlp_grads, earlier) = send_parts([kept[0]] + partial, (mlp_grads, shares[1][1]), True)
            shares[1] = (shares[1][0], earlier)
            mlp_share = data_sum(mlp_grads)
        mixed, attention_in = saved[5:]
        grad_attended, grad_after, sums2 = back_of_mlp(
            where, parts, grad_out, after, attended, projected, mods[l], picks_own
        )
        blocks = gather_blocks(grad_attended)
        partial, kept = attention_backward(l, blocks, (wq, wo), saved, tables, grad_after)
        grads, grad_attended, own, gain_sums[l], grad_after = kept
        attention_grads = attention_weight_grads(attention_in, grads, mixed, grad_attended, place.T)
        if l == 1:
            parts, (attention_grads, mlp_share) = send_parts([own] + partial, (attention_grads, mlp_share), True)
            attention_share = data_sum(attention_grads)
            sums1, grad_projected, grad_out = back_of_attention(
                where, parts, grad_after, state_kept, mods[1], picks_own, mods[0]
            )
            grad_blocks = gather_blocks(grad_projected)
            shares[1] = (mlp_share, attention_share)
        else:
            parts, attention_grads = send_parts([own] + partial, attention_grads, True)
            sums1, grad_state = back_of_attention(where, parts, grad_after, inputs, mods[0], picks_own, None)
        item_sums[l] = jnp.concatenate([sums1, sums2], axis=0)

    item_sums[1] = jnp.concatenate([item_sums[1], last_sums], axis=0)
    sums = jnp.stack(item_sums)[:, :, :items].transpose(0, 2, 1, 3).reshape(2 * items, 6 * width)
    gain_parts = jnp.concatenate([jnp.concatenate([g[0:1], g[1:2]], axis=1) for g in gain_sums])
    gain_parts = jnp.pad(gain_parts, ((0, 2 * items - 2), (0, 0)))
    pieces = [
        jnp.concatenate([lax.dynamic_slice_in_dim(sums, (tensor ^ k) * columns, columns, 1), gain_parts], axis=1)
        for k in range(group)
    ]
    got = send_parts(pieces)
    total = (got[0] + got[1]) + (got[2] + got[3])
    total, attention_grads, mlp_share = lax.optimization_barrier((total, attention_grads, mlp_share))
    shares[0] = (mlp_share, data_sum(attention_grads))
    last_partial[1:], total = lax.optimization_barrier((last_partial[1:], total))
    output = last_output(send_parts(last_partial), cache[1][2], mods[1], picks_own)
    layers = total[:, :columns].reshape(2, items, columns).astype(BF).astype(F32)
    gain_rows = jnp.pad(total[:2, None, columns:], ((0, 0), (0, items - 1), (0, 0)))
    layers = jnp.concatenate([layers, gain_rows], axis=2)
    mine = jnp.where(is_first, layers[0], layers[1])
    theirs = exchange(jnp.where(is_first, layers[1], layers[0]), "section", 1)
    gain_total = mine[0:1, columns:] + theirs[0:1, columns:]
    mods_grad = jnp.concatenate(
        [jnp.where(is_first, mine, theirs)[:, :columns], jnp.where(is_first, theirs, mine)[:, :columns]]
    )
    packed = jnp.concatenate(
        [mods_grad, scaled.astype(F32), jnp.pad(gain_total, ((0, 2 * items - 1), (0, 0)))], axis=1
    )
    gathered = gather_dp(packed)
    all_mods = gathered[:, :, :columns].astype(BF)
    deep = width // lax.axis_size("dp")
    scaled_share = lax.dynamic_slice_in_dim(gathered, columns + data * deep, deep, 2).astype(BF)
    grad_ada = jnp.einsum("nid,nic->dc", scaled_share, all_mods, preferred_element_type=F32)
    gain_total = jnp.sum(gathered[:, 0, columns + width :], axis=0)
    cond_value = conditioning[:, 0].astype(F32)
    sigma = jax.nn.sigmoid(cond_value)
    cond_part = jnp.einsum("ic,dc->id", mods_grad.astype(BF), modulator[0], preferred_element_type=F32)
    cond_part = cond_part.reshape(micro, items, width) * sigma * (1.0 + cond_value * (1.0 - sigma))
    grad_cond = group_sum(group_sum(cond_part, "section"), "tensor")
    half = LANE // 2
    gain_total = gain_total.reshape(2, LANE)
    grad_gains = jnp.concatenate([gain_total[:, :HALF], gain_total[:, half : half + HALF]], axis=1)
    mine = jnp.where(is_first, grad_state, output)
    theirs = exchange(jnp.where(is_first, output, grad_state), "section", 1)
    results = jnp.stack([jnp.where(is_first, mine, theirs), jnp.where(is_first, theirs, mine)])

    def joined(which):
        mine = jnp.where(is_first, shares[0][which], shares[1][which])
        theirs = exchange(jnp.where(is_first, shares[1][which], shares[0][which]), "section", 1)
        low = jnp.where(is_first, mine, theirs)
        high = jnp.where(is_first, theirs, mine)
        return jnp.concatenate([low, high], axis=0).astype(F32)

    size = down_weight.shape[1]
    mlp_grads = joined(0)
    grad_pair = jnp.stack([mlp_grads[:, :size], mlp_grads[:, size : 2 * size]])
    grad_down = mlp_grads[:, 2 * size :].T
    mine = jnp.where(is_first, shares[0][1], shares[1][1])
    theirs = exchange(jnp.where(is_first, shares[1][1], shares[0][1]), "section", 1)
    grad_qkv, grad_out_w = attention_results(where, mine, theirs)
    return (
        grad_ada[None],
        grad_qkv[None],
        grad_gains[None],
        grad_out_w[None],
        grad_pair[None],
        grad_down[None],
        grad_cond[:, None],
        results[None],
    )


def solution(mesh):
    return jax.shard_map(
        shards,
        mesh=mesh,
        in_specs=(
            P(None, "dp", None),
            P(None, "dp", None),
            P(None, "dp", None, None),
            P(None, "dp", None),
            P(None, None, "dp"),
            P("section", None, "tensor"),
            P("section", None, None, "tensor"),
            P("section", None, None),
            P("section", "tensor", None),
            P("section", None, None, "tensor"),
            P("section", "tensor", None),
        ),
        out_specs=(
            P("section", "dp", "tensor"),
            P("section", None, "dp", "tensor"),
            P("section", None, None),
            P("section", "tensor", "dp"),
            P("section", None, "dp", "tensor"),
            P("section", "tensor", "dp"),
            P(None, "dp", None, None),
            P("section", None, ("dp", "tensor"), None),
        ),
        check_vma=False,
    )
```

```python
import functools

import jax
import jax.numpy as jnp
from jax import lax
from jax.experimental import pallas as pl
from jax.experimental.pallas import tpu as pltpu
from jax.sharding import PartitionSpec as P
import numpy as np

HEAD = 72
HALF = HEAD // 2
LANE = 128
epsilon = 1e-06
BF = jnp.bfloat16
F32 = jnp.float32
HIGHEST = lax.Precision.HIGHEST
VM = pl.BlockSpec(memory_space=pltpu.VMEM)
SM = pl.BlockSpec(memory_space=pltpu.SMEM)
HB = pl.BlockSpec(memory_space=pltpu.HBM)
FREE = pl.BlockSpec(memory_space=pltpu.VMEM)


def nn(a, b):
    return lax.dot_general(a, b, (((1,), (0,)), ((), ())), preferred_element_type=F32)


def nt(a, b):
    return lax.dot_general(a, b, (((1,), (1,)), ((), ())), preferred_element_type=F32)


def tn(a, b):
    return lax.dot_general(a, b, (((0,), (0,)), ((), ())), preferred_element_type=F32)


def call(body, outs, in_specs, scratch=(), name=None, kept=0, limit=24, aliases={}):
    small = len(outs) - kept
    kernel = pl.pallas_call(
        body,
        out_shape=[pltpu.VMEM(o.shape, o.dtype) for o in outs[:small]] + [pltpu.HBM(o.shape, o.dtype) for o in outs[small:]],
        in_specs=in_specs,
        out_specs=[VM] * small + [HB] * kept,
        scratch_shapes=list(scratch),
        input_output_aliases=aliases,
        compiler_params=pltpu.CompilerParams(vmem_limit_bytes=limit * 2**20),
        cost_estimate=pl.CostEstimate(flops=1000, bytes_accessed=1000, transcendentals=0),
        name=name,
    )

    def run(*args):
        spaces = {id(HB): pltpu.HBM, id(VM): pltpu.VMEM}
        placed = [
            pltpu.with_memory_space_constraint(arg, spaces[id(spec)]) if id(spec) in spaces else arg
            for arg, spec in zip(args, in_specs)
        ]
        return kernel(*placed)

    return run


def shape(dims, dtype):
    return jax.ShapeDtypeStruct(dims, dtype)


def fetch(is_own, own, other, where, sem):
    @pl.when(is_own)
    def _():
        pltpu.make_async_copy(own, where, sem).start()

    @pl.when(jnp.logical_not(is_own))
    def _():
        pltpu.make_async_copy(other, where, sem).start()


def arrived(own, where, sem):
    pltpu.make_async_copy(own, where, sem).wait()


def load(pairs, sems):
    made = [pltpu.make_async_copy(there, here, sems.at[i]) for i, (there, here) in enumerate(pairs)]
    for one in made:
        one.start()
    return made


def finish(copies):
    for one in copies:
        one.wait()


def rows_of(whole, where_ref, here):
    share = whole.shape[1] // 4
    pairs = []
    for k in range(here.shape[0] // share):
        there = pl.ds(pl.multiple_of((where_ref[1] ^ k) * share, LANE), share)
        pairs.append((whole.at[where_ref[0], there], here.at[pl.ds(k * share, share)]))
    return pairs


def own_rows(whole, where_ref, here):
    return rows_of(whole, where_ref, here) if len(whole.shape) == 3 else [(whole, here)]


def inverse_rms(value):
    return lax.rsqrt(jnp.mean(value * value, axis=-1, keepdims=True) + epsilon)


def norm_back(grad, normed, inverse):
    return inverse * (grad - normed * jnp.mean(grad * normed, axis=-1, keepdims=True))


def token_mod(picks, mods_ref, part):
    width = mods_ref.shape[1] // 6
    return nn(picks, mods_ref[:, part * width : (part + 1) * width])


def image_sums(picks, value):
    return lax.dot_general(
        picks.astype(F32),
        value,
        (((0,), (0,)), ((), ())),
        precision=HIGHEST,
        preferred_element_type=F32,
    )


def swap_halves(value):
    return pltpu.roll(value, LANE // 2, 1)


def rotate(value, cosine, sine):
    return value * cosine + swap_halves(value) * sine


def unrotate(grad, cosine, sine):
    return grad * cosine - swap_halves(grad) * sine


def head_mean(value):
    return nn(value.astype(BF), jnp.full((LANE, LANE), 1.0, BF)) * (1.0 / HEAD)


def head_inverse(raw):
    return lax.rsqrt(head_mean(raw * raw) + epsilon)


def split_store(value, rows, block_refs):
    own = block_refs[0]
    share = own.shape[0]
    for k, ref in enumerate(block_refs):
        ref[:, rows] = value[k * share : (k + 1) * share].astype(ref.dtype)


def modulation_part(conditioning, modulator_t):
    micro, items = conditioning.shape[0], conditioning.shape[2]
    columns, width = modulator_t.shape
    step = 5 * LANE
    spans = [(j, min(step, columns - j)) for j in range(0, columns, step)]

    def body(cond_ref, mod_in, scaled_ref, part_ref, mod_ref, sems):
        copies = load([(mod_in.at[pl.ds(j, size)], mod_ref.at[pl.ds(j, size)]) for j, size in spans], sems)
        cond = jnp.concatenate([cond_ref[m, 0].astype(F32) for m in range(micro)], axis=0)
        scaled = (cond * jax.nn.sigmoid(cond)).astype(BF)
        scaled_ref[...] = scaled
        for copy, (j, size) in zip(copies, spans):
            copy.wait()
            part_ref[:, j : j + size] = nt(scaled, mod_ref[j : j + size]).astype(BF)

    return call(
        body,
        [shape((micro * items, width), BF), shape((micro * items, columns), BF)],
        [FREE, HB],
        [pltpu.VMEM((columns, width), BF), pltpu.SemaphoreType.DMA((len(spans),))],
        name="modulation_part",
        limit=12,
    )(conditioning, modulator_t)


def modulation_rows(pieces, gains, where, place_one):
    rows, columns = pieces[0].shape
    count = len(pieces)
    items = rows // 2

    def body(where_ref, *refs):
        piece_refs, (ga, gb, one_ref, own_ref, send_ref, gains_ref) = refs[:count], refs[count:]
        section, tensor = where_ref[0], where_ref[1]
        values = [ref[...].astype(F32) for ref in piece_refs]
        ordered = []
        for j in range(count):
            picked = jnp.zeros_like(values[0])
            for k in range(count):
                picked = jnp.where((tensor ^ k) == j, values[k], picked)
            ordered.append(picked)
        whole = jnp.concatenate(ordered, axis=1)
        blank = jnp.zeros((8 - items, whole.shape[1]), F32)
        first = jnp.concatenate([whole[:items], blank], axis=0)
        second = jnp.concatenate([whole[items:], blank], axis=0)
        own_ref[...] = jnp.where(section == 0, first, second).astype(BF)
        send_ref[...] = jnp.where(section == 0, second, first).astype(BF)
        a, b = ga[...], gb[...]
        first = jnp.where(section == 0, a, b)
        second = jnp.where(section == 0, b, a)
        both = jnp.concatenate([first, second, jnp.zeros((4, first.shape[1]), F32)], axis=0)
        gains_ref[...] = lax.dot_general(
            both, one_ref[...], (((1,), (0,)), ((), ())), precision=HIGHEST, preferred_element_type=F32
        )

    return call(
        body,
        [shape((8, count * columns), BF)] * 2 + [shape((8, LANE), F32)],
        [SM] + [VM] * count + [FREE] * 3,
        name="modulation_rows",
        limit=8,
    )(where, *pieces, *gains, place_one)


def prepare_tables(where, lengths, positions, rates):
    rows = positions.shape[2]
    share = rows // 4
    items = lengths.shape[2]

    def body(where_ref, len_ref, pos_ref, rate_ref, cos_ref, sin_ref, segc_ref, segr_ref, picks_ref, own_ref):
        section, tensor = where_ref[0], where_ref[1]

        def segments(index):
            place = (tensor ^ (index // share)) * share + index % share
            segment = jnp.zeros_like(index)
            end = 0
            for i in range(items):
                end = end + len_ref[section, 0, i]
                segment += (place >= end).astype(jnp.int32)
            return segment

        column = segments(lax.broadcasted_iota(jnp.int32, (rows, 1), 0))
        segc_ref[...] = column
        segr_ref[...] = segments(lax.broadcasted_iota(jnp.int32, (1, rows), 1))
        picks = jnp.where(column == lax.broadcasted_iota(jnp.int32, (rows, 8), 1), 1.0, 0.0).astype(BF)
        picks_ref[...] = picks
        own_ref[...] = picks[:share]
        blocks = [
            pos_ref[section, :, pl.ds(pl.multiple_of((tensor ^ k) * share, LANE), share)] for k in range(4)
        ]
        place = jnp.concatenate(blocks, axis=1).astype(F32)
        lane = lax.broadcasted_iota(jnp.int32, (LANE // 2, rows), 0)
        phase = jnp.where(lane < HEAD // 4, place[0:1], place[1:2]) * rate_ref[...]
        cosine = jnp.where(lane < HALF, jnp.cos(phase), 0.0)
        sine = jnp.where(lane < HALF, jnp.sin(phase), 0.0)
        cos_ref[...] = jnp.concatenate([cosine, cosine], axis=0).T
        sin_ref[...] = jnp.concatenate([-sine, sine], axis=0).T

    return call(
        body,
        [
            shape((rows, LANE), F32),
            shape((rows, LANE), F32),
            shape((rows, 1), jnp.int32),
            shape((1, rows), jnp.int32),
            shape((rows, 8), BF),
            shape((share, 8), BF),
        ],
        [SM, SM, FREE, FREE],
        name="prepare_tables",
        limit=16,
    )(where, lengths, positions, rates)


def prepare_weights(where, source, place, begun=None, only=None):
    wq, wo = source
    narrow, width = wq.shape[1:]
    padded = place.shape[1]

    def body(where_ref, wq_in, wo_in, place_ref, *refs):
        wq_out, wo_out, wq_ref, wo_ref, wide_ref, tall_ref, sems, out_sems = refs if begun is None else refs[2:]
        section = where_ref[0]

        def make(layer):
            copies = load([(wq_in.at[i], wq_ref.at[i]) for i in range(3)] + [(wo_in, wo_ref)], sems)
            outs = []
            for i in range(3):
                copies[i].wait()
                wide_ref[i] = tn(wq_ref[i], place_ref[...]).astype(BF)
                outs += load([(wide_ref.at[i], wq_out.at[layer, i])], out_sems.at[pl.ds(i, 1)])
            copies[3].wait()
            tall_ref[...] = tn(place_ref[...], wo_ref[...]).astype(BF)
            finish(outs + load([(tall_ref, wo_out.at[layer])], out_sems.at[pl.ds(3, 1)]))

        if only is None:
            make(section)
        else:

            @pl.when(section == only)
            def _():
                make(1 - only)

    args = [where, wq, wo, place] + ([] if begun is None else list(begun))
    return call(
        body,
        [shape((2, 3, width, padded), BF), shape((2, padded, width), BF)],
        [SM, HB, HB, FREE] + ([] if begun is None else [HB, HB]),
        [
            pltpu.VMEM((3, narrow, width), BF),
            pltpu.VMEM((narrow, width), BF),
            pltpu.VMEM((3, width, padded), BF),
            pltpu.VMEM((padded, width), BF),
            pltpu.SemaphoreType.DMA((4,)),
            pltpu.SemaphoreType.DMA((4,)),
        ],
        name="prepare_weights",
        limit=24,
        kept=2,
        aliases={} if begun is None else {4: 0, 5: 1},
    )(*args)


def last_ahead(where, cotangent, down_own, down_got, mods, picks):
    rows = picks.shape[0]
    size, width = down_own.shape

    def body(where_ref, cot_in, wd_a, wd_b, mods_ref, picks_ref, gp_out, gh_out, gp_ref, gh_ref, wd_ref, sems):
        copies = load(rows_of(cot_in, where_ref, gp_ref), sems)
        fetch(where_ref[0] == 1, wd_a, wd_b, wd_ref, sems.at[4])
        finish(copies)
        gp_ref[...] = (gp_ref[...].astype(F32) * token_mod(picks_ref[...], mods_ref, 5)).astype(BF)
        outs = load([(gp_ref, gp_out)], sems)
        arrived(wd_a, wd_ref, sems.at[4])
        gh_ref[...] = nt(gp_ref[...], wd_ref[...]).astype(BF)
        finish(outs + load([(gh_ref, gh_out)], sems.at[pl.ds(1, 1)]))

    return call(
        body,
        [shape((rows, width), BF), shape((rows, size), BF)],
        [SM] + [HB] * 3 + [VM] * 2,
        [
            pltpu.VMEM((rows, width), BF),
            pltpu.VMEM((rows, size), BF),
            pltpu.VMEM((size, width), BF),
            pltpu.SemaphoreType.DMA((5,)),
        ],
        name="last_ahead",
        limit=16,
        kept=2,
    )(where, cotangent, down_own, down_got, mods, picks)


def attention_forward(layer, where, blocks, weights, tables, mods, picks, carried=()):
    wq, wo = weights
    cosine, sine, gains, seg_col, seg_row = tables
    padded, width = wo.shape[1:]
    heads = padded // LANE
    raw_input = len(blocks) == 1
    rows = cosine.shape[0]
    share = rows // 4
    scale = HEAD**-0.5
    QB = 512

    def body(where_ref, *refs):
        refs = list(refs)
        in_refs = [refs.pop(0) for _ in blocks]
        wq_in, wo_in, cos_ref, sin_ref, gain_ref, segc_ref, segr_ref, mods_ref, picks_ref = refs[:9]
        refs = refs[9:]
        carried_refs = [refs.pop(0) for _ in carried]
        p_refs = [refs.pop(0) for _ in range(4)]
        state_ref = refs.pop(0) if raw_input else None
        kept = [refs.pop(0) for _ in range(7)]
        carried_outs = [refs.pop(0) for _ in carried]
        wq_ref, wo_ref, mask_ref = refs[:3]
        here = refs[3:10]
        sems, out_sems, carried_sems, a_x_ref, x_sems = refs[10:]
        if raw_input:
            x_ref = a_x_ref
            x_copies = load(rows_of(in_refs[0], where_ref, x_ref), x_sems)
        qraw_ref, kraw_ref, qrot_ref, krot_ref, v_ref, mixed_ref, a_ref = here
        pairs = [(wq_in.at[layer, i], wq_ref.at[i]) for i in range(3)] + [(wo_in.at[layer], wo_ref)]
        weights_in = load(pairs[:1], sems)

        def keep(i):
            pltpu.make_async_copy(here[i], kept[i], out_sems.at[i]).start()

        if raw_input:
            picked = picks_ref[...]
            shift1 = token_mod(picked, mods_ref, 0)
            scale1 = token_mod(picked, mods_ref, 1)
            finish(x_copies)
            state_ref[...] = x_ref[:share]
            x = x_ref[...].astype(F32)
            a_ref[...] = (x * inverse_rms(x) * (1.0 + scale1) + shift1).astype(BF)
        else:
            for k, ref in enumerate(in_refs):
                a_ref[k * share : (k + 1) * share] = ref[...]
        mask_ref[...] = jnp.where(segc_ref[...] == segr_ref[...], 1.0, 0.0).astype(BF)
        cos = cos_ref[...]
        sin = sin_ref[...]
        for i, (raw_out, rot_out) in enumerate(((qraw_ref, qrot_ref), (kraw_ref, krot_ref))):
            weights_in[i].wait()
            if i == 0:
                weights_in += load(pairs[1:], sems.at[pl.ds(1, 3)])
                carried_copies = load(list(zip(carried_refs, carried_outs)), carried_sems)
                keep(6)
            gain = gain_ref[2 * layer + i : 2 * layer + i + 1]
            all_raw = nn(a_ref[...], wq_ref[i])
            for h in range(heads):
                at = slice(h * LANE, (h + 1) * LANE)
                raw = all_raw[:, at]
                raw_out[:, at] = raw.astype(BF)
                turned = rotate(raw * head_inverse(raw) * gain, cos, sin)
                rot_out[:, at] = turned.astype(BF)
            keep(i)
            keep(2 + i)
        weights_in[2].wait()
        one = jnp.where(lax.broadcasted_iota(jnp.int32, (1, padded), 1) % LANE == LANE - 1, 1.0, 0.0)
        v_ref[...] = (nn(a_ref[...], wq_ref[2]) + one).astype(BF)
        keep(4)

        for j in range(rows // QB):
            at_rows = slice(j * QB, (j + 1) * QB)
            for h in range(heads):
                at = slice(h * LANE, (h + 1) * LANE)
                scores = nt(qrot_ref[at_rows, at], krot_ref[:, at]) * scale
                grown = jnp.exp(scores).astype(BF) * mask_ref[at_rows]
                mixed = nn(grown, v_ref[:, at])
                mixed_ref[at_rows, at] = (mixed * (1.0 / mixed[:, LANE - 1 :])).astype(BF)
        keep(5)
        weights_in[3].wait()
        step = 3 * LANE
        for j in range(width // step):
            at = slice(j * step, (j + 1) * step)
            split_store(nn(mixed_ref[...], wo_ref[:, at]), at, p_refs)
        for i in range(7):
            pltpu.make_async_copy(here[i], kept[i], out_sems.at[i]).wait()
        finish(carried_copies)

    outs = [shape((share, width), BF)] * (5 if raw_input else 4)
    saved_shapes = [shape((rows, padded), BF)] * 6 + [shape((rows, width), BF)]
    result = call(
        body,
        outs + saved_shapes + [shape(c.shape, c.dtype) for c in carried],
        [SM] + ([HB] if raw_input else [VM] * 4) + [HB] * 2 + [VM] * (7 + len(carried)),
        [
            pltpu.VMEM((3, width, padded), BF),
            pltpu.VMEM((padded, width), BF),
            pltpu.VMEM((rows, rows), BF),
        ] + [pltpu.VMEM(s.shape, BF) for s in saved_shapes] + [
            pltpu.SemaphoreType.DMA((4,)),
            pltpu.SemaphoreType.DMA((7,)),
            pltpu.SemaphoreType.DMA((max(1, len(carried)),)),
            pltpu.VMEM((rows if raw_input else 16, width), BF),
            pltpu.SemaphoreType.DMA((4,)),
        ],
        name=f"attention_forward_{layer}",
        limit=28,
        kept=7 + len(carried),
    )(where, *blocks, wq, wo, cosine, sine, gains, seg_col, seg_row, mods, picks, *carried)
    n = len(outs)
    return list(result[:4]), list(result[4:n]), list(result[n : n + 7]), list(result[n + 7 :])


def add_parts(refs):
    total = refs[0][...].astype(F32)
    for ref in refs[1:]:
        total += ref[...].astype(F32)
    return total


def after_attention(parts, state, mods, picks):
    dims = state.shape

    def body(p0, p1, p2, p3, state_ref, mods_ref, picks_ref, mlp_ref, attended_ref, after_ref):
        picked = picks_ref[...]
        attended = add_parts((p0, p1, p2, p3))
        attended_ref[...] = attended.astype(BF)
        after = state_ref[...].astype(F32) + token_mod(picked, mods_ref, 2) * attended
        after_ref[...] = after
        normed = after * inverse_rms(after)
        mlp_ref[...] = (normed * (1.0 + token_mod(picked, mods_ref, 4)) + token_mod(picked, mods_ref, 3)).astype(BF)

    return call(
        body,
        [shape(dims, BF), shape(dims, BF), shape(dims, F32)],
        [VM] * 7,
        name="after_attention",
        limit=8,
    )(*parts, state, mods, picks)


def after_mlp(parts, after, mods, picks, mods_next):
    dims = after.shape

    def body(p0, p1, p2, p3, after_ref, mods_ref, picks_ref, next_ref, in_ref, projected_ref, state_ref):
        picked = picks_ref[...]
        projected = add_parts((p0, p1, p2, p3))
        output = after_ref[...] + token_mod(picked, mods_ref, 5) * projected
        low = output.astype(BF)
        state_ref[...] = low
        state = low.astype(F32)
        normed = state * inverse_rms(state)
        in_ref[...] = (normed * (1.0 + token_mod(picked, next_ref, 1)) + token_mod(picked, next_ref, 0)).astype(BF)
        projected_ref[...] = projected.astype(BF)

    return call(
        body,
        [shape(dims, BF)] * 3,
        [VM] * 8,
        name="after_mlp",
        limit=8,
    )(*parts, after, mods, picks, mods_next)


def last_output(parts, after, mods, picks):
    dims = after.shape

    def body(p0_in, p1, p2, p3, after_in, mods_ref, picks_ref, output_ref, p0, after_ref, sems):
        copies = load([(p0_in, p0), (after_in, after_ref)], sems)
        gate2 = token_mod(picks_ref[...], mods_ref, 5)
        finish(copies)
        output_ref[...] = after_ref[...] + gate2 * add_parts((p0, p1, p2, p3))

    return call(
        body,
        [shape(dims, F32)],
        [HB] + [VM] * 3 + [HB] + [VM] * 2,
        [pltpu.VMEM(dims, BF), pltpu.VMEM(dims, F32), pltpu.SemaphoreType.DMA((2,))],
        name="last_output",
        limit=8,
    )(*parts, after, mods, picks)[0]


def last_projection(layer, where, hidden, weights, cotangent, picks):
    wd_own, wd_got = weights[2:]
    rows, size = hidden.shape
    width = wd_own.shape[1]
    share = rows // 4
    step = 3 * LANE

    def body(where_ref, hid_in, wd_a, wd_b, cot_in, picks_ref, p0, p1, p2, p3, sums_out,
             hid_ref, wd_ref, g_ref, q0, q1, q2, q3, sums_ref, sems, cot_sems, out_sems):
        fetch(where_ref[0] == layer, wd_a, wd_b, wd_ref, sems.at[0])
        copies = load([(hid_in, hid_ref)], sems.at[pl.ds(1, 1)]) + load(rows_of(cot_in, where_ref, g_ref), cot_sems)
        arrived(wd_a, wd_ref, sems.at[0])
        finish(copies)
        picked = picks_ref[...]
        for j in range(width // step):
            at = slice(j * step, (j + 1) * step)
            part = nn(hid_ref[...], wd_ref[:, at])
            split_store(part, at, (q0, q1, q2, q3))
            sums_ref[0, :, at] = image_sums(picked, g_ref[:, at].astype(F32) * part)
        finish(load([(q0, p0), (q1, p1), (q2, p2), (q3, p3), (sums_ref, sums_out)], out_sems))

    sums = (1, picks.shape[1], width)
    result = call(
        body,
        [shape((share, width), BF)] * 4 + [shape(sums, F32)],
        [SM] + [HB] * 4 + [VM],
        [
            pltpu.VMEM((rows, size), BF),
            pltpu.VMEM((size, width), BF),
            pltpu.VMEM((rows, width), BF),
        ]
        + [pltpu.VMEM((share, width), BF)] * 4
        + [
            pltpu.VMEM(sums, F32),
            pltpu.SemaphoreType.DMA((2,)),
            pltpu.SemaphoreType.DMA((4,)),
            pltpu.SemaphoreType.DMA((5,)),
        ],
        name="last_projection",
        limit=16,
        kept=5,
    )(where, hidden, wd_own, wd_got, cotangent, picks)
    return list(result[:4]), result[4]


def attention_results(where, mine, theirs):
    half, columns = mine.shape
    narrow = columns // 4
    eye = jnp.eye(2 * half, dtype=BF)

    def body(where_ref, mine_ref, theirs_ref, eye_ref, qkv_out, out_out, qkv_ref, out_ref, sems):
        a, b = mine_ref[...].astype(F32), theirs_ref[...].astype(F32)
        first = where_ref[0] == 0
        full = jnp.concatenate([jnp.where(first, a, b), jnp.where(first, b, a)], axis=0)
        for i in range(3):
            qkv_ref[i] = full[:, i * narrow : (i + 1) * narrow]
        copies = load([(qkv_ref, qkv_out)], sems)
        out_ref[...] = tn(full[:, 3 * narrow :].astype(BF), eye_ref[...])
        finish(copies + load([(out_ref, out_out)], sems.at[pl.ds(1, 1)]))

    return call(
        body,
        [shape((3, 2 * half, narrow), F32), shape((narrow, 2 * half), F32)],
        [SM, VM, VM, FREE],
        [
            pltpu.VMEM((3, 2 * half, narrow), F32),
            pltpu.VMEM((narrow, 2 * half), F32),
            pltpu.SemaphoreType.DMA((2,)),
        ],
        name="attention_results",
        limit=12,
        kept=2,
    )(where, mine, theirs, eye)


def mlp_forward(layer, blocks, weights, section, carried, late):
    gu_own, gu_got, wd_own, wd_got = weights
    hidden_size, width = wd_own.shape
    share = blocks[0].shape[0]
    rows = share * 4
    chunk = 2 * LANE
    chunks = hidden_size // chunk

    def body(sec_ref, b0, b1, b2, b3, gu_a, gu_b, wd_a, wd_b, attended_ref, after_ref,
             *refs):
        refs = list(refs)
        p_refs = [] if late else [refs.pop(0) for _ in range(4)]
        hid_out, c1_out, c2_out, a_out, attended_out, after_out = refs[:6]
        refs = refs[6:]
        p_outs = [refs.pop(0) for _ in range(4)] if late else []
        a_ref, gu_ref, wd_ref, hid_ref, c1_ref, c2_ref, sems, out_sems, carried_sems = refs[:9]
        if late:
            p_refs, p_sems = refs[9:13], refs[13]
        own = sec_ref[0] == layer
        for j in range(chunks):
            at = pl.ds(j * chunk, chunk)
            for i in range(2):
                fetch(own, gu_a.at[i, :, at], gu_b.at[i, :, at], gu_ref.at[i, :, at], sems.at[2 * j + i])
        fetch(own, wd_a, wd_b, wd_ref, sems.at[2 * chunks])
        carried_copies = load([(attended_ref, attended_out), (after_ref, after_out)], carried_sems)
        for k, ref in enumerate((b0, b1, b2, b3)):
            a_ref[k * share : (k + 1) * share] = ref[...]
        for j in range(chunks):
            at = slice(j * chunk, (j + 1) * chunk)
            for i in range(2):
                arrived(gu_a.at[i, :, pl.ds(j * chunk, chunk)], gu_ref.at[i, :, pl.ds(j * chunk, chunk)], sems.at[2 * j + i])
            gate = nn(a_ref[...], gu_ref[0, :, at])
            up = nn(a_ref[...], gu_ref[1, :, at])
            sigma = jax.nn.sigmoid(gate)
            silu = gate * sigma
            hid_ref[:, at] = (silu * up).astype(BF)
            c1_ref[:, at] = (up * (sigma + silu * (1.0 - sigma))).astype(BF)
            c2_ref[:, at] = silu.astype(BF)
        kept = load([(hid_ref, hid_out), (c1_ref, c1_out), (c2_ref, c2_out), (a_ref, a_out)], out_sems)
        arrived(wd_a, wd_ref, sems.at[2 * chunks])
        step = 3 * LANE
        for j in range(width // step):
            at = slice(j * step, (j + 1) * step)
            split_store(nn(hid_ref[...], wd_ref[:, at]), at, p_refs)
        if late:
            kept += load(list(zip(p_refs, p_outs)), p_sems)
        finish(kept + carried_copies)

    parts = [shape((share, width), BF)] * 4
    outs = ([] if late else parts) + [shape((rows, hidden_size), BF)] * 3 + [shape((rows, width), BF)]
    outs += [shape(c.shape, c.dtype) for c in carried] + (parts if late else [])
    result = call(
        body,
        outs,
        [SM] + [VM] * 4 + [HB] * 4 + [VM] * 2,
        [
            pltpu.VMEM((rows, width), BF),
            pltpu.VMEM(gu_own.shape, BF),
            pltpu.VMEM(wd_own.shape, BF),
        ]
        + [pltpu.VMEM((rows, hidden_size), BF)] * 3
        + [
            pltpu.SemaphoreType.DMA((2 * chunks + 1,)),
            pltpu.SemaphoreType.DMA((4,)),
            pltpu.SemaphoreType.DMA((2,)),
        ]
        + ([pltpu.VMEM((share, width), BF)] * 4 + [pltpu.SemaphoreType.DMA((4,))] if late else []),
        name=f"mlp_forward_{layer}",
        kept=10 if late else 6,
    )(section, *blocks, gu_own, gu_got, wd_own, wd_got, *carried)
    result = list(result)
    partial = result[6:] if late else result[:4]
    result = result[:6] if late else result[4:]
    return partial, result[:4], result[4:]


def mlp_backward(layer, where, blocks, weights, saved, carried):
    gu_own, gu_got, wd_own, wd_got = weights
    c1, c2 = saved
    hidden_size, width = wd_own.shape
    rows = c1.shape[0]
    share = rows // 4
    chunk = 3 * LANE
    chunks = hidden_size // chunk

    def body(where_ref, *refs):
        refs = list(refs)
        in_refs = [refs.pop(0) for _ in blocks]
        gu_a, gu_b, wd_a, wd_b, c1_in, c2_in = refs[:6]
        refs = refs[6:]
        carried_refs = [refs.pop(0) for _ in carried]
        p_refs = [refs.pop(0) for _ in range(3)]
        outs = [refs.pop(0) for _ in range(4)]
        carried_outs = [refs.pop(0) for _ in carried]
        gu_ref, wd_ref, c1_ref, c2_ref, gg_ref, gup_ref, gp_ref, p0, sems, in_sems, out_sems, carried_sems = refs
        own = where_ref[0] == layer
        for j in range(chunks):
            at = pl.ds(j * chunk, chunk)
            fetch(own, wd_a.at[at], wd_b.at[at], wd_ref.at[at], sems.at[j])
        saved_copies = load([(c1_in, c1_ref), (c2_in, c2_ref)], in_sems)
        for i in range(2):
            fetch(own, gu_a.at[i], gu_b.at[i], gu_ref.at[i], sems.at[chunks + i])
        kept = load(list(zip(carried_refs, carried_outs)), carried_sems)
        for k, ref in enumerate(in_refs):
            gp_ref[k * share : (k + 1) * share] = ref[...]

        def keep(i, here):
            kept.append(pltpu.make_async_copy(here, outs[i], out_sems.at[i]))
            kept[-1].start()

        keep(0, gp_ref)
        for j in range(chunks):
            at = slice(j * chunk, (j + 1) * chunk)
            arrived(wd_a.at[pl.ds(j * chunk, chunk)], wd_ref.at[pl.ds(j * chunk, chunk)], sems.at[j])
            grad_hidden = nt(gp_ref[...], wd_ref[at])
            if j == 0:
                finish(saved_copies)
            gg_ref[:, at] = (grad_hidden * c1_ref[:, at].astype(F32)).astype(BF)
            gup_ref[:, at] = (grad_hidden * c2_ref[:, at].astype(F32)).astype(BF)
        keep(1, gg_ref)
        keep(2, gup_ref)
        for i in range(2):
            arrived(gu_a.at[i], gu_ref.at[i], sems.at[chunks + i])
        step = 3 * LANE
        for j in range(width // step):
            at = slice(j * step, (j + 1) * step)
            split_store(nt(gg_ref[...], gu_ref[0, at]) + nt(gup_ref[...], gu_ref[1, at]), at, [p0] + p_refs)
        keep(3, p0)
        finish(kept)

    outs = [shape((share, width), BF)] * 3
    outs += [shape((rows, width), BF)] + [shape((rows, hidden_size), BF)] * 2 + [shape((share, width), BF)]
    outs += [shape(c.shape, c.dtype) for c in carried]
    result = call(
        body,
        outs,
        [SM] + [VM] * 4 + [HB] * 6 + [VM] * len(carried),
        [
            pltpu.VMEM(gu_own.shape, BF),
            pltpu.VMEM(wd_own.shape, BF),
        ]
        + [pltpu.VMEM((rows, hidden_size), BF)] * 4
        + [
            pltpu.VMEM((rows, width), BF),
            pltpu.VMEM((share, width), BF),
            pltpu.SemaphoreType.DMA((chunks + 2,)),
            pltpu.SemaphoreType.DMA((2,)),
            pltpu.SemaphoreType.DMA((4,)),
            pltpu.SemaphoreType.DMA((max(1, len(carried)),)),
        ],
        name=f"mlp_backward_{layer}",
        kept=4 + len(carried),
    )(where, *blocks, gu_own, gu_got, wd_own, wd_got, c1, c2, *carried)
    return list(result[:3]), list(result[3:6]), list(result[6:])


def mlp_last(layer, blocks, weights, ahead, section, carried):
    gu_own, gu_got = weights[:2]
    grad_projected, grad_hidden = ahead
    rows, size = grad_hidden.shape
    width = gu_own.shape[1]
    share = rows // 4
    chunk = 2 * LANE
    chunks = size // chunk
    step = LANE

    def body(sec_ref, b0, b1, b2, b3, gu_a, gu_b, gp_in, gh_in, attended_ref, after_ref,
             gg_ref, gup_ref, out, hid_out, attended_out, after_out,
             a_ref, gu_ref, hid_ref, gh_ref, gp_ref, full_ref, sems, in_sems, out_sems, kept_sems):
        own = sec_ref[0] == layer
        for j in range(chunks):
            at = pl.ds(j * chunk, chunk)
            for i in range(2):
                fetch(own, gu_a.at[i, :, at], gu_b.at[i, :, at], gu_ref.at[i, :, at], sems.at[2 * j + i])
        ins = load([(gh_in, gh_ref), (gp_in, gp_ref)], in_sems)
        kept = load([(attended_ref, attended_out), (after_ref, after_out)], kept_sems)
        for k, ref in enumerate((b0, b1, b2, b3)):
            a_ref[k * share : (k + 1) * share] = ref[...]
        for j in range(chunks):
            at = slice(j * chunk, (j + 1) * chunk)
            for i in range(2):
                here = pl.ds(j * chunk, chunk)
                arrived(gu_a.at[i, :, here], gu_ref.at[i, :, here], sems.at[2 * j + i])
            gate = nn(a_ref[...], gu_ref[0, :, at])
            up = nn(a_ref[...], gu_ref[1, :, at])
            if j == 0:
                ins[0].wait()
            sigma = jax.nn.sigmoid(gate)
            silu = gate * sigma
            grad = gh_ref[:, at].astype(F32)
            hid_ref[:, at] = (silu * up).astype(BF)
            gg_ref[:, at] = (grad * (up * (sigma + silu * (1.0 - sigma)))).astype(BF)
            gup_ref[:, at] = (grad * silu).astype(BF)
        kept += load([(hid_ref, hid_out)], kept_sems.at[pl.ds(2, 1)])
        ins[1].wait()
        for j in range(width // step):
            at = slice(j * step, (j + 1) * step)
            left = a_ref[:, at]
            full_ref[at, :size] = tn(left, gg_ref[...]).astype(BF)
            full_ref[at, size : 2 * size] = tn(left, gup_ref[...]).astype(BF)
            full_ref[at, 2 * size :] = tn(gp_ref[:, at], hid_ref[...]).astype(BF)
            here = pl.ds(j * step, step)
            kept += load([(full_ref.at[here], out.at[here])], out_sems.at[pl.ds(j, 1)])
        finish(kept)

    result = call(
        body,
        [shape((rows, size), BF)] * 2
        + [shape((width, 3 * size), BF), shape((rows, size), BF)]
        + [shape(c.shape, c.dtype) for c in carried],
        [SM] + [VM] * 4 + [HB] * 4 + [VM] * 2,
        [
            pltpu.VMEM((rows, width), BF),
            pltpu.VMEM(gu_own.shape, BF),
            pltpu.VMEM((rows, size), BF),
            pltpu.VMEM((rows, size), BF),
            pltpu.VMEM((rows, width), BF),
            pltpu.VMEM((width, 3 * size), BF),
            pltpu.SemaphoreType.DMA((2 * chunks,)),
            pltpu.SemaphoreType.DMA((2,)),
            pltpu.SemaphoreType.DMA((width // step,)),
            pltpu.SemaphoreType.DMA((3,)),
        ],
        name=f"mlp_last_{layer}",
        kept=4,
        limit=28,
    )(section, *blocks, gu_own, gu_got, grad_projected, grad_hidden, *carried)
    return list(result[:2]), result[2], result[3], list(result[4:])


def mlp_input_grad(layer, section, grad_gate, grad_up, weights):
    gu_own, gu_got = weights[:2]
    rows = grad_gate.shape[0]
    width = gu_own.shape[1]
    share = rows // 4
    step = 3 * LANE

    def body(sec_ref, gg_ref, gup_ref, gu_a, gu_b, p1, p2, p3, p0_out, p0, gu_ref, sems, out_sems):
        own = sec_ref[0] == layer
        spans = [pl.ds(j * step, step) for j in range(width // step)]
        for j, at in enumerate(spans):
            for i in range(2):
                fetch(own, gu_a.at[i, at], gu_b.at[i, at], gu_ref.at[i, at], sems.at[2 * j + i])
        for j, at in enumerate(spans):
            for i in range(2):
                arrived(gu_a.at[i, at], gu_ref.at[i, at], sems.at[2 * j + i])
            here = slice(j * step, (j + 1) * step)
            split_store(
                nt(gg_ref[...], gu_ref[0, here]) + nt(gup_ref[...], gu_ref[1, here]), here, (p0, p1, p2, p3)
            )
        finish(load([(p0, p0_out)], out_sems))

    result = call(
        body,
        [shape((share, width), BF)] * 4,
        [SM, VM, VM, HB, HB],
        [
            pltpu.VMEM((share, width), BF),
            pltpu.VMEM(gu_own.shape, BF),
            pltpu.SemaphoreType.DMA((2 * (width // step),)),
            pltpu.SemaphoreType.DMA((1,)),
        ],
        name="mlp_input_grad",
        kept=1,
        limit=16,
    )(section, grad_gate, grad_up, gu_own, gu_got)
    return [result[3]] + list(result[:3])


def mlp_weight_grads(mlp_in, grads, hidden):
    grad_projected, grad_gate, grad_up = grads
    rows, width = grad_projected.shape
    size = hidden.shape[1]
    step = 3 * LANE

    def body(a_in, gg_in, gu_in, gp_in, hid_in, *refs):
        out, a_ref, gg_ref, gu_ref, gp_ref, hid_ref, full_ref, in_sems, sems = refs
        ins = load([(a_in, a_ref), (gg_in, gg_ref), (gu_in, gu_ref), (gp_in, gp_ref), (hid_in, hid_ref)], in_sems)
        kept = []
        finish(ins[:2])
        for j in range(width // step):
            at = slice(j * step, (j + 1) * step)
            left = a_ref[:, at]
            full_ref[at, :size] = tn(left, gg_ref[...]).astype(BF)
            if j == 0:
                ins[2].wait()
            full_ref[at, size : 2 * size] = tn(left, gu_ref[...]).astype(BF)
            if j == 0:
                finish(ins[3:])
            full_ref[at, 2 * size :] = tn(gp_ref[:, at], hid_ref[...]).astype(BF)
            here = pl.ds(j * step, step)
            kept.append(pltpu.make_async_copy(full_ref.at[here], out.at[here], sems.at[j]))
            kept[-1].start()
        finish(kept)

    result = call(
        body,
        [shape((width, 3 * size), BF)],
        [HB] * 5,
        [pltpu.VMEM((rows, width), BF)]
        + [pltpu.VMEM((rows, size), BF)] * 2
        + [
            pltpu.VMEM((rows, width), BF),
            pltpu.VMEM((rows, size), BF),
            pltpu.VMEM((width, 3 * size), BF),
            pltpu.SemaphoreType.DMA((5,)),
            pltpu.SemaphoreType.DMA((width // step,)),
        ],
        name="mlp_weight_grads",
        kept=1,
    )(mlp_in, grad_gate, grad_up, grad_projected, hidden)
    return result[0]


def attention_backward(layer, blocks, weights, saved, tables, grad_after):
    wq, wo = weights
    cosine, sine, gains, seg_col, seg_row = tables
    rows, padded = saved[0].shape
    width = wo.shape[2]
    heads = padded // LANE
    share = rows // 4
    scale = HEAD**-0.5
    QB = 512

    def body(b0, b1, b2, b3, wq_in, wo_in, qraw_in, kraw_in, qrot_in, krot_in, v_in,
             cos_ref, sin_ref, gain_ref, segc_ref, segr_ref, grad_ref,
             p1, p2, p3, g_out, ga_out, p0_out, ggain_out, grad_out,
             wq_ref, wo_ref, qraw_ref, kraw_ref, qrot_ref, krot_ref, v_ref, mask_ref,
             ga_ref, gmix_ref, gq_ref, gk_ref, g_ref, p0, ggain_ref, sems, in_sems):
        ins = [(wo_in.at[layer], wo_ref)]
        ins += [(qrot_in, qrot_ref), (krot_in, krot_ref), (v_in, v_ref), (qraw_in, qraw_ref), (kraw_in, kraw_ref)]
        ins += [(wq_in.at[layer, i], wq_ref.at[i]) for i in range(3)]
        ins = load(ins, in_sems)
        for k, ref in enumerate((b0, b1, b2, b3)):
            ga_ref[k * share : (k + 1) * share] = ref[...]
        kept = []

        def keep(here, there):
            kept.append(pltpu.make_async_copy(here, there, sems.at[len(kept)]))
            kept[-1].start()

        keep(ga_ref, ga_out)
        keep(grad_ref, grad_out)
        mask_ref[...] = jnp.where(segc_ref[...] == segr_ref[...], 1.0, 0.0).astype(BF)
        ins[0].wait()
        gmix_ref[...] = nt(ga_ref[...], wo_ref[...]).astype(BF)
        finish(ins[1:4])
        for h in range(heads):
            at = slice(h * LANE, (h + 1) * LANE)
            for j in range(rows // QB):
                at_rows = slice(j * QB, (j + 1) * QB)
                query = qrot_ref[at_rows, at]
                grad_mixed = gmix_ref[at_rows, at]
                scores = nt(krot_ref[:, at], query) * scale
                grown = (jnp.exp(scores).astype(BF) * mask_ref[:, at_rows]).astype(F32)
                weights_t = grown * (1.0 / jnp.sum(grown, axis=0, keepdims=True))
                grad_weights = nt(v_ref[:, at], grad_mixed)
                add_v = nn(weights_t.astype(BF), grad_mixed)
                product = weights_t * grad_weights
                delta = jnp.sum(product, axis=0, keepdims=True)
                grad_scores = (product - weights_t * delta).astype(BF)
                gq_ref[at_rows, at] = tn(grad_scores, krot_ref[:, at])
                add_k = nn(grad_scores, query)
                total_v = add_v if j == 0 else total_v + add_v
                total_k = add_k if j == 0 else total_k + add_k
            gk_ref[:, at] = total_k
            g_ref[:, 2 * padded + h * LANE : 2 * padded + (h + 1) * LANE] = total_v.astype(BF)
        cos = cos_ref[...]
        sin = sin_ref[...]
        finish(ins[4:6])
        ggain_ref[...] = jnp.zeros_like(ggain_ref)
        for i, (raw_ref, grad_ref) in enumerate(((qraw_ref, gq_ref), (kraw_ref, gk_ref))):
            gain = gain_ref[2 * layer + i : 2 * layer + i + 1]
            gain_sum = jnp.zeros((1, LANE), F32)
            for h in range(heads):
                at = slice(h * LANE, (h + 1) * LANE)
                raw = raw_ref[:, at].astype(F32)
                inverse = head_inverse(raw)
                normed = raw * inverse
                turned = unrotate(grad_ref[:, at], cos, sin) * scale
                product = turned * normed
                gain_sum += jnp.sum(product, axis=0, keepdims=True)
                back = inverse * (turned * gain - normed * head_mean(product * gain))
                g_ref[:, i * padded + h * LANE : i * padded + (h + 1) * LANE] = back.astype(BF)
            ggain_ref[i : i + 1] = gain_sum
        keep(g_ref, g_out)
        keep(ggain_ref, ggain_out)
        finish(ins[6:])
        step = 3 * LANE
        for j in range(width // step):
            at = slice(j * step, (j + 1) * step)
            total = nt(g_ref[:, :padded], wq_ref[0, at])
            total += nt(g_ref[:, padded : 2 * padded], wq_ref[1, at])
            total += nt(g_ref[:, 2 * padded :], wq_ref[2, at])
            split_store(total, at, (p0, p1, p2, p3))
        keep(p0, p0_out)
        finish(kept)

    outs = [shape((share, width), BF)] * 3
    outs += [shape((rows, 3 * padded), BF), shape((rows, width), BF), shape((share, width), BF), shape((8, LANE), F32)]
    outs += [shape(grad_after.shape, F32)]
    result = call(
        body,
        outs,
        [VM] * 4 + [HB] * 7 + [VM] * 6,
        [
            pltpu.VMEM((3, width, padded), BF),
            pltpu.VMEM((padded, width), BF),
        ]
        + [pltpu.VMEM((rows, padded), BF)] * 5
        + [
            pltpu.VMEM((rows, rows), BF),
            pltpu.VMEM((rows, width), BF),
            pltpu.VMEM((rows, padded), BF),
            pltpu.VMEM((rows, padded), F32),
            pltpu.VMEM((rows, padded), F32),
            pltpu.VMEM((rows, 3 * padded), BF),
            pltpu.VMEM((share, width), BF),
            pltpu.VMEM((8, LANE), F32),
            pltpu.SemaphoreType.DMA((5,)),
            pltpu.SemaphoreType.DMA((9,)),
        ],
        name=f"attention_backward_{layer}",
        limit=32,
        kept=5,
    )(*blocks, wq, wo, *saved[:5], cosine, sine, gains, seg_col, seg_row, grad_after)
    return list(result[:3]), list(result[3:])


def attention_weight_grads(attention_in, grads, mixed, grad_attended, place):
    rows, width = attention_in.shape
    padded, narrow = place.shape
    step = 3 * LANE


    def body(a_in, g_in, mixed_in, ga_in, place_ref, out, a_ref, g_ref, mixed_ref, ga_ref, right_ref, full_ref, in_sems, sems):
        ins = load([(g_in, g_ref), (mixed_in, mixed_ref), (a_in, a_ref), (ga_in, ga_ref)], in_sems)
        finish(ins[:2])
        for i in range(3):
            right_ref[i] = nn(g_ref[:, i * padded : (i + 1) * padded], place_ref[...]).astype(BF)
        right_ref[3] = nn(mixed_ref[...], place_ref[...]).astype(BF)
        finish(ins[2:])
        kept = []
        for j in range(width // step):
            at = slice(j * step, (j + 1) * step)
            left = a_ref[:, at]
            for i in range(3):
                full_ref[at, i * narrow : (i + 1) * narrow] = tn(left, right_ref[i]).astype(BF)
            full_ref[at, 3 * narrow :] = tn(ga_ref[:, at], right_ref[3]).astype(BF)
            here = pl.ds(j * step, step)
            kept.append(pltpu.make_async_copy(full_ref.at[here], out.at[here], sems.at[j]))
            kept[-1].start()
        finish(kept)

    result = call(
        body,
        [shape((width, 4 * narrow), BF)],
        [HB] * 4 + [FREE],
        [
            pltpu.VMEM((rows, width), BF),
            pltpu.VMEM((rows, 3 * padded), BF),
            pltpu.VMEM((rows, padded), BF),
            pltpu.VMEM((rows, width), BF),
            pltpu.VMEM((4, rows, narrow), BF),
            pltpu.VMEM((width, 4 * narrow), BF),
            pltpu.SemaphoreType.DMA((4,)),
            pltpu.SemaphoreType.DMA((width // step,)),
        ],
        name="attention_weight_grads",
        kept=1,
    )(attention_in, grads, mixed, grad_attended, place)
    return result[0]


def back_of_mlp(where, parts, grad_out, after, attended, projected, mods, picks):
    dims = after.shape
    extra = [] if projected is None else [projected]
    sums = (3 + len(extra), picks.shape[1], dims[1])

    def body(where_ref, p0_in, p1, p2, p3, g_in, after_in, attended_in, *refs):
        refs = list(refs)
        extra_refs = [refs.pop(0) for _ in extra]
        (mods_ref, picks_ref, ga_ref, grad_ref, sums_out,
         p0, g_ref, after_ref, attended_ref, projected_ref, sums_ref, sems, out_sems) = refs
        pairs = [(p0_in, p0), (after_in, after_ref)] + own_rows(g_in, where_ref, g_ref)
        ins = load(pairs + [(attended_in, attended_ref)] + [(ref, projected_ref) for ref in extra_refs], sems)
        picked = picks_ref[...]
        scale2 = token_mod(picked, mods_ref, 4)
        gate1 = token_mod(picked, mods_ref, 2)
        finish(ins[:2])
        grad_in = add_parts((p0, p1, p2, p3))
        after = after_ref[...]
        inverse = inverse_rms(after)
        normed = after * inverse
        finish(ins[2:])
        g = g_ref[...].astype(F32)
        grad_after = g + norm_back(grad_in * (1.0 + scale2), normed, inverse)
        sums_ref[0] = image_sums(picked, grad_after * attended_ref[...].astype(F32))
        sums_ref[1] = image_sums(picked, grad_in)
        sums_ref[2] = image_sums(picked, grad_in * normed)
        if extra:
            sums_ref[3] = image_sums(picked, g * projected_ref[...].astype(F32))
        kept = load([(sums_ref, sums_out)], out_sems)
        grad_ref[...] = grad_after
        ga_ref[...] = (grad_after * gate1).astype(BF)
        finish(kept)

    return call(
        body,
        [shape(dims, BF), shape(dims, F32), shape(sums, F32)],
        [SM, HB] + [VM] * 3 + [HB] * (3 + len(extra)) + [VM] * 2,
        [
            pltpu.VMEM(dims, BF),
            pltpu.VMEM(dims, BF),
            pltpu.VMEM(dims, F32),
            pltpu.VMEM(dims, BF),
            pltpu.VMEM(dims, BF),
            pltpu.VMEM(sums, F32),
            pltpu.SemaphoreType.DMA((5,)),
            pltpu.SemaphoreType.DMA((1,)),
        ],
        name="back_of_mlp",
        limit=10,
        kept=1,
    )(where, *parts, grad_out, after, attended, *extra, mods, picks)


def back_of_attention(where, parts, grad_after, state, mods, picks, mods_below):
    first = mods_below is None
    dims = grad_after.shape

    def body(where_ref, p0_in, p1, p2, p3, grad_in_ref, state_in, mods_ref, picks_ref, *refs):
        refs = list(refs)
        below_ref = None if first else refs.pop(0)
        sums_ref = refs.pop(0)
        gp_ref = None if first else refs.pop(0)
        out_ref, p0, grad_ref, state_ref, sems = refs
        ins = load([(p0_in, p0), (grad_in_ref, grad_ref)] + own_rows(state_in, where_ref, state_ref), sems)
        picked = picks_ref[...]
        scale1 = token_mod(picked, mods_ref, 1)
        finish(ins)
        grad_in = add_parts((p0, p1, p2, p3))
        state = state_ref[...].astype(F32)
        inverse = inverse_rms(state)
        normed = state * inverse
        grad_state = grad_ref[...] + norm_back(grad_in * (1.0 + scale1), normed, inverse)
        out_ref[...] = grad_state.astype(out_ref.dtype)
        if not first:
            gp_ref[...] = (grad_state.astype(BF).astype(F32) * token_mod(picked, below_ref, 5)).astype(BF)
        sums_ref[0] = image_sums(picked, grad_in)
        sums_ref[1] = image_sums(picked, grad_in * normed)

    outs = [shape((2, picks.shape[1], dims[1]), F32)] + ([shape(dims, F32)] if first else [shape(dims, BF)] * 2)
    extra = () if first else (mods_below,)
    return call(
        body,
        outs,
        [SM, HB] + [VM] * 3 + [HB] * 2 + [VM] * (2 + len(extra)),
        [
            pltpu.VMEM(dims, BF),
            pltpu.VMEM(dims, F32),
            pltpu.VMEM(dims, BF),
            pltpu.SemaphoreType.DMA((3,)),
        ],
        name="back_of_attention",
        limit=10,
    )(where, *parts, grad_after, state, mods, picks, *extra)


def exchange(value, axis, k):
    return lax.ppermute(value, axis, [(i, i ^ k) for i in range(lax.axis_size(axis))])


def handed_on(value):
    def body(source, target):
        target[...] = source[...]

    return call(body, [shape(value.shape, value.dtype)], [VM], name="handed_on", limit=4)(value)[0]


def in_order(got, order):
    for place, k in enumerate(order):
        for _ in range(len(order) - 1 - place):
            got[k] = handed_on(got[k])


def send_parts(parts, beside=None, whole=False):
    got = {k: exchange(parts[k], "tensor", k) for k in (3, 1, 2)}
    if beside is not None and not whole:
        got[1], beside = lax.optimization_barrier((got[1], beside))
    if whole:
        got, beside = lax.optimization_barrier((got, beside))
    else:
        in_order(got, (1, 2, 3))
    result = [parts[0], got[1], got[2], got[3]]
    return result if beside is None else (result, beside)


def gather_blocks(own):
    got = {k: exchange(own, "tensor", k) for k in (3, 1, 2)}
    in_order(got, (3, 2, 1))
    return [own, got[1], got[2], got[3]]


def group_sum(value, axis):
    k = 1
    while k < lax.axis_size(axis):
        value = value + exchange(value, axis, k)
        k *= 2
    return value


def gather_dp(value):
    count = lax.axis_size("dp")
    if count > 4:
        return lax.all_gather(value, "dp", axis=0)
    me = lax.axis_index("dp")
    got = [value] + [exchange(value, "dp", k) for k in range(1, count)]
    stacked = jnp.stack(got)
    return jnp.stack([lax.dynamic_index_in_dim(stacked, me ^ j, 0, keepdims=False) for j in range(count)])


def head_places(heads):
    place = np.zeros((heads * HEAD, heads * LANE), np.float32)
    for h in range(heads):
        for j in range(HEAD):
            place[h * HEAD + j, h * LANE + (j // HALF) * (LANE // 2) + j % HALF] = 1.0
    return place


def shards(
    inputs,
    cotangent,
    conditioning,
    lengths,
    positions,
    modulator,
    projections,
    norm_gains,
    out_weight,
    gate_up,
    down_weight,
):
    section = lax.axis_index("section")
    other = 1 - section
    tensor = lax.axis_index("tensor")
    data = lax.axis_index("dp")
    micro, _, width = inputs.shape
    rows = inputs.shape[1]
    group = lax.axis_size("tensor")
    share = rows // group
    items = lengths.shape[2]
    narrow = projections.shape[3]
    heads = narrow // HEAD
    columns = modulator.shape[2]
    sec = section.reshape(1).astype(jnp.int32)

    where = jnp.stack([section, tensor]).astype(jnp.int32)
    is_first = section == 0

    where = jnp.stack([section, tensor]).astype(jnp.int32)
    is_first = section == 0
    place = jnp.asarray(head_places(heads), BF)
    place_one = jnp.asarray(head_places(1), F32)

    own = (jnp.swapaxes(projections[0], 1, 2), out_weight[0])
    got = [exchange(value, "section", 1) for value in own]
    got_gains = exchange(norm_gains[0], "section", 1)
    scaled, part = modulation_part(conditioning, jnp.swapaxes(modulator[0], 0, 1))
    pieces = gather_blocks(part)
    quarter = HEAD // 4
    rates = 10000.0 ** (-jnp.arange(quarter).astype(F32) / quarter)
    rates = jnp.concatenate([rates, rates, jnp.zeros(LANE // 2 - HALF, F32)])[:, None]
    where_late, part = lax.optimization_barrier((where, part))
    cosine, sine, seg_col, seg_row, picks, picks_own = prepare_tables(where_late, lengths, positions, rates)
    wq, wo = prepare_weights(where_late, own, place)
    pieces, got, cosine, wq = lax.optimization_barrier((pieces, got, cosine, wq))
    mods_own, mods_send, gains = modulation_rows([part] + pieces[1:], (norm_gains[0], got_gains), where, place_one)
    mods_got = exchange(mods_send, "section", 1)
    gu_send, wd_send, mods_got = lax.optimization_barrier((gate_up[0], down_weight[0], mods_got))
    mods = [jnp.where(is_first, mods_own, mods_got), jnp.where(is_first, mods_got, mods_own)]
    gu_got = exchange(gu_send, "section", 1)
    wd_got = exchange(wd_send, "section", 1)
    mlp_weights = (gate_up[0], gu_got, down_weight[0], wd_got)
    wq, mods_first = lax.optimization_barrier((wq, mods[0]))
    mods[0] = mods_first
    wq, wo = prepare_weights(where, got, place, (wq, wo), 1)
    tables = (cosine, sine, gains, seg_col, seg_row)

    cache = []
    attention_blocks = [inputs]
    carried = ()
    for l in range(2):
        partial, state, saved, kept = attention_forward(
            l, where, attention_blocks, (wq, wo), tables, mods[l], picks, carried
        )
        if l == 0:
            state = state[0]
            wq, mixed = lax.optimization_barrier((wq, saved[5]))
            saved[5] = mixed
            wq, wo = prepare_weights(where, got, place, (wq, wo), 0)
            parts, wq = send_parts(partial, wq)
        else:
            parts = send_parts(partial)
            cache[0].append(kept[0])
            state = carried[1]
            state_kept = kept[1]
        mlp_in, attended, after = after_attention(parts, state, mods[l], picks_own)
        if l == 1:
            grads, mlp_grads, hidden, kept = mlp_last(
                l, gather_blocks(mlp_in), mlp_weights, ahead, sec, (attended, after)
            )
            cache.append([saved] + kept)
            break
        partial, mlp_saved, kept = mlp_forward(l, gather_blocks(mlp_in), mlp_weights, sec, (attended, after), False)
        cache.append([saved, mlp_saved] + kept)
        if l == 0:
            where_late, partial[0] = lax.optimization_barrier((where, partial[0]))
            ahead = last_ahead(where_late, cotangent, down_weight[0], wd_got, mods[1], picks)
            parts, ahead = send_parts(partial, ahead)
            attention_in, projected, state = after_mlp(parts, after, mods[0], picks_own, mods[1])
            carried = (projected, state)
            attention_blocks = gather_blocks(attention_in)

    item_sums = [None, None]
    gain_sums = [None, None]
    shares = [None, None]

    def data_sum(value):
        return lax.psum_scatter(value, ("dp", "section"), scatter_dimension=0, tiled=True)

    for l in (1, 0):
        if l == 1:
            saved, attended, after = cache[1]
            mlp_share = data_sum(mlp_grads)
            partial = mlp_input_grad(l, sec, *grads, mlp_weights)
            where_late, partial[0] = lax.optimization_barrier((where, partial[0]))
            last_partial, last_sums = last_projection(l, where_late, hidden, mlp_weights, cotangent, picks)
            parts, last_sums = send_parts(partial, last_sums, True)
            grad_out = cotangent
            projected = None
        else:
            saved, (hidden, c1, c2, mlp_in), attended, after = cache[0][:4]
            partial, grads, kept = mlp_backward(
                l, where, grad_blocks, mlp_weights, (c1, c2), [grad_out]
            )
            projected = cache[0][4]
            grad_out = kept[1]
            mlp_grads = mlp_weight_grads(mlp_in, grads, hidden)
            parts, (mlp_grads, earlier) = send_parts([kept[0]] + partial, (mlp_grads, shares[1][1]), True)
            shares[1] = (shares[1][0], earlier)
            mlp_share = data_sum(mlp_grads)
        mixed, attention_in = saved[5:]
        grad_attended, grad_after, sums2 = back_of_mlp(
            where, parts, grad_out, after, attended, projected, mods[l], picks_own
        )
        blocks = gather_blocks(grad_attended)
        partial, kept = attention_backward(l, blocks, (wq, wo), saved, tables, grad_after)
        grads, grad_attended, own, gain_sums[l], grad_after = kept
        attention_grads = attention_weight_grads(attention_in, grads, mixed, grad_attended, place.T)
        if l == 1:
            parts, (attention_grads, mlp_share) = send_parts([own] + partial, (attention_grads, mlp_share), True)
            attention_share = data_sum(attention_grads)
            sums1, grad_projected, grad_out = back_of_attention(
                where, parts, grad_after, state_kept, mods[1], picks_own, mods[0]
            )
            grad_blocks = gather_blocks(grad_projected)
            shares[1] = (mlp_share, attention_share)
        else:
            parts, attention_grads = send_parts([own] + partial, attention_grads, True)
            sums1, grad_state = back_of_attention(where, parts, grad_after, inputs, mods[0], picks_own, None)
        item_sums[l] = jnp.concatenate([sums1, sums2], axis=0)

    item_sums[1] = jnp.concatenate([item_sums[1], last_sums], axis=0)
    sums = jnp.stack(item_sums)[:, :, :items].transpose(0, 2, 1, 3).reshape(2 * items, 6 * width)
    gain_parts = jnp.concatenate([jnp.concatenate([g[0:1], g[1:2]], axis=1) for g in gain_sums])
    gain_parts = jnp.pad(gain_parts, ((0, 2 * items - 2), (0, 0)))
    pieces = [
        jnp.concatenate([lax.dynamic_slice_in_dim(sums, (tensor ^ k) * columns, columns, 1), gain_parts], axis=1)
        for k in range(group)
    ]
    got = send_parts(pieces)
    total = (got[0] + got[1]) + (got[2] + got[3])
    total, attention_grads, mlp_share = lax.optimization_barrier((total, attention_grads, mlp_share))
    shares[0] = (mlp_share, data_sum(attention_grads))
    last_partial[1:], total = lax.optimization_barrier((last_partial[1:], total))
    output = last_output(send_parts(last_partial), cache[1][2], mods[1], picks_own)
    layers = total[:, :columns].reshape(2, items, columns).astype(BF).astype(F32)
    gain_rows = jnp.pad(total[:2, None, columns:], ((0, 0), (0, items - 1), (0, 0)))
    layers = jnp.concatenate([layers, gain_rows], axis=2)
    mine = jnp.where(is_first, layers[0], layers[1])
    theirs = exchange(jnp.where(is_first, layers[1], layers[0]), "section", 1)
    gain_total = mine[0:1, columns:] + theirs[0:1, columns:]
    mods_grad = jnp.concatenate(
        [jnp.where(is_first, mine, theirs)[:, :columns], jnp.where(is_first, theirs, mine)[:, :columns]]
    )
    packed = jnp.concatenate(
        [mods_grad, scaled.astype(F32), jnp.pad(gain_total, ((0, 2 * items - 1), (0, 0)))], axis=1
    )
    gathered = gather_dp(packed)
    all_mods = gathered[:, :, :columns].astype(BF)
    deep = width // lax.axis_size("dp")
    scaled_share = lax.dynamic_slice_in_dim(gathered, columns + data * deep, deep, 2).astype(BF)
    grad_ada = jnp.einsum("nid,nic->dc", scaled_share, all_mods, preferred_element_type=F32)
    gain_total = jnp.sum(gathered[:, 0, columns + width :], axis=0)
    cond_value = conditioning[:, 0].astype(F32)
    sigma = jax.nn.sigmoid(cond_value)
    cond_part = jnp.einsum("ic,dc->id", mods_grad.astype(BF), modulator[0], preferred_element_type=F32)
    cond_part = cond_part.reshape(micro, items, width) * sigma * (1.0 + cond_value * (1.0 - sigma))
    grad_cond = group_sum(group_sum(cond_part, "section"), "tensor")
    half = LANE // 2
    gain_total = gain_total.reshape(2, LANE)
    grad_gains = jnp.concatenate([gain_total[:, :HALF], gain_total[:, half : half + HALF]], axis=1)
    mine = jnp.where(is_first, grad_state, output)
    theirs = exchange(jnp.where(is_first, output, grad_state), "section", 1)
    results = jnp.stack([jnp.where(is_first, mine, theirs), jnp.where(is_first, theirs, mine)])

    def joined(which):
        mine = jnp.where(is_first, shares[0][which], shares[1][which])
        theirs = exchange(jnp.where(is_first, shares[1][which], shares[0][which]), "section", 1)
        low = jnp.where(is_first, mine, theirs)
        high = jnp.where(is_first, theirs, mine)
        return jnp.concatenate([low, high], axis=0).astype(F32)

    size = down_weight.shape[1]
    mlp_grads = joined(0)
    grad_pair = jnp.stack([mlp_grads[:, :size], mlp_grads[:, size : 2 * size]])
    grad_down = mlp_grads[:, 2 * size :].T
    mine = jnp.where(is_first, shares[0][1], shares[1][1])
    theirs = exchange(jnp.where(is_first, shares[1][1], shares[0][1]), "section", 1)
    grad_qkv, grad_out_w = attention_results(where, mine, theirs)
    return (
        grad_ada[None],
        grad_qkv[None],
        grad_gains[None],
        grad_out_w[None],
        grad_pair[None],
        grad_down[None],
        grad_cond[:, None],
        results[None],
    )


def solution(mesh):
    return jax.shard_map(
        shards,
        mesh=mesh,
        in_specs=(
            P(None, "dp", None),
            P(None, "dp", None),
            P(None, "dp", None, None),
            P(None, "dp", None),
            P(None, None, "dp"),
            P("section", None, "tensor"),
            P("section", None, None, "tensor"),
            P("section", None, None),
            P("section", "tensor", None),
            P("section", None, None, "tensor"),
            P("section", "tensor", None),
        ),
        out_specs=(
            P("section", "dp", "tensor"),
            P("section", None, "dp", "tensor"),
            P("section", None, None),
            P("section", "tensor", "dp"),
            P("section", None, "dp", "tensor"),
            P("section", "tensor", "dp"),
            P(None, "dp", None, None),
            P("section", None, ("dp", "tensor"), None),
        ),
        check_vma=False,
    )
```
